128 devices in a mesh: bx: 8 (over y, core), by: 16 (over x, z).
Axes of the slice: x: 4, y: 4, z: 4, core: 2. Of those that a mesh axis runs over, the one named last changes fastest.
Arguments:
- src_pos: int32 [2, 128, 16384], P(None, ('bx', 'by')), may hold values from 0 to 4095, as said below
- src_amp: float32 [2, 128, 16384], P(None, ('bx', 'by')), may hold values from -18 to 18
- box_slots: int32 [128, 256, 64], P(('bx', 'by')), may hold values from -1 to 16383, as said below
Outputs:
- weights: float32 [16, 8, 16, 16, 2, 256], P(None, 'bx', None, 'by')
The draws below stay inside these ranges and needn't reach their ends.
Inputs may be any that keep to these rules, and one draw needn't show every extreme that they name: `box_slots`: each row lists the received slots of the sources in that leaf box of that owner: 1 to 64 distinct slots first, then -1; in every owner some box lists exactly 64; no slot is listed twice for one owner. `src_pos`: A send slot to owner g holds a source inside g's block of leaf boxes, and inside leaf box b of g where g lists that slot for b.
All inputs are finite; a program needn't handle non-finite values.
Results may differ from the reference program's by a relative error of at most 0.0038.
Values sent between devices are 32-bit elements; how exact they have to be, the bound alone decides.
No kernel may reach another device: no remote copies, remote signals or barrier semaphores. Data moves between devices by JAX's collectives and lax.ppermute only.
A program may use at most 128 MiB of HBM per device.

```python
import math
import jax
import jax.numpy as jnp
import numpy as np
from jax import lax

LEAF_BOXES = 16
CHEB_POINTS = 16
BOX_NODES = 256
GRID_CELLS = 4096
PHASE_BAND = 1024
BOX_SOURCES = 64
PEER_SLOTS = 128
N_BX = 8
N_BY = 16


def reversed_lookup_drawn(length):
    bit_count = length.bit_length() - 1
    lookup = np.zeros(length, dtype=np.int32)
    for number in range(length):
        result = 0
        for position in range(bit_count):
            result = result | (number >> position & 1) << bit_count - 1 - position
        lookup[number] = result
    return lookup


def owner_layout(key):
    owners = N_BX * N_BY
    boxes = LEAF_BOXES * LEAF_BOXES
    slot_total = boxes * BOX_SOURCES
    cell_first = GRID_CELLS // (LEAF_BOXES * N_BX)
    cell_second = GRID_CELLS // (LEAF_BOXES * N_BY)
    lookup_first = jnp.asarray(reversed_lookup_drawn(N_BX))
    lookup_second = jnp.asarray(reversed_lookup_drawn(N_BY))

    def per_owner(owner_id):
        subkeys = jax.random.split(jax.random.fold_in(key, owner_id), 6)
        counts = jax.random.randint(subkeys[0], (boxes,), 1, BOX_SOURCES + 1)
        busiest = jax.random.randint(subkeys[1], (), 0, boxes)
        counts = counts.at[busiest].set(BOX_SOURCES)
        shuffled = jax.random.permutation(subkeys[2], slot_total).astype(jnp.int32)
        starts = jnp.cumsum(counts) - counts
        offsets = jnp.arange(BOX_SOURCES, dtype=jnp.int32)
        position = starts[:, None] + offsets[None, :]
        is_live = offsets[None, :] < counts[:, None]
        slot_lists = jnp.where(is_live, shuffled[jnp.minimum(position, slot_total - 1)], -1)
        box_ids = jnp.broadcast_to(jnp.arange(boxes, dtype=jnp.int32)[:, None], slot_lists.shape)
        target = jnp.where(is_live, slot_lists, slot_total).reshape(-1)
        filler = jax.random.randint(subkeys[3], (slot_total,), 0, boxes)
        slot_box = filler.at[target].set(box_ids.reshape(-1), mode='drop')
        column = owner_id // N_BY
        owner_row = owner_id % N_BY
        first_coord = (lookup_first[column] * LEAF_BOXES + slot_box // LEAF_BOXES) * cell_first + jax.random.randint(subkeys[4], (slot_total,), 0, cell_first)
        second_coord = (lookup_second[owner_row] * LEAF_BOXES + slot_box % LEAF_BOXES) * cell_second + jax.random.randint(subkeys[5], (slot_total,), 0, cell_second)
        return (slot_lists.astype(jnp.int32), jnp.stack([first_coord, second_coord]).astype(jnp.int32))
    slot_lists, coords = jax.vmap(per_owner)(jnp.arange(owners, dtype=jnp.int32))
    coords = coords.reshape(owners, 2, owners, slot_total // owners).transpose(1, 2, 0, 3).reshape(2, owners, slot_total)
    return (slot_lists, coords)


def draw_src_pos(key, part):
    layout = owner_layout(key)
    return layout[1]


def draw_box_slots(key, part):
    layout = owner_layout(key)
    return layout[0]


def block_scale(stream_key, dims, cuts, least, top_value):
    loudness = 1.0
    for dim, parts in cuts:
        steps = jax.random.uniform(jax.random.fold_in(jax.random.fold_in(stream_key, 6), dim), (parts,), jnp.float32, least / len(cuts), top_value / len(cuts))
        loudness = loudness * jnp.repeat(jnp.exp(steps), dims[dim] // parts).reshape((-1,) + (1,) * (len(dims) - 1 - dim))
    return loudness


def bell_draw(key, dims, deviation, reach, cuts=(), kind=jnp.bfloat16):
    drawn = deviation * jax.random.normal(key, dims, jnp.float32)
    if cuts:
        drawn = drawn * block_scale(key, dims, cuts, -0.22, 0.18)
    return jnp.clip(drawn, -reach, reach).astype(kind)


def setup_inputs(seed: int = 0) -> dict:
    arg_keys = jax.random.split(jax.random.key(seed), 4)
    src_pos = draw_src_pos(jax.random.fold_in(arg_keys[3], 71), 0)
    src_amp = bell_draw(arg_keys[1], (2, N_BX * N_BY, N_BX * N_BY * PEER_SLOTS), 3.0, 18.0, ((1, 128),), jnp.float32)
    box_slots = draw_box_slots(jax.random.fold_in(arg_keys[3], 71), 0)
    return {"src_pos": src_pos, "src_amp": src_amp, "box_slots": box_slots}


TWO_PI = 2.0 * math.pi

def chebyshev_points(point_count):
    indices = np.arange(point_count)
    return (1.0 - np.cos(np.pi * (2 * indices + 1) / (2 * point_count))) / 2.0

def barycentric(point_count):
    points = chebyshev_points(point_count)
    result = np.ones(point_count)
    for basis_index in range(point_count):
        for other_index in range(point_count):
            if other_index != basis_index:
                result[basis_index] = result[basis_index] / (points[basis_index] - points[other_index])
    return result

def child_matrix(point_count, halves, child_index):
    if halves == 1:
        return np.eye(point_count)
    points = chebyshev_points(point_count)
    factors = barycentric(point_count)
    inside = (child_index + points) / 2.0
    matrix = np.ones((point_count, point_count))
    for basis_index in range(point_count):
        for other_index in range(point_count):
            if other_index != basis_index:
                matrix[:, basis_index] = matrix[:, basis_index] * (inside - points[other_index])
        matrix[:, basis_index] = matrix[:, basis_index] * factors[basis_index]
    return matrix

def stacked_matrix(point_count, halves_first, halves_second):
    pieces = [np.kron(child_matrix(point_count, halves_first, a), child_matrix(point_count, halves_second, b)) for a in range(halves_first) for b in range(halves_second)]
    return np.concatenate(pieces, axis=0).astype(np.float32)

def reversed_lookup(length):
    bit_count = length.bit_length() - 1
    lookup = np.zeros(length, dtype=np.int32)
    for number in range(length):
        result = 0
        for position in range(bit_count):
            result = result | (number >> position & 1) << bit_count - 1 - position
        lookup[number] = result
    return lookup

def lagrange_values(location):
    points = chebyshev_points(CHEB_POINTS).astype(np.float32)
    factors = barycentric(CHEB_POINTS).astype(np.float32)
    columns = []
    for basis_index in range(CHEB_POINTS):
        product = jnp.full(location.shape, factors[basis_index], jnp.float32)
        for other_index in range(CHEB_POINTS):
            if other_index != basis_index:
                product = product * (location - points[other_index])
        columns.append(product)
    return jnp.stack(columns, axis=-1)

def phase_angle(first_target, second_target, first_source, second_source):
    velocity = (2.0 + jnp.sin(TWO_PI * first_target) * jnp.sin(TWO_PI * second_target)) * 0.125
    radius = jnp.sqrt(first_source * first_source + second_source * second_source)
    return TWO_PI * PHASE_BAND * (first_target * first_source + second_target * second_source + velocity * radius)

def advance(stacked, center_first, center_second, low_first, low_second, width_first, width_second):
    pair_count = stacked.shape[0]
    halves_first = stacked.shape[1]
    halves_second = stacked.shape[2]
    children = center_first.shape[1]
    points = jnp.asarray(chebyshev_points(CHEB_POINTS).astype(np.float32))
    offset_first = (jnp.arange(halves_first, dtype=jnp.float32)[:, None] + points[None, :]) * (width_first / halves_first)
    offset_second = (jnp.arange(halves_second, dtype=jnp.float32)[:, None] + points[None, :]) * (width_second / halves_second)
    node_first = low_first[:, None, None] + offset_first[None]
    node_second = low_second[:, None, None] + offset_second[None]
    angles = phase_angle(center_first[:, :, None, None, None, None], center_second[:, :, None, None, None, None], node_first[:, None, :, None, :, None], node_second[:, None, None, :, None, :])
    angles = angles.reshape(pair_count, children, halves_first, halves_second, BOX_NODES)
    cosine = jnp.cos(angles)
    sine_values = jnp.sin(angles)
    real_part = stacked[:, None, :, :, 0]
    imaginary = stacked[:, None, :, :, 1]
    turned = jnp.stack([real_part * cosine - imaginary * sine_values, real_part * sine_values + imaginary * cosine], axis=2)
    turned = turned.reshape(pair_count * children * 2, halves_first * halves_second * BOX_NODES)
    summed = jnp.dot(turned, jnp.asarray(stacked_matrix(CHEB_POINTS, halves_first, halves_second)), precision=lax.Precision.HIGHEST, preferred_element_type=jnp.float32)
    summed = summed.reshape(pair_count, children, 2, BOX_NODES)
    parent_first = low_first[:, None] + points[None, :] * width_first
    parent_second = low_second[:, None] + points[None, :] * width_second
    reverted = phase_angle(center_first[:, :, None, None], center_second[:, :, None, None], parent_first[:, None, :, None], parent_second[:, None, None, :]).reshape(pair_count, children, BOX_NODES)
    cosine_back = jnp.cos(reverted)
    sine_back = jnp.sin(reverted)
    real_sum = summed[:, :, 0]
    imaginary_sum = summed[:, :, 1]
    return jnp.stack([real_sum * cosine_back + imaginary_sum * sine_back, imaginary_sum * cosine_back - real_sum * sine_back], axis=2)

def advance_blocks(stacked, center_first, center_second, low_first, low_second, width_first, width_second, block_rows):
    pair_count = stacked.shape[0]
    if pair_count <= block_rows:
        return advance(stacked, center_first, center_second, low_first, low_second, width_first, width_second)
    block_count = pair_count // block_rows

    def one_block(items):
        return advance(items[0], items[1], items[2], items[3], items[4], width_first, width_second)
    outcome = lax.map(one_block, (stacked.reshape((block_count, block_rows) + stacked.shape[1:]), center_first.reshape(block_count, block_rows, -1), center_second.reshape(block_count, block_rows, -1), low_first.reshape(block_count, block_rows), low_second.reshape(block_count, block_rows)))
    return outcome.reshape((pair_count,) + outcome.shape[2:])

def level_step(weights, anchor_first, anchor_second, span_first, span_second, block_rows):
    target_rows, target_cols, source_rows, source_cols = weights.shape[:4]
    halves_first = 2 if source_rows > 1 else 1
    halves_second = 2 if source_cols > 1 else 1
    parent_rows = source_rows // halves_first
    parent_cols = source_cols // halves_second
    pair_count = target_rows * target_cols * parent_rows * parent_cols
    children = halves_first * halves_second
    stacked = weights.reshape(target_rows, target_cols, parent_rows, halves_first, parent_cols, halves_second, 2, BOX_NODES)
    stacked = stacked.transpose(0, 1, 2, 4, 3, 5, 6, 7).reshape(pair_count, halves_first, halves_second, 2, BOX_NODES)
    flat_index = jnp.arange(pair_count, dtype=jnp.int32)
    parent_second = flat_index % parent_cols
    remainder = flat_index // parent_cols
    parent_first = remainder % parent_rows
    remainder = remainder // parent_rows
    target_second = remainder % target_cols
    target_first = remainder // target_cols
    child_first = jnp.arange(halves_first, dtype=jnp.int32)
    child_second = jnp.arange(halves_second, dtype=jnp.int32)
    index_first = target_first[:, None, None] * halves_first + child_first[None, :, None] + 0 * child_second[None, None, :]
    index_second = target_second[:, None, None] * halves_second + child_second[None, None, :] + 0 * child_first[None, :, None]
    center_first = ((index_first.astype(jnp.float32) + 0.5) / (target_rows * halves_first)).reshape(pair_count, children)
    center_second = ((index_second.astype(jnp.float32) + 0.5) / (target_cols * halves_second)).reshape(pair_count, children)
    width_first = span_first / parent_rows
    width_second = span_second / parent_cols
    low_first = anchor_first + parent_first.astype(jnp.float32) * width_first
    low_second = anchor_second + parent_second.astype(jnp.float32) * width_second
    outcome = advance_blocks(stacked, center_first, center_second, low_first, low_second, width_first, width_second, block_rows)
    outcome = outcome.reshape(target_rows, target_cols, parent_rows, parent_cols, halves_first, halves_second, 2, BOX_NODES)
    outcome = outcome.transpose(0, 4, 1, 5, 2, 3, 6, 7)
    return outcome.reshape(target_rows * halves_first, target_cols * halves_second, parent_rows, parent_cols, 2, BOX_NODES)

def deposit(arrived, slot_lists, block_first, block_second, column_count, row_count):
    box_total = slot_lists.shape[0]
    valid = (slot_lists >= 0).astype(jnp.float32)
    picked = jnp.take(arrived, jnp.maximum(slot_lists, 0), axis=1)
    cell_first = GRID_CELLS // (LEAF_BOXES * column_count)
    cell_second = GRID_CELLS // (LEAF_BOXES * row_count)
    box_id = jnp.arange(box_total, dtype=jnp.int32)
    low_first = ((block_first * LEAF_BOXES + box_id // LEAF_BOXES) * cell_first).astype(jnp.float32)
    low_second = ((block_second * LEAF_BOXES + box_id % LEAF_BOXES) * cell_second).astype(jnp.float32)
    basis_first = lagrange_values((picked[0] - low_first[:, None]) / cell_first)
    basis_second = lagrange_values((picked[1] - low_second[:, None]) / cell_second)
    angles = phase_angle(0.5, 0.5, picked[0] / GRID_CELLS, picked[1] / GRID_CELLS)
    cosine = jnp.cos(angles)
    sine_values = jnp.sin(angles)
    source_real = valid * (picked[2] * cosine - picked[3] * sine_values)
    source_imaginary = valid * (picked[2] * sine_values + picked[3] * cosine)
    weighted = jnp.stack([source_real, source_imaginary], axis=2)[:, :, :, None] * basis_second[:, :, None, :]
    summed = jnp.einsum('bsp,bsrq->brpq', basis_first, weighted, precision=lax.Precision.HIGHEST).reshape(box_total, 2, BOX_NODES)
    points = jnp.asarray(chebyshev_points(CHEB_POINTS).astype(np.float32))
    node_first = (low_first[:, None] + points[None, :] * cell_first) / GRID_CELLS
    node_second = (low_second[:, None] + points[None, :] * cell_second) / GRID_CELLS
    reverted = phase_angle(0.5, 0.5, node_first[:, :, None], node_second[:, None, :]).reshape(box_total, BOX_NODES)
    cosine_back = jnp.cos(reverted)
    sine_back = jnp.sin(reverted)
    real_sum = summed[:, 0]
    imaginary_sum = summed[:, 1]
    return jnp.stack([real_sum * cosine_back + imaginary_sum * sine_back, imaginary_sum * cosine_back - real_sum * sine_back], axis=1)

def reference(src_pos, src_amp, box_slots):
    owners = N_BX * N_BY
    lookup_first = jnp.asarray(reversed_lookup(N_BX))
    lookup_second = jnp.asarray(reversed_lookup(N_BY))

    def one_owner(owner_id):
        column = owner_id // N_BY
        owner_row = owner_id % N_BY
        start_slot = (owner_id * PEER_SLOTS).astype(jnp.int32)
        position = lax.dynamic_slice_in_dim(src_pos, start_slot, PEER_SLOTS, axis=2)
        amplitude = lax.dynamic_slice_in_dim(src_amp, start_slot, PEER_SLOTS, axis=2)
        arrived = jnp.concatenate([position.reshape(2, -1).astype(jnp.float32) + 0.5, amplitude.reshape(2, -1)], axis=0)
        slot_lists = lax.dynamic_index_in_dim(box_slots, owner_id.astype(jnp.int32), 0, keepdims=False)
        return deposit(arrived, slot_lists, lookup_first[column], lookup_second[owner_row], N_BX, N_BY)
    leaves = lax.map(one_owner, jnp.arange(owners, dtype=jnp.int32))
    leaves = leaves.reshape(N_BX, N_BY, LEAF_BOXES, LEAF_BOXES, 2, BOX_NODES)
    leaves = leaves[reversed_lookup(N_BX)][:, reversed_lookup(N_BY)]
    weights = leaves.transpose(0, 2, 1, 3, 4, 5).reshape(1, 1, LEAF_BOXES * N_BX, LEAF_BOXES * N_BY, 2, BOX_NODES)
    for level_num in range((LEAF_BOXES * N_BY).bit_length() - 1):
        weights = level_step(weights, 0.0, 0.0, 1.0, 1.0, 1024)
    return weights.reshape(LEAF_BOXES, N_BX, LEAF_BOXES, N_BY, 2, BOX_NODES)
```

```python
import functools
import math

import jax
import jax.numpy as jnp
import numpy as np
from jax import lax
from jax.experimental import pallas as pl
from jax.experimental.pallas import tpu as pltpu
from jax.sharding import PartitionSpec as P

NODES = 16
BOX_NODES = 256
DEVICES = 128
LEAVES = 16
BX = 8
BY = 16
BAND = 1024
F32 = jnp.float32
BF16 = jnp.bfloat16
ROUNDER = 12582912.0
SIN = (6.28305581, -41.33121471, 81.36682035, -74.47802935, 32.78144238)
COS = (0.99995995, -19.73105034, 64.67355678, -82.40422428, 45.64775943)


def chebyshev_points(point_count):
    indices = np.arange(point_count)
    return (1.0 - np.cos(np.pi * (2 * indices + 1) / (2 * point_count))) / 2.0


def lagrange_matrix(locations):
    points = chebyshev_points(NODES)
    matrix = np.ones((len(locations), NODES))
    for own in range(NODES):
        for other in range(NODES):
            if other != own:
                matrix[:, own] *= (locations - points[other]) / (points[own] - points[other])
    return matrix


def child_matrix(halves, child):
    if halves == 1:
        return np.eye(NODES)
    return lagrange_matrix((child + chebyshev_points(NODES)) / 2.0)


def stacked_matrix(halves_first, halves_second):
    pieces = [
        np.kron(child_matrix(halves_first, a), child_matrix(halves_second, b))
        for a in range(halves_first)
        for b in range(halves_second)
    ]
    return np.concatenate(pieces, axis=0)


def two_parts(matrix):
    exact = np.asarray(matrix, np.float32)
    high = exact.astype(jnp.bfloat16)
    low = (exact - high.astype(np.float32)).astype(jnp.bfloat16)
    return high, low


def velocity(first, second):
    return (2.0 + np.sin(2 * np.pi * first) * np.sin(2 * np.pi * second)) / 8.0


def bits(value, count):
    return [(value >> (count - 1 - k)) & 1 for k in range(count)]


def speed_change(first, second, level, split_first=True):
    count_second = 2.0**level
    count_first = 2.0 ** (level if split_first else level - 1)
    new = velocity((first + 0.5) / count_first, (second + 0.5) / count_second)
    above_first = first >> 1 if split_first else first
    old = velocity(
        (above_first + 0.5) / 2.0 ** (level - 1), ((second >> 1) + 0.5) / 2.0 ** (level - 1)
    )
    return new - old


def inner_speeds():
    table = np.zeros((4, 4, 8, 8))
    for child in range(4):
        x, y = bits(child, 2)
        for row in range(8):
            r0, r1, r2 = bits(row, 3)
            for sub in range(8):
                s0, s1, s2 = bits(sub, 3)
                table[0, child, row, sub] = speed_change(x, y, 1)
                table[1, child, row, sub] = speed_change(2 * r0 + x, 2 * r1 + y, 2)
                first, second = 2 * s0 + r2, 2 * s1 + s2
                table[2, child, row, sub] = speed_change(2 * first + x, 2 * second + y, 3)
                first, second = 2 * first + r0, 2 * second + r1
                table[3, child, row, sub] = speed_change(2 * first + x, 2 * second + y, 4)
    return table.reshape(1024).astype(np.float32)


def outer_speeds():
    tables = np.zeros((DEVICES, 7, 256))
    for device in range(DEVICES):
        coarse_first = device >> 3
        for child in range(4):
            x, y = bits(child, 2)
            for row in range(8):
                r0, r1, r2 = bits(row, 3)
                for sub in range(8):
                    s0, s1, s2 = bits(sub, 3)
                    place = child * 64 + row * 8 + sub
                    second = 2 * (device & 7) + s2
                    tables[device, 0, place] = speed_change(
                        2 * coarse_first + x, 2 * second + y, 5
                    )
                    tables[device, 1, place] = speed_change(
                        4 * coarse_first + 2 * r0 + x, 4 * second + 2 * r1 + y, 6
                    )
                    second = 2 * (device & 7) + r2
                    tables[device, 2, place] = speed_change(
                        8 * coarse_first + 4 * s0 + 2 * r0 + x,
                        8 * second + 4 * s1 + 2 * s2 + y,
                        7,
                    )
        for child in range(2):
            for row in range(16):
                r0, r1, r2, r3 = bits(row, 4)
                for sub in range(8):
                    s0, s1, s2 = bits(sub, 3)
                    place = child * 128 + row * 8 + sub
                    first = 8 * coarse_first + 4 * s0 + 2 * r2 + r0
                    second = 2 * (device & 7) + r3
                    second = 16 * second + 8 * s1 + 4 * s2 + 2 * r1 + child
                    tables[device, 3, place] = speed_change(first, second, 8, False)
                    tables[device, 4, place] = velocity((first + 0.5) / 128, (second + 0.5) / 256)
                    tables[device, 5, place] = 8 * (first + 0.5)
                    tables[device, 6, place] = 4 * (second + 0.5)
    return tables.reshape(DEVICES, 7 * 256).astype(np.float32)


def node_tables():
    points = chebyshev_points(NODES).astype(np.float32).astype(np.float64)
    first = np.repeat(points, NODES)
    second = np.tile(points, NODES)
    rows = np.zeros((16, BOX_NODES))
    for child in range(4):
        x, y = bits(child, 2)
        turns = (2 * x - 1) * 2 * first + (2 * y - 1) * second
        rows[child] = turns - np.round(turns)
    for child in range(2):
        rows[4 + child] = (2 * child - 1) * second
    rows[6] = 2 * first
    rows[7] = second
    rows[8] = np.round(first * 8192) / 8192
    rows[9] = first - rows[8]
    rows[10] = np.round(second * 8192) / 8192
    rows[11] = second - rows[10]
    rows[12] = BAND * np.sqrt(first * first + second * second)
    return rows.astype(np.float32)


def basis_factors():
    points = chebyshev_points(NODES)
    return [
        float(np.float32(1.0 / np.prod([points[own] - points[k] for k in range(NODES) if k != own])))
        for own in range(NODES)
    ]


def second_basis():
    small = lagrange_matrix((np.arange(16) + 0.5) / 16.0)
    whole = np.zeros((16, 32, 32, 16))
    for k in range(32):
        whole[:, k, k, :] = small
    return whole.reshape(512, 512)


def turn(turns):
    part = turns - ((turns + ROUNDER) - ROUNDER)
    square = part * part
    sine = SIN[4]
    cosine = COS[4]
    for k in (3, 2, 1, 0):
        sine = sine * square + SIN[k]
        cosine = cosine * square + COS[k]
    return cosine, sine * part


def split(value):
    high = value.astype(BF16)
    return high, (value - high.astype(F32)).astype(BF16)


def bit(value, place):
    return (value >> place) & 1


def make_turns(table, first_line, box, level_number, speeds, speed_row, node, base_row, children, rows):
    scale = 4.0 * 2.0 ** (level_number - 1)
    pairs = rows // 2

    def step(index, carry):
        source = index // pairs
        pair = lax.rem(index, pairs)
        radius = []
        for k in range(2):
            first, second = box(source, 2 * pair + k)
            along = first + node[6:7, :]
            across = second + node[7:8, :]
            radius.append(scale * jnp.sqrt(along * along + across * across))
        radius = jnp.concatenate([jnp.broadcast_to(value, (8, BOX_NODES)) for value in radius])
        for child in range(children):
            place = pl.multiple_of(speed_row + child * rows * 8 + pair * 16, 16)
            change = speeds[pl.ds(place, 16), :]
            change = jnp.concatenate([change, change], axis=1)
            cosine, sine = turn(change * radius + node[base_row + child : base_row + child + 1, :])
            line = first_line + index * children + child
            table[line, 0] = cosine
            table[line, 1] = sine
        return carry

    lax.fori_loop(0, (4 if children == 4 else 2) * pairs, step, 0)


def level(read, table, first_line, high, low, matrix, children, rows):
    sources = 4 if children == 4 else 2
    pairs = rows // 2
    for source in range(sources):
        lanes = slice(source * BOX_NODES, (source + 1) * BOX_NODES)
        for pair in range(pairs):
            group = source * rows + 2 * pair
            real, imaginary = (
                jnp.concatenate([read(group, part), read(group + 1, part)]) for part in range(2)
            )
            for child in range(children):
                line = first_line + (source * pairs + pair) * children + child
                cosine = table[line, 0]
                sine = table[line, 1]
                for part, value in enumerate(
                    (real * cosine - imaginary * sine, real * sine + imaginary * cosine)
                ):
                    place = (child * 2 + part) * rows * 8 + pair * 16
                    value_high, value_low = split(value)
                    high[place : place + 16, lanes] = value_high
                    low[place : place + 16, lanes] = value_low
        operand = jnp.concatenate([high[:, lanes], low[:, lanes], high[:, lanes]], axis=1)
        weights = matrix[source * 768 : (source + 1) * 768, :]
        part = jnp.dot(operand, weights, preferred_element_type=F32)
        total = part if source == 0 else total + part
    return total


def three_parts(matrix):
    high, low = two_parts(matrix)
    high = high.reshape(-1, BOX_NODES, BOX_NODES)
    low = low.reshape(-1, BOX_NODES, BOX_NODES)
    return np.stack([high, high, low], axis=1).reshape(-1, BOX_NODES)


def sub_bits():
    row = lax.broadcasted_iota(jnp.int32, (8, BOX_NODES), 0)
    return [bit(row, 2 - k).astype(F32) for k in range(3)]


def find_mask(slots, mask, high_hot, low_hot, total):
    iota = lax.broadcasted_iota(jnp.int32, (16, 128), 0).astype(F32)
    rows = [(iota + 16.0 * k).astype(BF16) for k in range(8)]
    one = jnp.ones((16, 128), BF16)
    zero = jnp.zeros((16, 128), BF16)
    total[...] = jnp.zeros_like(total)

    def step(index, carry):
        block = slots[pl.ds(pl.multiple_of(index * 16, 16), 16), :]
        block = jnp.concatenate([block[:8], block[8:]], axis=1)
        high = (block >> 7).astype(F32)
        low = (block & 127).astype(F32)
        for k in range(8):
            for source, hot in ((high, high_hot), (low, low_hot)):
                value = jnp.broadcast_to(source[k : k + 1], (16, 128)).astype(BF16)
                for place in range(8):
                    hot[16 * place : 16 * (place + 1), 128 * k : 128 * (k + 1)] = jnp.where(
                        value == rows[place], one, zero
                    )
        total[...] += lax.dot_general(
            high_hot[...], low_hot[...], (((1,), (1,)), ((), ())), preferred_element_type=F32
        )
        return carry

    lax.fori_loop(0, 16, step, 0)
    mask[...] = jnp.where(total[...] > 0.5, 1.0, 0.0)


def store_level(table, table_far, leave, index, size=64):
    lines = pl.ds(64 * index, size)
    return pltpu.make_async_copy(table.at[lines], table_far.at[lines], leave.at[index])


def fetch_level(table_far, table, arrive, index, size=64):
    lines = pl.ds(64 * index, size)
    return pltpu.make_async_copy(table_far.at[lines], table.at[lines], arrive.at[index])


def inner_turns_kernel(
    block,
    slots_far,
    node_far,
    speeds_far,
    mask,
    table_far,
    slots,
    node,
    speeds,
    table,
    high_hot,
    low_hot,
    total,
    arrive,
    leave,
):
    fetches = [
        pltpu.make_async_copy(far, near, arrive.at[k])
        for k, (far, near) in enumerate(
            ((slots_far, slots), (node_far, node), (speeds_far, speeds))
        )
    ]
    for fetch in fetches:
        fetch.start()
    fetches[0].wait()
    find_mask(slots, mask, high_hot, low_hot, total)
    for fetch in fetches[1:]:
        fetch.wait()
    stores = [store_level(table, table_far, leave, k) for k in range(4)]
    sub = sub_bits()
    block_first = block[0]
    block_second = block[1]

    def box(source, row):
        first = block_first * 16 + bit(source, 1) + 2 * bit(row, 2)
        second = block_second * 16 + bit(source, 0) + 2 * bit(row, 1) + 8 * bit(row, 0)
        return (
            2.0 * first.astype(F32) + (8.0 * sub[0] + 16.0 * sub[2]),
            second.astype(F32) + 4.0 * sub[1],
        )

    make_turns(table, 0, box, 1, speeds, 0, node, 0, 4, 8)
    stores[0].start()

    def box(source, row):
        first = block_first * 8 + bit(source, 1)
        second = block_second * 8 + bit(source, 0) + 4 * bit(row, 0)
        return (
            2.0 * first.astype(F32) + (4.0 * sub[0] + 8.0 * sub[2]),
            second.astype(F32) + 2.0 * sub[1],
        )

    make_turns(table, 64, box, 2, speeds, 256, node, 0, 4, 8)
    stores[1].start()

    def box(source, row):
        first = block_first * 4 + bit(source, 1) + 2 * bit(row, 2)
        second = block_second * 4 + bit(source, 0) + 2 * bit(row, 1)
        return 2.0 * first.astype(F32), second.astype(F32)

    make_turns(table, 128, box, 3, speeds, 512, node, 0, 4, 8)
    stores[2].start()

    def box(source, row):
        first = block_first * 2 + bit(source, 1)
        second = block_second * 2 + bit(source, 0)
        return 2.0 * first.astype(F32), second.astype(F32)

    make_turns(table, 192, box, 4, speeds, 768, node, 0, 4, 8)
    stores[3].start()
    for store in stores:
        store.wait()


def outer_turns_kernel(node, speeds, table_far, table, leave):
    stores = [store_level(table, table_far, leave, k, 64 if k < 3 else 48) for k in range(4)]
    sub = sub_bits()

    def box(source, row):
        first = bit(source, 1) + 2 * bit(row, 2) + 4 * bit(row, 1)
        second = bit(source, 0) + 2 * bit(row, 0)
        return 2.0 * first.astype(F32), second.astype(F32) + (4.0 * sub[0] + 8.0 * sub[1])

    make_turns(table, 0, box, 5, speeds, 0, node, 0, 4, 8)
    stores[0].start()

    def box(source, row):
        first = bit(source, 1) + 2 * bit(row, 0)
        second = bit(source, 0)
        return 2.0 * first.astype(F32), second.astype(F32) + (2.0 * sub[0] + 4.0 * sub[1])

    make_turns(table, 64, box, 6, speeds, 256, node, 0, 4, 8)
    stores[1].start()

    def box(source, row):
        first = bit(source, 1)
        second = bit(source, 0) + 2 * bit(row, 1)
        return 2.0 * first.astype(F32), second.astype(F32)

    make_turns(table, 128, box, 7, speeds, 512, node, 0, 4, 8)
    stores[2].start()

    def box(source, row):
        return jnp.float32(0.0), source.astype(F32)

    make_turns(table, 192, box, 8, speeds, 768, node, 4, 2, 16)

    def last(index, carry):
        def column(table):
            value = speeds[pl.ds(pl.multiple_of(256 * table + index * 16, 16), 16), :]
            return jnp.concatenate([value, value], axis=1)

        first = column(5)
        second = column(6)
        turns = first * node[8:9, :]
        turns = turns - ((turns + ROUNDER) - ROUNDER)
        across = second * node[10:11, :]
        across = across - ((across + ROUNDER) - ROUNDER)
        around = column(4) * node[12:13, :]
        around = around - ((around + ROUNDER) - ROUNDER)
        turns = turns + across + around + first * node[9:10, :] + second * node[11:12, :]
        cosine, sine = turn(turns)
        table[224 + index, 0] = cosine
        table[224 + index, 1] = sine
        return carry

    lax.fori_loop(0, 16, last, 0)
    stores[3].start()
    for store in stores:
        store.wait()


def deposit(
    arrived, mask, second, fetch_second, state, wide, cells, hots, spreads, grid
):
    points = [float(value) for value in chebyshev_points(NODES).astype(np.float32)]
    factors = basis_factors()

    def source_step(index, carry):
        rows = pl.ds(pl.multiple_of(index * 16, 16), 16)
        first, second, real, imaginary = (
            arrived[pl.ds(index * 64 + k, 16, stride=4), :] for k in range(4)
        )
        whole_first = first.astype(jnp.int32)
        whole_second = second.astype(jnp.int32)
        along = first + 0.5
        across = second + 0.5
        eighths = jnp.bitwise_and(whole_first + whole_second + 1, 7).astype(F32)
        cosine, sine = turn(
            0.125 * eighths + 0.0625 * jnp.sqrt(along * along + across * across)
        )
        live = mask[rows, :]
        real = real * live
        imaginary = imaginary * live
        turned = (real * cosine - imaginary * sine, real * sine + imaginary * cosine)
        place = jnp.bitwise_and(whole_first, 31).astype(F32) * 0.03125 + 0.015625
        cells[0, rows, :] = jnp.bitwise_and(whole_second, 15).astype(F32)
        x = [bit(whole_first, 5 + k) for k in range(4)]
        y = [bit(whole_second, 4 + k) for k in range(4)]
        cells[1, rows, :] = (x[0] * 8 + y[0] * 4 + x[1] * 2 + y[1]).astype(F32)
        cells[2, rows, :] = (y[3] * 8 + x[2] * 4 + y[2] * 2 + x[3]).astype(F32)
        away = [place - value for value in points]
        before = [None] * NODES
        after = [None] * NODES
        for p in range(1, NODES):
            before[p] = away[p - 1] if p == 1 else before[p - 1] * away[p - 1]
            q = NODES - 1 - p
            after[q] = away[q + 1] if p == 1 else after[q + 1] * away[q + 1]
        for p in range(NODES):
            if p == 0:
                value = after[0]
            elif p == NODES - 1:
                value = before[p]
            else:
                value = before[p] * after[p]
            value = value * factors[p]
            for part in range(2):
                wide[pl.ds(index * 512 + part * 16 + p, 16, stride=32), :] = value * turned[part]
        return carry

    lax.fori_loop(0, 8, source_step, 0)

    iota = lax.broadcasted_iota(jnp.int32, (16, 128), 0).astype(F32).astype(BF16)
    one = jnp.ones((16, 128), BF16)
    zero = jnp.zeros((16, 128), BF16)
    both = jnp.zeros((32, 128), BF16)

    def build(chunk, hot, spread):
        for k in range(8):
            sender = chunk * 8 + k
            lanes = slice(128 * k, 128 * (k + 1))

            def row(number, height):
                value = cells[number, pl.ds(sender, 1), :]
                return jnp.broadcast_to(value, (height, 128)).astype(BF16)

            value = wide[pl.ds(pl.multiple_of(sender * 32, 32), 32), :].astype(BF16)
            cell = row(0, 32)
            for c in range(16):
                spread[32 * c : 32 * (c + 1), lanes] = jnp.where(
                    cell == jnp.full((32, 128), c, BF16), value, both
                )
            inside = jnp.where(row(2, 16) == iota, one, zero)
            above = row(1, 16)
            for c in range(16):
                hot[16 * c : 16 * (c + 1), lanes] = jnp.where(
                    above == jnp.full((16, 128), c, BF16), inside, zero
                )

    def add(hot, spread):
        grid[...] += lax.dot_general(
            spread[...], hot[...], (((1,), (1,)), ((), ())), preferred_element_type=F32
        )

    grid[...] = jnp.zeros_like(grid)
    build(0, hots[0], spreads[0])

    def spread_step(index, carry):
        build(2 * index + 1, hots[1], spreads[1])
        add(hots[0], spreads[0])
        build(jnp.minimum(2 * index + 2, 15), hots[0], spreads[0])
        add(hots[1], spreads[1])
        return carry

    lax.fori_loop(0, 8, spread_step, 0)

    grid_high, grid_low = split(grid[...].T)
    fetch_second.wait()
    result = jnp.dot(
        jnp.concatenate([grid_high, grid_low, grid_high], axis=1),
        second[...],
        preferred_element_type=F32,
    )
    for group in range(32):
        for part in range(2):
            state[group, part] = result[
                8 * group : 8 * group + 8, BOX_NODES * part : BOX_NODES * (part + 1)
            ]


def pieces(result):
    for child in range(4):
        for row in range(8):
            start = child * 128 + row * 8
            yield bits(child, 2), bits(row, 3), [
                result[start + 64 * part : start + 64 * part + 8, :] for part in range(2)
            ]


def halves(value):
    return value[:, :128], value[:, 128:]


def inner_kernel(
    arrived,
    mask,
    second_far,
    table_far,
    matrix,
    out,
    second,
    table,
    arrive,
    wide,
    cells,
    hots,
    spreads,
    grid,
    state,
    turned,
    high,
    low,
):
    fetch_second = pltpu.make_async_copy(second_far, second, arrive.at[4])
    fetch_second.start()
    fetches = [fetch_level(table_far, table, arrive, k) for k in range(4)]
    for fetch in fetches:
        fetch.start()
    deposit(arrived, mask, second, fetch_second, state, wide, cells, hots, spreads, grid)

    def run(number, read):
        fetches[number - 1].wait()
        return level(read, table, 64 * (number - 1), high, low, matrix, 4, 8)

    def read(group, part):
        return state[group, part]

    for (x, y), (r0, r1, r2), values in pieces(run(1, read)):
        for part in range(2):
            state[(2 * r0 + r1) * 8 + x * 4 + y * 2 + r2, part] = values[part]

    for (x, y), (r0, r1, r2), values in pieces(run(2, read)):
        start = ((r2 * 2 + x) * 8 + r0 * 4 + r1 * 2 + y) * 8
        for part in range(2):
            for half, value in enumerate(halves(values[part])):
                turned[2 * part + half, start : start + 8, :] = value

    def across(group, part):
        b2x, b2y, b3x, b3y, t2x = bits(group, 5)
        start = (b3y * 2 + t2x) * 64 + b2x * 4 + b2y * 2 + b3x
        return jnp.concatenate(
            [turned.at[2 * part + half][pl.ds(start, 8, stride=8), :] for half in range(2)], axis=1
        )

    for (x, y), (r0, r1, r2), values in pieces(run(3, across)):
        for part in range(2):
            state[(2 * r0 + r1) * 8 + x * 4 + y * 2 + r2, part] = values[part]

    for (x, y), (r0, r1, r2), values in pieces(run(4, read)):
        device = r2 * 32 + r0 * 16 + x * 8 + r1
        for upper in range(2):
            for part in range(2):
                for half, value in enumerate(halves(values[part])):
                    start = (device + 64 * upper) * 8 + y * 4 + half * 2 + part
                    out[pl.ds(start, 4, stride=16), :] = value[4 * upper : 4 * upper + 4]


def outer_kernel(
    arrived, table_far, matrix, last_far, out, table, last, arrive, state, turned, high, low
):
    fetches = [
        fetch_level(table_far, table, arrive, k, 64 if k < 3 else 48) for k in range(4)
    ]
    fetch_last = pltpu.make_async_copy(last_far, last, arrive.at[4])
    for fetch in fetches:
        fetch.start()
    fetch_last.start()

    def first_read(group, part):
        i2, j3, i1, i0, j2 = bits(group, 5)
        source = i2 * 64 + i1 * 32 + i0 * 16 + j3 * 8 + j2 * 4
        return jnp.concatenate(
            [
                arrived[pl.ds(source * 8 + half * 2 + part, 8, stride=4), :]
                for half in range(2)
            ],
            axis=1,
        )

    def run(number, read):
        fetches[number - 5].wait()
        return level(read, table, 64 * (number - 5), high, low, matrix, 4, 8)

    def read(group, part):
        return state[group, part]

    for (x, y), (i1, i0, j2), values in pieces(run(5, first_read)):
        for part in range(2):
            state[(2 * i1 + j2) * 8 + x * 4 + y * 2 + i0, part] = values[part]

    for (x, y), (r0, r1, i0), values in pieces(run(6, read)):
        start = ((i0 * 2 + x) * 8 + r0 * 4 + r1 * 2 + y) * 8
        for part in range(2):
            for half, value in enumerate(halves(values[part])):
                turned[2 * part + half, start : start + 8, :] = value

    def across(group, part):
        i0, j1, t6x, j0, pair = bits(group, 5)
        start = (i0 * 2 + t6x) * 64 + j1 * 4 + j0 * 2 + pair
        return jnp.concatenate(
            [turned.at[2 * part + half][pl.ds(start, 8, stride=8), :] for half in range(2)], axis=1
        )

    for (x, y), (t6x, j0, pair), values in pieces(run(7, across)):
        for part in range(2):
            state[j0 * 16 + x * 8 + y * 4 + t6x * 2 + pair, part] = values[part]

    fetches[3].wait()
    fetch_last.wait()
    result = level(read, table, 192, high, low, last, 2, 16)
    for child in range(2):
        for row in range(16):
            t7x, t7y, t6x, pair = bits(row, 4)
            start = child * 256 + row * 8
            line = 224 + child * 8 + row // 2
            cosine = table[line, 0, 8 * (row % 2) : 8 * (row % 2) + 8, :]
            sine = table[line, 1, 8 * (row % 2) : 8 * (row % 2) + 8, :]
            real = result[start : start + 8, :]
            imaginary = result[start + 128 : start + 136, :]
            device = t6x * 32 + t7x * 16 + t7y * 2 + child
            for part, whole in enumerate(
                (real * cosine + imaginary * sine, imaginary * cosine - real * sine)
            ):
                for half, value in enumerate(halves(whole)):
                    for upper in range(2):
                        place = (device + 64 * upper) * 8 + pair * 4 + half * 2 + part
                        out[pl.ds(place, 4, stride=32), :] = value[4 * upper : 4 * upper + 4]


def vmem(count):
    return [pl.BlockSpec(memory_space=pltpu.VMEM)] * count


def smem(count):
    return [pl.BlockSpec(memory_space=pltpu.SMEM)] * count


def far(count):
    return [pl.BlockSpec(memory_space=pl.ANY)] * count


def inner_turns(block, slots):
    speeds = np.repeat(inner_speeds()[:, None], 128, axis=1)
    return pl.pallas_call(
        inner_turns_kernel,
        out_shape=[
            jax.ShapeDtypeStruct((128, 128), F32),
            jax.ShapeDtypeStruct((256, 2, 16, 256), F32),
        ],
        in_specs=smem(1) + far(3),
        out_specs=vmem(1) + far(1),
        scratch_shapes=[
            pltpu.VMEM((256, 64), jnp.int32),
            pltpu.VMEM((16, 256), F32),
            pltpu.VMEM((1024, 128), F32),
            pltpu.VMEM((256, 2, 16, 256), F32),
            pltpu.VMEM((128, 1024), BF16),
            pltpu.VMEM((128, 1024), BF16),
            pltpu.VMEM((128, 128), F32),
            pltpu.SemaphoreType.DMA((3,)),
            pltpu.SemaphoreType.DMA((4,)),
        ],
        name="inner_turns",
        compiler_params=pltpu.CompilerParams(vmem_limit_bytes=48 << 20),
    )(block, slots, jnp.asarray(node_tables()), jnp.asarray(speeds))


def outer_turns(speeds):
    return pl.pallas_call(
        outer_turns_kernel,
        out_shape=jax.ShapeDtypeStruct((240, 2, 16, 256), F32),
        in_specs=vmem(2),
        out_specs=far(1)[0],
        scratch_shapes=[
            pltpu.VMEM((240, 2, 16, 256), F32),
            pltpu.SemaphoreType.DMA((4,)),
        ],
        name="outer_turns",
        compiler_params=pltpu.CompilerParams(vmem_limit_bytes=48 << 20),
    )(jnp.asarray(node_tables()), speeds)


LEVEL_SCRATCH = [
    pltpu.VMEM((32, 2, 8, 256), F32),
    pltpu.VMEM((4, 256, 128), F32),
    pltpu.VMEM((512, 1024), BF16),
    pltpu.VMEM((512, 1024), BF16),
]


def inner_levels(arrived, mask, table):
    second_high, second_low = two_parts(second_basis())
    second = np.concatenate([second_high, second_high, second_low], axis=0)
    return pl.pallas_call(
        inner_kernel,
        out_shape=jax.ShapeDtypeStruct((1024, 128), F32),
        in_specs=vmem(2) + far(2) + vmem(1),
        out_specs=vmem(1)[0],
        scratch_shapes=[
            pltpu.VMEM((1536, 512), BF16),
            pltpu.VMEM((256, 2, 16, 256), F32),
            pltpu.SemaphoreType.DMA((5,)),
            pltpu.VMEM((4096, 128), F32),
            pltpu.VMEM((3, 128, 128), F32),
            [pltpu.VMEM((256, 1024), BF16)] * 2,
            [pltpu.VMEM((512, 1024), BF16)] * 2,
            pltpu.VMEM((512, 256), F32),
        ]
        + LEVEL_SCRATCH,
        name="inner",
        compiler_params=pltpu.CompilerParams(vmem_limit_bytes=48 << 20),
    )(
        arrived,
        mask,
        jnp.asarray(second),
        table,
        jnp.asarray(three_parts(stacked_matrix(2, 2))),
    )


def outer_levels(arrived, table):
    return pl.pallas_call(
        outer_kernel,
        out_shape=jax.ShapeDtypeStruct((1024, 128), F32),
        in_specs=vmem(1) + far(1) + vmem(1) + far(1),
        out_specs=vmem(1)[0],
        scratch_shapes=[
            pltpu.VMEM((240, 2, 16, 256), F32),
            pltpu.VMEM((1536, 256), BF16),
            pltpu.SemaphoreType.DMA((5,)),
        ]
        + LEVEL_SCRATCH,
        name="outer",
        compiler_params=pltpu.CompilerParams(vmem_limit_bytes=48 << 20),
    )(
        arrived,
        table,
        jnp.asarray(three_parts(stacked_matrix(2, 2))),
        jnp.asarray(three_parts(stacked_matrix(1, 2))),
    )


def reverse_bits(number, bit_count):
    result = jnp.zeros_like(number)
    for position in range(bit_count):
        result = result + jnp.left_shift(
            jnp.bitwise_and(jnp.right_shift(number, position), 1), bit_count - 1 - position
        )
    return result


def exchange(array):
    return lax.all_to_all(array, ("bx", "by"), split_axis=0, concat_axis=0, tiled=True)


def shards(src_pos, src_amp, box_slots):
    column = lax.axis_index("bx")
    row = lax.axis_index("by")
    device = column * BY + row
    block = jnp.stack([reverse_bits(column, 3), reverse_bits(row, 4)]).astype(jnp.int32)
    payload = jnp.concatenate([src_pos[:, 0, :].astype(F32), src_amp[:, 0, :]], axis=0)
    payload = payload.reshape(4, DEVICES, 128).transpose(1, 0, 2)
    arrived = exchange(payload).reshape(512, 128)
    mask, table = inner_turns(block, box_slots[0])
    arrived, mask, table = lax.optimization_barrier((arrived, mask, table))
    weights = inner_levels(arrived, mask, table)
    weights = exchange(weights.reshape(DEVICES, 8, 128)).reshape(1024, 128)
    speeds = lax.dynamic_index_in_dim(jnp.asarray(outer_speeds()), device, 0, keepdims=False)
    speeds = jnp.broadcast_to(speeds[:, None], (7 * 256, 128))
    weights = outer_levels(weights, outer_turns(speeds))
    weights = exchange(weights.reshape(DEVICES, 8, 128))
    weights = weights.reshape(LEAVES, LEAVES, 2, 2, 128).transpose(0, 1, 3, 2, 4)
    return weights.reshape(LEAVES, 1, LEAVES, 1, 2, BOX_NODES)


def solution(mesh):
    return jax.shard_map(
        shards,
        mesh=mesh,
        in_specs=(
            P(None, ("bx", "by"), None),
            P(None, ("bx", "by"), None),
            P(("bx", "by"), None, None),
        ),
        out_specs=P(None, "bx", None, "by", None, None),
        check_vma=False,
    )
```

```python
import functools
import math

import jax
import jax.numpy as jnp
import numpy as np
from jax import lax
from jax.experimental import pallas as pl
from jax.experimental.pallas import tpu as pltpu
from jax.sharding import PartitionSpec as P

NODES = 16
BOX_NODES = 256
DEVICES = 128
LEAVES = 16
BX = 8
BY = 16
BAND = 1024
F32 = jnp.float32
BF16 = jnp.bfloat16
ROUNDER = 12582912.0
SIN = (6.28305581, -41.33121471, 81.36682035, -74.47802935, 32.78144238)
COS = (0.99995995, -19.73105034, 64.67355678, -82.40422428, 45.64775943)


def chebyshev_points(point_count):
    indices = np.arange(point_count)
    return (1.0 - np.cos(np.pi * (2 * indices + 1) / (2 * point_count))) / 2.0


def lagrange_matrix(locations):
    points = chebyshev_points(NODES)
    matrix = np.ones((len(locations), NODES))
    for own in range(NODES):
        for other in range(NODES):
            if other != own:
                matrix[:, own] *= (locations - points[other]) / (points[own] - points[other])
    return matrix


def child_matrix(halves, child):
    if halves == 1:
        return np.eye(NODES)
    return lagrange_matrix((child + chebyshev_points(NODES)) / 2.0)


def stacked_matrix(halves_first, halves_second):
    pieces = [
        np.kron(child_matrix(halves_first, a), child_matrix(halves_second, b))
        for a in range(halves_first)
        for b in range(halves_second)
    ]
    return np.concatenate(pieces, axis=0)


def two_parts(matrix):
    exact = np.asarray(matrix, np.float32)
    high = exact.astype(jnp.bfloat16)
    low = (exact - high.astype(np.float32)).astype(jnp.bfloat16)
    return high, low


def velocity(first, second):
    return (2.0 + np.sin(2 * np.pi * first) * np.sin(2 * np.pi * second)) / 8.0


def bits(value, count):
    return [(value >> (count - 1 - k)) & 1 for k in range(count)]


def speed_change(first, second, level, split_first=True):
    count_second = 2.0**level
    count_first = 2.0 ** (level if split_first else level - 1)
    new = velocity((first + 0.5) / count_first, (second + 0.5) / count_second)
    above_first = first >> 1 if split_first else first
    old = velocity(
        (above_first + 0.5) / 2.0 ** (level - 1), ((second >> 1) + 0.5) / 2.0 ** (level - 1)
    )
    return new - old


def inner_speeds():
    table = np.zeros((4, 4, 8, 8))
    for child in range(4):
        x, y = bits(child, 2)
        for row in range(8):
            r0, r1, r2 = bits(row, 3)
            for sub in range(8):
                s0, s1, s2 = bits(sub, 3)
                table[0, child, row, sub] = speed_change(x, y, 1)
                table[1, child, row, sub] = speed_change(2 * r0 + x, 2 * r1 + y, 2)
                first, second = 2 * s0 + r2, 2 * s1 + s2
                table[2, child, row, sub] = speed_change(2 * first + x, 2 * second + y, 3)
                first, second = 2 * first + r0, 2 * second + r1
                table[3, child, row, sub] = speed_change(2 * first + x, 2 * second + y, 4)
    return table.reshape(1024).astype(np.float32)


def outer_speeds():
    tables = np.zeros((DEVICES, 7, 256))
    for device in range(DEVICES):
        coarse_first = device >> 3
        for child in range(4):
            x, y = bits(child, 2)
            for row in range(8):
                r0, r1, r2 = bits(row, 3)
                for sub in range(8):
                    s0, s1, s2 = bits(sub, 3)
                    place = child * 64 + row * 8 + sub
                    second = 2 * (device & 7) + s2
                    tables[device, 0, place] = speed_change(
                        2 * coarse_first + x, 2 * second + y, 5
                    )
                    tables[device, 1, place] = speed_change(
                        4 * coarse_first + 2 * r0 + x, 4 * second + 2 * r1 + y, 6
                    )
                    second = 2 * (device & 7) + r2
                    tables[device, 2, place] = speed_change(
                        8 * coarse_first + 4 * s0 + 2 * r0 + x,
                        8 * second + 4 * s1 + 2 * s2 + y,
                        7,
                    )
        for child in range(2):
            for row in range(16):
                r0, r1, r2, r3 = bits(row, 4)
                for sub in range(8):
                    s0, s1, s2 = bits(sub, 3)
                    place = child * 128 + row * 8 + sub
                    first = 8 * coarse_first + 4 * s0 + 2 * r2 + r0
                    second = 2 * (device & 7) + r3
                    second = 16 * second + 8 * s1 + 4 * s2 + 2 * r1 + child
                    tables[device, 3, place] = speed_change(first, second, 8, False)
                    tables[device, 4, place] = velocity((first + 0.5) / 128, (second + 0.5) / 256)
                    tables[device, 5, place] = 8 * (first + 0.5)
                    tables[device, 6, place] = 4 * (second + 0.5)
    return tables.reshape(DEVICES, 7 * 256).astype(np.float32)


def node_tables():
    points = chebyshev_points(NODES).astype(np.float32).astype(np.float64)
    first = np.repeat(points, NODES)
    second = np.tile(points, NODES)
    rows = np.zeros((16, BOX_NODES))
    for child in range(4):
        x, y = bits(child, 2)
        turns = (2 * x - 1) * 2 * first + (2 * y - 1) * second
        rows[child] = turns - np.round(turns)
    for child in range(2):
        rows[4 + child] = (2 * child - 1) * second
    rows[6] = 2 * first
    rows[7] = second
    rows[8] = np.round(first * 8192) / 8192
    rows[9] = first - rows[8]
    rows[10] = np.round(second * 8192) / 8192
    rows[11] = second - rows[10]
    rows[12] = BAND * np.sqrt(first * first + second * second)
    return rows.astype(np.float32)


def basis_factors():
    points = chebyshev_points(NODES)
    return [
        float(np.float32(1.0 / np.prod([points[own] - points[k] for k in range(NODES) if k != own])))
        for own in range(NODES)
    ]


def second_basis():
    small = lagrange_matrix((np.arange(16) + 0.5) / 16.0)
    whole = np.zeros((16, 32, 32, 16))
    for k in range(32):
        whole[:, k, k, :] = small
    return whole.reshape(512, 512)


def turn(turns):
    part = turns - ((turns + ROUNDER) - ROUNDER)
    square = part * part
    sine = SIN[4]
    cosine = COS[4]
    for k in (3, 2, 1, 0):
        sine = sine * square + SIN[k]
        cosine = cosine * square + COS[k]
    return cosine, sine * part


def split(value):
    high = value.astype(BF16)
    return high, (value - high.astype(F32)).astype(BF16)


def bit(value, place):
    return (value >> place) & 1


def make_turns(table, first_line, box, level_number, speeds, speed_row, node, base_row, children, rows):
    scale = 4.0 * 2.0 ** (level_number - 1)
    pairs = rows // 2

    def step(index, carry):
        source = index // pairs
        pair = lax.rem(index, pairs)
        radius = []
        for k in range(2):
            first, second = box(source, 2 * pair + k)
            along = first + node[6:7, :]
            across = second + node[7:8, :]
            radius.append(scale * jnp.sqrt(along * along + across * across))
        radius = jnp.concatenate([jnp.broadcast_to(value, (8, BOX_NODES)) for value in radius])
        for child in range(children):
            place = pl.multiple_of(speed_row + child * rows * 8 + pair * 16, 16)
            change = speeds[pl.ds(place, 16), :]
            change = jnp.concatenate([change, change], axis=1)
            cosine, sine = turn(change * radius + node[base_row + child : base_row + child + 1, :])
            line = first_line + index * children + child
            table[line, 0] = cosine
            table[line, 1] = sine
        return carry

    lax.fori_loop(0, (4 if children == 4 else 2) * pairs, step, 0)


def level(read, table, first_line, high, low, matrix, children, rows):
    sources = 4 if children == 4 else 2
    pairs = rows // 2

    def step(index, carry):
        source = index // pairs
        pair = index % pairs
        lanes = pl.ds(pl.multiple_of(source * BOX_NODES, BOX_NODES), BOX_NODES)
        group = source * rows + 2 * pair
        real, imaginary = (
            jnp.concatenate([read(group, part), read(group + 1, part)]) for part in range(2)
        )
        for child in range(children):
            line = first_line + index * children + child
            cosine = table[line, 0]
            sine = table[line, 1]
            for part, value in enumerate(
                (real * cosine - imaginary * sine, real * sine + imaginary * cosine)
            ):
                place = pl.multiple_of((child * 2 + part) * rows * 8 + pair * 16, 16)
                value_high, value_low = split(value)
                high[pl.ds(place, 16), lanes] = value_high
                low[pl.ds(place, 16), lanes] = value_low
        return carry

    lax.fori_loop(0, sources * pairs, step, 0)
    pieces = []
    for source in range(sources):
        lanes = slice(source * BOX_NODES, (source + 1) * BOX_NODES)
        pieces += [high[:, lanes], low[:, lanes], high[:, lanes]]
    return jnp.dot(jnp.concatenate(pieces, axis=1), matrix[...], preferred_element_type=F32)


def three_parts(matrix):
    high, low = two_parts(matrix)
    high = high.reshape(-1, BOX_NODES, BOX_NODES)
    low = low.reshape(-1, BOX_NODES, BOX_NODES)
    return np.stack([high, high, low], axis=1).reshape(-1, BOX_NODES)


def sub_bits():
    row = lax.broadcasted_iota(jnp.int32, (8, BOX_NODES), 0)
    return [bit(row, 2 - k).astype(F32) for k in range(3)]


def find_mask(slots, mask, columns, high_hot, low_hot, total):
    iota = lax.broadcasted_iota(jnp.int32, (16, 128), 0).astype(F32)
    rows = [(iota + 16.0 * k).astype(BF16) for k in range(8)]
    lane = lax.broadcasted_iota(jnp.int32, (128, 128), 1).astype(F32).astype(BF16)
    one = jnp.ones((16, 128), BF16)
    zero = jnp.zeros((16, 128), BF16)
    ones = jnp.ones((128, 128), BF16)
    zeros = jnp.zeros((128, 128), BF16)
    total[...] = jnp.zeros_like(total)
    block = jnp.concatenate([slots[:128, :], slots[128:, :]], axis=1)
    columns[0] = (block >> 7).astype(F32)
    columns[1] = (block & 127).astype(F32).T

    def step(index, carry):
        high = columns[0, pl.ds(pl.multiple_of(index * 8, 8), 8), :]
        low = pltpu.roll(columns[1], lax.rem(128 - index * 8, 128), 1)
        for k in range(8):
            value = jnp.broadcast_to(high[k : k + 1], (16, 128)).astype(BF16)
            for place in range(8):
                high_hot[16 * place : 16 * (place + 1), 128 * k : 128 * (k + 1)] = jnp.where(
                    value == rows[place], one, zero
                )
            value = jnp.broadcast_to(low[:, k : k + 1], (128, 128)).astype(BF16)
            low_hot[128 * k : 128 * (k + 1), :] = jnp.where(value == lane, ones, zeros)
        total[...] += jnp.dot(high_hot[...], low_hot[...], preferred_element_type=F32)
        return carry

    lax.fori_loop(0, 16, step, 0)
    mask[...] = jnp.where(total[...] > 0.5, 1.0, 0.0)


def store_level(table, table_far, leave, index, size=64):
    lines = pl.ds(64 * index, size)
    return pltpu.make_async_copy(table.at[lines], table_far.at[lines], leave.at[index])


def fetch_level(table_far, table, arrive, index, size=64):
    lines = pl.ds(64 * index, size)
    return pltpu.make_async_copy(table_far.at[lines], table.at[lines], arrive.at[index])


def inner_turns_kernel(
    block,
    slots_far,
    node_far,
    speeds_far,
    mask,
    table_far,
    slots,
    node,
    speeds,
    table,
    columns,
    high_hot,
    low_hot,
    total,
    arrive,
    leave,
):
    fetches = [
        pltpu.make_async_copy(far, near, arrive.at[k])
        for k, (far, near) in enumerate(
            ((slots_far, slots), (node_far, node), (speeds_far, speeds))
        )
    ]
    for fetch in fetches:
        fetch.start()
    fetches[0].wait()
    find_mask(slots, mask, columns, high_hot, low_hot, total)
    for fetch in fetches[1:]:
        fetch.wait()
    stores = [store_level(table, table_far, leave, k) for k in range(4)]
    sub = sub_bits()
    block_first = block[0]
    block_second = block[1]

    def box(source, row):
        first = block_first * 16 + bit(source, 1) + 2 * bit(row, 2)
        second = block_second * 16 + bit(source, 0) + 2 * bit(row, 1) + 8 * bit(row, 0)
        return (
            2.0 * first.astype(F32) + (8.0 * sub[0] + 16.0 * sub[2]),
            second.astype(F32) + 4.0 * sub[1],
        )

    make_turns(table, 0, box, 1, speeds, 0, node, 0, 4, 8)
    stores[0].start()

    def box(source, row):
        first = block_first * 8 + bit(source, 1)
        second = block_second * 8 + bit(source, 0) + 4 * bit(row, 0)
        return (
            2.0 * first.astype(F32) + (4.0 * sub[0] + 8.0 * sub[2]),
            second.astype(F32) + 2.0 * sub[1],
        )

    make_turns(table, 64, box, 2, speeds, 256, node, 0, 4, 8)
    stores[1].start()

    def box(source, row):
        first = block_first * 4 + bit(source, 1) + 2 * bit(row, 2)
        second = block_second * 4 + bit(source, 0) + 2 * bit(row, 1)
        return 2.0 * first.astype(F32), second.astype(F32)

    make_turns(table, 128, box, 3, speeds, 512, node, 0, 4, 8)
    stores[2].start()

    def box(source, row):
        first = block_first * 2 + bit(source, 1)
        second = block_second * 2 + bit(source, 0)
        return 2.0 * first.astype(F32), second.astype(F32)

    make_turns(table, 192, box, 4, speeds, 768, node, 0, 4, 8)
    stores[3].start()
    for store in stores:
        store.wait()


def outer_turns_kernel(node, speeds, table_far, table, leave):
    stores = [store_level(table, table_far, leave, k, 64 if k < 3 else 48) for k in range(4)]
    sub = sub_bits()

    def box(source, row):
        first = bit(source, 1) + 2 * bit(row, 2) + 4 * bit(row, 1)
        second = bit(source, 0) + 2 * bit(row, 0)
        return 2.0 * first.astype(F32), second.astype(F32) + (4.0 * sub[0] + 8.0 * sub[1])

    make_turns(table, 0, box, 5, speeds, 0, node, 0, 4, 8)
    stores[0].start()

    def box(source, row):
        first = bit(source, 1) + 2 * bit(row, 0)
        second = bit(source, 0)
        return 2.0 * first.astype(F32), second.astype(F32) + (2.0 * sub[0] + 4.0 * sub[1])

    make_turns(table, 64, box, 6, speeds, 256, node, 0, 4, 8)
    stores[1].start()

    def box(source, row):
        first = bit(source, 1)
        second = bit(source, 0) + 2 * bit(row, 1)
        return 2.0 * first.astype(F32), second.astype(F32)

    make_turns(table, 128, box, 7, speeds, 512, node, 0, 4, 8)
    stores[2].start()

    def box(source, row):
        return jnp.float32(0.0), source.astype(F32)

    make_turns(table, 192, box, 8, speeds, 768, node, 4, 2, 16)

    def last(index, carry):
        def column(table):
            value = speeds[pl.ds(pl.multiple_of(256 * table + index * 16, 16), 16), :]
            return jnp.concatenate([value, value], axis=1)

        first = column(5)
        second = column(6)
        turns = first * node[8:9, :]
        turns = turns - ((turns + ROUNDER) - ROUNDER)
        across = second * node[10:11, :]
        across = across - ((across + ROUNDER) - ROUNDER)
        around = column(4) * node[12:13, :]
        around = around - ((around + ROUNDER) - ROUNDER)
        turns = turns + across + around + first * node[9:10, :] + second * node[11:12, :]
        cosine, sine = turn(turns)
        table[224 + index, 0] = cosine
        table[224 + index, 1] = sine
        return carry

    lax.fori_loop(0, 16, last, 0)
    stores[3].start()
    for store in stores:
        store.wait()


def deposit(
    arrived, mask, second, fetch_second, state, wide, cells, hots, spreads, grid
):
    points = [float(value) for value in chebyshev_points(NODES).astype(np.float32)]
    factors = basis_factors()

    def source_step(index, carry):
        rows = pl.ds(pl.multiple_of(index * 16, 16), 16)
        first, second, real, imaginary = (
            arrived[pl.ds(index * 64 + k, 16, stride=4), :] for k in range(4)
        )
        whole_first = first.astype(jnp.int32)
        whole_second = second.astype(jnp.int32)
        along = first + 0.5
        across = second + 0.5
        eighths = jnp.bitwise_and(whole_first + whole_second + 1, 7).astype(F32)
        cosine, sine = turn(
            0.125 * eighths + 0.0625 * jnp.sqrt(along * along + across * across)
        )
        live = mask[rows, :]
        real = real * live
        imaginary = imaginary * live
        turned = (real * cosine - imaginary * sine, real * sine + imaginary * cosine)
        place = jnp.bitwise_and(whole_first, 31).astype(F32) * 0.03125 + 0.015625
        cells[0, rows, :] = jnp.bitwise_and(whole_second, 15).astype(F32)
        x = [bit(whole_first, 5 + k) for k in range(4)]
        y = [bit(whole_second, 4 + k) for k in range(4)]
        high = x[0] * 128 + y[0] * 64 + x[1] * 32 + y[1] * 16
        low = y[3] * 8 + x[2] * 4 + y[2] * 2 + x[3]
        cells[1, rows, :] = (high + low).astype(F32)
        away = [place - value for value in points]
        before = [None] * NODES
        after = [None] * NODES
        for p in range(1, NODES):
            before[p] = away[p - 1] if p == 1 else before[p - 1] * away[p - 1]
            q = NODES - 1 - p
            after[q] = away[q + 1] if p == 1 else after[q + 1] * away[q + 1]
        for p in range(NODES):
            if p == 0:
                value = after[0]
            elif p == NODES - 1:
                value = before[p]
            else:
                value = before[p] * after[p]
            value = value * factors[p]
            for part in range(2):
                wide[pl.ds(index * 512 + part * 16 + p, 16, stride=32), :] = value * turned[part]
        return carry

    lax.fori_loop(0, 8, source_step, 0)
    cells[1] = cells[1].T

    lanes_low = lax.broadcasted_iota(jnp.int32, (128, 128), 1).astype(F32)
    lanes_high = (lanes_low + 128.0).astype(BF16)
    lanes_low = lanes_low.astype(BF16)
    one = jnp.ones((128, 128), BF16)
    zero = jnp.zeros((128, 128), BF16)
    both = jnp.zeros((32, 128), BF16)

    def build(chunk, hot, spread):
        boxes = pltpu.roll(cells[1], lax.rem(128 - chunk * 8, 128), 1)
        for k in range(8):
            sender = chunk * 8 + k
            lanes = slice(128 * k, 128 * (k + 1))
            value = wide[pl.ds(pl.multiple_of(sender * 32, 32), 32), :].astype(BF16)
            cell = jnp.broadcast_to(cells[0, pl.ds(sender, 1), :], (32, 128)).astype(BF16)
            for c in range(16):
                spread[32 * c : 32 * (c + 1), lanes] = jnp.where(
                    cell == jnp.full((32, 128), c, BF16), value, both
                )
            box = jnp.broadcast_to(boxes[:, k : k + 1], (128, 128)).astype(BF16)
            hot[lanes, :128] = jnp.where(box == lanes_low, one, zero)
            hot[lanes, 128:] = jnp.where(box == lanes_high, one, zero)

    def add(hot, spread):
        grid[...] += jnp.dot(spread[...], hot[...], preferred_element_type=F32)

    grid[...] = jnp.zeros_like(grid)
    build(0, hots[0], spreads[0])

    def spread_step(index, carry):
        build(2 * index + 1, hots[1], spreads[1])
        add(hots[0], spreads[0])
        build(jnp.minimum(2 * index + 2, 15), hots[0], spreads[0])
        add(hots[1], spreads[1])
        return carry

    lax.fori_loop(0, 8, spread_step, 0)

    grid_high, grid_low = split(grid[...].T)
    fetch_second.wait()
    result = jnp.dot(
        jnp.concatenate([grid_high, grid_low, grid_high], axis=1),
        second[...],
        preferred_element_type=F32,
    )
    for group in range(32):
        for part in range(2):
            state[group, part] = result[
                8 * group : 8 * group + 8, BOX_NODES * part : BOX_NODES * (part + 1)
            ]


def pieces(result):
    for child in range(4):
        for row in range(8):
            start = child * 128 + row * 8
            yield bits(child, 2), bits(row, 3), [
                result[start + 64 * part : start + 64 * part + 8, :] for part in range(2)
            ]


def halves(value):
    return value[:, :128], value[:, 128:]


def inner_kernel(
    arrived,
    mask,
    second_far,
    table_far,
    matrix_far,
    out,
    second,
    matrix,
    table,
    arrive,
    wide,
    cells,
    hots,
    spreads,
    grid,
    state,
    turned,
    high,
    low,
):
    fetch_second = pltpu.make_async_copy(second_far, second, arrive.at[4])
    fetch_second.start()
    fetches = [fetch_level(table_far, table, arrive, k) for k in range(4)]
    for fetch in fetches:
        fetch.start()
    fetch_matrix = pltpu.make_async_copy(matrix_far, matrix, arrive.at[5])
    fetch_matrix.start()
    deposit(arrived, mask, second, fetch_second, state, wide, cells, hots, spreads, grid)
    fetch_matrix.wait()

    def run(number, read):
        fetches[number - 1].wait()
        return level(read, table, 64 * (number - 1), high, low, matrix, 4, 8)

    def read(group, part):
        return state[group, part]

    for (x, y), (r0, r1, r2), values in pieces(run(1, read)):
        for part in range(2):
            state[(2 * r0 + r1) * 8 + x * 4 + y * 2 + r2, part] = values[part]

    for (x, y), (r0, r1, r2), values in pieces(run(2, read)):
        start = ((r2 * 2 + x) * 8 + r0 * 4 + r1 * 2 + y) * 8
        for part in range(2):
            for half, value in enumerate(halves(values[part])):
                turned[2 * part + half, start : start + 8, :] = value

    def across(group, part):
        b2x, b2y, b3x, b3y, t2x = bits(group, 5)
        start = (b3y * 2 + t2x) * 64 + b2x * 4 + b2y * 2 + b3x
        return jnp.concatenate(
            [turned.at[2 * part + half][pl.ds(start, 8, stride=8), :] for half in range(2)], axis=1
        )

    for (x, y), (r0, r1, r2), values in pieces(run(3, across)):
        for part in range(2):
            state[(2 * r0 + r1) * 8 + x * 4 + y * 2 + r2, part] = values[part]

    for (x, y), (r0, r1, r2), values in pieces(run(4, read)):
        device = r2 * 32 + r0 * 16 + x * 8 + r1
        for upper in range(2):
            for part in range(2):
                for half, value in enumerate(halves(values[part])):
                    start = (device + 64 * upper) * 8 + y * 4 + half * 2 + part
                    out[pl.ds(start, 4, stride=16), :] = value[4 * upper : 4 * upper + 4]


def outer_kernel(
    arrived, table_far, matrix_far, last_far, out, table, matrix, last, arrive, state, turned, high, low
):
    fetches = [
        fetch_level(table_far, table, arrive, k, 64 if k < 3 else 48) for k in range(4)
    ]
    fetch_last = pltpu.make_async_copy(last_far, last, arrive.at[4])
    fetch_matrix = pltpu.make_async_copy(matrix_far, matrix, arrive.at[5])
    fetches[0].start()
    fetch_matrix.start()
    for fetch in fetches[1:]:
        fetch.start()
    fetch_last.start()
    fetch_matrix.wait()

    def first_read(group, part):
        i2, j3, i1, i0, j2 = bits(group, 5)
        source = i2 * 64 + i1 * 32 + i0 * 16 + j3 * 8 + j2 * 4
        return jnp.concatenate(
            [
                arrived[pl.ds(source * 8 + half * 2 + part, 8, stride=4), :]
                for half in range(2)
            ],
            axis=1,
        )

    def run(number, read):
        fetches[number - 5].wait()
        return level(read, table, 64 * (number - 5), high, low, matrix, 4, 8)

    def read(group, part):
        return state[group, part]

    for (x, y), (i1, i0, j2), values in pieces(run(5, first_read)):
        for part in range(2):
            state[(2 * i1 + j2) * 8 + x * 4 + y * 2 + i0, part] = values[part]

    for (x, y), (r0, r1, i0), values in pieces(run(6, read)):
        start = ((i0 * 2 + x) * 8 + r0 * 4 + r1 * 2 + y) * 8
        for part in range(2):
            for half, value in enumerate(halves(values[part])):
                turned[2 * part + half, start : start + 8, :] = value

    def across(group, part):
        i0, j1, t6x, j0, pair = bits(group, 5)
        start = (i0 * 2 + t6x) * 64 + j1 * 4 + j0 * 2 + pair
        return jnp.concatenate(
            [turned.at[2 * part + half][pl.ds(start, 8, stride=8), :] for half in range(2)], axis=1
        )

    for (x, y), (t6x, j0, pair), values in pieces(run(7, across)):
        for part in range(2):
            state[j0 * 16 + x * 8 + y * 4 + t6x * 2 + pair, part] = values[part]

    fetches[3].wait()
    fetch_last.wait()
    result = level(read, table, 192, high, low, last, 2, 16)
    for child in range(2):
        for row in range(16):
            t7x, t7y, t6x, pair = bits(row, 4)
            start = child * 256 + row * 8
            line = 224 + child * 8 + row // 2
            cosine = table[line, 0, 8 * (row % 2) : 8 * (row % 2) + 8, :]
            sine = table[line, 1, 8 * (row % 2) : 8 * (row % 2) + 8, :]
            real = result[start : start + 8, :]
            imaginary = result[start + 128 : start + 136, :]
            device = t6x * 32 + t7x * 16 + t7y * 2 + child
            for part, whole in enumerate(
                (real * cosine + imaginary * sine, imaginary * cosine - real * sine)
            ):
                for half, value in enumerate(halves(whole)):
                    for upper in range(2):
                        place = (device + 64 * upper) * 8 + pair * 4 + half * 2 + part
                        out[pl.ds(place, 4, stride=32), :] = value[4 * upper : 4 * upper + 4]


def vmem(count):
    return [pl.BlockSpec(memory_space=pltpu.VMEM)] * count


def smem(count):
    return [pl.BlockSpec(memory_space=pltpu.SMEM)] * count


def far(count):
    return [pl.BlockSpec(memory_space=pltpu.HBM)] * count


def inner_turns(block, slots):
    speeds = np.repeat(inner_speeds()[:, None], 128, axis=1)
    return pl.pallas_call(
        inner_turns_kernel,
        out_shape=[
            jax.ShapeDtypeStruct((128, 128), F32),
            jax.ShapeDtypeStruct((256, 2, 16, 256), F32),
        ],
        in_specs=smem(1) + far(3),
        out_specs=vmem(1) + far(1),
        scratch_shapes=[
            pltpu.VMEM((256, 64), jnp.int32),
            pltpu.VMEM((16, 256), F32),
            pltpu.VMEM((1024, 128), F32),
            pltpu.VMEM((256, 2, 16, 256), F32),
            pltpu.VMEM((2, 128, 128), F32),
            pltpu.VMEM((128, 1024), BF16),
            pltpu.VMEM((1024, 128), BF16),
            pltpu.VMEM((128, 128), F32),
            pltpu.SemaphoreType.DMA((3,)),
            pltpu.SemaphoreType.DMA((4,)),
        ],
        name="inner_turns",
        compiler_params=pltpu.CompilerParams(vmem_limit_bytes=48 << 20),
    )(block, slots, jnp.asarray(node_tables()), jnp.asarray(speeds))


def outer_turns(speeds):
    return pl.pallas_call(
        outer_turns_kernel,
        out_shape=jax.ShapeDtypeStruct((240, 2, 16, 256), F32),
        in_specs=vmem(2),
        out_specs=far(1)[0],
        scratch_shapes=[
            pltpu.VMEM((240, 2, 16, 256), F32),
            pltpu.SemaphoreType.DMA((4,)),
        ],
        name="outer_turns",
        compiler_params=pltpu.CompilerParams(vmem_limit_bytes=48 << 20),
    )(jnp.asarray(node_tables()), speeds)


LEVEL_SCRATCH = [
    pltpu.VMEM((32, 2, 8, 256), F32),
    pltpu.VMEM((4, 256, 128), F32),
    pltpu.VMEM((512, 1024), BF16),
    pltpu.VMEM((512, 1024), BF16),
]


def inner_levels(arrived, mask, table):
    second_high, second_low = two_parts(second_basis())
    second = np.concatenate([second_high, second_high, second_low], axis=0)
    return pl.pallas_call(
        inner_kernel,
        out_shape=jax.ShapeDtypeStruct((1024, 128), F32),
        in_specs=vmem(2) + far(3),
        out_specs=vmem(1)[0],
        scratch_shapes=[
            pltpu.VMEM((1536, 512), BF16),
            pltpu.VMEM((3072, 256), BF16),
            pltpu.VMEM((256, 2, 16, 256), F32),
            pltpu.SemaphoreType.DMA((6,)),
            pltpu.VMEM((4096, 128), F32),
            pltpu.VMEM((2, 128, 128), F32),
            [pltpu.VMEM((1024, 256), BF16)] * 2,
            [pltpu.VMEM((512, 1024), BF16)] * 2,
            pltpu.VMEM((512, 256), F32),
        ]
        + LEVEL_SCRATCH,
        name="inner",
        compiler_params=pltpu.CompilerParams(vmem_limit_bytes=48 << 20),
    )(
        arrived,
        mask,
        jnp.asarray(second),
        table,
        jnp.asarray(three_parts(stacked_matrix(2, 2))),
    )


def outer_levels(arrived, table):
    return pl.pallas_call(
        outer_kernel,
        out_shape=jax.ShapeDtypeStruct((1024, 128), F32),
        in_specs=vmem(1) + far(3),
        out_specs=vmem(1)[0],
        scratch_shapes=[
            pltpu.VMEM((240, 2, 16, 256), F32),
            pltpu.VMEM((3072, 256), BF16),
            pltpu.VMEM((1536, 256), BF16),
            pltpu.SemaphoreType.DMA((6,)),
        ]
        + LEVEL_SCRATCH,
        name="outer",
        compiler_params=pltpu.CompilerParams(vmem_limit_bytes=48 << 20),
    )(
        arrived,
        table,
        jnp.asarray(three_parts(stacked_matrix(2, 2))),
        jnp.asarray(three_parts(stacked_matrix(1, 2))),
    )


def reverse_bits(number, bit_count):
    result = jnp.zeros_like(number)
    for position in range(bit_count):
        result = result + jnp.left_shift(
            jnp.bitwise_and(jnp.right_shift(number, position), 1), bit_count - 1 - position
        )
    return result


def exchange(array):
    return lax.all_to_all(array, ("bx", "by"), split_axis=0, concat_axis=0, tiled=True)


def shards(src_pos, src_amp, box_slots):
    column = lax.axis_index("bx")
    row = lax.axis_index("by")
    device = column * BY + row
    block = jnp.stack([reverse_bits(column, 3), reverse_bits(row, 4)]).astype(jnp.int32)
    payload = jnp.concatenate([src_pos[:, 0, :].astype(F32), src_amp[:, 0, :]], axis=0)
    payload = payload.reshape(4, DEVICES, 128).transpose(1, 0, 2)
    arrived = exchange(payload).reshape(512, 128)
    mask, table = inner_turns(block, box_slots[0])
    arrived, mask, table = lax.optimization_barrier((arrived, mask, table))
    weights = inner_levels(arrived, mask, table)
    weights = exchange(weights.reshape(DEVICES, 8, 128)).reshape(1024, 128)
    speeds = lax.dynamic_index_in_dim(jnp.asarray(outer_speeds()), device, 0, keepdims=False)
    speeds = jnp.broadcast_to(speeds[:, None], (7 * 256, 128))
    weights = outer_levels(weights, outer_turns(speeds))
    weights = exchange(weights.reshape(DEVICES, 8, 128))
    weights = weights.reshape(LEAVES, LEAVES, 2, 2, 128).transpose(0, 1, 3, 2, 4)
    return weights.reshape(LEAVES, 1, LEAVES, 1, 2, BOX_NODES)


def solution(mesh):
    return jax.shard_map(
        shards,
        mesh=mesh,
        in_specs=(
            P(None, ("bx", "by"), None),
            P(None, ("bx", "by"), None),
            P(("bx", "by"), None, None),
        ),
        out_specs=P(None, "bx", None, "by", None, None),
        check_vma=False,
    )
```

```python
import functools
import math

import jax
import jax.numpy as jnp
import numpy as np
from jax import lax
from jax.experimental import pallas as pl
from jax.experimental.pallas import tpu as pltpu
from jax.sharding import PartitionSpec as P

NODES = 16
BOX_NODES = 256
DEVICES = 128
LEAVES = 16
BX = 8
BY = 16
BAND = 1024
F32 = jnp.float32
BF16 = jnp.bfloat16
ROUNDER = 12582912.0
SIN = (6.28305581, -41.33121471, 81.36682035, -74.47802935, 32.78144238)
COS = (0.99995995, -19.73105034, 64.67355678, -82.40422428, 45.64775943)


def chebyshev_points(point_count):
    indices = np.arange(point_count)
    return (1.0 - np.cos(np.pi * (2 * indices + 1) / (2 * point_count))) / 2.0


def lagrange_matrix(locations):
    points = chebyshev_points(NODES)
    matrix = np.ones((len(locations), NODES))
    for own in range(NODES):
        for other in range(NODES):
            if other != own:
                matrix[:, own] *= (locations - points[other]) / (points[own] - points[other])
    return matrix


def child_matrix(halves, child):
    if halves == 1:
        return np.eye(NODES)
    return lagrange_matrix((child + chebyshev_points(NODES)) / 2.0)


def stacked_matrix(halves_first, halves_second):
    pieces = [
        np.kron(child_matrix(halves_first, a), child_matrix(halves_second, b))
        for a in range(halves_first)
        for b in range(halves_second)
    ]
    return np.concatenate(pieces, axis=0)


def two_parts(matrix):
    exact = np.asarray(matrix, np.float32)
    high = exact.astype(jnp.bfloat16)
    low = (exact - high.astype(np.float32)).astype(jnp.bfloat16)
    return high, low


def velocity(first, second):
    return (2.0 + np.sin(2 * np.pi * first) * np.sin(2 * np.pi * second)) / 8.0


def bits(value, count):
    return [(value >> (count - 1 - k)) & 1 for k in range(count)]


def speed_change(first, second, level, split_first=True):
    count_second = 2.0**level
    count_first = 2.0 ** (level if split_first else level - 1)
    new = velocity((first + 0.5) / count_first, (second + 0.5) / count_second)
    above_first = first >> 1 if split_first else first
    old = velocity(
        (above_first + 0.5) / 2.0 ** (level - 1), ((second >> 1) + 0.5) / 2.0 ** (level - 1)
    )
    return new - old


def inner_speeds():
    table = np.zeros((4, 4, 8, 8))
    for child in range(4):
        x, y = bits(child, 2)
        for row in range(8):
            r0, r1, r2 = bits(row, 3)
            for sub in range(8):
                s0, s1, s2 = bits(sub, 3)
                table[0, child, row, sub] = speed_change(x, y, 1)
                table[1, child, row, sub] = speed_change(2 * r0 + x, 2 * r1 + y, 2)
                first, second = 2 * s0 + r2, 2 * s1 + s2
                table[2, child, row, sub] = speed_change(2 * first + x, 2 * second + y, 3)
                first, second = 2 * first + r0, 2 * second + r1
                table[3, child, row, sub] = speed_change(2 * first + x, 2 * second + y, 4)
    return table.reshape(1024).astype(np.float32)


def outer_speeds():
    tables = np.zeros((DEVICES, 7, 256))
    for device in range(DEVICES):
        coarse_first = device >> 3
        for child in range(4):
            x, y = bits(child, 2)
            for row in range(8):
                r0, r1, r2 = bits(row, 3)
                for sub in range(8):
                    s0, s1, s2 = bits(sub, 3)
                    place = child * 64 + row * 8 + sub
                    second = 2 * (device & 7) + s2
                    tables[device, 0, place] = speed_change(
                        2 * coarse_first + x, 2 * second + y, 5
                    )
                    tables[device, 1, place] = speed_change(
                        4 * coarse_first + 2 * r0 + x, 4 * second + 2 * r1 + y, 6
                    )
                    second = 2 * (device & 7) + r2
                    tables[device, 2, place] = speed_change(
                        8 * coarse_first + 4 * s0 + 2 * r0 + x,
                        8 * second + 4 * s1 + 2 * s2 + y,
                        7,
                    )
        for child in range(2):
            for row in range(16):
                r0, r1, r2, r3 = bits(row, 4)
                for sub in range(8):
                    s0, s1, s2 = bits(sub, 3)
                    place = child * 128 + row * 8 + sub
                    first = 8 * coarse_first + 4 * s0 + 2 * r2 + r0
                    second = 2 * (device & 7) + r3
                    second = 16 * second + 8 * s1 + 4 * s2 + 2 * r1 + child
                    tables[device, 3, place] = speed_change(first, second, 8, False)
                    tables[device, 4, place] = velocity((first + 0.5) / 128, (second + 0.5) / 256)
                    tables[device, 5, place] = 8 * (first + 0.5)
                    tables[device, 6, place] = 4 * (second + 0.5)
    return tables.reshape(DEVICES, 7 * 256).astype(np.float32)


def node_tables():
    points = chebyshev_points(NODES).astype(np.float32).astype(np.float64)
    first = np.repeat(points, NODES)
    second = np.tile(points, NODES)
    rows = np.zeros((16, BOX_NODES))
    for child in range(4):
        x, y = bits(child, 2)
        turns = (2 * x - 1) * 2 * first + (2 * y - 1) * second
        rows[child] = turns - np.round(turns)
    for child in range(2):
        rows[4 + child] = (2 * child - 1) * second
    rows[6] = 2 * first
    rows[7] = second
    rows[8] = np.round(first * 8192) / 8192
    rows[9] = first - rows[8]
    rows[10] = np.round(second * 8192) / 8192
    rows[11] = second - rows[10]
    rows[12] = BAND * np.sqrt(first * first + second * second)
    return rows.astype(np.float32)


def basis_factors():
    points = chebyshev_points(NODES)
    return [
        float(np.float32(1.0 / np.prod([points[own] - points[k] for k in range(NODES) if k != own])))
        for own in range(NODES)
    ]


def second_basis():
    small = lagrange_matrix((np.arange(16) + 0.5) / 16.0)
    whole = np.zeros((16, 32, 32, 16))
    for k in range(32):
        whole[:, k, k, :] = small
    return whole.reshape(512, 512)


def turn(turns):
    part = turns - ((turns + ROUNDER) - ROUNDER)
    square = part * part
    sine = SIN[4]
    cosine = COS[4]
    for k in (3, 2, 1, 0):
        sine = sine * square + SIN[k]
        cosine = cosine * square + COS[k]
    return cosine, sine * part


def split(value):
    high = value.astype(BF16)
    return high, (value - high.astype(F32)).astype(BF16)


def bit(value, place):
    return (value >> place) & 1


def make_turns(table, first_line, box, level_number, speeds, speed_row, node, base_row, children, rows):
    scale = 4.0 * 2.0 ** (level_number - 1)
    pairs = rows // 2

    def step(index, carry):
        source = index // pairs
        pair = lax.rem(index, pairs)
        radius = []
        for k in range(2):
            first, second = box(source, 2 * pair + k)
            along = first + node[6:7, :]
            across = second + node[7:8, :]
            radius.append(scale * jnp.sqrt(along * along + across * across))
        radius = jnp.concatenate([jnp.broadcast_to(value, (8, BOX_NODES)) for value in radius])
        for child in range(children):
            place = pl.multiple_of(speed_row + child * rows * 8 + pair * 16, 16)
            change = speeds[pl.ds(place, 16), :]
            change = jnp.concatenate([change, change], axis=1)
            cosine, sine = turn(change * radius + node[base_row + child : base_row + child + 1, :])
            line = first_line + index * children + child
            table[line, 0] = cosine
            table[line, 1] = sine
        return carry

    lax.fori_loop(0, (4 if children == 4 else 2) * pairs, step, 0)


def level(read, table, first_line, high, low, matrix, children, rows, ready, matrix_ready=None):
    sources = 4 if children == 4 else 2
    pairs = rows // 2
    for source in range(sources):
        lanes = slice(source * BOX_NODES, (source + 1) * BOX_NODES)
        if source < len(ready):
            ready[source].wait()
        for pair in range(pairs):
            group = source * rows + 2 * pair
            real, imaginary = (
                jnp.concatenate([read(group, part), read(group + 1, part)]) for part in range(2)
            )
            for child in range(children):
                line = first_line + (source * pairs + pair) * children + child
                cosine = table[line, 0]
                sine = table[line, 1]
                for part, value in enumerate(
                    (real * cosine - imaginary * sine, real * sine + imaginary * cosine)
                ):
                    place = (child * 2 + part) * rows * 8 + pair * 16
                    value_high, value_low = split(value)
                    high[place : place + 16, lanes] = value_high
                    low[place : place + 16, lanes] = value_low
    pieces = []
    for source in range(sources):
        lanes = slice(source * BOX_NODES, (source + 1) * BOX_NODES)
        pieces += [high[:, lanes], low[:, lanes], high[:, lanes]]
    if matrix_ready is not None:
        matrix_ready.wait()
    return jnp.dot(jnp.concatenate(pieces, axis=1), matrix[...], preferred_element_type=F32)


def three_parts(matrix):
    high, low = two_parts(matrix)
    high = high.reshape(-1, BOX_NODES, BOX_NODES)
    low = low.reshape(-1, BOX_NODES, BOX_NODES)
    return np.stack([high, high, low], axis=1).reshape(-1, BOX_NODES)


def matrices():
    return np.concatenate([three_parts(stacked_matrix(2, 2)), three_parts(stacked_matrix(1, 2))])


def sub_bits():
    row = lax.broadcasted_iota(jnp.int32, (8, BOX_NODES), 0)
    return [bit(row, 2 - k).astype(F32) for k in range(3)]


def find_mask(slots, mask, entries, high_hot, low_hot, total):
    iota = lax.broadcasted_iota(jnp.int32, (16, 128), 0).astype(F32)
    rows = [iota + 16.0 * k for k in range(8)]
    block = jnp.concatenate([slots[:, :128], slots[:, 128:]], axis=0)
    entries[0] = (block >> 7).astype(F32)
    entries[1] = (block & 127).astype(F32)

    def step(index, carry):
        for source, hot in enumerate((high_hot, low_hot)):
            block = entries[source, pl.ds(pl.multiple_of(index * 8, 8), 8), :]
            for k in range(8):
                value = jnp.broadcast_to(block[k : k + 1], (16, 128))
                lanes = pl.ds(pl.multiple_of(index * 1024 + 128 * k, 128), 128)
                for place in range(8):
                    hot[16 * place : 16 * (place + 1), lanes] = jnp.where(
                        value == rows[place], 1.0, 0.0
                    ).astype(BF16)
        return carry

    lax.fori_loop(0, 16, step, 0)
    total[...] = jnp.zeros_like(total)

    def add(index, carry):
        lanes = pl.ds(pl.multiple_of(index * 4096, 4096), 4096)
        total[...] += lax.dot_general(
            high_hot[:, lanes],
            low_hot[:, lanes],
            (((1,), (1,)), ((), ())),
            preferred_element_type=F32,
        )
        return carry

    lax.fori_loop(0, 4, add, 0)
    mask[...] = jnp.where(total[...] > 0.5, 1.0, 0.0)


def store_level(table, table_far, leave, index, size=64):
    lines = pl.ds(64 * index, size)
    return pltpu.make_async_copy(table.at[lines], table_far.at[lines], leave.at[index])


def fetch_level(table_far, table, arrive, index, size=64):
    lines = pl.ds(64 * index, size)
    return pltpu.make_async_copy(table_far.at[lines], table.at[lines], arrive.at[index])


def inner_turns_kernel(
    block,
    slots_far,
    node_far,
    speeds_far,
    mask,
    table_far,
    slots,
    node,
    speeds,
    table,
    entries,
    high_hot,
    low_hot,
    total,
    arrive,
    leave,
):
    fetches = [
        pltpu.make_async_copy(far, near, arrive.at[k])
        for k, (far, near) in enumerate(
            ((slots_far, slots), (node_far, node), (speeds_far, speeds))
        )
    ]
    for fetch in fetches:
        fetch.start()
    fetches[0].wait()
    find_mask(slots, mask, entries, high_hot, low_hot, total)
    for fetch in fetches[1:]:
        fetch.wait()
    stores = [store_level(table, table_far, leave, k) for k in range(4)]
    sub = sub_bits()
    block_first = block[0]
    block_second = block[1]

    def box(source, row):
        first = block_first * 16 + bit(source, 1) + 2 * bit(row, 2)
        second = block_second * 16 + bit(source, 0) + 2 * bit(row, 1) + 8 * bit(row, 0)
        return (
            2.0 * first.astype(F32) + (8.0 * sub[0] + 16.0 * sub[2]),
            second.astype(F32) + 4.0 * sub[1],
        )

    make_turns(table, 0, box, 1, speeds, 0, node, 0, 4, 8)
    stores[0].start()

    def box(source, row):
        first = block_first * 8 + bit(source, 1)
        second = block_second * 8 + bit(source, 0) + 4 * bit(row, 0)
        return (
            2.0 * first.astype(F32) + (4.0 * sub[0] + 8.0 * sub[2]),
            second.astype(F32) + 2.0 * sub[1],
        )

    make_turns(table, 64, box, 2, speeds, 256, node, 0, 4, 8)
    stores[1].start()

    def box(source, row):
        first = block_first * 4 + bit(source, 1) + 2 * bit(row, 2)
        second = block_second * 4 + bit(source, 0) + 2 * bit(row, 1)
        return 2.0 * first.astype(F32), second.astype(F32)

    make_turns(table, 128, box, 3, speeds, 512, node, 0, 4, 8)
    stores[2].start()

    def box(source, row):
        first = block_first * 2 + bit(source, 1)
        second = block_second * 2 + bit(source, 0)
        return 2.0 * first.astype(F32), second.astype(F32)

    make_turns(table, 192, box, 4, speeds, 768, node, 0, 4, 8)
    stores[3].start()
    for store in stores:
        store.wait()


def outer_turns_kernel(node, speeds, table_far, table, leave):
    stores = [store_level(table, table_far, leave, k, 64 if k < 3 else 48) for k in range(4)]
    sub = sub_bits()

    def box(source, row):
        first = bit(source, 1) + 2 * bit(row, 2) + 4 * bit(row, 1)
        second = bit(source, 0) + 2 * bit(row, 0)
        return 2.0 * first.astype(F32), second.astype(F32) + (4.0 * sub[0] + 8.0 * sub[1])

    make_turns(table, 0, box, 5, speeds, 0, node, 0, 4, 8)
    stores[0].start()

    def box(source, row):
        first = bit(source, 1) + 2 * bit(row, 0)
        second = bit(source, 0)
        return 2.0 * first.astype(F32), second.astype(F32) + (2.0 * sub[0] + 4.0 * sub[1])

    make_turns(table, 64, box, 6, speeds, 256, node, 0, 4, 8)
    stores[1].start()

    def box(source, row):
        first = bit(source, 1)
        second = bit(source, 0) + 2 * bit(row, 1)
        return 2.0 * first.astype(F32), second.astype(F32)

    make_turns(table, 128, box, 7, speeds, 512, node, 0, 4, 8)
    stores[2].start()

    def box(source, row):
        return jnp.float32(0.0), source.astype(F32)

    make_turns(table, 192, box, 8, speeds, 768, node, 4, 2, 16)

    def last(index, carry):
        def column(table):
            value = speeds[pl.ds(pl.multiple_of(256 * table + index * 16, 16), 16), :]
            return jnp.concatenate([value, value], axis=1)

        first = column(5)
        second = column(6)
        turns = first * node[8:9, :]
        turns = turns - ((turns + ROUNDER) - ROUNDER)
        across = second * node[10:11, :]
        across = across - ((across + ROUNDER) - ROUNDER)
        around = column(4) * node[12:13, :]
        around = around - ((around + ROUNDER) - ROUNDER)
        turns = turns + across + around + first * node[9:10, :] + second * node[11:12, :]
        cosine, sine = turn(turns)
        table[224 + index, 0] = cosine
        table[224 + index, 1] = sine
        return carry

    lax.fori_loop(0, 16, last, 0)
    stores[3].start()
    for store in stores:
        store.wait()


def deposit(
    arrived, mask, second, fetch_second, state, wide, cells, hots, spreads, grid
):
    points = [float(value) for value in chebyshev_points(NODES).astype(np.float32)]
    factors = basis_factors()

    def source_step(index, carry):
        rows = pl.ds(pl.multiple_of(index * 16, 16), 16)
        first, second, real, imaginary = (
            arrived[pl.ds(index * 64 + k, 16, stride=4), :] for k in range(4)
        )
        whole_first = first.astype(jnp.int32)
        whole_second = second.astype(jnp.int32)
        along = first + 0.5
        across = second + 0.5
        eighths = jnp.bitwise_and(whole_first + whole_second + 1, 7).astype(F32)
        cosine, sine = turn(
            0.125 * eighths + 0.0625 * jnp.sqrt(along * along + across * across)
        )
        live = mask[rows, :]
        real = real * live
        imaginary = imaginary * live
        turned = (real * cosine - imaginary * sine, real * sine + imaginary * cosine)
        place = jnp.bitwise_and(whole_first, 31).astype(F32) * 0.03125 + 0.015625
        cells[0, rows, :] = jnp.bitwise_and(whole_second, 15).astype(F32)
        x = [bit(whole_first, 5 + k) for k in range(4)]
        y = [bit(whole_second, 4 + k) for k in range(4)]
        cells[1, rows, :] = (x[0] * 8 + y[0] * 4 + x[1] * 2 + y[1]).astype(F32)
        cells[2, rows, :] = (y[3] * 8 + x[2] * 4 + y[2] * 2 + x[3]).astype(F32)
        away = [place - value for value in points]
        before = [None] * NODES
        after = [None] * NODES
        for p in range(1, NODES):
            before[p] = away[p - 1] if p == 1 else before[p - 1] * away[p - 1]
            q = NODES - 1 - p
            after[q] = away[q + 1] if p == 1 else after[q + 1] * away[q + 1]
        for p in range(NODES):
            if p == 0:
                value = after[0]
            elif p == NODES - 1:
                value = before[p]
            else:
                value = before[p] * after[p]
            value = value * factors[p]
            for part in range(2):
                wide[pl.ds(index * 512 + part * 16 + p, 16, stride=32), :] = value * turned[part]
        return carry

    lax.fori_loop(0, 8, source_step, 0)

    iota = lax.broadcasted_iota(jnp.int32, (16, 128), 0).astype(F32)

    def build(chunk, hot, spread):
        for k in range(16):
            sender = chunk * 16 + k
            lanes = slice(128 * k, 128 * (k + 1))

            def row(number):
                return jnp.broadcast_to(cells[number, pl.ds(sender, 1), :], (8, 128))

            values = wide[pl.ds(pl.multiple_of(sender * 32, 32), 32), :]
            cell = row(0)
            for c in range(16):
                chosen = jnp.concatenate([cell == float(c)] * 4)
                spread[32 * c : 32 * (c + 1), lanes] = jnp.where(chosen, values, 0.0).astype(BF16)
            low = row(2)
            inside = jnp.where(jnp.concatenate([low, low]) == iota, 1.0, 0.0)
            above = row(1)
            for c in range(16):
                chosen = jnp.concatenate([above == float(c)] * 2)
                hot[16 * c : 16 * (c + 1), lanes] = jnp.where(chosen, inside, 0.0).astype(BF16)

    def add(hot, spread):
        grid[...] += lax.dot_general(
            spread[...], hot[...], (((1,), (1,)), ((), ())), preferred_element_type=F32
        )

    grid[...] = jnp.zeros_like(grid)
    build(0, hots[0], spreads[0])

    def spread_step(index, carry):
        add(hots[0], spreads[0])
        build(2 * index + 1, hots[1], spreads[1])
        add(hots[1], spreads[1])
        build(jnp.minimum(2 * index + 2, 7), hots[0], spreads[0])
        return carry

    lax.fori_loop(0, 4, spread_step, 0)

    grid_high, grid_low = split(grid[...].T)
    fetch_second.wait()
    result = jnp.dot(
        jnp.concatenate([grid_high, grid_low, grid_high], axis=1),
        second[...],
        preferred_element_type=F32,
    )
    for group in range(32):
        for part in range(2):
            state[group, part] = result[
                8 * group : 8 * group + 8, BOX_NODES * part : BOX_NODES * (part + 1)
            ]


def pieces(result):
    for child in range(4):
        for row in range(8):
            start = child * 128 + row * 8
            yield bits(child, 2), bits(row, 3), [
                result[start + 64 * part : start + 64 * part + 8, :] for part in range(2)
            ]


def halves(value):
    return value[:, :128], value[:, 128:]


def inner_kernel(
    arrived,
    mask,
    second_far,
    table_far,
    matrix_far,
    out,
    second,
    matrix,
    table,
    arrive,
    wide,
    cells,
    hots,
    spreads,
    grid,
    state,
    turned,
    high,
    low,
):
    fetch_second = pltpu.make_async_copy(second_far, second, arrive.at[4])
    fetch_second.start()
    fetches = [fetch_level(table_far, table, arrive, k) for k in range(4)]
    for fetch in fetches:
        fetch.start()
    fetch_matrix = pltpu.make_async_copy(matrix_far.at[pl.ds(0, 3072)], matrix, arrive.at[5])
    fetch_matrix.start()
    deposit(arrived, mask, second, fetch_second, state, wide, cells, hots, spreads, grid)

    def run(number, read):
        return level(
            read,
            table,
            64 * (number - 1),
            high,
            low,
            matrix,
            4,
            8,
            fetches[number - 1 : number],
            fetch_matrix if number == 1 else None,
        )

    def read(group, part):
        return state[group, part]

    for (x, y), (r0, r1, r2), values in pieces(run(1, read)):
        for part in range(2):
            state[(2 * r0 + r1) * 8 + x * 4 + y * 2 + r2, part] = values[part]

    for (x, y), (r0, r1, r2), values in pieces(run(2, read)):
        start = ((r2 * 2 + x) * 8 + r0 * 4 + r1 * 2 + y) * 8
        for part in range(2):
            for half, value in enumerate(halves(values[part])):
                turned[2 * part + half, start : start + 8, :] = value

    def across(group, part):
        b2x, b2y, b3x, b3y, t2x = bits(group, 5)
        start = (b3y * 2 + t2x) * 64 + b2x * 4 + b2y * 2 + b3x
        return jnp.concatenate(
            [turned.at[2 * part + half][pl.ds(start, 8, stride=8), :] for half in range(2)], axis=1
        )

    for (x, y), (r0, r1, r2), values in pieces(run(3, across)):
        for part in range(2):
            state[(2 * r0 + r1) * 8 + x * 4 + y * 2 + r2, part] = values[part]

    for (x, y), (r0, r1, r2), values in pieces(run(4, read)):
        device = r2 * 32 + r0 * 16 + x * 8 + r1
        for upper in range(2):
            for part in range(2):
                for half, value in enumerate(halves(values[part])):
                    start = (device + 64 * upper) * 8 + y * 4 + half * 2 + part
                    out[pl.ds(start, 4, stride=16), :] = value[4 * upper : 4 * upper + 4]


def outer_kernel(
    arrived, table_far, matrix_far, out, table, matrix, last, arrive, state, turned, high, low
):
    first = [
        pltpu.make_async_copy(
            table_far.at[pl.ds(16 * k, 16)], table.at[pl.ds(16 * k, 16)], arrive.at[6 + k]
        )
        for k in range(4)
    ]
    fetches = [
        fetch_level(table_far, table, arrive, k, 64 if k < 3 else 48) for k in range(1, 4)
    ]
    fetch_matrix = pltpu.make_async_copy(matrix_far.at[pl.ds(0, 3072)], matrix, arrive.at[5])
    fetch_last = pltpu.make_async_copy(matrix_far.at[pl.ds(3072, 1536)], last, arrive.at[4])
    for fetch in first + [fetch_matrix] + fetches + [fetch_last]:
        fetch.start()

    def first_read(group, part):
        i2, j3, i1, i0, j2 = bits(group, 5)
        source = i2 * 64 + i1 * 32 + i0 * 16 + j3 * 8 + j2 * 4
        return jnp.concatenate(
            [
                arrived[pl.ds(source * 8 + half * 2 + part, 8, stride=4), :]
                for half in range(2)
            ],
            axis=1,
        )

    def run(number, read):
        return level(
            read,
            table,
            64 * (number - 5),
            high,
            low,
            matrix,
            4,
            8,
            first if number == 5 else fetches[number - 6 : number - 5],
            fetch_matrix if number == 5 else None,
        )

    def read(group, part):
        return state[group, part]

    for (x, y), (i1, i0, j2), values in pieces(run(5, first_read)):
        for part in range(2):
            state[(2 * i1 + j2) * 8 + x * 4 + y * 2 + i0, part] = values[part]

    for (x, y), (r0, r1, i0), values in pieces(run(6, read)):
        start = ((i0 * 2 + x) * 8 + r0 * 4 + r1 * 2 + y) * 8
        for part in range(2):
            for half, value in enumerate(halves(values[part])):
                turned[2 * part + half, start : start + 8, :] = value

    def across(group, part):
        i0, j1, t6x, j0, pair = bits(group, 5)
        start = (i0 * 2 + t6x) * 64 + j1 * 4 + j0 * 2 + pair
        return jnp.concatenate(
            [turned.at[2 * part + half][pl.ds(start, 8, stride=8), :] for half in range(2)], axis=1
        )

    for (x, y), (t6x, j0, pair), values in pieces(run(7, across)):
        for part in range(2):
            state[j0 * 16 + x * 8 + y * 4 + t6x * 2 + pair, part] = values[part]

    result = level(read, table, 192, high, low, last, 2, 16, fetches[2:], fetch_last)
    for child in range(2):
        for row in range(16):
            t7x, t7y, t6x, pair = bits(row, 4)
            start = child * 256 + row * 8
            line = 224 + child * 8 + row // 2
            cosine = table[line, 0, 8 * (row % 2) : 8 * (row % 2) + 8, :]
            sine = table[line, 1, 8 * (row % 2) : 8 * (row % 2) + 8, :]
            real = result[start : start + 8, :]
            imaginary = result[start + 128 : start + 136, :]
            device = t6x * 32 + t7x * 16 + t7y * 2 + child
            for part, whole in enumerate(
                (real * cosine + imaginary * sine, imaginary * cosine - real * sine)
            ):
                for half, value in enumerate(halves(whole)):
                    for upper in range(2):
                        place = (device + 64 * upper) * 8 + pair * 4 + half * 2 + part
                        out[pl.ds(place, 4, stride=32), :] = value[4 * upper : 4 * upper + 4]


def vmem(count):
    return [pl.BlockSpec(memory_space=pltpu.VMEM)] * count


def smem(count):
    return [pl.BlockSpec(memory_space=pltpu.SMEM)] * count


def far(count):
    return [pl.BlockSpec(memory_space=pltpu.HBM)] * count


def payload_kernel(place_far, amp_far, out_far, place, amp, out, arrive, leave):
    fetches = [
        pltpu.make_async_copy(place_far, place, arrive.at[0]),
        pltpu.make_async_copy(amp_far, amp, arrive.at[1]),
    ]
    for fetch in fetches:
        fetch.start()
    for fetch in fetches:
        fetch.wait()
    for k in range(2):
        out[pl.ds(k, DEVICES, stride=4), :] = place[k].astype(F32)
        out[pl.ds(2 + k, DEVICES, stride=4), :] = amp[k]
    store = pltpu.make_async_copy(out, out_far, leave)
    store.start()
    store.wait()


def make_payload(place, amp):
    return pl.pallas_call(
        payload_kernel,
        out_shape=jax.ShapeDtypeStruct((4 * DEVICES, 128), F32),
        in_specs=far(2),
        out_specs=far(1)[0],
        scratch_shapes=[
            pltpu.VMEM((2, DEVICES, 128), jnp.int32),
            pltpu.VMEM((2, DEVICES, 128), F32),
            pltpu.VMEM((4 * DEVICES, 128), F32),
            pltpu.SemaphoreType.DMA((2,)),
            pltpu.SemaphoreType.DMA,
        ],
        name="payload",
        compiler_params=pltpu.CompilerParams(vmem_limit_bytes=60 << 20),
    )(place, amp)


def inner_turns(block, slots):
    speeds = np.repeat(inner_speeds()[:, None], 128, axis=1)
    return pl.pallas_call(
        inner_turns_kernel,
        out_shape=[
            jax.ShapeDtypeStruct((128, 128), F32),
            jax.ShapeDtypeStruct((256, 2, 16, 256), F32),
        ],
        in_specs=smem(1) + far(3),
        out_specs=vmem(1) + far(1),
        scratch_shapes=[
            pltpu.VMEM((64, 256), jnp.int32),
            pltpu.VMEM((16, 256), F32),
            pltpu.VMEM((1024, 128), F32),
            pltpu.VMEM((256, 2, 16, 256), F32),
            pltpu.VMEM((2, 128, 128), F32),
            pltpu.VMEM((128, 16384), BF16),
            pltpu.VMEM((128, 16384), BF16),
            pltpu.VMEM((128, 128), F32),
            pltpu.SemaphoreType.DMA((3,)),
            pltpu.SemaphoreType.DMA((4,)),
        ],
        name="inner_turns",
        compiler_params=pltpu.CompilerParams(vmem_limit_bytes=60 << 20),
    )(block, slots, jnp.asarray(node_tables()), jnp.asarray(speeds))


def outer_turns(speeds):
    return pl.pallas_call(
        outer_turns_kernel,
        out_shape=jax.ShapeDtypeStruct((240, 2, 16, 256), F32),
        in_specs=vmem(2),
        out_specs=far(1)[0],
        scratch_shapes=[
            pltpu.VMEM((240, 2, 16, 256), F32),
            pltpu.SemaphoreType.DMA((4,)),
        ],
        name="outer_turns",
        compiler_params=pltpu.CompilerParams(vmem_limit_bytes=59 << 20),
    )(jnp.asarray(node_tables()), speeds)


LEVEL_SCRATCH = [
    pltpu.VMEM((32, 2, 8, 256), F32),
    pltpu.VMEM((4, 256, 128), F32),
    pltpu.VMEM((512, 1024), BF16),
    pltpu.VMEM((512, 1024), BF16),
]


def inner_levels(arrived, mask, table):
    second_high, second_low = two_parts(second_basis())
    second = np.concatenate([second_high, second_high, second_low], axis=0)
    return pl.pallas_call(
        inner_kernel,
        out_shape=jax.ShapeDtypeStruct((1024, 128), F32),
        in_specs=vmem(2) + far(3),
        out_specs=vmem(1)[0],
        scratch_shapes=[
            pltpu.VMEM((1536, 512), BF16),
            pltpu.VMEM((3072, 256), BF16),
            pltpu.VMEM((256, 2, 16, 256), F32),
            pltpu.SemaphoreType.DMA((6,)),
            pltpu.VMEM((4096, 128), F32),
            pltpu.VMEM((3, 128, 128), F32),
            [pltpu.VMEM((256, 2048), BF16)] * 2,
            [pltpu.VMEM((512, 2048), BF16)] * 2,
            pltpu.VMEM((512, 256), F32),
        ]
        + LEVEL_SCRATCH,
        name="inner",
        compiler_params=pltpu.CompilerParams(vmem_limit_bytes=59 << 20),
    )(
        arrived,
        mask,
        jnp.asarray(second),
        table,
        jnp.asarray(matrices()),
    )


def outer_levels(arrived, table):
    return pl.pallas_call(
        outer_kernel,
        out_shape=jax.ShapeDtypeStruct((1024, 128), F32),
        in_specs=vmem(1) + far(2),
        out_specs=vmem(1)[0],
        scratch_shapes=[
            pltpu.VMEM((240, 2, 16, 256), F32),
            pltpu.VMEM((3072, 256), BF16),
            pltpu.VMEM((1536, 256), BF16),
            pltpu.SemaphoreType.DMA((10,)),
        ]
        + LEVEL_SCRATCH,
        name="outer",
        compiler_params=pltpu.CompilerParams(vmem_limit_bytes=59 << 20),
    )(
        arrived,
        table,
        jnp.asarray(matrices()),
    )


def reverse_bits(number, bit_count):
    result = jnp.zeros_like(number)
    for position in range(bit_count):
        result = result + jnp.left_shift(
            jnp.bitwise_and(jnp.right_shift(number, position), 1), bit_count - 1 - position
        )
    return result


def exchange(array):
    return lax.all_to_all(array, ("bx", "by"), split_axis=0, concat_axis=0, tiled=True)


def shards(src_pos, src_amp, box_slots):
    column = lax.axis_index("bx")
    row = lax.axis_index("by")
    device = column * BY + row
    block = jnp.stack([reverse_bits(column, 3), reverse_bits(row, 4)]).astype(jnp.int32)
    payload = make_payload(src_pos.reshape(2, DEVICES, 128), src_amp.reshape(2, DEVICES, 128))
    arrived = exchange(payload.reshape(DEVICES, 4, 128)).reshape(512, 128)
    mask, table = inner_turns(block, box_slots[0].T)
    arrived, mask, table = lax.optimization_barrier((arrived, mask, table))
    weights = inner_levels(arrived, mask, table)
    weights = exchange(weights.reshape(DEVICES, 8, 128)).reshape(1024, 128)
    speeds = lax.dynamic_index_in_dim(jnp.asarray(outer_speeds()), device, 0, keepdims=False)
    speeds = jnp.broadcast_to(speeds[:, None], (7 * 256, 128))
    weights = outer_levels(weights, outer_turns(speeds))
    weights = exchange(weights.reshape(DEVICES, 8, 128))
    weights = weights.reshape(LEAVES, LEAVES, 2, 2, 128)
    weights = jnp.concatenate([weights[:, :, 0], weights[:, :, 1]], axis=-1)
    return weights.reshape(LEAVES, 1, LEAVES, 1, 2, BOX_NODES)


def solution(mesh):
    return jax.shard_map(
        shards,
        mesh=mesh,
        in_specs=(
            P(None, ("bx", "by"), None),
            P(None, ("bx", "by"), None),
            P(("bx", "by"), None, None),
        ),
        out_specs=P(None, "bx", None, "by", None, None),
        check_vma=False,
    )
```

```python
import functools
import math

import jax
import jax.numpy as jnp
import numpy as np
from jax import lax
from jax.experimental import pallas as pl
from jax.experimental.pallas import tpu as pltpu
from jax.sharding import PartitionSpec as P

NODES = 16
BOX_NODES = 256
DEVICES = 128
LEAVES = 16
BX = 8
BY = 16
BAND = 1024
F32 = jnp.float32
BF16 = jnp.bfloat16
ROUNDER = 12582912.0
SIN = (6.28305581, -41.33121471, 81.36682035, -74.47802935, 32.78144238)
COS = (0.99995995, -19.73105034, 64.67355678, -82.40422428, 45.64775943)


def chebyshev_points(point_count):
    indices = np.arange(point_count)
    return (1.0 - np.cos(np.pi * (2 * indices + 1) / (2 * point_count))) / 2.0


def lagrange_matrix(locations):
    points = chebyshev_points(NODES)
    matrix = np.ones((len(locations), NODES))
    for own in range(NODES):
        for other in range(NODES):
            if other != own:
                matrix[:, own] *= (locations - points[other]) / (points[own] - points[other])
    return matrix


def child_matrix(halves, child):
    if halves == 1:
        return np.eye(NODES)
    return lagrange_matrix((child + chebyshev_points(NODES)) / 2.0)


def stacked_matrix(halves_first, halves_second):
    pieces = [
        np.kron(child_matrix(halves_first, a), child_matrix(halves_second, b))
        for a in range(halves_first)
        for b in range(halves_second)
    ]
    return np.concatenate(pieces, axis=0)


def two_parts(matrix):
    exact = np.asarray(matrix, np.float32)
    high = exact.astype(jnp.bfloat16)
    low = (exact - high.astype(np.float32)).astype(jnp.bfloat16)
    return high, low


def velocity(first, second):
    return (2.0 + np.sin(2 * np.pi * first) * np.sin(2 * np.pi * second)) / 8.0


def bits(value, count):
    return [(value >> (count - 1 - k)) & 1 for k in range(count)]


def speed_change(first, second, level, split_first=True):
    count_second = 2.0**level
    count_first = 2.0 ** (level if split_first else level - 1)
    new = velocity((first + 0.5) / count_first, (second + 0.5) / count_second)
    above_first = first >> 1 if split_first else first
    old = velocity(
        (above_first + 0.5) / 2.0 ** (level - 1), ((second >> 1) + 0.5) / 2.0 ** (level - 1)
    )
    return new - old


def inner_speeds():
    table = np.zeros((4, 4, 8, 8))
    for child in range(4):
        x, y = bits(child, 2)
        for row in range(8):
            r0, r1, r2 = bits(row, 3)
            for sub in range(8):
                s0, s1, s2 = bits(sub, 3)
                table[0, child, row, sub] = speed_change(x, y, 1)
                table[1, child, row, sub] = speed_change(2 * r0 + x, 2 * r1 + y, 2)
                first, second = 2 * s0 + r2, 2 * s1 + s2
                table[2, child, row, sub] = speed_change(2 * first + x, 2 * second + y, 3)
                first, second = 2 * first + r0, 2 * second + r1
                table[3, child, row, sub] = speed_change(2 * first + x, 2 * second + y, 4)
    return table.reshape(1024).astype(np.float32)


def outer_speeds():
    tables = np.zeros((DEVICES, 7, 256))
    for device in range(DEVICES):
        coarse_first = device >> 3
        for child in range(4):
            x, y = bits(child, 2)
            for row in range(8):
                r0, r1, r2 = bits(row, 3)
                for sub in range(8):
                    s0, s1, s2 = bits(sub, 3)
                    place = child * 64 + row * 8 + sub
                    second = 2 * (device & 7) + s2
                    tables[device, 0, place] = speed_change(
                        2 * coarse_first + x, 2 * second + y, 5
                    )
                    tables[device, 1, place] = speed_change(
                        4 * coarse_first + 2 * r0 + x, 4 * second + 2 * r1 + y, 6
                    )
                    second = 2 * (device & 7) + r2
                    tables[device, 2, place] = speed_change(
                        8 * coarse_first + 4 * s0 + 2 * r0 + x,
                        8 * second + 4 * s1 + 2 * s2 + y,
                        7,
                    )
        for child in range(2):
            for row in range(16):
                r0, r1, r2, r3 = bits(row, 4)
                for sub in range(8):
                    s0, s1, s2 = bits(sub, 3)
                    place = child * 128 + row * 8 + sub
                    first = 8 * coarse_first + 4 * s0 + 2 * r2 + r0
                    second = 2 * (device & 7) + r3
                    second = 16 * second + 8 * s1 + 4 * s2 + 2 * r1 + child
                    tables[device, 3, place] = speed_change(first, second, 8, False)
                    tables[device, 4, place] = velocity((first + 0.5) / 128, (second + 0.5) / 256)
                    tables[device, 5, place] = 8 * (first + 0.5)
                    tables[device, 6, place] = 4 * (second + 0.5)
    return tables.reshape(DEVICES, 7 * 256).astype(np.float32)


def node_tables():
    points = chebyshev_points(NODES).astype(np.float32).astype(np.float64)
    first = np.repeat(points, NODES)
    second = np.tile(points, NODES)
    rows = np.zeros((16, BOX_NODES))
    for child in range(4):
        x, y = bits(child, 2)
        turns = (2 * x - 1) * 2 * first + (2 * y - 1) * second
        rows[child] = turns - np.round(turns)
    for child in range(2):
        rows[4 + child] = (2 * child - 1) * second
    rows[6] = 2 * first
    rows[7] = second
    rows[8] = np.round(first * 8192) / 8192
    rows[9] = first - rows[8]
    rows[10] = np.round(second * 8192) / 8192
    rows[11] = second - rows[10]
    rows[12] = BAND * np.sqrt(first * first + second * second)
    return rows.astype(np.float32)


def basis_factors():
    points = chebyshev_points(NODES)
    return [
        float(np.float32(1.0 / np.prod([points[own] - points[k] for k in range(NODES) if k != own])))
        for own in range(NODES)
    ]


def second_basis():
    small = lagrange_matrix((np.arange(16) + 0.5) / 16.0)
    whole = np.zeros((16, 32, 32, 16))
    for k in range(32):
        whole[:, k, k, :] = small
    return whole.reshape(512, 512)


def turn(turns):
    part = turns - ((turns + ROUNDER) - ROUNDER)
    square = part * part
    sine = SIN[4]
    cosine = COS[4]
    for k in (3, 2, 1, 0):
        sine = sine * square + SIN[k]
        cosine = cosine * square + COS[k]
    return cosine, sine * part


def split(value):
    high = value.astype(BF16)
    return high, (value - high.astype(F32)).astype(BF16)


def bit(value, place):
    return (value >> place) & 1


def make_turns(table, first_line, box, level_number, speeds, speed_row, node, base_row, children, rows):
    scale = 4.0 * 2.0 ** (level_number - 1)
    pairs = rows // 2

    def step(index, carry):
        source = index // pairs
        pair = lax.rem(index, pairs)
        radius = []
        for k in range(2):
            first, second = box(source, 2 * pair + k)
            along = first + node[6:7, :]
            across = second + node[7:8, :]
            radius.append(scale * jnp.sqrt(along * along + across * across))
        radius = jnp.concatenate([jnp.broadcast_to(value, (8, BOX_NODES)) for value in radius])
        for child in range(children):
            place = pl.multiple_of(speed_row + child * rows * 8 + pair * 16, 16)
            change = speeds[pl.ds(place, 16), :]
            change = jnp.concatenate([change, change], axis=1)
            cosine, sine = turn(change * radius + node[base_row + child : base_row + child + 1, :])
            line = first_line + index * children + child
            table[line, 0] = cosine
            table[line, 1] = sine
        return carry

    lax.fori_loop(0, (4 if children == 4 else 2) * pairs, step, 0)


def level(read, table, first_line, high, low, matrix, children, rows, ready, matrix_ready=None):
    sources = 4 if children == 4 else 2
    pairs = rows // 2
    for source in range(sources):
        lanes = slice(source * BOX_NODES, (source + 1) * BOX_NODES)
        if source < len(ready):
            ready[source].wait()
        for pair in range(pairs):
            group = source * rows + 2 * pair
            real, imaginary = (
                jnp.concatenate([read(group, part), read(group + 1, part)]) for part in range(2)
            )
            for child in range(children):
                line = first_line + (source * pairs + pair) * children + child
                cosine = table[line, 0]
                sine = table[line, 1]
                for part, value in enumerate(
                    (real * cosine - imaginary * sine, real * sine + imaginary * cosine)
                ):
                    place = (child * 2 + part) * rows * 8 + pair * 16
                    value_high, value_low = split(value)
                    high[place : place + 16, lanes] = value_high
                    low[place : place + 16, lanes] = value_low
    if matrix_ready is not None:
        matrix_ready.wait()
    columns = sources * BOX_NODES
    both = jnp.dot(high[:, :columns], matrix[...], preferred_element_type=F32)
    rest = jnp.dot(low[:, :columns], matrix[:, :BOX_NODES], preferred_element_type=F32)
    return both[:, :BOX_NODES] + (both[:, BOX_NODES:] + rest)


def matrices():
    basis = second_basis()
    rows = [
        stacked_matrix(2, 2),
        stacked_matrix(1, 2),
        basis[:, :256],
        basis[:, 256:],
    ]
    return np.concatenate(two_parts(np.concatenate(rows)), axis=1)


def sub_bits():
    row = lax.broadcasted_iota(jnp.int32, (8, BOX_NODES), 0)
    return [bit(row, 2 - k).astype(F32) for k in range(3)]


def find_mask(slots, mask, entries, high_hot, low_hot, total):
    iota = lax.broadcasted_iota(jnp.int32, (16, 128), 0).astype(F32)
    rows = [(iota + 16.0 * k).astype(BF16) for k in range(8)]
    one = jnp.ones((16, 128), BF16)
    zero = jnp.zeros((16, 128), BF16)
    block = jnp.concatenate([slots[:, :128], slots[:, 128:]], axis=0)
    entries[0] = (block >> 7).astype(F32)
    entries[1] = (block & 127).astype(F32)

    def step(index, carry):
        for source, hot in enumerate((high_hot, low_hot)):
            block = entries[source, pl.ds(pl.multiple_of(index * 8, 8), 8), :]
            for k in range(8):
                value = jnp.broadcast_to(block[k : k + 1], (16, 128)).astype(BF16)
                lanes = pl.ds(pl.multiple_of(index * 1024 + 128 * k, 128), 128)
                for place in range(8):
                    hot[16 * place : 16 * (place + 1), lanes] = jnp.where(
                        value == rows[place], one, zero
                    )
        return carry

    lax.fori_loop(0, 16, step, 0)
    total[...] = jnp.zeros_like(total)

    def add(index, carry):
        lanes = pl.ds(pl.multiple_of(index * 4096, 4096), 4096)
        total[...] += lax.dot_general(
            high_hot[:, lanes],
            low_hot[:, lanes],
            (((1,), (1,)), ((), ())),
            preferred_element_type=F32,
        )
        return carry

    lax.fori_loop(0, 4, add, 0)
    mask[...] = jnp.where(total[...] > 0.5, 1.0, 0.0)


def store_level(table, table_far, leave, index, size=64):
    lines = pl.ds(64 * index, size)
    return pltpu.make_async_copy(table.at[lines], table_far.at[lines], leave.at[index])


def fetch_level(table_far, table, arrive, index, size=64):
    lines = pl.ds(64 * index, size)
    return pltpu.make_async_copy(table_far.at[lines], table.at[lines], arrive.at[index])


def inner_turns_kernel(
    block,
    slots_far,
    node_far,
    speeds_far,
    mask,
    table_far,
    slots,
    node,
    speeds,
    table,
    entries,
    high_hot,
    low_hot,
    total,
    arrive,
    leave,
):
    fetches = [
        pltpu.make_async_copy(far, near, arrive.at[k])
        for k, (far, near) in enumerate(
            ((slots_far, slots), (node_far, node), (speeds_far, speeds))
        )
    ]
    for fetch in fetches:
        fetch.start()
    fetches[0].wait()
    find_mask(slots, mask, entries, high_hot, low_hot, total)
    for fetch in fetches[1:]:
        fetch.wait()
    stores = [store_level(table, table_far, leave, k) for k in range(4)]
    sub = sub_bits()
    block_first = block[0]
    block_second = block[1]

    def box(source, row):
        first = block_first * 16 + bit(source, 1) + 2 * bit(row, 2)
        second = block_second * 16 + bit(source, 0) + 2 * bit(row, 1) + 8 * bit(row, 0)
        return (
            2.0 * first.astype(F32) + (8.0 * sub[0] + 16.0 * sub[2]),
            second.astype(F32) + 4.0 * sub[1],
        )

    make_turns(table, 0, box, 1, speeds, 0, node, 0, 4, 8)
    stores[0].start()

    def box(source, row):
        first = block_first * 8 + bit(source, 1)
        second = block_second * 8 + bit(source, 0) + 4 * bit(row, 0)
        return (
            2.0 * first.astype(F32) + (4.0 * sub[0] + 8.0 * sub[2]),
            second.astype(F32) + 2.0 * sub[1],
        )

    make_turns(table, 64, box, 2, speeds, 256, node, 0, 4, 8)
    stores[1].start()

    def box(source, row):
        first = block_first * 4 + bit(source, 1) + 2 * bit(row, 2)
        second = block_second * 4 + bit(source, 0) + 2 * bit(row, 1)
        return 2.0 * first.astype(F32), second.astype(F32)

    make_turns(table, 128, box, 3, speeds, 512, node, 0, 4, 8)
    stores[2].start()

    def box(source, row):
        first = block_first * 2 + bit(source, 1)
        second = block_second * 2 + bit(source, 0)
        return 2.0 * first.astype(F32), second.astype(F32)

    make_turns(table, 192, box, 4, speeds, 768, node, 0, 4, 8)
    stores[3].start()
    for store in stores:
        store.wait()


def outer_turns_kernel(node, speeds, table_far, table, leave):
    stores = [store_level(table, table_far, leave, k, 64 if k < 3 else 48) for k in range(4)]
    sub = sub_bits()

    def box(source, row):
        first = bit(source, 1) + 2 * bit(row, 2) + 4 * bit(row, 1)
        second = bit(source, 0) + 2 * bit(row, 0)
        return 2.0 * first.astype(F32), second.astype(F32) + (4.0 * sub[0] + 8.0 * sub[1])

    make_turns(table, 0, box, 5, speeds, 0, node, 0, 4, 8)
    stores[0].start()

    def box(source, row):
        first = bit(source, 1) + 2 * bit(row, 0)
        second = bit(source, 0)
        return 2.0 * first.astype(F32), second.astype(F32) + (2.0 * sub[0] + 4.0 * sub[1])

    make_turns(table, 64, box, 6, speeds, 256, node, 0, 4, 8)
    stores[1].start()

    def box(source, row):
        first = bit(source, 1)
        second = bit(source, 0) + 2 * bit(row, 1)
        return 2.0 * first.astype(F32), second.astype(F32)

    make_turns(table, 128, box, 7, speeds, 512, node, 0, 4, 8)
    stores[2].start()

    def box(source, row):
        return jnp.float32(0.0), source.astype(F32)

    make_turns(table, 192, box, 8, speeds, 768, node, 4, 2, 16)

    def last(index, carry):
        def column(table):
            value = speeds[pl.ds(pl.multiple_of(256 * table + index * 16, 16), 16), :]
            return jnp.concatenate([value, value], axis=1)

        first = column(5)
        second = column(6)
        turns = first * node[8:9, :]
        turns = turns - ((turns + ROUNDER) - ROUNDER)
        across = second * node[10:11, :]
        across = across - ((across + ROUNDER) - ROUNDER)
        around = column(4) * node[12:13, :]
        around = around - ((around + ROUNDER) - ROUNDER)
        turns = turns + across + around + first * node[9:10, :] + second * node[11:12, :]
        cosine, sine = turn(turns)
        table[224 + index, 0] = cosine
        table[224 + index, 1] = sine
        return carry

    lax.fori_loop(0, 16, last, 0)
    stores[3].start()
    for store in stores:
        store.wait()


def deposit(
    arrived, mask, second, fetch_second, state, wide, cells, hots, spreads, grid
):
    points = [float(value) for value in chebyshev_points(NODES).astype(np.float32)]
    factors = basis_factors()

    def source_step(index, carry):
        rows = pl.ds(pl.multiple_of(index * 16, 16), 16)
        first, second, real, imaginary = (
            arrived[pl.ds(index * 64 + k, 16, stride=4), :] for k in range(4)
        )
        whole_first = first.astype(jnp.int32)
        whole_second = second.astype(jnp.int32)
        along = first + 0.5
        across = second + 0.5
        eighths = jnp.bitwise_and(whole_first + whole_second + 1, 7).astype(F32)
        cosine, sine = turn(
            0.125 * eighths + 0.0625 * jnp.sqrt(along * along + across * across)
        )
        live = mask[rows, :]
        real = real * live
        imaginary = imaginary * live
        turned = (real * cosine - imaginary * sine, real * sine + imaginary * cosine)
        place = jnp.bitwise_and(whole_first, 31).astype(F32) * 0.03125 + 0.015625
        cells[0, rows, :] = jnp.bitwise_and(whole_second, 15).astype(F32)
        x = [bit(whole_first, 5 + k) for k in range(4)]
        y = [bit(whole_second, 4 + k) for k in range(4)]
        cells[1, rows, :] = (x[0] * 8 + y[0] * 4 + x[1] * 2 + y[1]).astype(F32)
        cells[2, rows, :] = (y[3] * 8 + x[2] * 4 + y[2] * 2 + x[3]).astype(F32)
        away = [place - value for value in points]
        before = [None] * NODES
        after = [None] * NODES
        for p in range(1, NODES):
            before[p] = away[p - 1] if p == 1 else before[p - 1] * away[p - 1]
            q = NODES - 1 - p
            after[q] = away[q + 1] if p == 1 else after[q + 1] * away[q + 1]
        for p in range(NODES):
            if p == 0:
                value = after[0]
            elif p == NODES - 1:
                value = before[p]
            else:
                value = before[p] * after[p]
            value = value * factors[p]
            for part in range(2):
                wide[pl.ds(index * 512 + part * 16 + p, 16, stride=32), :] = value * turned[part]
        return carry

    lax.fori_loop(0, 8, source_step, 0)

    iota = lax.broadcasted_iota(jnp.int32, (16, 128), 0).astype(F32).astype(BF16)
    one = jnp.ones((16, 128), BF16)
    zero = jnp.zeros((16, 128), BF16)
    both = jnp.zeros((32, 128), BF16)

    def build(chunk, hot, spread):
        for k in range(16):
            sender = chunk * 16 + k
            lanes = slice(128 * k, 128 * (k + 1))

            def row(number, height):
                value = cells[number, pl.ds(sender, 1), :]
                return jnp.broadcast_to(value, (height, 128)).astype(BF16)

            value = wide[pl.ds(pl.multiple_of(sender * 32, 32), 32), :].astype(BF16)
            cell = row(0, 32)
            for c in range(16):
                spread[32 * c : 32 * (c + 1), lanes] = jnp.where(
                    cell == jnp.full((32, 128), c, BF16), value, both
                )
            inside = jnp.where(row(2, 16) == iota, one, zero)
            above = row(1, 16)
            for c in range(16):
                hot[16 * c : 16 * (c + 1), lanes] = jnp.where(
                    above == jnp.full((16, 128), c, BF16), inside, zero
                )

    def add(hot, spread):
        grid[...] += lax.dot_general(
            hot[...], spread[...], (((1,), (1,)), ((), ())), preferred_element_type=F32
        )

    grid[...] = jnp.zeros_like(grid)
    build(0, hots[0], spreads[0])

    def spread_step(index, carry):
        add(hots[0], spreads[0])
        build(2 * index + 1, hots[1], spreads[1])
        add(hots[1], spreads[1])
        build(jnp.minimum(2 * index + 2, 7), hots[0], spreads[0])
        return carry

    lax.fori_loop(0, 4, spread_step, 0)

    grid_high, grid_low = split(grid[...])
    fetch_second.wait()
    for part in range(2):
        basis = second[512 * part : 512 * (part + 1), :]
        result = jnp.dot(grid_high, basis, preferred_element_type=F32)
        rest = jnp.dot(grid_low, basis[:, :BOX_NODES], preferred_element_type=F32)
        result = result[:, :BOX_NODES] + (result[:, BOX_NODES:] + rest)
        for group in range(32):
            state[group, part] = result[8 * group : 8 * group + 8, :]


def pieces(result):
    for child in range(4):
        for row in range(8):
            start = child * 128 + row * 8
            yield bits(child, 2), bits(row, 3), [
                result[start + 64 * part : start + 64 * part + 8, :] for part in range(2)
            ]


def halves(value):
    return value[:, :128], value[:, 128:]


def inner_kernel(
    arrived,
    mask,
    table_far,
    matrix_far,
    out,
    second,
    matrix,
    table,
    arrive,
    wide,
    cells,
    hots,
    spreads,
    grid,
    state,
    turned,
    high,
    low,
):
    fetch_second = pltpu.make_async_copy(matrix_far.at[pl.ds(1536, 1024)], second, arrive.at[4])
    fetch_second.start()
    fetches = [fetch_level(table_far, table, arrive, k) for k in range(4)]
    for fetch in fetches:
        fetch.start()
    fetch_matrix = pltpu.make_async_copy(matrix_far.at[pl.ds(0, 1024)], matrix, arrive.at[5])
    fetch_matrix.start()
    deposit(arrived, mask, second, fetch_second, state, wide, cells, hots, spreads, grid)

    def run(number, read):
        return level(
            read,
            table,
            64 * (number - 1),
            high,
            low,
            matrix,
            4,
            8,
            fetches[number - 1 : number],
            fetch_matrix if number == 1 else None,
        )

    def read(group, part):
        return state[group, part]

    for (x, y), (r0, r1, r2), values in pieces(run(1, read)):
        for part in range(2):
            state[(2 * r0 + r1) * 8 + x * 4 + y * 2 + r2, part] = values[part]

    for (x, y), (r0, r1, r2), values in pieces(run(2, read)):
        start = ((r2 * 2 + x) * 8 + r0 * 4 + r1 * 2 + y) * 8
        for part in range(2):
            for half, value in enumerate(halves(values[part])):
                turned[2 * part + half, start : start + 8, :] = value

    def across(group, part):
        b2x, b2y, b3x, b3y, t2x = bits(group, 5)
        start = (b3y * 2 + t2x) * 64 + b2x * 4 + b2y * 2 + b3x
        return jnp.concatenate(
            [turned.at[2 * part + half][pl.ds(start, 8, stride=8), :] for half in range(2)], axis=1
        )

    for (x, y), (r0, r1, r2), values in pieces(run(3, across)):
        for part in range(2):
            state[(2 * r0 + r1) * 8 + x * 4 + y * 2 + r2, part] = values[part]

    for (x, y), (r0, r1, r2), values in pieces(run(4, read)):
        device = r2 * 32 + r0 * 16 + x * 8 + r1
        for upper in range(2):
            for part in range(2):
                for half, value in enumerate(halves(values[part])):
                    start = (device + 64 * upper) * 8 + y * 4 + half * 2 + part
                    out[pl.ds(start, 4, stride=16), :] = value[4 * upper : 4 * upper + 4]


def outer_kernel(
    arrived, table_far, matrix_far, out, table, matrix, last, arrive, state, turned, high, low
):
    first = [
        pltpu.make_async_copy(
            table_far.at[pl.ds(16 * k, 16)], table.at[pl.ds(16 * k, 16)], arrive.at[6 + k]
        )
        for k in range(4)
    ]
    fetches = [
        fetch_level(table_far, table, arrive, k, 64 if k < 3 else 48) for k in range(1, 4)
    ]
    fetch_matrix = pltpu.make_async_copy(matrix_far.at[pl.ds(0, 1024)], matrix, arrive.at[5])
    fetch_last = pltpu.make_async_copy(matrix_far.at[pl.ds(1024, 512)], last, arrive.at[4])
    for fetch in first + [fetch_matrix] + fetches + [fetch_last]:
        fetch.start()

    def first_read(group, part):
        i2, j3, i1, i0, j2 = bits(group, 5)
        source = i2 * 64 + i1 * 32 + i0 * 16 + j3 * 8 + j2 * 4
        return jnp.concatenate(
            [
                arrived[pl.ds(source * 8 + half * 2 + part, 8, stride=4), :]
                for half in range(2)
            ],
            axis=1,
        )

    def run(number, read):
        return level(
            read,
            table,
            64 * (number - 5),
            high,
            low,
            matrix,
            4,
            8,
            first if number == 5 else fetches[number - 6 : number - 5],
            fetch_matrix if number == 5 else None,
        )

    def read(group, part):
        return state[group, part]

    for (x, y), (i1, i0, j2), values in pieces(run(5, first_read)):
        for part in range(2):
            state[(2 * i1 + j2) * 8 + x * 4 + y * 2 + i0, part] = values[part]

    for (x, y), (r0, r1, i0), values in pieces(run(6, read)):
        start = ((i0 * 2 + x) * 8 + r0 * 4 + r1 * 2 + y) * 8
        for part in range(2):
            for half, value in enumerate(halves(values[part])):
                turned[2 * part + half, start : start + 8, :] = value

    def across(group, part):
        i0, j1, t6x, j0, pair = bits(group, 5)
        start = (i0 * 2 + t6x) * 64 + j1 * 4 + j0 * 2 + pair
        return jnp.concatenate(
            [turned.at[2 * part + half][pl.ds(start, 8, stride=8), :] for half in range(2)], axis=1
        )

    for (x, y), (t6x, j0, pair), values in pieces(run(7, across)):
        for part in range(2):
            state[j0 * 16 + x * 8 + y * 4 + t6x * 2 + pair, part] = values[part]

    result = level(read, table, 192, high, low, last, 2, 16, fetches[2:], fetch_last)
    for child in range(2):
        for row in range(16):
            t7x, t7y, t6x, pair = bits(row, 4)
            start = child * 256 + row * 8
            line = 224 + child * 8 + row // 2
            cosine = table[line, 0, 8 * (row % 2) : 8 * (row % 2) + 8, :]
            sine = table[line, 1, 8 * (row % 2) : 8 * (row % 2) + 8, :]
            real = result[start : start + 8, :]
            imaginary = result[start + 128 : start + 136, :]
            device = t6x * 32 + t7x * 16 + t7y * 2 + child
            for part, whole in enumerate(
                (real * cosine + imaginary * sine, imaginary * cosine - real * sine)
            ):
                for half, value in enumerate(halves(whole)):
                    for upper in range(2):
                        place = (device + 64 * upper) * 8 + pair * 4 + half * 2 + part
                        out[pl.ds(place, 4, stride=32), :] = value[4 * upper : 4 * upper + 4]


def vmem(count):
    return [pl.BlockSpec(memory_space=pltpu.VMEM)] * count


def smem(count):
    return [pl.BlockSpec(memory_space=pltpu.SMEM)] * count


def far(count):
    return [pl.BlockSpec(memory_space=pltpu.HBM)] * count


def payload_kernel(place_far, amp_far, out_far, place, amp, out, arrive, leave):
    fetches = [
        pltpu.make_async_copy(place_far, place, arrive.at[0]),
        pltpu.make_async_copy(amp_far, amp, arrive.at[1]),
    ]
    for fetch in fetches:
        fetch.start()
    for fetch in fetches:
        fetch.wait()
    for k in range(2):
        out[pl.ds(k, DEVICES, stride=4), :] = place[k].astype(F32)
        out[pl.ds(2 + k, DEVICES, stride=4), :] = amp[k]
    store = pltpu.make_async_copy(out, out_far, leave)
    store.start()
    store.wait()


def make_payload(place, amp):
    return pl.pallas_call(
        payload_kernel,
        out_shape=jax.ShapeDtypeStruct((4 * DEVICES, 128), F32),
        in_specs=far(2),
        out_specs=far(1)[0],
        scratch_shapes=[
            pltpu.VMEM((2, DEVICES, 128), jnp.int32),
            pltpu.VMEM((2, DEVICES, 128), F32),
            pltpu.VMEM((4 * DEVICES, 128), F32),
            pltpu.SemaphoreType.DMA((2,)),
            pltpu.SemaphoreType.DMA,
        ],
        name="payload",
        compiler_params=pltpu.CompilerParams(vmem_limit_bytes=60 << 20),
    )(place, amp)


def inner_turns(block, slots):
    speeds = np.repeat(inner_speeds()[:, None], 128, axis=1)
    return pl.pallas_call(
        inner_turns_kernel,
        out_shape=[
            jax.ShapeDtypeStruct((128, 128), F32),
            jax.ShapeDtypeStruct((256, 2, 16, 256), F32),
        ],
        in_specs=smem(1) + far(3),
        out_specs=vmem(1) + far(1),
        scratch_shapes=[
            pltpu.VMEM((64, 256), jnp.int32),
            pltpu.VMEM((16, 256), F32),
            pltpu.VMEM((1024, 128), F32),
            pltpu.VMEM((256, 2, 16, 256), F32),
            pltpu.VMEM((2, 128, 128), F32),
            pltpu.VMEM((128, 16384), BF16),
            pltpu.VMEM((128, 16384), BF16),
            pltpu.VMEM((128, 128), F32),
            pltpu.SemaphoreType.DMA((3,)),
            pltpu.SemaphoreType.DMA((4,)),
        ],
        name="inner_turns",
        compiler_params=pltpu.CompilerParams(vmem_limit_bytes=60 << 20),
    )(block, slots, jnp.asarray(node_tables()), jnp.asarray(speeds))


def outer_turns(speeds):
    return pl.pallas_call(
        outer_turns_kernel,
        out_shape=jax.ShapeDtypeStruct((240, 2, 16, 256), F32),
        in_specs=vmem(2),
        out_specs=far(1)[0],
        scratch_shapes=[
            pltpu.VMEM((240, 2, 16, 256), F32),
            pltpu.SemaphoreType.DMA((4,)),
        ],
        name="outer_turns",
        compiler_params=pltpu.CompilerParams(vmem_limit_bytes=52 << 20),
    )(jnp.asarray(node_tables()), speeds)


LEVEL_SCRATCH = [
    pltpu.VMEM((32, 2, 8, 256), F32),
    pltpu.VMEM((4, 256, 128), F32),
    pltpu.VMEM((512, 1024), BF16),
    pltpu.VMEM((512, 1024), BF16),
]


def inner_levels(arrived, mask, table):
    return pl.pallas_call(
        inner_kernel,
        out_shape=jax.ShapeDtypeStruct((1024, 128), F32),
        in_specs=vmem(2) + far(2),
        out_specs=vmem(1)[0],
        scratch_shapes=[
            pltpu.VMEM((1024, 512), BF16),
            pltpu.VMEM((1024, 512), BF16),
            pltpu.VMEM((256, 2, 16, 256), F32),
            pltpu.SemaphoreType.DMA((6,)),
            pltpu.VMEM((4096, 128), F32),
            pltpu.VMEM((3, 128, 128), F32),
            [pltpu.VMEM((256, 2048), BF16)] * 2,
            [pltpu.VMEM((512, 2048), BF16)] * 2,
            pltpu.VMEM((256, 512), F32),
        ]
        + LEVEL_SCRATCH,
        name="inner",
        compiler_params=pltpu.CompilerParams(vmem_limit_bytes=52 << 20),
    )(
        arrived,
        mask,
        table,
        jnp.asarray(matrices()),
    )


def outer_levels(arrived, table):
    return pl.pallas_call(
        outer_kernel,
        out_shape=jax.ShapeDtypeStruct((1024, 128), F32),
        in_specs=vmem(1) + far(2),
        out_specs=vmem(1)[0],
        scratch_shapes=[
            pltpu.VMEM((240, 2, 16, 256), F32),
            pltpu.VMEM((1024, 512), BF16),
            pltpu.VMEM((512, 512), BF16),
            pltpu.SemaphoreType.DMA((10,)),
        ]
        + LEVEL_SCRATCH,
        name="outer",
        compiler_params=pltpu.CompilerParams(vmem_limit_bytes=52 << 20),
    )(
        arrived,
        table,
        jnp.asarray(matrices()),
    )


def reverse_bits(number, bit_count):
    result = jnp.zeros_like(number)
    for position in range(bit_count):
        result = result + jnp.left_shift(
            jnp.bitwise_and(jnp.right_shift(number, position), 1), bit_count - 1 - position
        )
    return result


def exchange(array):
    return lax.all_to_all(array, ("bx", "by"), split_axis=0, concat_axis=0, tiled=True)


def shards(src_pos, src_amp, box_slots):
    column = lax.axis_index("bx")
    row = lax.axis_index("by")
    device = column * BY + row
    block = jnp.stack([reverse_bits(column, 3), reverse_bits(row, 4)]).astype(jnp.int32)
    payload = make_payload(src_pos.reshape(2, DEVICES, 128), src_amp.reshape(2, DEVICES, 128))
    arrived = exchange(payload.reshape(DEVICES, 4, 128)).reshape(512, 128)
    mask, table = inner_turns(block, box_slots[0].T)
    arrived, mask, table = lax.optimization_barrier((arrived, mask, table))
    weights = inner_levels(arrived, mask, table)
    weights = exchange(weights.reshape(DEVICES, 8, 128)).reshape(1024, 128)
    speeds = lax.dynamic_index_in_dim(jnp.asarray(outer_speeds()), device, 0, keepdims=False)
    speeds = jnp.broadcast_to(speeds[:, None], (7 * 256, 128))
    weights = outer_levels(weights, outer_turns(speeds))
    weights = exchange(weights.reshape(DEVICES, 8, 128))
    weights = weights.reshape(LEAVES, LEAVES, 2, 2, 128)
    weights = jnp.concatenate([weights[:, :, 0], weights[:, :, 1]], axis=-1)
    return weights.reshape(LEAVES, 1, LEAVES, 1, 2, BOX_NODES)


def solution(mesh):
    return jax.shard_map(
        shards,
        mesh=mesh,
        in_specs=(
            P(None, ("bx", "by"), None),
            P(None, ("bx", "by"), None),
            P(("bx", "by"), None, None),
        ),
        out_specs=P(None, "bx", None, "by", None, None),
        check_vma=False,
    )
```

```python
import functools
import math

import jax
import jax.numpy as jnp
import numpy as np
from jax import lax
from jax.experimental import pallas as pl
from jax.experimental.pallas import tpu as pltpu
from jax.sharding import PartitionSpec as P

NODES = 16
BOX_NODES = 256
DEVICES = 128
LEAVES = 16
BX = 8
BY = 16
BAND = 1024
F32 = jnp.float32
BF16 = jnp.bfloat16
ROUNDER = 12582912.0
SIN = (6.28305581, -41.33121471, 81.36682035, -74.47802935, 32.78144238)
COS = (0.99995995, -19.73105034, 64.67355678, -82.40422428, 45.64775943)


def chebyshev_points(point_count):
    indices = np.arange(point_count)
    return (1.0 - np.cos(np.pi * (2 * indices + 1) / (2 * point_count))) / 2.0


def lagrange_matrix(locations):
    points = chebyshev_points(NODES)
    matrix = np.ones((len(locations), NODES))
    for own in range(NODES):
        for other in range(NODES):
            if other != own:
                matrix[:, own] *= (locations - points[other]) / (points[own] - points[other])
    return matrix


def child_matrix(halves, child):
    if halves == 1:
        return np.eye(NODES)
    return lagrange_matrix((child + chebyshev_points(NODES)) / 2.0)


def stacked_matrix(halves_first, halves_second):
    pieces = [
        np.kron(child_matrix(halves_first, a), child_matrix(halves_second, b))
        for a in range(halves_first)
        for b in range(halves_second)
    ]
    return np.concatenate(pieces, axis=0)


def two_parts(matrix):
    exact = np.asarray(matrix, np.float32)
    high = exact.astype(jnp.bfloat16)
    low = (exact - high.astype(np.float32)).astype(jnp.bfloat16)
    return high, low


def velocity(first, second):
    return (2.0 + np.sin(2 * np.pi * first) * np.sin(2 * np.pi * second)) / 8.0


def bits(value, count):
    return [(value >> (count - 1 - k)) & 1 for k in range(count)]


def speed_change(first, second, level, split_first=True):
    count_second = 2.0**level
    count_first = 2.0 ** (level if split_first else level - 1)
    new = velocity((first + 0.5) / count_first, (second + 0.5) / count_second)
    above_first = first >> 1 if split_first else first
    old = velocity(
        (above_first + 0.5) / 2.0 ** (level - 1), ((second >> 1) + 0.5) / 2.0 ** (level - 1)
    )
    return new - old


def inner_speeds():
    table = np.zeros((4, 4, 8, 8))
    for child in range(4):
        x, y = bits(child, 2)
        for row in range(8):
            r0, r1, r2 = bits(row, 3)
            for sub in range(8):
                s0, s1, s2 = bits(sub, 3)
                table[0, child, row, sub] = speed_change(x, y, 1)
                table[1, child, row, sub] = speed_change(2 * r0 + x, 2 * r1 + y, 2)
                first, second = 2 * s0 + r2, 2 * s1 + s2
                table[2, child, row, sub] = speed_change(2 * first + x, 2 * second + y, 3)
                first, second = 2 * first + r0, 2 * second + r1
                table[3, child, row, sub] = speed_change(2 * first + x, 2 * second + y, 4)
    return table.reshape(1024).astype(np.float32)


def outer_speeds():
    tables = np.zeros((DEVICES, 7, 256))
    for device in range(DEVICES):
        coarse_first = device >> 3
        for child in range(4):
            x, y = bits(child, 2)
            for row in range(8):
                r0, r1, r2 = bits(row, 3)
                for sub in range(8):
                    s0, s1, s2 = bits(sub, 3)
                    place = child * 64 + row * 8 + sub
                    second = 2 * (device & 7) + s2
                    tables[device, 0, place] = speed_change(
                        2 * coarse_first + x, 2 * second + y, 5
                    )
                    tables[device, 1, place] = speed_change(
                        4 * coarse_first + 2 * r0 + x, 4 * second + 2 * r1 + y, 6
                    )
                    second = 2 * (device & 7) + r2
                    tables[device, 2, place] = speed_change(
                        8 * coarse_first + 4 * s0 + 2 * r0 + x,
                        8 * second + 4 * s1 + 2 * s2 + y,
                        7,
                    )
        for child in range(2):
            for row in range(16):
                r0, r1, r2, r3 = bits(row, 4)
                for sub in range(8):
                    s0, s1, s2 = bits(sub, 3)
                    place = child * 128 + row * 8 + sub
                    first = 8 * coarse_first + 4 * s0 + 2 * r2 + r0
                    second = 2 * (device & 7) + r3
                    second = 16 * second + 8 * s1 + 4 * s2 + 2 * r1 + child
                    tables[device, 3, place] = speed_change(first, second, 8, False)
                    tables[device, 4, place] = velocity((first + 0.5) / 128, (second + 0.5) / 256)
                    tables[device, 5, place] = 8 * (first + 0.5)
                    tables[device, 6, place] = 4 * (second + 0.5)
    return tables.reshape(DEVICES, 7 * 256).astype(np.float32)


def node_tables():
    points = chebyshev_points(NODES).astype(np.float32).astype(np.float64)
    first = np.repeat(points, NODES)
    second = np.tile(points, NODES)
    rows = np.zeros((24, BOX_NODES))
    for child in range(4):
        x, y = bits(child, 2)
        turns = (2 * x - 1) * 2 * first + (2 * y - 1) * second
        rows[child] = turns - np.round(turns)
    for child in range(2):
        rows[4 + child] = (2 * child - 1) * second
    rows[6] = 2 * first
    rows[7] = second
    rows[8] = np.round(first * 8192) / 8192
    rows[9] = first - rows[8]
    rows[10] = np.round(second * 8192) / 8192
    rows[11] = second - rows[10]
    for child in range(2):
        rows[16 + 2 * child] = np.cos(2 * np.pi * rows[child])
        rows[17 + 2 * child] = np.sin(2 * np.pi * rows[child])
    rows[12] = BAND * np.sqrt(first * first + second * second)
    return rows.astype(np.float32)


def basis_factors():
    points = chebyshev_points(NODES)
    return [
        float(np.float32(1.0 / np.prod([points[own] - points[k] for k in range(NODES) if k != own])))
        for own in range(NODES)
    ]


def second_basis():
    small = lagrange_matrix((np.arange(16) + 0.5) / 16.0)
    whole = np.zeros((16, 32, 32, 16))
    for k in range(32):
        whole[:, k, k, :] = small
    return whole.reshape(512, 512)


def turn(turns):
    part = turns - ((turns + ROUNDER) - ROUNDER)
    square = part * part
    sine = SIN[4]
    cosine = COS[4]
    for k in (3, 2, 1, 0):
        sine = sine * square + SIN[k]
        cosine = cosine * square + COS[k]
    return cosine, sine * part


def split(value):
    high = value.astype(BF16)
    return high, (value - high.astype(F32)).astype(BF16)


def bit(value, place):
    return (value >> place) & 1


def make_turns(
    table, first_line, box, level_number, speeds, speed_row, node, base_row, children, rows, stores=()
):
    scale = 4.0 * 2.0 ** (level_number - 1)
    pairs = rows // 2

    def step(index, carry):
        source = index // pairs
        pair = lax.rem(index, pairs)
        radius = []
        for k in range(2):
            first, second = box(source, 2 * pair + k)
            along = first + node[6:7, :]
            across = second + node[7:8, :]
            radius.append(scale * jnp.sqrt(along * along + across * across))
        radius = jnp.concatenate([jnp.broadcast_to(value, (8, BOX_NODES)) for value in radius])
        for child in range(children):
            place = pl.multiple_of(speed_row + child * rows * 8 + pair * 16, 16)
            change = speeds[pl.ds(place, 16), :]
            change = jnp.concatenate([change, change], axis=1)
            cosine, sine = turn(change * radius + node[base_row + child : base_row + child + 1, :])
            line = first_line + index * children + child
            table[line, 0] = cosine
            table[line, 1] = sine
        return carry

    if not stores:
        lax.fori_loop(0, (4 if children == 4 else 2) * pairs, step, 0)
    for source, store in enumerate(stores):
        lax.fori_loop(source * pairs, (source + 1) * pairs, step, 0)
        store.start()


def make_first_turns(table, box, node):
    def step(index, carry):
        radius = []
        for k in range(2):
            first, second = box(index // 4, 2 * (index % 4) + k)
            along = first + node[6:7, :]
            across = second + node[7:8, :]
            radius.append(0.5 * jnp.sqrt(along * along + across * across))
        cosine, sine = turn(jnp.concatenate(radius))
        for kind in range(2):
            base_cosine = node[16 + 2 * kind : 17 + 2 * kind, :]
            base_sine = node[17 + 2 * kind : 18 + 2 * kind, :]
            cosines = base_cosine * cosine
            sines = base_sine * sine
            mixed = base_sine * cosine
            other = base_cosine * sine
            line = 4 * index + kind
            mirror = 4 * index + 3 - kind
            if kind == 0:
                table[line, 0] = cosines - sines
                table[line, 1] = mixed + other
                table[mirror, 0] = cosines + sines
                table[mirror, 1] = other - mixed
            else:
                table[line, 0] = cosines + sines
                table[line, 1] = mixed - other
                table[mirror, 0] = cosines - sines
                table[mirror, 1] = -mixed - other
        return carry

    lax.fori_loop(0, 16, step, 0)


def level(read, table, first_line, high, low, matrix, children, rows, ready, matrix_ready=None):
    sources = 4 if children == 4 else 2
    pairs = rows // 2
    columns = sources * BOX_NODES
    results = []
    for first in range(0, children, children // 2):
        chosen = range(first, first + children // 2)
        for source in range(sources):
            lanes = slice(source * BOX_NODES, (source + 1) * BOX_NODES)
            if first == 0 and source < len(ready):
                ready[source].wait()
            for pair in range(pairs):
                group = source * rows + 2 * pair
                real, imaginary = (
                    jnp.concatenate([read(group, part), read(group + 1, part)])
                    for part in range(2)
                )
                for child in chosen:
                    line = first_line + (source * pairs + pair) * children + child
                    cosine = table[line, 0]
                    sine = table[line, 1]
                    for part, value in enumerate(
                        (real * cosine - imaginary * sine, real * sine + imaginary * cosine)
                    ):
                        place = (child * 2 + part) * rows * 8 + pair * 16
                        value_high, value_low = split(value)
                        high[place : place + 16, lanes] = value_high
                        low[place : place + 16, lanes] = value_low
        if first == 0 and matrix_ready is not None:
            matrix_ready.wait()
        places = slice(first * 2 * rows * 8, (first + children // 2) * 2 * rows * 8)
        both = jnp.dot(high[places, :columns], matrix[...], preferred_element_type=F32)
        rest = jnp.dot(
            low[places, :columns], matrix[:, :BOX_NODES], preferred_element_type=F32
        )
        results.append(both[:, :BOX_NODES] + (both[:, BOX_NODES:] + rest))
    return jnp.concatenate(results)


def matrices():
    basis = second_basis()
    rows = [
        stacked_matrix(2, 2),
        stacked_matrix(1, 2),
        basis[:, :256],
        basis[:, 256:],
    ]
    return np.concatenate(two_parts(np.concatenate(rows)), axis=1)


def sub_bits():
    row = lax.broadcasted_iota(jnp.int32, (8, BOX_NODES), 0)
    return [bit(row, 2 - k).astype(F32) for k in range(3)]


def find_mask(slots, table, entries, high_hot, low_hot, total):
    iota = lax.broadcasted_iota(jnp.int32, (16, 128), 0).astype(F32)
    rows = [(iota + 16.0 * k).astype(BF16) for k in range(8)]
    one = jnp.ones((16, 128), BF16)
    zero = jnp.zeros((16, 128), BF16)
    block = jnp.concatenate([slots[:, :128], slots[:, 128:]], axis=0)
    entries[0] = (block >> 7).astype(F32)
    entries[1] = (block & 127).astype(F32)

    def step(index, carry):
        for source, hot in enumerate((high_hot, low_hot)):
            for side in range(2):
                start = pl.multiple_of(index * 8 + 64 * side, 8)
                block = entries[source, pl.ds(start, 8), :]
                for k in range(8):
                    value = jnp.broadcast_to(block[k : k + 1], (16, 128)).astype(BF16)
                    lanes = pl.ds(pl.multiple_of(index * 1024 + 128 * k, 128), 128)
                    for place in range(8):
                        line = 128 * side + 16 * place
                        hot[line : line + 16, lanes] = jnp.where(value == rows[place], one, zero)
        return carry

    lax.fori_loop(0, 8, step, 0)
    total[...] = jnp.zeros_like(total)

    def add(index, carry):
        lanes = pl.ds(pl.multiple_of(index * 4096, 4096), 4096)
        total[...] += lax.dot_general(
            high_hot[:, lanes],
            low_hot[:, lanes],
            (((1,), (1,)), ((), ())),
            preferred_element_type=F32,
        )
        return carry

    lax.fori_loop(0, 2, add, 0)
    mask = jnp.where(total[:128, :128] + total[128:, 128:] > 0.5, 1.0, 0.0)
    for k in range(8):
        lanes = slice(128 * (k % 2), 128 * (k % 2 + 1))
        table[256 + k // 4, k // 2 % 2, :, lanes] = mask[16 * k : 16 * (k + 1)]


def store_level(table, table_far, leave, index, size=64, first=0):
    lines = pl.ds(size * index, size)
    place = leave.at[index if first == 0 else first + index % 4]
    return pltpu.make_async_copy(table.at[lines], table_far.at[lines], place)


def fetch_level(table_far, table, arrive, index, size=64):
    lines = pl.ds(64 * index, size)
    return pltpu.make_async_copy(table_far.at[lines], table.at[lines], arrive.at[index])


def fetch_mask_lines(table_far, table, place):
    lines = pl.ds(256, 2)
    return pltpu.make_async_copy(table_far.at[lines], table.at[lines], place)


def inner_turns_kernel(
    block_first_ref,
    block_second_ref,
    slots_far,
    node_far,
    speeds_far,
    table_far,
    slots,
    node,
    speeds,
    table,
    entries,
    high_hot,
    low_hot,
    total,
    arrive,
    leave,
):
    fetches = [
        pltpu.make_async_copy(far, near, arrive.at[k])
        for k, (far, near) in enumerate(
            ((slots_far, slots), (node_far, node), (speeds_far, speeds))
        )
    ]
    for fetch in fetches:
        fetch.start()
    fetches[0].wait()
    find_mask(slots, table, entries, high_hot, low_hot, total)
    for fetch in fetches[1:]:
        fetch.wait()
    stores = [store_level(table, table_far, leave, k) for k in range(3)]
    stores += [store_level(table, table_far, leave, 12 + k, 16, 3) for k in range(4)]
    store_mask = store_level(table, table_far, leave, 128, 2, 7)
    store_mask.start()
    sub = sub_bits()
    block_first = block_first_ref[0]
    block_second = block_second_ref[0]

    def box(source, row):
        first = block_first * 16 + bit(source, 1) + 2 * bit(row, 2)
        second = block_second * 16 + bit(source, 0) + 2 * bit(row, 1) + 8 * bit(row, 0)
        return (
            2.0 * first.astype(F32) + (8.0 * sub[0] + 16.0 * sub[2]),
            second.astype(F32) + 4.0 * sub[1],
        )

    make_first_turns(table, box, node)
    stores[0].start()

    def box(source, row):
        first = block_first * 8 + bit(source, 1)
        second = block_second * 8 + bit(source, 0) + 4 * bit(row, 0)
        return (
            2.0 * first.astype(F32) + (4.0 * sub[0] + 8.0 * sub[2]),
            second.astype(F32) + 2.0 * sub[1],
        )

    make_turns(table, 64, box, 2, speeds, 256, node, 0, 4, 8)
    stores[1].start()

    def box(source, row):
        first = block_first * 4 + bit(source, 1) + 2 * bit(row, 2)
        second = block_second * 4 + bit(source, 0) + 2 * bit(row, 1)
        return 2.0 * first.astype(F32), second.astype(F32)

    make_turns(table, 128, box, 3, speeds, 512, node, 0, 4, 8)
    stores[2].start()

    def box(source, row):
        first = block_first * 2 + bit(source, 1)
        second = block_second * 2 + bit(source, 0)
        return 2.0 * first.astype(F32), second.astype(F32)

    make_turns(table, 192, box, 4, speeds, 768, node, 0, 4, 8, stores[3:])
    for store in stores + [store_mask]:
        store.wait()


def outer_turns_kernel(node, speeds, table_far, table, leave):
    stores = [store_level(table, table_far, leave, k) for k in range(3)]
    stores += [store_level(table, table_far, leave, 12 + k, 16, 3) for k in range(3)]
    sub = sub_bits()

    def box(source, row):
        first = bit(source, 1) + 2 * bit(row, 2) + 4 * bit(row, 1)
        second = bit(source, 0) + 2 * bit(row, 0)
        return 2.0 * first.astype(F32), second.astype(F32) + (4.0 * sub[0] + 8.0 * sub[1])

    make_turns(table, 0, box, 5, speeds, 0, node, 0, 4, 8)
    stores[0].start()

    def box(source, row):
        first = bit(source, 1) + 2 * bit(row, 0)
        second = bit(source, 0)
        return 2.0 * first.astype(F32), second.astype(F32) + (2.0 * sub[0] + 4.0 * sub[1])

    make_turns(table, 64, box, 6, speeds, 256, node, 0, 4, 8)
    stores[1].start()

    def box(source, row):
        first = bit(source, 1)
        second = bit(source, 0) + 2 * bit(row, 1)
        return 2.0 * first.astype(F32), second.astype(F32)

    make_turns(table, 128, box, 7, speeds, 512, node, 0, 4, 8)
    stores[2].start()

    def box(source, row):
        return jnp.float32(0.0), source.astype(F32)

    make_turns(table, 192, box, 8, speeds, 768, node, 4, 2, 16, stores[3:5])

    def last(index, carry):
        def column(table):
            value = speeds[pl.ds(pl.multiple_of(256 * table + index * 16, 16), 16), :]
            return jnp.concatenate([value, value], axis=1)

        first = column(5)
        second = column(6)
        turns = first * node[8:9, :]
        turns = turns - ((turns + ROUNDER) - ROUNDER)
        across = second * node[10:11, :]
        across = across - ((across + ROUNDER) - ROUNDER)
        around = column(4) * node[12:13, :]
        around = around - ((around + ROUNDER) - ROUNDER)
        turns = turns + across + around + first * node[9:10, :] + second * node[11:12, :]
        cosine, sine = turn(turns)
        table[224 + index, 0] = cosine
        table[224 + index, 1] = sine
        return carry

    lax.fori_loop(0, 16, last, 0)
    stores[5].start()
    for store in stores:
        store.wait()


def deposit(
    arrived, table, second, fetch_second, state, wide, cells, hots, spreads, grid
):
    points = [float(value) for value in chebyshev_points(NODES).astype(np.float32)]
    factors = basis_factors()

    def source_step(index, carry):
        rows = pl.ds(pl.multiple_of(index * 16, 16), 16)
        first, second, real, imaginary = (
            arrived[pl.ds(index * 64 + k, 16, stride=4), :] for k in range(4)
        )
        whole_first = first.astype(jnp.int32)
        whole_second = second.astype(jnp.int32)
        along = first + 0.5
        across = second + 0.5
        eighths = jnp.bitwise_and(whole_first + whole_second + 1, 7).astype(F32)
        cosine, sine = turn(
            0.125 * eighths + 0.0625 * jnp.sqrt(along * along + across * across)
        )
        lanes = pl.ds(pl.multiple_of(index % 2 * 128, 128), 128)
        live = table[256 + index // 4, index // 2 % 2, :, lanes]
        real = real * live
        imaginary = imaginary * live
        turned = (real * cosine - imaginary * sine, real * sine + imaginary * cosine)
        place = jnp.bitwise_and(whole_first, 31).astype(F32) * 0.03125 + 0.015625
        cells[0, rows, :] = jnp.bitwise_and(whole_second, 15).astype(F32)
        x = [bit(whole_first, 5 + k) for k in range(4)]
        y = [bit(whole_second, 4 + k) for k in range(4)]
        cells[1, rows, :] = (x[0] * 8 + y[0] * 4 + x[1] * 2 + y[1]).astype(F32)
        cells[2, rows, :] = (y[3] * 8 + x[2] * 4 + y[2] * 2 + x[3]).astype(F32)
        away = [place - value for value in points]
        before = [None] * NODES
        after = [None] * NODES
        for p in range(1, NODES):
            before[p] = away[p - 1] if p == 1 else before[p - 1] * away[p - 1]
            q = NODES - 1 - p
            after[q] = away[q + 1] if p == 1 else after[q + 1] * away[q + 1]
        for p in range(NODES):
            if p == 0:
                value = after[0]
            elif p == NODES - 1:
                value = before[p]
            else:
                value = before[p] * after[p]
            value = value * factors[p]
            for part in range(2):
                wide[pl.ds(index * 512 + part * 16 + p, 16, stride=32), :] = value * turned[part]
        return carry

    lax.fori_loop(0, 8, source_step, 0)

    iota = lax.broadcasted_iota(jnp.int32, (16, 128), 0).astype(F32).astype(BF16)
    one = jnp.ones((16, 128), BF16)
    zero = jnp.zeros((16, 128), BF16)

    def build(chunk, hot, spread):
        for k in range(16):
            sender = chunk * 16 + k
            lanes = slice(128 * k, 128 * (k + 1))

            def row(number, height):
                value = cells[number, pl.ds(sender, 1), :]
                return jnp.broadcast_to(value, (height, 128)).astype(BF16)

            value = wide[pl.ds(pl.multiple_of(sender * 32, 32), 32), :].astype(BF16)
            cell = row(0, 16)
            for c in range(16):
                chosen = cell == jnp.full((16, 128), c, BF16)
                for part in range(2):
                    spread[32 * c + 16 * part : 32 * c + 16 * (part + 1), lanes] = jnp.where(
                        chosen, value[16 * part : 16 * (part + 1)], zero
                    )
            inside = jnp.where(row(2, 16) == iota, one, zero)
            above = row(1, 16)
            for c in range(16):
                hot[16 * c : 16 * (c + 1), lanes] = jnp.where(
                    above == jnp.full((16, 128), c, BF16), inside, zero
                )

    def product(hot, spread):
        return lax.dot_general(
            hot[...], spread[...], (((1,), (1,)), ((), ())), preferred_element_type=F32
        )

    grid[...] = jnp.zeros_like(grid)

    def spread_step(index, carry):
        for k in range(2):
            build(2 * index + k, hots[k], spreads[k])
        parts = [product(hots[k], spreads[k]) for k in range(2)]
        grid[...] += parts[0] + parts[1]
        return carry

    lax.fori_loop(0, 4, spread_step, 0)

    grid_high, grid_low = split(grid[...])
    fetch_second.wait()
    for part in range(2):
        basis = second[512 * part : 512 * (part + 1), :]
        result = jnp.dot(grid_high, basis, preferred_element_type=F32)
        rest = jnp.dot(grid_low, basis[:, :BOX_NODES], preferred_element_type=F32)
        result = result[:, :BOX_NODES] + (result[:, BOX_NODES:] + rest)
        for group in range(32):
            state[group, part] = result[8 * group : 8 * group + 8, :]


def pieces(result):
    for child in range(4):
        for row in range(8):
            start = child * 128 + row * 8
            yield bits(child, 2), bits(row, 3), [
                result[start + 64 * part : start + 64 * part + 8, :] for part in range(2)
            ]


def halves(value):
    return value[:, :128], value[:, 128:]


def inner_kernel(
    arrived,
    table_far,
    matrix_far,
    out,
    second,
    matrix,
    table,
    arrive,
    wide,
    cells,
    hots,
    spreads,
    grid,
    state,
    turned,
    high,
    low,
):
    fetch_mask = fetch_mask_lines(table_far, table, arrive.at[6])
    fetch_mask.start()
    fetch_second = pltpu.make_async_copy(matrix_far.at[pl.ds(1536, 1024)], second, arrive.at[4])
    fetch_second.start()
    fetches = [fetch_level(table_far, table, arrive, k) for k in range(4)]
    for fetch in fetches:
        fetch.start()
    fetch_matrix = pltpu.make_async_copy(matrix_far.at[pl.ds(0, 1024)], matrix, arrive.at[5])
    fetch_matrix.start()
    fetch_mask.wait()
    deposit(arrived, table, second, fetch_second, state, wide, cells, hots, spreads, grid)

    def run(number, read):
        return level(
            read,
            table,
            64 * (number - 1),
            high,
            low,
            matrix,
            4,
            8,
            fetches[number - 1 : number],
            fetch_matrix if number == 1 else None,
        )

    def read(group, part):
        return state[group, part]

    for (x, y), (r0, r1, r2), values in pieces(run(1, read)):
        for part in range(2):
            state[(2 * r0 + r1) * 8 + x * 4 + y * 2 + r2, part] = values[part]

    for (x, y), (r0, r1, r2), values in pieces(run(2, read)):
        start = ((r2 * 2 + x) * 8 + r0 * 4 + r1 * 2 + y) * 8
        for part in range(2):
            for half, value in enumerate(halves(values[part])):
                turned[2 * part + half, start : start + 8, :] = value

    def across(group, part):
        b2x, b2y, b3x, b3y, t2x = bits(group, 5)
        start = (b3y * 2 + t2x) * 64 + b2x * 4 + b2y * 2 + b3x
        return jnp.concatenate(
            [turned.at[2 * part + half][pl.ds(start, 8, stride=8), :] for half in range(2)], axis=1
        )

    for (x, y), (r0, r1, r2), values in pieces(run(3, across)):
        for part in range(2):
            state[(2 * r0 + r1) * 8 + x * 4 + y * 2 + r2, part] = values[part]

    for (x, y), (r0, r1, r2), values in pieces(run(4, read)):
        device = r2 * 32 + r0 * 16 + x * 8 + r1
        for upper in range(2):
            for part in range(2):
                for half, value in enumerate(halves(values[part])):
                    start = (device + 64 * upper) * 8 + y * 4 + half * 2 + part
                    out[pl.ds(start, 4, stride=16), :] = value[4 * upper : 4 * upper + 4]


def outer_kernel(
    arrived, table_far, matrix_far, out, table, matrix, last, arrive, state, turned, high, low
):
    first = [
        pltpu.make_async_copy(
            table_far.at[pl.ds(16 * k, 16)], table.at[pl.ds(16 * k, 16)], arrive.at[6 + k]
        )
        for k in range(4)
    ]
    fetches = [
        fetch_level(table_far, table, arrive, k, 64 if k < 3 else 48) for k in range(1, 4)
    ]
    fetch_matrix = pltpu.make_async_copy(matrix_far.at[pl.ds(0, 1024)], matrix, arrive.at[5])
    fetch_last = pltpu.make_async_copy(matrix_far.at[pl.ds(1024, 512)], last, arrive.at[4])
    for fetch in first + [fetch_matrix] + fetches + [fetch_last]:
        fetch.start()

    def first_read(group, part):
        i2, j3, i1, i0, j2 = bits(group, 5)
        source = i2 * 64 + i1 * 32 + i0 * 16 + j3 * 8 + j2 * 4
        return jnp.concatenate(
            [
                arrived[pl.ds(source * 8 + half * 2 + part, 8, stride=4), :]
                for half in range(2)
            ],
            axis=1,
        )

    def run(number, read):
        return level(
            read,
            table,
            64 * (number - 5),
            high,
            low,
            matrix,
            4,
            8,
            first if number == 5 else fetches[number - 6 : number - 5],
            fetch_matrix if number == 5 else None,
        )

    def read(group, part):
        return state[group, part]

    for (x, y), (i1, i0, j2), values in pieces(run(5, first_read)):
        for part in range(2):
            state[(2 * i1 + j2) * 8 + x * 4 + y * 2 + i0, part] = values[part]

    for (x, y), (r0, r1, i0), values in pieces(run(6, read)):
        start = ((i0 * 2 + x) * 8 + r0 * 4 + r1 * 2 + y) * 8
        for part in range(2):
            for half, value in enumerate(halves(values[part])):
                turned[2 * part + half, start : start + 8, :] = value

    def across(group, part):
        i0, j1, t6x, j0, pair = bits(group, 5)
        start = (i0 * 2 + t6x) * 64 + j1 * 4 + j0 * 2 + pair
        return jnp.concatenate(
            [turned.at[2 * part + half][pl.ds(start, 8, stride=8), :] for half in range(2)], axis=1
        )

    for (x, y), (t6x, j0, pair), values in pieces(run(7, across)):
        for part in range(2):
            state[j0 * 16 + x * 8 + y * 4 + t6x * 2 + pair, part] = values[part]

    result = level(read, table, 192, high, low, last, 2, 16, fetches[2:], fetch_last)
    for child in range(2):
        for row in range(16):
            t7x, t7y, t6x, pair = bits(row, 4)
            start = child * 256 + row * 8
            line = 224 + child * 8 + row // 2
            cosine = table[line, 0, 8 * (row % 2) : 8 * (row % 2) + 8, :]
            sine = table[line, 1, 8 * (row % 2) : 8 * (row % 2) + 8, :]
            real = result[start : start + 8, :]
            imaginary = result[start + 128 : start + 136, :]
            device = t6x * 32 + t7x * 16 + t7y * 2 + child
            for part, whole in enumerate(
                (real * cosine + imaginary * sine, imaginary * cosine - real * sine)
            ):
                for half, value in enumerate(halves(whole)):
                    for upper in range(2):
                        place = (device + 64 * upper) * 8 + pair * 4 + half * 2 + part
                        out[pl.ds(place, 4, stride=32), :] = value[4 * upper : 4 * upper + 4]


def vmem(count):
    return [pl.BlockSpec(memory_space=pltpu.VMEM)] * count


def smem(count):
    return [pl.BlockSpec(memory_space=pltpu.SMEM)] * count


def far(count):
    return [pl.BlockSpec(memory_space=pltpu.HBM)] * count


def payload_kernel(place_far, amp_far, out_far, place, amp, out, arrive, leave):
    fetches = [
        pltpu.make_async_copy(place_far, place, arrive.at[0]),
        pltpu.make_async_copy(amp_far, amp, arrive.at[1]),
    ]
    for fetch in fetches:
        fetch.start()
    for fetch in fetches:
        fetch.wait()
    for k in range(2):
        out[pl.ds(k, DEVICES, stride=4), :] = place[k].astype(F32)
        out[pl.ds(2 + k, DEVICES, stride=4), :] = amp[k]
    store = pltpu.make_async_copy(out, out_far, leave)
    store.start()
    store.wait()


def make_payload(place, amp):
    return pl.pallas_call(
        payload_kernel,
        out_shape=jax.ShapeDtypeStruct((4 * DEVICES, 128), F32),
        in_specs=far(2),
        out_specs=far(1)[0],
        scratch_shapes=[
            pltpu.VMEM((2, DEVICES, 128), jnp.int32),
            pltpu.VMEM((2, DEVICES, 128), F32),
            pltpu.VMEM((4 * DEVICES, 128), F32),
            pltpu.SemaphoreType.DMA((2,)),
            pltpu.SemaphoreType.DMA,
        ],
        name="payload",
        compiler_params=pltpu.CompilerParams(vmem_limit_bytes=60 << 20),
    )(place, amp)


def inner_turns(block_first, block_second, slots):
    speeds = np.repeat(inner_speeds()[:, None], 128, axis=1)
    return pl.pallas_call(
        inner_turns_kernel,
        out_shape=jax.ShapeDtypeStruct((258, 2, 16, 256), F32),
        in_specs=smem(2) + far(3),
        out_specs=far(1)[0],
        scratch_shapes=[
            pltpu.VMEM((64, 256), jnp.int32),
            pltpu.VMEM((24, 256), F32),
            pltpu.VMEM((1024, 128), F32),
            pltpu.VMEM((258, 2, 16, 256), F32),
            pltpu.VMEM((2, 128, 128), F32),
            pltpu.VMEM((256, 8192), BF16),
            pltpu.VMEM((256, 8192), BF16),
            pltpu.VMEM((256, 256), F32),
            pltpu.SemaphoreType.DMA((3,)),
            pltpu.SemaphoreType.DMA((8,)),
        ],
        name="inner_turns",
        compiler_params=pltpu.CompilerParams(vmem_limit_bytes=60 << 20),
    )(block_first, block_second, slots, jnp.asarray(node_tables()), jnp.asarray(speeds))


def outer_turns(speeds):
    return pl.pallas_call(
        outer_turns_kernel,
        out_shape=jax.ShapeDtypeStruct((240, 2, 16, 256), F32),
        in_specs=vmem(2),
        out_specs=far(1)[0],
        scratch_shapes=[
            pltpu.VMEM((240, 2, 16, 256), F32),
            pltpu.SemaphoreType.DMA((7,)),
        ],
        name="outer_turns",
        compiler_params=pltpu.CompilerParams(vmem_limit_bytes=52 << 20),
    )(jnp.asarray(node_tables()), speeds)


LEVEL_SCRATCH = [
    pltpu.VMEM((32, 2, 8, 256), F32),
    pltpu.VMEM((4, 256, 128), F32),
    pltpu.VMEM((512, 1024), BF16),
    pltpu.VMEM((512, 1024), BF16),
]


def inner_levels(arrived, table):
    return pl.pallas_call(
        inner_kernel,
        out_shape=jax.ShapeDtypeStruct((1024, 128), F32),
        in_specs=vmem(1) + far(2),
        out_specs=vmem(1)[0],
        scratch_shapes=[
            pltpu.VMEM((1024, 512), BF16),
            pltpu.VMEM((1024, 512), BF16),
            pltpu.VMEM((258, 2, 16, 256), F32),
            pltpu.SemaphoreType.DMA((7,)),
            pltpu.VMEM((4096, 128), F32),
            pltpu.VMEM((3, 128, 128), F32),
            [pltpu.VMEM((256, 2048), BF16)] * 2,
            [pltpu.VMEM((512, 2048), BF16)] * 2,
            pltpu.VMEM((256, 512), F32),
        ]
        + LEVEL_SCRATCH,
        name="inner",
        compiler_params=pltpu.CompilerParams(vmem_limit_bytes=52 << 20),
    )(
        arrived,
        table,
        jnp.asarray(matrices()),
    )


def outer_levels(arrived, table):
    return pl.pallas_call(
        outer_kernel,
        out_shape=jax.ShapeDtypeStruct((1024, 128), F32),
        in_specs=vmem(1) + far(2),
        out_specs=vmem(1)[0],
        scratch_shapes=[
            pltpu.VMEM((240, 2, 16, 256), F32),
            pltpu.VMEM((1024, 512), BF16),
            pltpu.VMEM((512, 512), BF16),
            pltpu.SemaphoreType.DMA((10,)),
        ]
        + LEVEL_SCRATCH,
        name="outer",
        compiler_params=pltpu.CompilerParams(vmem_limit_bytes=52 << 20),
    )(
        arrived,
        table,
        jnp.asarray(matrices()),
    )


def reverse_bits(number, bit_count):
    result = jnp.zeros_like(number)
    for position in range(bit_count):
        result = result + jnp.left_shift(
            jnp.bitwise_and(jnp.right_shift(number, position), 1), bit_count - 1 - position
        )
    return result


def exchange(array):
    return lax.all_to_all(array, ("bx", "by"), split_axis=0, concat_axis=0, tiled=True)


def shards(src_pos, src_amp, box_slots):
    column = lax.axis_index("bx")
    row = lax.axis_index("by")
    device = column * BY + row
    block_first = reverse_bits(column, 3).astype(jnp.int32).reshape(1)
    block_second = reverse_bits(row, 4).astype(jnp.int32).reshape(1)
    payload = make_payload(src_pos.reshape(2, DEVICES, 128), src_amp.reshape(2, DEVICES, 128))
    arrived = exchange(payload.reshape(DEVICES, 4, 128)).reshape(512, 128)
    table = inner_turns(block_first, block_second, box_slots[0].T)
    arrived, table = lax.optimization_barrier((arrived, table))
    weights = inner_levels(arrived, table)
    weights = exchange(weights.reshape(DEVICES, 8, 128)).reshape(1024, 128)
    speeds = lax.dynamic_index_in_dim(jnp.asarray(outer_speeds()), device, 0, keepdims=False)
    speeds = jnp.broadcast_to(speeds[:, None], (7 * 256, 128))
    weights = outer_levels(weights, outer_turns(speeds))
    weights = exchange(weights.reshape(DEVICES, 8, 128))
    weights = weights.reshape(LEAVES, LEAVES, 2, 2, 128)
    weights = jnp.concatenate([weights[:, :, 0], weights[:, :, 1]], axis=-1)
    return weights.reshape(LEAVES, 1, LEAVES, 1, 2, BOX_NODES)


def solution(mesh):
    return jax.shard_map(
        shards,
        mesh=mesh,
        in_specs=(
            P(None, ("bx", "by"), None),
            P(None, ("bx", "by"), None),
            P(("bx", "by"), None, None),
        ),
        out_specs=P(None, "bx", None, "by", None, None),
        check_vma=False,
    )
```

```python
import functools
import math

import jax
import jax.numpy as jnp
import numpy as np
from jax import lax
from jax.experimental import pallas as pl
from jax.experimental.pallas import tpu as pltpu
from jax.sharding import PartitionSpec as P

NODES = 16
BOX_NODES = 256
DEVICES = 128
LEAVES = 16
BX = 8
BY = 16
BAND = 1024
F32 = jnp.float32
BF16 = jnp.bfloat16
ROUNDER = 12582912.0
SIN = (6.28305581, -41.33121471, 81.36682035, -74.47802935, 32.78144238)
COS = (0.99995995, -19.73105034, 64.67355678, -82.40422428, 45.64775943)


def chebyshev_points(point_count):
    indices = np.arange(point_count)
    return (1.0 - np.cos(np.pi * (2 * indices + 1) / (2 * point_count))) / 2.0


def lagrange_matrix(locations):
    points = chebyshev_points(NODES)
    matrix = np.ones((len(locations), NODES))
    for own in range(NODES):
        for other in range(NODES):
            if other != own:
                matrix[:, own] *= (locations - points[other]) / (points[own] - points[other])
    return matrix


def child_matrix(halves, child):
    if halves == 1:
        return np.eye(NODES)
    return lagrange_matrix((child + chebyshev_points(NODES)) / 2.0)


def stacked_matrix(halves_first, halves_second):
    pieces = [
        np.kron(child_matrix(halves_first, a), child_matrix(halves_second, b))
        for a in range(halves_first)
        for b in range(halves_second)
    ]
    return np.concatenate(pieces, axis=0)


def two_parts(matrix):
    exact = np.asarray(matrix, np.float32)
    high = exact.astype(jnp.bfloat16)
    low = (exact - high.astype(np.float32)).astype(jnp.bfloat16)
    return high, low


def velocity(first, second):
    return (2.0 + np.sin(2 * np.pi * first) * np.sin(2 * np.pi * second)) / 8.0


def bits(value, count):
    return [(value >> (count - 1 - k)) & 1 for k in range(count)]


def speed_change(first, second, level, split_first=True):
    count_second = 2.0**level
    count_first = 2.0 ** (level if split_first else level - 1)
    new = velocity((first + 0.5) / count_first, (second + 0.5) / count_second)
    above_first = first >> 1 if split_first else first
    old = velocity(
        (above_first + 0.5) / 2.0 ** (level - 1), ((second >> 1) + 0.5) / 2.0 ** (level - 1)
    )
    return new - old


def inner_speeds():
    table = np.zeros((4, 4, 8, 8))
    for child in range(4):
        x, y = bits(child, 2)
        for row in range(8):
            r0, r1, r2 = bits(row, 3)
            for sub in range(8):
                s0, s1, s2 = bits(sub, 3)
                table[0, child, row, sub] = speed_change(x, y, 1)
                table[1, child, row, sub] = speed_change(2 * r0 + x, 2 * r1 + y, 2)
                first, second = 2 * s0 + r2, 2 * s1 + s2
                table[2, child, row, sub] = speed_change(2 * first + x, 2 * second + y, 3)
                first, second = 2 * first + r0, 2 * second + r1
                table[3, child, row, sub] = speed_change(2 * first + x, 2 * second + y, 4)
    return table.reshape(1024).astype(np.float32)


def outer_speeds():
    tables = np.zeros((DEVICES, 7, 256))
    for device in range(DEVICES):
        coarse_first = device >> 3
        for child in range(4):
            x, y = bits(child, 2)
            for row in range(8):
                r0, r1, r2 = bits(row, 3)
                for sub in range(8):
                    s0, s1, s2 = bits(sub, 3)
                    place = child * 64 + row * 8 + sub
                    second = 2 * (device & 7) + s2
                    tables[device, 0, place] = speed_change(
                        2 * coarse_first + x, 2 * second + y, 5
                    )
                    tables[device, 1, place] = speed_change(
                        4 * coarse_first + 2 * r0 + x, 4 * second + 2 * r1 + y, 6
                    )
                    second = 2 * (device & 7) + r2
                    tables[device, 2, place] = speed_change(
                        8 * coarse_first + 4 * s0 + 2 * r0 + x,
                        8 * second + 4 * s1 + 2 * s2 + y,
                        7,
                    )
        for child in range(2):
            for row in range(16):
                r0, r1, r2, r3 = bits(row, 4)
                for sub in range(8):
                    s0, s1, s2 = bits(sub, 3)
                    place = child * 128 + row * 8 + sub
                    first = 8 * coarse_first + 4 * s0 + 2 * r2 + r0
                    second = 2 * (device & 7) + r3
                    second = 16 * second + 8 * s1 + 4 * s2 + 2 * r1 + child
                    tables[device, 3, place] = speed_change(first, second, 8, False)
                    tables[device, 4, place] = velocity((first + 0.5) / 128, (second + 0.5) / 256)
                    tables[device, 5, place] = 8 * (first + 0.5)
                    tables[device, 6, place] = 4 * (second + 0.5)
    return tables.reshape(DEVICES, 7 * 256).astype(np.float32)


def node_tables():
    points = chebyshev_points(NODES).astype(np.float32).astype(np.float64)
    first = np.repeat(points, NODES)
    second = np.tile(points, NODES)
    rows = np.zeros((24, BOX_NODES))
    for child in range(4):
        x, y = bits(child, 2)
        turns = (2 * x - 1) * 2 * first + (2 * y - 1) * second
        rows[child] = turns - np.round(turns)
    for child in range(2):
        rows[4 + child] = (2 * child - 1) * second
    rows[6] = 2 * first
    rows[7] = second
    rows[8] = np.round(first * 8192) / 8192
    rows[9] = first - rows[8]
    rows[10] = np.round(second * 8192) / 8192
    rows[11] = second - rows[10]
    for child in range(2):
        rows[16 + 2 * child] = np.cos(2 * np.pi * rows[child])
        rows[17 + 2 * child] = np.sin(2 * np.pi * rows[child])
    rows[12] = BAND * np.sqrt(first * first + second * second)
    return rows.astype(np.float32)


def basis_factors():
    points = chebyshev_points(NODES)
    return [
        float(np.float32(1.0 / np.prod([points[own] - points[k] for k in range(NODES) if k != own])))
        for own in range(NODES)
    ]


def second_basis():
    small = lagrange_matrix((np.arange(16) + 0.5) / 16.0)
    whole = np.zeros((16, 32, 32, 16))
    for k in range(32):
        whole[:, k, k, :] = small
    return whole.reshape(512, 512)


def turn(turns):
    part = turns - ((turns + ROUNDER) - ROUNDER)
    square = part * part
    sine = SIN[4]
    cosine = COS[4]
    for k in (3, 2, 1, 0):
        sine = sine * square + SIN[k]
        cosine = cosine * square + COS[k]
    return cosine, sine * part


def split(value):
    high = value.astype(BF16)
    return high, (value - high.astype(F32)).astype(BF16)


def bit(value, place):
    return (value >> place) & 1


def make_turns(
    table, first_line, box, level_number, speeds, speed_row, node, base_row, children, rows, stores=()
):
    scale = 4.0 * 2.0 ** (level_number - 1)
    pairs = rows // 2

    def step(index, carry):
        source = index // pairs
        pair = lax.rem(index, pairs)
        radius = []
        for k in range(2):
            first, second = box(source, 2 * pair + k)
            along = first + node[6:7, :]
            across = second + node[7:8, :]
            radius.append(scale * jnp.sqrt(along * along + across * across))
        radius = jnp.concatenate([jnp.broadcast_to(value, (8, BOX_NODES)) for value in radius])
        for child in range(children):
            place = pl.multiple_of(speed_row + child * rows * 8 + pair * 16, 16)
            change = speeds[pl.ds(place, 16), :]
            change = jnp.concatenate([change, change], axis=1)
            cosine, sine = turn(change * radius + node[base_row + child : base_row + child + 1, :])
            line = first_line + index * children + child
            table[line, 0] = cosine
            table[line, 1] = sine
        return carry

    if not stores:
        lax.fori_loop(0, (4 if children == 4 else 2) * pairs, step, 0)
    for source, store in enumerate(stores):
        lax.fori_loop(source * pairs, (source + 1) * pairs, step, 0)
        store.start()


def make_first_turns(table, box, node):
    def step(index, carry):
        radius = []
        for k in range(2):
            first, second = box(index // 4, 2 * (index % 4) + k)
            along = first + node[6:7, :]
            across = second + node[7:8, :]
            radius.append(0.5 * jnp.sqrt(along * along + across * across))
        cosine, sine = turn(jnp.concatenate(radius))
        for kind in range(2):
            base_cosine = node[16 + 2 * kind : 17 + 2 * kind, :]
            base_sine = node[17 + 2 * kind : 18 + 2 * kind, :]
            cosines = base_cosine * cosine
            sines = base_sine * sine
            mixed = base_sine * cosine
            other = base_cosine * sine
            line = 4 * index + kind
            mirror = 4 * index + 3 - kind
            if kind == 0:
                table[line, 0] = cosines - sines
                table[line, 1] = mixed + other
                table[mirror, 0] = cosines + sines
                table[mirror, 1] = other - mixed
            else:
                table[line, 0] = cosines + sines
                table[line, 1] = mixed - other
                table[mirror, 0] = cosines - sines
                table[mirror, 1] = -mixed - other
        return carry

    lax.fori_loop(0, 16, step, 0)


def level(
    read, table, first_line, highs, lows, matrix, children, rows, by_rows, ready, emit, matrix_ready=None
):
    sources = 4 if children == 4 else 2
    pairs = rows // 2
    columns = sources * BOX_NODES
    for half in range(2):
        high, low = highs[half], lows[half]
        if by_rows:
            chosen = list(range(children))
            near = list(range(half * pairs // 2, (half + 1) * pairs // 2))
        else:
            chosen = list(range(half * children // 2, (half + 1) * children // 2))
            near = list(range(pairs))
        height = 16 * len(near)
        for source in range(sources):
            lanes = slice(source * BOX_NODES, (source + 1) * BOX_NODES)
            if half == 0 and source < len(ready):
                ready[source].wait()
            for spot, pair in enumerate(near):
                group = source * rows + 2 * pair
                real, imaginary = (
                    jnp.concatenate([read(group, part), read(group + 1, part)])
                    for part in range(2)
                )
                for number, child in enumerate(chosen):
                    line = first_line + (source * pairs + pair) * children + child
                    cosine = table[line, 0]
                    sine = table[line, 1]
                    for part, value in enumerate(
                        (real * cosine - imaginary * sine, real * sine + imaginary * cosine)
                    ):
                        place = (number * 2 + part) * height + spot * 16
                        value_high, value_low = split(value)
                        high[place : place + 16, lanes] = value_high
                        low[place : place + 16, lanes] = value_low
        if half == 0 and matrix_ready is not None:
            matrix_ready.wait()
        both = jnp.dot(high[:, :columns], matrix[...], preferred_element_type=F32)
        rest = jnp.dot(low[:, :columns], matrix[:, :BOX_NODES], preferred_element_type=F32)
        result = both[:, :BOX_NODES] + (both[:, BOX_NODES:] + rest)
        for number, child in enumerate(chosen):
            for spot, pair in enumerate(near):
                for k in range(2):
                    start = number * 2 * height + spot * 16 + 8 * k
                    emit(
                        child,
                        2 * pair + k,
                        [result[start + height * part : start + height * part + 8] for part in range(2)],
                    )


def matrices():
    basis = second_basis()
    rows = [
        stacked_matrix(2, 2),
        stacked_matrix(1, 2),
        basis[:, :256],
        basis[:, 256:],
    ]
    return np.concatenate(two_parts(np.concatenate(rows)), axis=1)


def sub_bits():
    row = lax.broadcasted_iota(jnp.int32, (8, BOX_NODES), 0)
    return [bit(row, 2 - k).astype(F32) for k in range(3)]


def find_mask(slots, table, entries, high_hot, low_hot):
    iota = lax.broadcasted_iota(jnp.int32, (16, 128), 0).astype(F32)
    rows = [(iota + 16.0 * k).astype(BF16) for k in range(8)]
    one = jnp.ones((16, 128), BF16)
    zero = jnp.zeros((16, 128), BF16)
    block = jnp.concatenate([slots[:, :128], slots[:, 128:]], axis=0)
    entries[0] = (block >> 7).astype(F32)
    entries[1] = (block & 127).astype(F32)

    def step(index, carry):
        for source, hot in enumerate((high_hot, low_hot)):
            for side in range(2):
                start = pl.multiple_of(index * 8 + 64 * side, 8)
                block = entries[source, pl.ds(start, 8), :]
                for k in range(8):
                    value = jnp.broadcast_to(block[k : k + 1], (16, 128)).astype(BF16)
                    lanes = pl.ds(pl.multiple_of(index * 1024 + 128 * k, 128), 128)
                    for place in range(8):
                        line = 128 * side + 16 * place
                        hot[line : line + 16, lanes] = jnp.where(value == rows[place], one, zero)
        return carry

    lax.fori_loop(0, 8, step, 0)
    parts = [
        lax.dot_general(
            high_hot[:, 4096 * k : 4096 * (k + 1)],
            low_hot[:, 4096 * k : 4096 * (k + 1)],
            (((1,), (1,)), ((), ())),
            preferred_element_type=F32,
        )
        for k in range(2)
    ]
    total = parts[0] + parts[1]
    mask = jnp.where(total[:128, :128] + total[128:, 128:] > 0.5, 1.0, 0.0)
    for k in range(8):
        lanes = slice(128 * (k % 2), 128 * (k % 2 + 1))
        table[256 + k // 4, k // 2 % 2, :, lanes] = mask[16 * k : 16 * (k + 1)]


def store_level(table, table_far, leave, index, size=64, first=0):
    lines = pl.ds(size * index, size)
    place = leave.at[index if first == 0 else first + index % 4]
    return pltpu.make_async_copy(table.at[lines], table_far.at[lines], place)


def fetch_level(table_far, table, arrive, index, size=64):
    lines = pl.ds(64 * index, size)
    return pltpu.make_async_copy(table_far.at[lines], table.at[lines], arrive.at[index])


def fetch_mask_lines(table_far, table, place):
    lines = pl.ds(256, 2)
    return pltpu.make_async_copy(table_far.at[lines], table.at[lines], place)


def inner_turns_kernel(
    block_first_ref,
    block_second_ref,
    slots_far,
    node_far,
    speeds_far,
    table_far,
    slots,
    node,
    speeds,
    table,
    entries,
    high_hot,
    low_hot,
    arrive,
    leave,
):
    fetches = [
        pltpu.make_async_copy(far, near, arrive.at[k])
        for k, (far, near) in enumerate(
            ((slots_far, slots), (node_far, node), (speeds_far, speeds))
        )
    ]
    for fetch in fetches:
        fetch.start()
    fetches[0].wait()
    find_mask(slots, table, entries, high_hot, low_hot)
    for fetch in fetches[1:]:
        fetch.wait()
    stores = [store_level(table, table_far, leave, k) for k in range(3)]
    stores += [store_level(table, table_far, leave, 12 + k, 16, 3) for k in range(4)]
    store_mask = store_level(table, table_far, leave, 128, 2, 7)
    store_mask.start()
    sub = sub_bits()
    block_first = block_first_ref[0]
    block_second = block_second_ref[0]

    def box(source, row):
        first = block_first * 16 + bit(source, 1) + 2 * bit(row, 2)
        second = block_second * 16 + bit(source, 0) + 2 * bit(row, 1) + 8 * bit(row, 0)
        return (
            2.0 * first.astype(F32) + (8.0 * sub[0] + 16.0 * sub[2]),
            second.astype(F32) + 4.0 * sub[1],
        )

    make_first_turns(table, box, node)
    stores[0].start()

    def box(source, row):
        first = block_first * 8 + bit(source, 1)
        second = block_second * 8 + bit(source, 0) + 4 * bit(row, 0)
        return (
            2.0 * first.astype(F32) + (4.0 * sub[0] + 8.0 * sub[2]),
            second.astype(F32) + 2.0 * sub[1],
        )

    make_turns(table, 64, box, 2, speeds, 256, node, 0, 4, 8)
    stores[1].start()

    def box(source, row):
        first = block_first * 4 + bit(source, 1) + 2 * bit(row, 2)
        second = block_second * 4 + bit(source, 0) + 2 * bit(row, 1)
        return 2.0 * first.astype(F32), second.astype(F32)

    make_turns(table, 128, box, 3, speeds, 512, node, 0, 4, 8)
    stores[2].start()

    def box(source, row):
        first = block_first * 2 + bit(source, 1)
        second = block_second * 2 + bit(source, 0)
        return 2.0 * first.astype(F32), second.astype(F32)

    make_turns(table, 192, box, 4, speeds, 768, node, 0, 4, 8, stores[3:])
    for store in stores + [store_mask]:
        store.wait()


def outer_turns_kernel(node, speeds, table_far, table, leave):
    stores = [store_level(table, table_far, leave, k) for k in range(3)]
    stores += [store_level(table, table_far, leave, 12 + k, 16, 3) for k in range(3)]
    sub = sub_bits()

    def box(source, row):
        first = bit(source, 1) + 2 * bit(row, 2) + 4 * bit(row, 1)
        second = bit(source, 0) + 2 * bit(row, 0)
        return 2.0 * first.astype(F32), second.astype(F32) + (4.0 * sub[0] + 8.0 * sub[1])

    make_turns(table, 0, box, 5, speeds, 0, node, 0, 4, 8)
    stores[0].start()

    def box(source, row):
        first = bit(source, 1) + 2 * bit(row, 0)
        second = bit(source, 0)
        return 2.0 * first.astype(F32), second.astype(F32) + (2.0 * sub[0] + 4.0 * sub[1])

    make_turns(table, 64, box, 6, speeds, 256, node, 0, 4, 8)
    stores[1].start()

    def box(source, row):
        first = bit(source, 1)
        second = bit(source, 0) + 2 * bit(row, 1)
        return 2.0 * first.astype(F32), second.astype(F32)

    make_turns(table, 128, box, 7, speeds, 512, node, 0, 4, 8)
    stores[2].start()

    def box(source, row):
        return jnp.float32(0.0), source.astype(F32)

    make_turns(table, 192, box, 8, speeds, 768, node, 4, 2, 16, stores[3:5])

    def last(index, carry):
        def column(table):
            value = speeds[pl.ds(pl.multiple_of(256 * table + index * 16, 16), 16), :]
            return jnp.concatenate([value, value], axis=1)

        first = column(5)
        second = column(6)
        turns = first * node[8:9, :]
        turns = turns - ((turns + ROUNDER) - ROUNDER)
        across = second * node[10:11, :]
        across = across - ((across + ROUNDER) - ROUNDER)
        around = column(4) * node[12:13, :]
        around = around - ((around + ROUNDER) - ROUNDER)
        turns = turns + across + around + first * node[9:10, :] + second * node[11:12, :]
        cosine, sine = turn(turns)
        table[224 + index, 0] = cosine
        table[224 + index, 1] = sine
        return carry

    lax.fori_loop(0, 16, last, 0)
    stores[5].start()
    for store in stores:
        store.wait()


def deposit(
    arrived, table, second, fetch_second, state, wide, cells, hots, spreads, grid
):
    points = [float(value) for value in chebyshev_points(NODES).astype(np.float32)]
    factors = basis_factors()

    def source_step(index, carry):
        rows = pl.ds(pl.multiple_of(index * 16, 16), 16)
        first, second, real, imaginary = (
            arrived[pl.ds(index * 64 + k, 16, stride=4), :] for k in range(4)
        )
        whole_first = first.astype(jnp.int32)
        whole_second = second.astype(jnp.int32)
        along = first + 0.5
        across = second + 0.5
        eighths = jnp.bitwise_and(whole_first + whole_second + 1, 7).astype(F32)
        cosine, sine = turn(
            0.125 * eighths + 0.0625 * jnp.sqrt(along * along + across * across)
        )
        lanes = pl.ds(pl.multiple_of(index % 2 * 128, 128), 128)
        live = table[256 + index // 4, index // 2 % 2, :, lanes]
        real = real * live
        imaginary = imaginary * live
        turned = (real * cosine - imaginary * sine, real * sine + imaginary * cosine)
        place = jnp.bitwise_and(whole_first, 31).astype(F32) * 0.03125 + 0.015625
        cells[0, rows, :] = jnp.bitwise_and(whole_second, 15).astype(F32)
        x = [bit(whole_first, 5 + k) for k in range(4)]
        y = [bit(whole_second, 4 + k) for k in range(4)]
        cells[1, rows, :] = (x[0] * 8 + y[0] * 4 + x[1] * 2 + y[1]).astype(F32)
        cells[2, rows, :] = (y[3] * 8 + x[2] * 4 + y[2] * 2 + x[3]).astype(F32)
        away = [place - value for value in points]
        before = [None] * NODES
        after = [None] * NODES
        for p in range(1, NODES):
            before[p] = away[p - 1] if p == 1 else before[p - 1] * away[p - 1]
            q = NODES - 1 - p
            after[q] = away[q + 1] if p == 1 else after[q + 1] * away[q + 1]
        for p in range(NODES):
            if p == 0:
                value = after[0]
            elif p == NODES - 1:
                value = before[p]
            else:
                value = before[p] * after[p]
            value = value * factors[p]
            for part in range(2):
                wide[pl.ds(index * 512 + part * 16 + p, 16, stride=32), :] = value * turned[part]
        return carry

    lax.fori_loop(0, 8, source_step, 0)

    iota = lax.broadcasted_iota(jnp.int32, (16, 128), 0).astype(F32).astype(BF16)
    one = jnp.ones((16, 128), BF16)
    zero = jnp.zeros((16, 128), BF16)

    def build(chunk, hot, spread):
        for k in range(8):
            sender = chunk * 8 + k
            lanes = slice(128 * k, 128 * (k + 1))

            def row(number, height):
                value = cells[number, pl.ds(sender, 1), :]
                return jnp.broadcast_to(value, (height, 128)).astype(BF16)

            value = wide[pl.ds(pl.multiple_of(sender * 32, 32), 32), :].astype(BF16)
            cell = row(0, 16)
            for c in range(16):
                chosen = cell == jnp.full((16, 128), c, BF16)
                for part in range(2):
                    spread[32 * c + 16 * part : 32 * c + 16 * (part + 1), lanes] = jnp.where(
                        chosen, value[16 * part : 16 * (part + 1)], zero
                    )
            inside = jnp.where(row(2, 16) == iota, one, zero)
            above = row(1, 16)
            for c in range(16):
                hot[16 * c : 16 * (c + 1), lanes] = jnp.where(
                    above == jnp.full((16, 128), c, BF16), inside, zero
                )

    def product(hot, spread):
        return lax.dot_general(
            hot[...], spread[...], (((1,), (1,)), ((), ())), preferred_element_type=F32
        )

    grid[...] = jnp.zeros_like(grid)
    for k in range(2):
        build(k, hots[k], spreads[k])

    def spread_step(index, carry):
        for side in range(2):
            here, there = 2 * side, 2 - 2 * side
            parts = [product(hots[here + k], spreads[here + k]) for k in range(2)]
            for k in range(2):
                chunk = jnp.minimum(4 * index + 2 * side + 2 + k, 15)
                build(chunk, hots[there + k], spreads[there + k])
            grid[...] += parts[0] + parts[1]
        return carry

    lax.fori_loop(0, 4, spread_step, 0)

    grid_high, grid_low = split(grid[...])
    fetch_second.wait()
    for part in range(2):
        basis = second[512 * part : 512 * (part + 1), :]
        result = jnp.dot(grid_high, basis, preferred_element_type=F32)
        rest = jnp.dot(grid_low, basis[:, :BOX_NODES], preferred_element_type=F32)
        result = result[:, :BOX_NODES] + (result[:, BOX_NODES:] + rest)
        for group in range(32):
            state[group, part] = result[8 * group : 8 * group + 8, :]


def halves(value):
    return value[:, :128], value[:, 128:]


def inner_kernel(
    arrived,
    table_far,
    matrix_far,
    out,
    second,
    matrix,
    table,
    arrive,
    wide,
    cells,
    hots,
    spreads,
    grid,
    other,
    turned,
    highs,
    lows,
    state,
):
    fetch_mask = fetch_mask_lines(table_far, table, arrive.at[6])
    fetch_mask.start()
    fetch_second = pltpu.make_async_copy(matrix_far.at[pl.ds(1536, 1024)], second, arrive.at[4])
    fetch_second.start()
    fetches = [fetch_level(table_far, table, arrive, k) for k in range(4)]
    for fetch in fetches:
        fetch.start()
    fetch_matrix = pltpu.make_async_copy(matrix_far.at[pl.ds(0, 1024)], matrix, arrive.at[5])
    fetch_matrix.start()
    fetch_mask.wait()
    deposit(arrived, table, second, fetch_second, state, wide, cells, hots, spreads, grid)

    def run(number, read, emit):
        level(
            read,
            table,
            64 * (number - 1),
            highs,
            lows,
            matrix,
            4,
            8,
            number % 2 == 0,
            fetches[number - 1 : number],
            emit,
            fetch_matrix if number == 1 else None,
        )

    def leaf(group, part):
        return state[group, part]

    def read(group, part):
        return other[group, part]

    def keep(child, row, values):
        for part in range(2):
            other[(row // 2) * 8 + child * 2 + row % 2, part] = values[part]

    run(1, leaf, keep)

    def turn_over(child, row, values):
        start = ((row % 2 * 2 + child // 2) * 8 + row // 2 * 2 + child % 2) * 8
        for part in range(2):
            for half, value in enumerate(halves(values[part])):
                turned[2 * part + half, start : start + 8, :] = value

    run(2, read, turn_over)

    def across(group, part):
        b2x, b2y, b3x, b3y, t2x = bits(group, 5)
        start = (b3y * 2 + t2x) * 64 + b2x * 4 + b2y * 2 + b3x
        return jnp.concatenate(
            [turned.at[2 * part + half][pl.ds(start, 8, stride=8), :] for half in range(2)], axis=1
        )

    run(3, across, keep)

    def send(child, row, values):
        x, y = bits(child, 2)
        r0, r1, r2 = bits(row, 3)
        device = r2 * 32 + r0 * 16 + x * 8 + r1
        for upper in range(2):
            for part in range(2):
                for half, value in enumerate(halves(values[part])):
                    start = (device + 64 * upper) * 8 + y * 4 + half * 2 + part
                    out[pl.ds(start, 4, stride=16), :] = value[4 * upper : 4 * upper + 4]

    run(4, read, send)


def outer_kernel(
    arrived, table_far, matrix_far, out, table, matrix, last, arrive, state, turned, highs, lows
):
    first = [
        pltpu.make_async_copy(
            table_far.at[pl.ds(16 * k, 16)], table.at[pl.ds(16 * k, 16)], arrive.at[6 + k]
        )
        for k in range(4)
    ]
    fetches = [
        fetch_level(table_far, table, arrive, k, 64 if k < 3 else 48) for k in range(1, 4)
    ]
    fetch_matrix = pltpu.make_async_copy(matrix_far.at[pl.ds(0, 1024)], matrix, arrive.at[5])
    fetch_last = pltpu.make_async_copy(matrix_far.at[pl.ds(1024, 512)], last, arrive.at[4])
    for fetch in first + [fetch_matrix] + fetches + [fetch_last]:
        fetch.start()

    def first_read(group, part):
        i2, j3, i1, i0, j2 = bits(group, 5)
        source = i2 * 64 + i1 * 32 + i0 * 16 + j3 * 8 + j2 * 4
        return jnp.concatenate(
            [
                arrived[pl.ds(source * 8 + half * 2 + part, 8, stride=4), :]
                for half in range(2)
            ],
            axis=1,
        )

    def run(number, read, emit):
        level(
            read,
            table,
            64 * (number - 5),
            highs,
            lows,
            matrix,
            4,
            8,
            number % 2 == 0,
            first if number == 5 else fetches[number - 6 : number - 5],
            emit,
            fetch_matrix if number == 5 else None,
        )

    def read(group, part):
        return state[group, part]

    def keep(child, row, values):
        i1, i0, j2 = bits(row, 3)
        for part in range(2):
            state[(2 * i1 + j2) * 8 + child * 2 + i0, part] = values[part]

    run(5, first_read, keep)

    def turn_over(child, row, values):
        start = ((row % 2 * 2 + child // 2) * 8 + row // 2 * 2 + child % 2) * 8
        for part in range(2):
            for half, value in enumerate(halves(values[part])):
                turned[2 * part + half, start : start + 8, :] = value

    run(6, read, turn_over)

    def across(group, part):
        i0, j1, t6x, j0, pair = bits(group, 5)
        start = (i0 * 2 + t6x) * 64 + j1 * 4 + j0 * 2 + pair
        return jnp.concatenate(
            [turned.at[2 * part + half][pl.ds(start, 8, stride=8), :] for half in range(2)], axis=1
        )

    def keep_last(child, row, values):
        t6x, j0, pair = bits(row, 3)
        for part in range(2):
            state[j0 * 16 + child * 4 + t6x * 2 + pair, part] = values[part]

    run(7, across, keep_last)

    def send(child, row, values):
        t7x, t7y, t6x, pair = bits(row, 4)
        line = 224 + child * 8 + row // 2
        cosine = table[line, 0, 8 * (row % 2) : 8 * (row % 2) + 8, :]
        sine = table[line, 1, 8 * (row % 2) : 8 * (row % 2) + 8, :]
        real, imaginary = values
        device = t6x * 32 + t7x * 16 + t7y * 2 + child
        for part, whole in enumerate(
            (real * cosine + imaginary * sine, imaginary * cosine - real * sine)
        ):
            for half, value in enumerate(halves(whole)):
                for upper in range(2):
                    place = (device + 64 * upper) * 8 + pair * 4 + half * 2 + part
                    out[pl.ds(place, 4, stride=32), :] = value[4 * upper : 4 * upper + 4]

    level(
        read, table, 192, highs, lows, last, 2, 16, True, fetches[2:], send, fetch_last
    )


def vmem(count):
    return [pl.BlockSpec(memory_space=pltpu.VMEM)] * count


def smem(count):
    return [pl.BlockSpec(memory_space=pltpu.SMEM)] * count


def far(count):
    return [pl.BlockSpec(memory_space=pltpu.HBM)] * count


def payload_kernel(place_far, amp_far, out_far, place, amp, out, arrive, leave):
    fetches = [
        pltpu.make_async_copy(place_far, place, arrive.at[0]),
        pltpu.make_async_copy(amp_far, amp, arrive.at[1]),
    ]
    for fetch in fetches:
        fetch.start()
    for fetch in fetches:
        fetch.wait()
    for k in range(2):
        out[pl.ds(k, DEVICES, stride=4), :] = place[k].astype(F32)
        out[pl.ds(2 + k, DEVICES, stride=4), :] = amp[k]
    store = pltpu.make_async_copy(out, out_far, leave)
    store.start()
    store.wait()


def make_payload(place, amp):
    return pl.pallas_call(
        payload_kernel,
        out_shape=jax.ShapeDtypeStruct((4 * DEVICES, 128), F32),
        in_specs=far(2),
        out_specs=far(1)[0],
        scratch_shapes=[
            pltpu.VMEM((2, DEVICES, 128), jnp.int32),
            pltpu.VMEM((2, DEVICES, 128), F32),
            pltpu.VMEM((4 * DEVICES, 128), F32),
            pltpu.SemaphoreType.DMA((2,)),
            pltpu.SemaphoreType.DMA,
        ],
        name="payload",
        compiler_params=pltpu.CompilerParams(vmem_limit_bytes=60 << 20),
    )(place, amp)


def inner_turns(block_first, block_second, slots):
    speeds = np.repeat(inner_speeds()[:, None], 128, axis=1)
    return pl.pallas_call(
        inner_turns_kernel,
        out_shape=jax.ShapeDtypeStruct((258, 2, 16, 256), F32),
        in_specs=smem(2) + far(3),
        out_specs=far(1)[0],
        scratch_shapes=[
            pltpu.VMEM((64, 256), jnp.int32),
            pltpu.VMEM((24, 256), F32),
            pltpu.VMEM((1024, 128), F32),
            pltpu.VMEM((258, 2, 16, 256), F32),
            pltpu.VMEM((2, 128, 128), F32),
            pltpu.VMEM((256, 8192), BF16),
            pltpu.VMEM((256, 8192), BF16),
            pltpu.SemaphoreType.DMA((3,)),
            pltpu.SemaphoreType.DMA((8,)),
        ],
        name="inner_turns",
        compiler_params=pltpu.CompilerParams(vmem_limit_bytes=60 << 20),
    )(block_first, block_second, slots, jnp.asarray(node_tables()), jnp.asarray(speeds))


def outer_turns(speeds):
    return pl.pallas_call(
        outer_turns_kernel,
        out_shape=jax.ShapeDtypeStruct((240, 2, 16, 256), F32),
        in_specs=vmem(2),
        out_specs=far(1)[0],
        scratch_shapes=[
            pltpu.VMEM((240, 2, 16, 256), F32),
            pltpu.SemaphoreType.DMA((7,)),
        ],
        name="outer_turns",
        compiler_params=pltpu.CompilerParams(vmem_limit_bytes=52 << 20),
    )(jnp.asarray(node_tables()), speeds)


LEVEL_SCRATCH = [
    pltpu.VMEM((32, 2, 8, 256), F32),
    pltpu.VMEM((4, 256, 128), F32),
    [pltpu.VMEM((256, 1024), BF16)] * 2,
    [pltpu.VMEM((256, 1024), BF16)] * 2,
]


def inner_levels(arrived, table):
    return pl.pallas_call(
        inner_kernel,
        out_shape=jax.ShapeDtypeStruct((1024, 128), F32),
        in_specs=vmem(1) + far(2),
        out_specs=vmem(1)[0],
        scratch_shapes=[
            pltpu.VMEM((1024, 512), BF16),
            pltpu.VMEM((1024, 512), BF16),
            pltpu.VMEM((258, 2, 16, 256), F32),
            pltpu.SemaphoreType.DMA((7,)),
            pltpu.VMEM((4096, 128), F32),
            pltpu.VMEM((3, 128, 128), F32),
            [pltpu.VMEM((256, 1024), BF16)] * 4,
            [pltpu.VMEM((512, 1024), BF16)] * 4,
            pltpu.VMEM((256, 512), F32),
        ]
        + LEVEL_SCRATCH
        + LEVEL_SCRATCH[:1],
        name="inner",
        compiler_params=pltpu.CompilerParams(vmem_limit_bytes=52 << 20),
    )(
        arrived,
        table,
        jnp.asarray(matrices()),
    )


def outer_levels(arrived, table):
    return pl.pallas_call(
        outer_kernel,
        out_shape=jax.ShapeDtypeStruct((1024, 128), F32),
        in_specs=vmem(1) + far(2),
        out_specs=vmem(1)[0],
        scratch_shapes=[
            pltpu.VMEM((240, 2, 16, 256), F32),
            pltpu.VMEM((1024, 512), BF16),
            pltpu.VMEM((512, 512), BF16),
            pltpu.SemaphoreType.DMA((10,)),
        ]
        + LEVEL_SCRATCH,
        name="outer",
        compiler_params=pltpu.CompilerParams(vmem_limit_bytes=52 << 20),
    )(
        arrived,
        table,
        jnp.asarray(matrices()),
    )


def reverse_bits(number, bit_count):
    result = jnp.zeros_like(number)
    for position in range(bit_count):
        result = result + jnp.left_shift(
            jnp.bitwise_and(jnp.right_shift(number, position), 1), bit_count - 1 - position
        )
    return result


def exchange(array):
    return lax.all_to_all(array, ("bx", "by"), split_axis=0, concat_axis=0, tiled=True)


def shards(src_pos, src_amp, box_slots):
    column = lax.axis_index("bx")
    row = lax.axis_index("by")
    device = column * BY + row
    block_first = reverse_bits(column, 3).astype(jnp.int32).reshape(1)
    block_second = reverse_bits(row, 4).astype(jnp.int32).reshape(1)
    payload = make_payload(src_pos.reshape(2, DEVICES, 128), src_amp.reshape(2, DEVICES, 128))
    arrived = exchange(payload.reshape(DEVICES, 4, 128)).reshape(512, 128)
    table = inner_turns(block_first, block_second, box_slots[0].T)
    arrived, table = lax.optimization_barrier((arrived, table))
    weights = inner_levels(arrived, table)
    weights = exchange(weights.reshape(DEVICES, 8, 128)).reshape(1024, 128)
    speeds = lax.dynamic_index_in_dim(jnp.asarray(outer_speeds()), device, 0, keepdims=False)
    speeds = jnp.broadcast_to(speeds[:, None], (7 * 256, 128))
    weights = outer_levels(weights, outer_turns(speeds))
    weights = exchange(weights.reshape(DEVICES, 8, 128))
    weights = weights.reshape(LEAVES, LEAVES, 2, 2, 128)
    weights = jnp.concatenate([weights[:, :, 0], weights[:, :, 1]], axis=-1)
    return weights.reshape(LEAVES, 1, LEAVES, 1, 2, BOX_NODES)


def solution(mesh):
    return jax.shard_map(
        shards,
        mesh=mesh,
        in_specs=(
            P(None, ("bx", "by"), None),
            P(None, ("bx", "by"), None),
            P(("bx", "by"), None, None),
        ),
        out_specs=P(None, "bx", None, "by", None, None),
        check_vma=False,
    )
```

```python
import functools
import math

import jax
import jax.numpy as jnp
import numpy as np
from jax import lax
from jax.experimental import pallas as pl
from jax.experimental.pallas import tpu as pltpu
from jax.sharding import PartitionSpec as P

NODES = 16
BOX_NODES = 256
DEVICES = 128
LEAVES = 16
BX = 8
BY = 16
BAND = 1024
F32 = jnp.float32
BF16 = jnp.bfloat16
ROUNDER = 12582912.0
SIN = (6.28305581, -41.33121471, 81.36682035, -74.47802935, 32.78144238)
COS = (0.99995995, -19.73105034, 64.67355678, -82.40422428, 45.64775943)


def chebyshev_points(point_count):
    indices = np.arange(point_count)
    return (1.0 - np.cos(np.pi * (2 * indices + 1) / (2 * point_count))) / 2.0


def lagrange_matrix(locations):
    points = chebyshev_points(NODES)
    matrix = np.ones((len(locations), NODES))
    for own in range(NODES):
        for other in range(NODES):
            if other != own:
                matrix[:, own] *= (locations - points[other]) / (points[own] - points[other])
    return matrix


def child_matrix(halves, child):
    if halves == 1:
        return np.eye(NODES)
    return lagrange_matrix((child + chebyshev_points(NODES)) / 2.0)


def stacked_matrix(halves_first, halves_second):
    pieces = [
        np.kron(child_matrix(halves_first, a), child_matrix(halves_second, b))
        for a in range(halves_first)
        for b in range(halves_second)
    ]
    return np.concatenate(pieces, axis=0)


def two_parts(matrix):
    exact = np.asarray(matrix, np.float32)
    high = exact.astype(jnp.bfloat16)
    low = (exact - high.astype(np.float32)).astype(jnp.bfloat16)
    return high, low


def velocity(first, second):
    return (2.0 + np.sin(2 * np.pi * first) * np.sin(2 * np.pi * second)) / 8.0


def bits(value, count):
    return [(value >> (count - 1 - k)) & 1 for k in range(count)]


def speed_change(first, second, level, split_first=True):
    count_second = 2.0**level
    count_first = 2.0 ** (level if split_first else level - 1)
    new = velocity((first + 0.5) / count_first, (second + 0.5) / count_second)
    above_first = first >> 1 if split_first else first
    old = velocity(
        (above_first + 0.5) / 2.0 ** (level - 1), ((second >> 1) + 0.5) / 2.0 ** (level - 1)
    )
    return new - old


def inner_speeds():
    table = np.zeros((4, 4, 8, 8))
    for child in range(4):
        x, y = bits(child, 2)
        for row in range(8):
            r0, r1, r2 = bits(row, 3)
            for sub in range(8):
                s0, s1, s2 = bits(sub, 3)
                table[0, child, row, sub] = speed_change(x, y, 1)
                table[1, child, row, sub] = speed_change(2 * r0 + x, 2 * r1 + y, 2)
                first, second = 2 * s0 + r2, 2 * s1 + s2
                table[2, child, row, sub] = speed_change(2 * first + x, 2 * second + y, 3)
                first, second = 2 * first + r0, 2 * second + r1
                table[3, child, row, sub] = speed_change(2 * first + x, 2 * second + y, 4)
    return table.reshape(1024).astype(np.float32)


def outer_speeds():
    tables = np.zeros((DEVICES, 7, 256))
    for device in range(DEVICES):
        coarse_first = device >> 3
        for child in range(4):
            x, y = bits(child, 2)
            for row in range(8):
                r0, r1, r2 = bits(row, 3)
                for sub in range(8):
                    s0, s1, s2 = bits(sub, 3)
                    place = child * 64 + row * 8 + sub
                    second = 2 * (device & 7) + s2
                    tables[device, 0, place] = speed_change(
                        2 * coarse_first + x, 2 * second + y, 5
                    )
                    tables[device, 1, place] = speed_change(
                        4 * coarse_first + 2 * r0 + x, 4 * second + 2 * r1 + y, 6
                    )
                    second = 2 * (device & 7) + r2
                    tables[device, 2, place] = speed_change(
                        8 * coarse_first + 4 * s0 + 2 * r0 + x,
                        8 * second + 4 * s1 + 2 * s2 + y,
                        7,
                    )
        for child in range(2):
            for row in range(16):
                r0, r1, r2, r3 = bits(row, 4)
                for sub in range(8):
                    s0, s1, s2 = bits(sub, 3)
                    place = child * 128 + row * 8 + sub
                    first = 8 * coarse_first + 4 * s0 + 2 * r2 + r0
                    second = 2 * (device & 7) + r3
                    second = 16 * second + 8 * s1 + 4 * s2 + 2 * r1 + child
                    tables[device, 3, place] = speed_change(first, second, 8, False)
                    tables[device, 4, place] = velocity((first + 0.5) / 128, (second + 0.5) / 256)
                    tables[device, 5, place] = 8 * (first + 0.5)
                    tables[device, 6, place] = 4 * (second + 0.5)
    return tables.reshape(DEVICES, 7 * 256).astype(np.float32)


def node_tables():
    points = chebyshev_points(NODES).astype(np.float32).astype(np.float64)
    first = np.repeat(points, NODES)
    second = np.tile(points, NODES)
    rows = np.zeros((24, BOX_NODES))
    for child in range(4):
        x, y = bits(child, 2)
        turns = (2 * x - 1) * 2 * first + (2 * y - 1) * second
        rows[child] = turns - np.round(turns)
    for child in range(2):
        rows[4 + child] = (2 * child - 1) * second
    rows[6] = 2 * first
    rows[7] = second
    rows[8] = np.round(first * 8192) / 8192
    rows[9] = first - rows[8]
    rows[10] = np.round(second * 8192) / 8192
    rows[11] = second - rows[10]
    for child in range(2):
        rows[16 + 2 * child] = np.cos(2 * np.pi * rows[child])
        rows[17 + 2 * child] = np.sin(2 * np.pi * rows[child])
    rows[12] = BAND * np.sqrt(first * first + second * second)
    return rows.astype(np.float32)


def basis_factors():
    points = chebyshev_points(NODES)
    return [
        float(np.float32(1.0 / np.prod([points[own] - points[k] for k in range(NODES) if k != own])))
        for own in range(NODES)
    ]


def second_basis():
    small = lagrange_matrix((np.arange(16) + 0.5) / 16.0)
    whole = np.zeros((16, 32, 32, 16))
    for k in range(32):
        whole[:, k, k, :] = small
    return whole.reshape(512, 512)


def turn(turns):
    part = turns - ((turns + ROUNDER) - ROUNDER)
    square = part * part
    sine = SIN[4]
    cosine = COS[4]
    for k in (3, 2, 1, 0):
        sine = sine * square + SIN[k]
        cosine = cosine * square + COS[k]
    return cosine, sine * part


def split(value):
    high = value.astype(BF16)
    return high, (value - high.astype(F32)).astype(BF16)


def bit(value, place):
    return (value >> place) & 1


def make_turns(
    table, first_line, box, level_number, speeds, speed_row, node, base_row, children, rows, stores=()
):
    scale = 4.0 * 2.0 ** (level_number - 1)
    pairs = rows // 2

    def step(index, carry):
        source = index // pairs
        pair = lax.rem(index, pairs)
        radius = []
        for k in range(2):
            first, second = box(source, 2 * pair + k)
            along = first + node[6:7, :]
            across = second + node[7:8, :]
            radius.append(scale * jnp.sqrt(along * along + across * across))
        radius = jnp.concatenate([jnp.broadcast_to(value, (8, BOX_NODES)) for value in radius])
        for child in range(children):
            place = pl.multiple_of(speed_row + child * rows * 8 + pair * 16, 16)
            change = speeds[pl.ds(place, 16), :]
            change = jnp.concatenate([change, change], axis=1)
            cosine, sine = turn(change * radius + node[base_row + child : base_row + child + 1, :])
            line = first_line + index * children + child
            table[line, 0] = cosine
            table[line, 1] = sine
        return carry

    if not stores:
        lax.fori_loop(0, (4 if children == 4 else 2) * pairs, step, 0)
    for source, store in enumerate(stores):
        lax.fori_loop(source * pairs, (source + 1) * pairs, step, 0)
        store.start()


def make_first_turns(table, box, node):
    def step(index, carry):
        radius = []
        for k in range(2):
            first, second = box(index // 4, 2 * (index % 4) + k)
            along = first + node[6:7, :]
            across = second + node[7:8, :]
            radius.append(0.5 * jnp.sqrt(along * along + across * across))
        cosine, sine = turn(jnp.concatenate(radius))
        for kind in range(2):
            base_cosine = node[16 + 2 * kind : 17 + 2 * kind, :]
            base_sine = node[17 + 2 * kind : 18 + 2 * kind, :]
            cosines = base_cosine * cosine
            sines = base_sine * sine
            mixed = base_sine * cosine
            other = base_cosine * sine
            line = 4 * index + kind
            mirror = 4 * index + 3 - kind
            if kind == 0:
                table[line, 0] = cosines - sines
                table[line, 1] = mixed + other
                table[mirror, 0] = cosines + sines
                table[mirror, 1] = other - mixed
            else:
                table[line, 0] = cosines + sines
                table[line, 1] = mixed - other
                table[mirror, 0] = cosines - sines
                table[mirror, 1] = -mixed - other
        return carry

    lax.fori_loop(0, 16, step, 0)


def level(
    read, table, first_line, highs, lows, matrix, children, rows, ready, emit, matrix_ready=None
):
    sources = 4 if children == 4 else 2
    pairs = rows // 2
    parts = []
    for half in range(2):
        pieces = []
        for source in range(half * sources // 2, (half + 1) * sources // 2):
            lanes = slice(BOX_NODES * (source % 2), BOX_NODES * (source % 2 + 1))
            high, low = highs[half], lows[half]
            if source < len(ready):
                ready[source].wait()
            for pair in range(pairs):
                group = source * rows + 2 * pair
                real, imaginary = (
                    jnp.concatenate([read(group, part), read(group + 1, part)])
                    for part in range(2)
                )
                for child in range(children):
                    line = first_line + (source * pairs + pair) * children + child
                    cosine = table[line, 0]
                    sine = table[line, 1]
                    for part, value in enumerate(
                        (real * cosine - imaginary * sine, real * sine + imaginary * cosine)
                    ):
                        place = (child * 2 + part) * rows * 8 + pair * 16
                        value_high, value_low = split(value)
                        high[place : place + 16, lanes] = value_high
                        low[place : place + 16, lanes] = value_low
            pieces += [high[:, lanes], low[:, lanes], high[:, lanes]]
        if half == 0 and matrix_ready is not None:
            matrix_ready.wait()
        depth = 384 * sources
        parts.append(
            jnp.dot(
                jnp.concatenate(pieces, axis=1),
                matrix[depth * half : depth * (half + 1), :],
                preferred_element_type=F32,
            )
        )
    result = parts[0] + parts[1]
    for child in range(children):
        for row in range(rows):
            start = child * 2 * rows * 8 + row * 8
            emit(
                child,
                row,
                [result[start + rows * 8 * part : start + rows * 8 * part + 8] for part in range(2)],
            )


def three_parts(matrix):
    high, low = two_parts(matrix)
    high = high.reshape(-1, BOX_NODES, BOX_NODES)
    low = low.reshape(-1, BOX_NODES, BOX_NODES)
    return np.stack([high, high, low], axis=1).reshape(-1, BOX_NODES)


def matrices():
    high, low = two_parts(second_basis())
    basis = np.concatenate([high, high, low], axis=0)
    return np.concatenate(
        [
            three_parts(stacked_matrix(2, 2)),
            three_parts(stacked_matrix(1, 2)),
            basis[:, :256],
            basis[:, 256:],
        ]
    )


def sub_bits():
    row = lax.broadcasted_iota(jnp.int32, (8, BOX_NODES), 0)
    return [bit(row, 2 - k).astype(F32) for k in range(3)]


def find_mask(slots, table, entries, high_hot, low_hot):
    iota = lax.broadcasted_iota(jnp.int32, (16, 128), 0).astype(F32)
    rows = [(iota + 16.0 * k).astype(BF16) for k in range(8)]
    one = jnp.ones((16, 128), BF16)
    zero = jnp.zeros((16, 128), BF16)
    block = jnp.concatenate([slots[:, :128], slots[:, 128:]], axis=0)
    entries[0] = (block >> 7).astype(F32)
    entries[1] = (block & 127).astype(F32)

    def step(index, carry):
        for source, hot in enumerate((high_hot, low_hot)):
            for side in range(2):
                start = pl.multiple_of(index * 8 + 64 * side, 8)
                block = entries[source, pl.ds(start, 8), :]
                for k in range(8):
                    value = jnp.broadcast_to(block[k : k + 1], (16, 128)).astype(BF16)
                    lanes = pl.ds(pl.multiple_of(index * 1024 + 128 * k, 128), 128)
                    for place in range(8):
                        line = 128 * side + 16 * place
                        hot[line : line + 16, lanes] = jnp.where(value == rows[place], one, zero)
        return carry

    lax.fori_loop(0, 8, step, 0)
    parts = [
        lax.dot_general(
            high_hot[:, 4096 * k : 4096 * (k + 1)],
            low_hot[:, 4096 * k : 4096 * (k + 1)],
            (((1,), (1,)), ((), ())),
            preferred_element_type=F32,
        )
        for k in range(2)
    ]
    total = parts[0] + parts[1]
    mask = jnp.where(total[:128, :128] + total[128:, 128:] > 0.5, 1.0, 0.0)
    for k in range(8):
        lanes = slice(128 * (k % 2), 128 * (k % 2 + 1))
        table[256 + k // 4, k // 2 % 2, :, lanes] = mask[16 * k : 16 * (k + 1)]


def store_level(table, table_far, leave, index, size=64, first=0):
    lines = pl.ds(size * index, size)
    place = leave.at[index if first == 0 else first + index % 4]
    return pltpu.make_async_copy(table.at[lines], table_far.at[lines], place)


def fetch_level(table_far, table, arrive, index, size=64):
    lines = pl.ds(64 * index, size)
    return pltpu.make_async_copy(table_far.at[lines], table.at[lines], arrive.at[index])


def fetch_mask_lines(table_far, table, place):
    lines = pl.ds(256, 2)
    return pltpu.make_async_copy(table_far.at[lines], table.at[lines], place)


def inner_turns_kernel(
    block_first_ref,
    block_second_ref,
    slots_far,
    node_far,
    speeds_far,
    table_far,
    slots,
    node,
    speeds,
    table,
    entries,
    high_hot,
    low_hot,
    arrive,
    leave,
):
    fetches = [
        pltpu.make_async_copy(far, near, arrive.at[k])
        for k, (far, near) in enumerate(
            ((slots_far, slots), (node_far, node), (speeds_far, speeds))
        )
    ]
    for fetch in fetches:
        fetch.start()
    fetches[0].wait()
    find_mask(slots, table, entries, high_hot, low_hot)
    for fetch in fetches[1:]:
        fetch.wait()
    stores = [store_level(table, table_far, leave, k) for k in range(3)]
    stores += [store_level(table, table_far, leave, 12 + k, 16, 3) for k in range(4)]
    store_mask = store_level(table, table_far, leave, 128, 2, 7)
    store_mask.start()
    sub = sub_bits()
    block_first = block_first_ref[0]
    block_second = block_second_ref[0]

    def box(source, row):
        first = block_first * 16 + bit(source, 1) + 2 * bit(row, 2)
        second = block_second * 16 + bit(source, 0) + 2 * bit(row, 1) + 8 * bit(row, 0)
        return (
            2.0 * first.astype(F32) + (8.0 * sub[0] + 16.0 * sub[2]),
            second.astype(F32) + 4.0 * sub[1],
        )

    make_first_turns(table, box, node)
    stores[0].start()

    def box(source, row):
        first = block_first * 8 + bit(source, 1)
        second = block_second * 8 + bit(source, 0) + 4 * bit(row, 0)
        return (
            2.0 * first.astype(F32) + (4.0 * sub[0] + 8.0 * sub[2]),
            second.astype(F32) + 2.0 * sub[1],
        )

    make_turns(table, 64, box, 2, speeds, 256, node, 0, 4, 8)
    stores[1].start()

    def box(source, row):
        first = block_first * 4 + bit(source, 1) + 2 * bit(row, 2)
        second = block_second * 4 + bit(source, 0) + 2 * bit(row, 1)
        return 2.0 * first.astype(F32), second.astype(F32)

    make_turns(table, 128, box, 3, speeds, 512, node, 0, 4, 8)
    stores[2].start()

    def box(source, row):
        first = block_first * 2 + bit(source, 1)
        second = block_second * 2 + bit(source, 0)
        return 2.0 * first.astype(F32), second.astype(F32)

    make_turns(table, 192, box, 4, speeds, 768, node, 0, 4, 8, stores[3:])
    for store in stores + [store_mask]:
        store.wait()


def outer_turns_kernel(node, speeds, table_far, table, leave):
    stores = [store_level(table, table_far, leave, k) for k in range(3)]
    stores += [store_level(table, table_far, leave, 12 + k, 16, 3) for k in range(3)]
    sub = sub_bits()

    def box(source, row):
        first = bit(source, 1) + 2 * bit(row, 2) + 4 * bit(row, 1)
        second = bit(source, 0) + 2 * bit(row, 0)
        return 2.0 * first.astype(F32), second.astype(F32) + (4.0 * sub[0] + 8.0 * sub[1])

    make_turns(table, 0, box, 5, speeds, 0, node, 0, 4, 8)
    stores[0].start()

    def box(source, row):
        first = bit(source, 1) + 2 * bit(row, 0)
        second = bit(source, 0)
        return 2.0 * first.astype(F32), second.astype(F32) + (2.0 * sub[0] + 4.0 * sub[1])

    make_turns(table, 64, box, 6, speeds, 256, node, 0, 4, 8)
    stores[1].start()

    def box(source, row):
        first = bit(source, 1)
        second = bit(source, 0) + 2 * bit(row, 1)
        return 2.0 * first.astype(F32), second.astype(F32)

    make_turns(table, 128, box, 7, speeds, 512, node, 0, 4, 8)
    stores[2].start()

    def box(source, row):
        return jnp.float32(0.0), source.astype(F32)

    make_turns(table, 192, box, 8, speeds, 768, node, 4, 2, 16, stores[3:5])

    def last(index, carry):
        def column(table):
            value = speeds[pl.ds(pl.multiple_of(256 * table + index * 16, 16), 16), :]
            return jnp.concatenate([value, value], axis=1)

        first = column(5)
        second = column(6)
        turns = first * node[8:9, :]
        turns = turns - ((turns + ROUNDER) - ROUNDER)
        across = second * node[10:11, :]
        across = across - ((across + ROUNDER) - ROUNDER)
        around = column(4) * node[12:13, :]
        around = around - ((around + ROUNDER) - ROUNDER)
        turns = turns + across + around + first * node[9:10, :] + second * node[11:12, :]
        cosine, sine = turn(turns)
        table[224 + index, 0] = cosine
        table[224 + index, 1] = sine
        return carry

    lax.fori_loop(0, 16, last, 0)
    stores[5].start()
    for store in stores:
        store.wait()


def deposit(
    arrived, table, second, fetch_second, state, wide, cells, hots, spreads, grid
):
    points = [float(value) for value in chebyshev_points(NODES).astype(np.float32)]
    factors = basis_factors()

    def source_step(index, carry):
        rows = pl.ds(pl.multiple_of(index * 16, 16), 16)
        first, second, real, imaginary = (
            arrived[pl.ds(index * 64 + k, 16, stride=4), :] for k in range(4)
        )
        whole_first = first.astype(jnp.int32)
        whole_second = second.astype(jnp.int32)
        along = first + 0.5
        across = second + 0.5
        eighths = jnp.bitwise_and(whole_first + whole_second + 1, 7).astype(F32)
        cosine, sine = turn(
            0.125 * eighths + 0.0625 * jnp.sqrt(along * along + across * across)
        )
        lanes = pl.ds(pl.multiple_of(index % 2 * 128, 128), 128)
        live = table[256 + index // 4, index // 2 % 2, :, lanes]
        real = real * live
        imaginary = imaginary * live
        turned = (real * cosine - imaginary * sine, real * sine + imaginary * cosine)
        place = jnp.bitwise_and(whole_first, 31).astype(F32) * 0.03125 + 0.015625
        cells[0, rows, :] = jnp.bitwise_and(whole_second, 15).astype(F32)
        x = [bit(whole_first, 5 + k) for k in range(4)]
        y = [bit(whole_second, 4 + k) for k in range(4)]
        cells[1, rows, :] = (x[0] * 8 + y[0] * 4 + x[1] * 2 + y[1]).astype(F32)
        cells[2, rows, :] = (y[3] * 8 + x[2] * 4 + y[2] * 2 + x[3]).astype(F32)
        away = [place - value for value in points]
        before = [None] * NODES
        after = [None] * NODES
        for p in range(1, NODES):
            before[p] = away[p - 1] if p == 1 else before[p - 1] * away[p - 1]
            q = NODES - 1 - p
            after[q] = away[q + 1] if p == 1 else after[q + 1] * away[q + 1]
        for p in range(NODES):
            if p == 0:
                value = after[0]
            elif p == NODES - 1:
                value = before[p]
            else:
                value = before[p] * after[p]
            value = value * factors[p]
            for part in range(2):
                wide[pl.ds(index * 512 + part * 16 + p, 16, stride=32), :] = value * turned[part]
        return carry

    lax.fori_loop(0, 8, source_step, 0)

    iota = lax.broadcasted_iota(jnp.int32, (16, 128), 0).astype(F32).astype(BF16)
    one = jnp.ones((16, 128), BF16)
    zero = jnp.zeros((16, 128), BF16)

    def build(chunk, hot, spread):
        for k in range(16):
            sender = chunk * 16 + k
            lanes = slice(128 * k, 128 * (k + 1))

            def row(number, height):
                value = cells[number, pl.ds(sender, 1), :]
                return jnp.broadcast_to(value, (height, 128)).astype(BF16)

            value = wide[pl.ds(pl.multiple_of(sender * 32, 32), 32), :].astype(BF16)
            cell = row(0, 16)
            for c in range(16):
                chosen = cell == jnp.full((16, 128), c, BF16)
                for part in range(2):
                    spread[32 * c + 16 * part : 32 * c + 16 * (part + 1), lanes] = jnp.where(
                        chosen, value[16 * part : 16 * (part + 1)], zero
                    )
            inside = jnp.where(row(2, 16) == iota, one, zero)
            above = row(1, 16)
            for c in range(16):
                hot[16 * c : 16 * (c + 1), lanes] = jnp.where(
                    above == jnp.full((16, 128), c, BF16), inside, zero
                )

    def product(hot, spread):
        return lax.dot_general(
            spread[...], hot[...], (((1,), (1,)), ((), ())), preferred_element_type=F32
        )

    grid[...] = jnp.zeros_like(grid)

    def spread_step(index, carry):
        for k in range(2):
            build(2 * index + k, hots[k], spreads[k])
        parts = [product(hots[k], spreads[k]) for k in range(2)]
        grid[...] += parts[0] + parts[1]
        return carry

    lax.fori_loop(0, 4, spread_step, 0)

    grid_high, grid_low = split(grid[...].T)
    fetch_second.wait()
    operand = jnp.concatenate([grid_high, grid_low, grid_high], axis=1)
    for part in range(2):
        result = jnp.dot(
            operand, second[1536 * part : 1536 * (part + 1), :], preferred_element_type=F32
        )
        for group in range(32):
            state[group, part] = result[8 * group : 8 * group + 8, :]


def halves(value):
    return value[:, :128], value[:, 128:]


def inner_kernel(
    arrived,
    table_far,
    matrix_far,
    out,
    second,
    matrix,
    table,
    arrive,
    wide,
    cells,
    hots,
    spreads,
    grid,
    other,
    turned,
    highs,
    lows,
    state,
):
    fetch_mask = fetch_mask_lines(table_far, table, arrive.at[6])
    fetch_mask.start()
    fetch_second = pltpu.make_async_copy(matrix_far.at[pl.ds(4608, 3072)], second, arrive.at[4])
    fetch_second.start()
    fetches = [fetch_level(table_far, table, arrive, k) for k in range(4)]
    for fetch in fetches:
        fetch.start()
    fetch_matrix = pltpu.make_async_copy(matrix_far.at[pl.ds(0, 3072)], matrix, arrive.at[5])
    fetch_matrix.start()
    fetch_mask.wait()
    deposit(arrived, table, second, fetch_second, state, wide, cells, hots, spreads, grid)

    def run(number, read, emit):
        level(
            read,
            table,
            64 * (number - 1),
            highs,
            lows,
            matrix,
            4,
            8,
            fetches[number - 1 : number],
            emit,
            fetch_matrix if number == 1 else None,
        )

    def leaf(group, part):
        return state[group, part]

    def read(group, part):
        return other[group, part]

    def keep(child, row, values):
        for part in range(2):
            other[(row // 2) * 8 + child * 2 + row % 2, part] = values[part]

    run(1, leaf, keep)

    def turn_over(child, row, values):
        start = ((row % 2 * 2 + child // 2) * 8 + row // 2 * 2 + child % 2) * 8
        for part in range(2):
            for half, value in enumerate(halves(values[part])):
                turned[2 * part + half, start : start + 8, :] = value

    run(2, read, turn_over)

    def across(group, part):
        b2x, b2y, b3x, b3y, t2x = bits(group, 5)
        start = (b3y * 2 + t2x) * 64 + b2x * 4 + b2y * 2 + b3x
        return jnp.concatenate(
            [turned.at[2 * part + half][pl.ds(start, 8, stride=8), :] for half in range(2)], axis=1
        )

    run(3, across, keep)

    def send(child, row, values):
        x, y = bits(child, 2)
        r0, r1, r2 = bits(row, 3)
        device = r2 * 32 + r0 * 16 + x * 8 + r1
        for upper in range(2):
            for part in range(2):
                for half, value in enumerate(halves(values[part])):
                    start = (device + 64 * upper) * 8 + y * 4 + half * 2 + part
                    out[pl.ds(start, 4, stride=16), :] = value[4 * upper : 4 * upper + 4]

    run(4, read, send)


def outer_kernel(
    arrived, table_far, matrix_far, out, table, matrix, last, arrive, state, turned, highs, lows
):
    first = [
        pltpu.make_async_copy(
            table_far.at[pl.ds(16 * k, 16)], table.at[pl.ds(16 * k, 16)], arrive.at[6 + k]
        )
        for k in range(4)
    ]
    fetches = [
        fetch_level(table_far, table, arrive, k, 64 if k < 3 else 48) for k in range(1, 4)
    ]
    fetch_matrix = pltpu.make_async_copy(matrix_far.at[pl.ds(0, 3072)], matrix, arrive.at[5])
    fetch_last = pltpu.make_async_copy(matrix_far.at[pl.ds(3072, 1536)], last, arrive.at[4])
    for fetch in first + [fetch_matrix] + fetches + [fetch_last]:
        fetch.start()

    def first_read(group, part):
        i2, j3, i1, i0, j2 = bits(group, 5)
        source = i2 * 64 + i1 * 32 + i0 * 16 + j3 * 8 + j2 * 4
        return jnp.concatenate(
            [
                arrived[pl.ds(source * 8 + half * 2 + part, 8, stride=4), :]
                for half in range(2)
            ],
            axis=1,
        )

    def run(number, read, emit):
        level(
            read,
            table,
            64 * (number - 5),
            highs,
            lows,
            matrix,
            4,
            8,
            first if number == 5 else fetches[number - 6 : number - 5],
            emit,
            fetch_matrix if number == 5 else None,
        )

    def read(group, part):
        return state[group, part]

    def keep(child, row, values):
        i1, i0, j2 = bits(row, 3)
        for part in range(2):
            state[(2 * i1 + j2) * 8 + child * 2 + i0, part] = values[part]

    run(5, first_read, keep)

    def turn_over(child, row, values):
        start = ((row % 2 * 2 + child // 2) * 8 + row // 2 * 2 + child % 2) * 8
        for part in range(2):
            for half, value in enumerate(halves(values[part])):
                turned[2 * part + half, start : start + 8, :] = value

    run(6, read, turn_over)

    def across(group, part):
        i0, j1, t6x, j0, pair = bits(group, 5)
        start = (i0 * 2 + t6x) * 64 + j1 * 4 + j0 * 2 + pair
        return jnp.concatenate(
            [turned.at[2 * part + half][pl.ds(start, 8, stride=8), :] for half in range(2)], axis=1
        )

    def keep_last(child, row, values):
        t6x, j0, pair = bits(row, 3)
        for part in range(2):
            state[j0 * 16 + child * 4 + t6x * 2 + pair, part] = values[part]

    run(7, across, keep_last)

    def send(child, row, values):
        t7x, t7y, t6x, pair = bits(row, 4)
        line = 224 + child * 8 + row // 2
        cosine = table[line, 0, 8 * (row % 2) : 8 * (row % 2) + 8, :]
        sine = table[line, 1, 8 * (row % 2) : 8 * (row % 2) + 8, :]
        real, imaginary = values
        device = t6x * 32 + t7x * 16 + t7y * 2 + child
        for part, whole in enumerate(
            (real * cosine + imaginary * sine, imaginary * cosine - real * sine)
        ):
            for half, value in enumerate(halves(whole)):
                for upper in range(2):
                    place = (device + 64 * upper) * 8 + pair * 4 + half * 2 + part
                    out[pl.ds(place, 4, stride=32), :] = value[4 * upper : 4 * upper + 4]

    level(
        read, table, 192, highs, lows, last, 2, 16, fetches[2:], send, fetch_last
    )


def vmem(count):
    return [pl.BlockSpec(memory_space=pltpu.VMEM)] * count


def smem(count):
    return [pl.BlockSpec(memory_space=pltpu.SMEM)] * count


def far(count):
    return [pl.BlockSpec(memory_space=pltpu.HBM)] * count


def payload_kernel(place_far, amp_far, out_far, place, amp, out, arrive, leave):
    fetches = [
        pltpu.make_async_copy(place_far, place, arrive.at[0]),
        pltpu.make_async_copy(amp_far, amp, arrive.at[1]),
    ]
    for fetch in fetches:
        fetch.start()
    for fetch in fetches:
        fetch.wait()
    for k in range(2):
        out[pl.ds(k, DEVICES, stride=4), :] = place[k].astype(F32)
        out[pl.ds(2 + k, DEVICES, stride=4), :] = amp[k]
    store = pltpu.make_async_copy(out, out_far, leave)
    store.start()
    store.wait()


def make_payload(place, amp):
    return pl.pallas_call(
        payload_kernel,
        out_shape=jax.ShapeDtypeStruct((4 * DEVICES, 128), F32),
        in_specs=far(2),
        out_specs=far(1)[0],
        scratch_shapes=[
            pltpu.VMEM((2, DEVICES, 128), jnp.int32),
            pltpu.VMEM((2, DEVICES, 128), F32),
            pltpu.VMEM((4 * DEVICES, 128), F32),
            pltpu.SemaphoreType.DMA((2,)),
            pltpu.SemaphoreType.DMA,
        ],
        name="payload",
        compiler_params=pltpu.CompilerParams(vmem_limit_bytes=60 << 20),
    )(place, amp)


def inner_turns(block_first, block_second, slots):
    speeds = np.repeat(inner_speeds()[:, None], 128, axis=1)
    return pl.pallas_call(
        inner_turns_kernel,
        out_shape=jax.ShapeDtypeStruct((258, 2, 16, 256), F32),
        in_specs=smem(2) + far(3),
        out_specs=far(1)[0],
        scratch_shapes=[
            pltpu.VMEM((64, 256), jnp.int32),
            pltpu.VMEM((24, 256), F32),
            pltpu.VMEM((1024, 128), F32),
            pltpu.VMEM((258, 2, 16, 256), F32),
            pltpu.VMEM((2, 128, 128), F32),
            pltpu.VMEM((256, 8192), BF16),
            pltpu.VMEM((256, 8192), BF16),
            pltpu.SemaphoreType.DMA((3,)),
            pltpu.SemaphoreType.DMA((8,)),
        ],
        name="inner_turns",
        compiler_params=pltpu.CompilerParams(vmem_limit_bytes=60 << 20),
    )(block_first, block_second, slots, jnp.asarray(node_tables()), jnp.asarray(speeds))


def outer_turns(speeds):
    return pl.pallas_call(
        outer_turns_kernel,
        out_shape=jax.ShapeDtypeStruct((240, 2, 16, 256), F32),
        in_specs=vmem(2),
        out_specs=far(1)[0],
        scratch_shapes=[
            pltpu.VMEM((240, 2, 16, 256), F32),
            pltpu.SemaphoreType.DMA((7,)),
        ],
        name="outer_turns",
        compiler_params=pltpu.CompilerParams(vmem_limit_bytes=52 << 20),
    )(jnp.asarray(node_tables()), speeds)


LEVEL_SCRATCH = [
    pltpu.VMEM((32, 2, 8, 256), F32),
    pltpu.VMEM((4, 256, 128), F32),
    [pltpu.VMEM((512, 512), BF16)] * 2,
    [pltpu.VMEM((512, 512), BF16)] * 2,
]


def inner_levels(arrived, table):
    return pl.pallas_call(
        inner_kernel,
        out_shape=jax.ShapeDtypeStruct((1024, 128), F32),
        in_specs=vmem(1) + far(2),
        out_specs=vmem(1)[0],
        scratch_shapes=[
            pltpu.VMEM((3072, 256), BF16),
            pltpu.VMEM((3072, 256), BF16),
            pltpu.VMEM((258, 2, 16, 256), F32),
            pltpu.SemaphoreType.DMA((7,)),
            pltpu.VMEM((4096, 128), F32),
            pltpu.VMEM((3, 128, 128), F32),
            [pltpu.VMEM((256, 2048), BF16)] * 2,
            [pltpu.VMEM((512, 2048), BF16)] * 2,
            pltpu.VMEM((512, 256), F32),
        ]
        + LEVEL_SCRATCH
        + LEVEL_SCRATCH[:1],
        name="inner",
        compiler_params=pltpu.CompilerParams(vmem_limit_bytes=52 << 20),
    )(
        arrived,
        table,
        jnp.asarray(matrices()),
    )


def outer_levels(arrived, table):
    return pl.pallas_call(
        outer_kernel,
        out_shape=jax.ShapeDtypeStruct((1024, 128), F32),
        in_specs=vmem(1) + far(2),
        out_specs=vmem(1)[0],
        scratch_shapes=[
            pltpu.VMEM((240, 2, 16, 256), F32),
            pltpu.VMEM((3072, 256), BF16),
            pltpu.VMEM((1536, 256), BF16),
            pltpu.SemaphoreType.DMA((10,)),
        ]
        + LEVEL_SCRATCH,
        name="outer",
        compiler_params=pltpu.CompilerParams(vmem_limit_bytes=52 << 20),
    )(
        arrived,
        table,
        jnp.asarray(matrices()),
    )


def reverse_bits(number, bit_count):
    result = jnp.zeros_like(number)
    for position in range(bit_count):
        result = result + jnp.left_shift(
            jnp.bitwise_and(jnp.right_shift(number, position), 1), bit_count - 1 - position
        )
    return result


def exchange(array):
    return lax.all_to_all(array, ("bx", "by"), split_axis=0, concat_axis=0, tiled=True)


def shards(src_pos, src_amp, box_slots):
    column = lax.axis_index("bx")
    row = lax.axis_index("by")
    device = column * BY + row
    block_first = reverse_bits(column, 3).astype(jnp.int32).reshape(1)
    block_second = reverse_bits(row, 4).astype(jnp.int32).reshape(1)
    payload = make_payload(src_pos.reshape(2, DEVICES, 128), src_amp.reshape(2, DEVICES, 128))
    arrived = exchange(payload.reshape(DEVICES, 4, 128)).reshape(512, 128)
    table = inner_turns(block_first, block_second, box_slots[0].T)
    arrived, table = lax.optimization_barrier((arrived, table))
    weights = inner_levels(arrived, table)
    weights = exchange(weights.reshape(DEVICES, 8, 128)).reshape(1024, 128)
    speeds = lax.dynamic_index_in_dim(jnp.asarray(outer_speeds()), device, 0, keepdims=False)
    speeds = jnp.broadcast_to(speeds[:, None], (7 * 256, 128))
    weights = outer_levels(weights, outer_turns(speeds))
    weights = exchange(weights.reshape(DEVICES, 8, 128))
    weights = weights.reshape(LEAVES, LEAVES, 2, 2, 128)
    weights = jnp.concatenate([weights[:, :, 0], weights[:, :, 1]], axis=-1)
    return weights.reshape(LEAVES, 1, LEAVES, 1, 2, BOX_NODES)


def solution(mesh):
    return jax.shard_map(
        shards,
        mesh=mesh,
        in_specs=(
            P(None, ("bx", "by"), None),
            P(None, ("bx", "by"), None),
            P(("bx", "by"), None, None),
        ),
        out_specs=P(None, "bx", None, "by", None, None),
        check_vma=False,
    )
```

```python
import functools
import math

import jax
import jax.numpy as jnp
import numpy as np
from jax import lax
from jax.experimental import pallas as pl
from jax.experimental.pallas import tpu as pltpu
from jax.sharding import PartitionSpec as P

NODES = 16
BOX_NODES = 256
DEVICES = 128
LEAVES = 16
BX = 8
BY = 16
BAND = 1024
F32 = jnp.float32
BF16 = jnp.bfloat16
ROUNDER = 12582912.0
SIN = (6.28305581, -41.33121471, 81.36682035, -74.47802935, 32.78144238)
COS = (0.99995995, -19.73105034, 64.67355678, -82.40422428, 45.64775943)


def chebyshev_points(point_count):
    indices = np.arange(point_count)
    return (1.0 - np.cos(np.pi * (2 * indices + 1) / (2 * point_count))) / 2.0


def lagrange_matrix(locations):
    points = chebyshev_points(NODES)
    matrix = np.ones((len(locations), NODES))
    for own in range(NODES):
        for other in range(NODES):
            if other != own:
                matrix[:, own] *= (locations - points[other]) / (points[own] - points[other])
    return matrix


def child_matrix(halves, child):
    if halves == 1:
        return np.eye(NODES)
    return lagrange_matrix((child + chebyshev_points(NODES)) / 2.0)


def stacked_matrix(halves_first, halves_second):
    pieces = [
        np.kron(child_matrix(halves_first, a), child_matrix(halves_second, b))
        for a in range(halves_first)
        for b in range(halves_second)
    ]
    return np.concatenate(pieces, axis=0)


def two_parts(matrix):
    exact = np.asarray(matrix, np.float32)
    high = exact.astype(jnp.bfloat16)
    low = (exact - high.astype(np.float32)).astype(jnp.bfloat16)
    return high, low


def velocity(first, second):
    return (2.0 + np.sin(2 * np.pi * first) * np.sin(2 * np.pi * second)) / 8.0


def bits(value, count):
    return [(value >> (count - 1 - k)) & 1 for k in range(count)]


def speed_change(first, second, level, split_first=True):
    count_second = 2.0**level
    count_first = 2.0 ** (level if split_first else level - 1)
    new = velocity((first + 0.5) / count_first, (second + 0.5) / count_second)
    above_first = first >> 1 if split_first else first
    old = velocity(
        (above_first + 0.5) / 2.0 ** (level - 1), ((second >> 1) + 0.5) / 2.0 ** (level - 1)
    )
    return new - old


def inner_speeds():
    table = np.zeros((4, 4, 8, 8))
    for child in range(4):
        x, y = bits(child, 2)
        for row in range(8):
            r0, r1, r2 = bits(row, 3)
            for sub in range(8):
                s0, s1, s2 = bits(sub, 3)
                table[0, child, row, sub] = speed_change(x, y, 1)
                table[1, child, row, sub] = speed_change(2 * r0 + x, 2 * r1 + y, 2)
                first, second = 2 * s0 + r2, 2 * s1 + s2
                table[2, child, row, sub] = speed_change(2 * first + x, 2 * second + y, 3)
                first, second = 2 * first + r0, 2 * second + r1
                table[3, child, row, sub] = speed_change(2 * first + x, 2 * second + y, 4)
    return table.reshape(1024).astype(np.float32)


def outer_speeds():
    tables = np.zeros((DEVICES, 7, 256))
    for device in range(DEVICES):
        coarse_first = device >> 3
        for child in range(4):
            x, y = bits(child, 2)
            for row in range(8):
                r0, r1, r2 = bits(row, 3)
                for sub in range(8):
                    s0, s1, s2 = bits(sub, 3)
                    place = child * 64 + row * 8 + sub
                    second = 2 * (device & 7) + s2
                    tables[device, 0, place] = speed_change(
                        2 * coarse_first + x, 2 * second + y, 5
                    )
                    tables[device, 1, place] = speed_change(
                        4 * coarse_first + 2 * r0 + x, 4 * second + 2 * r1 + y, 6
                    )
                    second = 2 * (device & 7) + r2
                    tables[device, 2, place] = speed_change(
                        8 * coarse_first + 4 * s0 + 2 * r0 + x,
                        8 * second + 4 * s1 + 2 * s2 + y,
                        7,
                    )
        for child in range(2):
            for row in range(16):
                r0, r1, r2, r3 = bits(row, 4)
                for sub in range(8):
                    s0, s1, s2 = bits(sub, 3)
                    place = child * 128 + row * 8 + sub
                    first = 8 * coarse_first + 4 * s0 + 2 * r2 + r0
                    second = 2 * (device & 7) + r3
                    second = 16 * second + 8 * s1 + 4 * s2 + 2 * r1 + child
                    tables[device, 3, place] = speed_change(first, second, 8, False)
                    tables[device, 4, place] = velocity((first + 0.5) / 128, (second + 0.5) / 256)
                    tables[device, 5, place] = 8 * (first + 0.5)
                    tables[device, 6, place] = 4 * (second + 0.5)
    return tables.reshape(DEVICES, 7 * 256).astype(np.float32)


def node_tables():
    points = chebyshev_points(NODES).astype(np.float32).astype(np.float64)
    first = np.repeat(points, NODES)
    second = np.tile(points, NODES)
    rows = np.zeros((24, BOX_NODES))
    for child in range(4):
        x, y = bits(child, 2)
        turns = (2 * x - 1) * 2 * first + (2 * y - 1) * second
        rows[child] = turns - np.round(turns)
    for child in range(2):
        rows[4 + child] = (2 * child - 1) * second
    rows[6] = 2 * first
    rows[7] = second
    rows[8] = np.round(first * 8192) / 8192
    rows[9] = first - rows[8]
    rows[10] = np.round(second * 8192) / 8192
    rows[11] = second - rows[10]
    for child in range(2):
        rows[16 + 2 * child] = np.cos(2 * np.pi * rows[child])
        rows[17 + 2 * child] = np.sin(2 * np.pi * rows[child])
    rows[12] = BAND * np.sqrt(first * first + second * second)
    return rows.astype(np.float32)


def basis_factors():
    points = chebyshev_points(NODES)
    return [
        float(np.float32(1.0 / np.prod([points[own] - points[k] for k in range(NODES) if k != own])))
        for own in range(NODES)
    ]


def second_basis():
    small = lagrange_matrix((np.arange(16) + 0.5) / 16.0)
    whole = np.zeros((16, 32, 32, 16))
    for k in range(32):
        whole[:, k, k, :] = small
    return whole.reshape(512, 512)


def turn(turns):
    part = turns - ((turns + ROUNDER) - ROUNDER)
    square = part * part
    sine = SIN[4]
    cosine = COS[4]
    for k in (3, 2, 1, 0):
        sine = sine * square + SIN[k]
        cosine = cosine * square + COS[k]
    return cosine, sine * part


def split(value):
    high = value.astype(BF16)
    return high, (value - high.astype(F32)).astype(BF16)


def bit(value, place):
    return (value >> place) & 1


def make_turns(
    table, first_line, box, level_number, speeds, speed_row, node, base_row, children, rows, stores=()
):
    scale = 4.0 * 2.0 ** (level_number - 1)
    pairs = rows // 2

    def step(index, carry):
        source = index // pairs
        pair = lax.rem(index, pairs)
        radius = []
        for k in range(2):
            first, second = box(source, 2 * pair + k)
            along = first + node[6:7, :]
            across = second + node[7:8, :]
            radius.append(scale * jnp.sqrt(along * along + across * across))
        radius = jnp.concatenate([jnp.broadcast_to(value, (8, BOX_NODES)) for value in radius])
        for child in range(children):
            place = pl.multiple_of(speed_row + child * rows * 8 + pair * 16, 16)
            change = speeds[pl.ds(place, 16), :]
            change = jnp.concatenate([change, change], axis=1)
            cosine, sine = turn(change * radius + node[base_row + child : base_row + child + 1, :])
            line = first_line + index * children + child
            table[line, 0] = cosine
            table[line, 1] = sine
        return carry

    if not stores:
        lax.fori_loop(0, (4 if children == 4 else 2) * pairs, step, 0)
    for source, store in enumerate(stores):
        lax.fori_loop(source * pairs, (source + 1) * pairs, step, 0)
        store.start()


def make_first_turns(table, box, node):
    def step(index, carry):
        radius = []
        for k in range(2):
            first, second = box(index // 4, 2 * (index % 4) + k)
            along = first + node[6:7, :]
            across = second + node[7:8, :]
            radius.append(0.5 * jnp.sqrt(along * along + across * across))
        cosine, sine = turn(jnp.concatenate(radius))
        for kind in range(2):
            base_cosine = node[16 + 2 * kind : 17 + 2 * kind, :]
            base_sine = node[17 + 2 * kind : 18 + 2 * kind, :]
            cosines = base_cosine * cosine
            sines = base_sine * sine
            mixed = base_sine * cosine
            other = base_cosine * sine
            line = 4 * index + kind
            mirror = 4 * index + 3 - kind
            if kind == 0:
                table[line, 0] = cosines - sines
                table[line, 1] = mixed + other
                table[mirror, 0] = cosines + sines
                table[mirror, 1] = other - mixed
            else:
                table[line, 0] = cosines + sines
                table[line, 1] = mixed - other
                table[mirror, 0] = cosines - sines
                table[mirror, 1] = -mixed - other
        return carry

    lax.fori_loop(0, 16, step, 0)


def level(
    read, table, first_line, highs, lows, matrix, children, rows, by_rows, ready, emit, matrix_ready=None
):
    sources = 4 if children == 4 else 2
    pairs = rows // 2
    columns = sources * BOX_NODES
    for half in range(2):
        high, low = highs[half], lows[half]
        if by_rows:
            chosen = list(range(children))
            near = list(range(half * pairs // 2, (half + 1) * pairs // 2))
        else:
            chosen = list(range(half * children // 2, (half + 1) * children // 2))
            near = list(range(pairs))
        height = 16 * len(near)
        for source in range(sources):
            lanes = slice(source * BOX_NODES, (source + 1) * BOX_NODES)
            if half == 0 and source < len(ready):
                ready[source].wait()
            for spot, pair in enumerate(near):
                group = source * rows + 2 * pair
                real, imaginary = (
                    jnp.concatenate([read(group, part), read(group + 1, part)])
                    for part in range(2)
                )
                for number, child in enumerate(chosen):
                    line = first_line + (source * pairs + pair) * children + child
                    cosine = table[line, 0]
                    sine = table[line, 1]
                    for part, value in enumerate(
                        (real * cosine - imaginary * sine, real * sine + imaginary * cosine)
                    ):
                        place = (number * 2 + part) * height + spot * 16
                        value_high, value_low = split(value)
                        high[place : place + 16, lanes] = value_high
                        low[place : place + 16, lanes] = value_low
        if half == 0 and matrix_ready is not None:
            matrix_ready.wait()
        both = jnp.dot(high[:, :columns], matrix[...], preferred_element_type=F32)
        rest = jnp.dot(low[:, :columns], matrix[:, :BOX_NODES], preferred_element_type=F32)
        result = both[:, :BOX_NODES] + (both[:, BOX_NODES:] + rest)
        for number, child in enumerate(chosen):
            for spot, pair in enumerate(near):
                for k in range(2):
                    start = number * 2 * height + spot * 16 + 8 * k
                    emit(
                        child,
                        2 * pair + k,
                        [result[start + height * part : start + height * part + 8] for part in range(2)],
                    )


def matrices():
    basis = second_basis()
    rows = [
        stacked_matrix(2, 2),
        stacked_matrix(1, 2),
        basis[:, :256],
        basis[:, 256:],
    ]
    return np.concatenate(two_parts(np.concatenate(rows)), axis=1)


def sub_bits():
    row = lax.broadcasted_iota(jnp.int32, (8, BOX_NODES), 0)
    return [bit(row, 2 - k).astype(F32) for k in range(3)]


def find_mask(slots, table, entries, high_hot, low_hot):
    iota = lax.broadcasted_iota(jnp.int32, (16, 128), 0).astype(F32)
    rows = [(iota + 16.0 * k).astype(BF16) for k in range(8)]
    one = jnp.ones((16, 128), BF16)
    zero = jnp.zeros((16, 128), BF16)
    block = jnp.concatenate([slots[:, :128], slots[:, 128:]], axis=0)
    entries[0] = (block >> 7).astype(F32)
    entries[1] = (block & 127).astype(F32)

    def step(index, carry):
        for source, hot in enumerate((high_hot, low_hot)):
            for side in range(2):
                start = pl.multiple_of(index * 8 + 64 * side, 8)
                block = entries[source, pl.ds(start, 8), :]
                for k in range(8):
                    value = jnp.broadcast_to(block[k : k + 1], (16, 128)).astype(BF16)
                    lanes = pl.ds(pl.multiple_of(index * 1024 + 128 * k, 128), 128)
                    for place in range(8):
                        line = 128 * side + 16 * place
                        hot[line : line + 16, lanes] = jnp.where(value == rows[place], one, zero)
        return carry

    lax.fori_loop(0, 8, step, 0)
    parts = [
        lax.dot_general(
            high_hot[:, 4096 * k : 4096 * (k + 1)],
            low_hot[:, 4096 * k : 4096 * (k + 1)],
            (((1,), (1,)), ((), ())),
            preferred_element_type=F32,
        )
        for k in range(2)
    ]
    total = parts[0] + parts[1]
    mask = jnp.where(total[:128, :128] + total[128:, 128:] > 0.5, 1.0, 0.0)
    for k in range(8):
        lanes = slice(128 * (k % 2), 128 * (k % 2 + 1))
        table[256 + k // 4, k // 2 % 2, :, lanes] = mask[16 * k : 16 * (k + 1)]


def store_level(table, table_far, leave, index, size=64, first=0):
    lines = pl.ds(size * index, size)
    place = leave.at[index if first == 0 else first + index % 4]
    return pltpu.make_async_copy(table.at[lines], table_far.at[lines], place)


def fetch_level(table_far, table, arrive, index, size=64):
    lines = pl.ds(64 * index, size)
    return pltpu.make_async_copy(table_far.at[lines], table.at[lines], arrive.at[index])


def fetch_mask_lines(table_far, table, place):
    lines = pl.ds(256, 2)
    return pltpu.make_async_copy(table_far.at[lines], table.at[lines], place)


def inner_turns_kernel(
    block_first_ref,
    block_second_ref,
    slots_far,
    node_far,
    speeds_far,
    table_far,
    slots,
    node,
    speeds,
    table,
    entries,
    high_hot,
    low_hot,
    arrive,
    leave,
):
    fetches = [
        pltpu.make_async_copy(far, near, arrive.at[k])
        for k, (far, near) in enumerate(
            ((slots_far, slots), (node_far, node), (speeds_far, speeds))
        )
    ]
    for fetch in fetches:
        fetch.start()
    fetches[0].wait()
    find_mask(slots, table, entries, high_hot, low_hot)
    for fetch in fetches[1:]:
        fetch.wait()
    stores = [store_level(table, table_far, leave, k) for k in range(3)]
    stores += [store_level(table, table_far, leave, 12 + k, 16, 3) for k in range(4)]
    store_mask = store_level(table, table_far, leave, 128, 2, 7)
    store_mask.start()
    sub = sub_bits()
    block_first = block_first_ref[0]
    block_second = block_second_ref[0]

    def box(source, row):
        first = block_first * 16 + bit(source, 1) + 2 * bit(row, 2)
        second = block_second * 16 + bit(source, 0) + 2 * bit(row, 1) + 8 * bit(row, 0)
        return (
            2.0 * first.astype(F32) + (8.0 * sub[0] + 16.0 * sub[2]),
            second.astype(F32) + 4.0 * sub[1],
        )

    make_first_turns(table, box, node)
    stores[0].start()

    def box(source, row):
        first = block_first * 8 + bit(source, 1)
        second = block_second * 8 + bit(source, 0) + 4 * bit(row, 0)
        return (
            2.0 * first.astype(F32) + (4.0 * sub[0] + 8.0 * sub[2]),
            second.astype(F32) + 2.0 * sub[1],
        )

    make_turns(table, 64, box, 2, speeds, 256, node, 0, 4, 8)
    stores[1].start()

    def box(source, row):
        first = block_first * 4 + bit(source, 1) + 2 * bit(row, 2)
        second = block_second * 4 + bit(source, 0) + 2 * bit(row, 1)
        return 2.0 * first.astype(F32), second.astype(F32)

    make_turns(table, 128, box, 3, speeds, 512, node, 0, 4, 8)
    stores[2].start()

    def box(source, row):
        first = block_first * 2 + bit(source, 1)
        second = block_second * 2 + bit(source, 0)
        return 2.0 * first.astype(F32), second.astype(F32)

    make_turns(table, 192, box, 4, speeds, 768, node, 0, 4, 8, stores[3:])
    for store in stores + [store_mask]:
        store.wait()


def outer_turns_kernel(node, speeds, table_far, table, leave):
    stores = [store_level(table, table_far, leave, k) for k in range(3)]
    stores += [store_level(table, table_far, leave, 12 + k, 16, 3) for k in range(3)]
    sub = sub_bits()

    def box(source, row):
        first = bit(source, 1) + 2 * bit(row, 2) + 4 * bit(row, 1)
        second = bit(source, 0) + 2 * bit(row, 0)
        return 2.0 * first.astype(F32), second.astype(F32) + (4.0 * sub[0] + 8.0 * sub[1])

    make_turns(table, 0, box, 5, speeds, 0, node, 0, 4, 8)
    stores[0].start()

    def box(source, row):
        first = bit(source, 1) + 2 * bit(row, 0)
        second = bit(source, 0)
        return 2.0 * first.astype(F32), second.astype(F32) + (2.0 * sub[0] + 4.0 * sub[1])

    make_turns(table, 64, box, 6, speeds, 256, node, 0, 4, 8)
    stores[1].start()

    def box(source, row):
        first = bit(source, 1)
        second = bit(source, 0) + 2 * bit(row, 1)
        return 2.0 * first.astype(F32), second.astype(F32)

    make_turns(table, 128, box, 7, speeds, 512, node, 0, 4, 8)
    stores[2].start()

    def box(source, row):
        return jnp.float32(0.0), source.astype(F32)

    make_turns(table, 192, box, 8, speeds, 768, node, 4, 2, 16, stores[3:5])

    def last(index, carry):
        def column(table):
            value = speeds[pl.ds(pl.multiple_of(256 * table + index * 16, 16), 16), :]
            return jnp.concatenate([value, value], axis=1)

        first = column(5)
        second = column(6)
        turns = first * node[8:9, :]
        turns = turns - ((turns + ROUNDER) - ROUNDER)
        across = second * node[10:11, :]
        across = across - ((across + ROUNDER) - ROUNDER)
        around = column(4) * node[12:13, :]
        around = around - ((around + ROUNDER) - ROUNDER)
        turns = turns + across + around + first * node[9:10, :] + second * node[11:12, :]
        cosine, sine = turn(turns)
        table[224 + index, 0] = cosine
        table[224 + index, 1] = sine
        return carry

    lax.fori_loop(0, 16, last, 0)
    stores[5].start()
    for store in stores:
        store.wait()


def deposit(
    arrived, table, second, fetch_second, state, wide, cells, hots, spreads, grid
):
    points = [float(value) for value in chebyshev_points(NODES).astype(np.float32)]
    factors = basis_factors()

    def source_step(index, carry):
        rows = pl.ds(pl.multiple_of(index * 16, 16), 16)
        first, second, real, imaginary = (
            arrived[pl.ds(index * 64 + k, 16, stride=4), :] for k in range(4)
        )
        whole_first = first.astype(jnp.int32)
        whole_second = second.astype(jnp.int32)
        along = first + 0.5
        across = second + 0.5
        eighths = jnp.bitwise_and(whole_first + whole_second + 1, 7).astype(F32)
        cosine, sine = turn(
            0.125 * eighths + 0.0625 * jnp.sqrt(along * along + across * across)
        )
        lanes = pl.ds(pl.multiple_of(index % 2 * 128, 128), 128)
        live = table[256 + index // 4, index // 2 % 2, :, lanes]
        real = real * live
        imaginary = imaginary * live
        turned = (real * cosine - imaginary * sine, real * sine + imaginary * cosine)
        place = jnp.bitwise_and(whole_first, 31).astype(F32) * 0.03125 + 0.015625
        cells[0, rows, :] = jnp.bitwise_and(whole_second, 15).astype(F32)
        x = [bit(whole_first, 5 + k) for k in range(4)]
        y = [bit(whole_second, 4 + k) for k in range(4)]
        cells[1, rows, :] = (x[0] * 8 + y[0] * 4 + x[1] * 2 + y[1]).astype(F32)
        cells[2, rows, :] = (y[3] * 8 + x[2] * 4 + y[2] * 2 + x[3]).astype(F32)
        away = [place - value for value in points]
        before = [None] * NODES
        after = [None] * NODES
        for p in range(1, NODES):
            before[p] = away[p - 1] if p == 1 else before[p - 1] * away[p - 1]
            q = NODES - 1 - p
            after[q] = away[q + 1] if p == 1 else after[q + 1] * away[q + 1]
        for p in range(NODES):
            if p == 0:
                value = after[0]
            elif p == NODES - 1:
                value = before[p]
            else:
                value = before[p] * after[p]
            value = value * factors[p]
            for part in range(2):
                wide[pl.ds(index * 512 + part * 16 + p, 16, stride=32), :] = value * turned[part]
        return carry

    lax.fori_loop(0, 8, source_step, 0)

    iota = lax.broadcasted_iota(jnp.int32, (16, 128), 0).astype(F32).astype(BF16)
    one = jnp.ones((16, 128), BF16)
    zero = jnp.zeros((16, 128), BF16)

    def build(chunk, hot, spread):
        for k in range(16):
            sender = chunk * 16 + k
            lanes = slice(128 * k, 128 * (k + 1))

            def row(number, height):
                value = cells[number, pl.ds(sender, 1), :]
                return jnp.broadcast_to(value, (height, 128)).astype(BF16)

            value = wide[pl.ds(pl.multiple_of(sender * 32, 32), 32), :].astype(BF16)
            cell = row(0, 16)
            for c in range(16):
                chosen = cell == jnp.full((16, 128), c, BF16)
                for part in range(2):
                    spread[32 * c + 16 * part : 32 * c + 16 * (part + 1), lanes] = jnp.where(
                        chosen, value[16 * part : 16 * (part + 1)], zero
                    )
            inside = jnp.where(row(2, 16) == iota, one, zero)
            above = row(1, 16)
            for c in range(16):
                hot[16 * c : 16 * (c + 1), lanes] = jnp.where(
                    above == jnp.full((16, 128), c, BF16), inside, zero
                )

    grid[...] = jnp.zeros_like(grid)

    def spread_step(index, carry):
        for k in range(2):
            build(2 * index + k, hots[k], spreads[k])
        grid[...] += lax.dot_general(
            jnp.concatenate([hots[0][...], hots[1][...]], axis=1),
            jnp.concatenate([spreads[0][...], spreads[1][...]], axis=1),
            (((1,), (1,)), ((), ())),
            preferred_element_type=F32,
        )
        return carry

    lax.fori_loop(0, 4, spread_step, 0)

    grid_high, grid_low = split(grid[...])
    fetch_second.wait()
    for part in range(2):
        basis = second[512 * part : 512 * (part + 1), :]
        result = jnp.dot(grid_high, basis, preferred_element_type=F32)
        rest = jnp.dot(grid_low, basis[:, :BOX_NODES], preferred_element_type=F32)
        result = result[:, :BOX_NODES] + (result[:, BOX_NODES:] + rest)
        for group in range(32):
            state[group, part] = result[8 * group : 8 * group + 8, :]


def halves(value):
    return value[:, :128], value[:, 128:]


def inner_kernel(
    arrived,
    table_far,
    matrix_far,
    out,
    second,
    matrix,
    table,
    arrive,
    wide,
    cells,
    hots,
    spreads,
    grid,
    other,
    turned,
    highs,
    lows,
    state,
):
    fetch_mask = fetch_mask_lines(table_far, table, arrive.at[6])
    fetch_mask.start()
    fetch_second = pltpu.make_async_copy(matrix_far.at[pl.ds(1536, 1024)], second, arrive.at[4])
    fetch_second.start()
    fetches = [fetch_level(table_far, table, arrive, k) for k in range(4)]
    for fetch in fetches:
        fetch.start()
    fetch_matrix = pltpu.make_async_copy(matrix_far.at[pl.ds(0, 1024)], matrix, arrive.at[5])
    fetch_matrix.start()
    fetch_mask.wait()
    deposit(arrived, table, second, fetch_second, state, wide, cells, hots, spreads, grid)

    def run(number, read, emit):
        level(
            read,
            table,
            64 * (number - 1),
            highs,
            lows,
            matrix,
            4,
            8,
            number % 2 == 0,
            fetches[number - 1 : number],
            emit,
            fetch_matrix if number == 1 else None,
        )

    def leaf(group, part):
        return state[group, part]

    def read(group, part):
        return other[group, part]

    def keep(child, row, values):
        for part in range(2):
            other[(row // 2) * 8 + child * 2 + row % 2, part] = values[part]

    run(1, leaf, keep)

    def turn_over(child, row, values):
        start = ((row % 2 * 2 + child // 2) * 8 + row // 2 * 2 + child % 2) * 8
        for part in range(2):
            for half, value in enumerate(halves(values[part])):
                turned[2 * part + half, start : start + 8, :] = value

    run(2, read, turn_over)

    def across(group, part):
        b2x, b2y, b3x, b3y, t2x = bits(group, 5)
        start = (b3y * 2 + t2x) * 64 + b2x * 4 + b2y * 2 + b3x
        return jnp.concatenate(
            [turned.at[2 * part + half][pl.ds(start, 8, stride=8), :] for half in range(2)], axis=1
        )

    run(3, across, keep)

    def send(child, row, values):
        x, y = bits(child, 2)
        r0, r1, r2 = bits(row, 3)
        device = r2 * 32 + r0 * 16 + x * 8 + r1
        for upper in range(2):
            for part in range(2):
                for half, value in enumerate(halves(values[part])):
                    start = (device + 64 * upper) * 8 + y * 4 + half * 2 + part
                    out[pl.ds(start, 4, stride=16), :] = value[4 * upper : 4 * upper + 4]

    run(4, read, send)


def outer_kernel(
    arrived, table_far, matrix_far, out, table, matrix, last, arrive, state, turned, highs, lows
):
    first = [
        pltpu.make_async_copy(
            table_far.at[pl.ds(16 * k, 16)], table.at[pl.ds(16 * k, 16)], arrive.at[6 + k]
        )
        for k in range(4)
    ]
    fetches = [
        fetch_level(table_far, table, arrive, k, 64 if k < 3 else 48) for k in range(1, 4)
    ]
    fetch_matrix = pltpu.make_async_copy(matrix_far.at[pl.ds(0, 1024)], matrix, arrive.at[5])
    fetch_last = pltpu.make_async_copy(matrix_far.at[pl.ds(1024, 512)], last, arrive.at[4])
    for fetch in first + [fetch_matrix] + fetches + [fetch_last]:
        fetch.start()

    def first_read(group, part):
        i2, j3, i1, i0, j2 = bits(group, 5)
        source = i2 * 64 + i1 * 32 + i0 * 16 + j3 * 8 + j2 * 4
        return jnp.concatenate(
            [
                arrived[pl.ds(source * 8 + half * 2 + part, 8, stride=4), :]
                for half in range(2)
            ],
            axis=1,
        )

    def run(number, read, emit):
        level(
            read,
            table,
            64 * (number - 5),
            highs,
            lows,
            matrix,
            4,
            8,
            number % 2 == 0,
            first if number == 5 else fetches[number - 6 : number - 5],
            emit,
            fetch_matrix if number == 5 else None,
        )

    def read(group, part):
        return state[group, part]

    def keep(child, row, values):
        i1, i0, j2 = bits(row, 3)
        for part in range(2):
            state[(2 * i1 + j2) * 8 + child * 2 + i0, part] = values[part]

    run(5, first_read, keep)

    def turn_over(child, row, values):
        start = ((row % 2 * 2 + child // 2) * 8 + row // 2 * 2 + child % 2) * 8
        for part in range(2):
            for half, value in enumerate(halves(values[part])):
                turned[2 * part + half, start : start + 8, :] = value

    run(6, read, turn_over)

    def across(group, part):
        i0, j1, t6x, j0, pair = bits(group, 5)
        start = (i0 * 2 + t6x) * 64 + j1 * 4 + j0 * 2 + pair
        return jnp.concatenate(
            [turned.at[2 * part + half][pl.ds(start, 8, stride=8), :] for half in range(2)], axis=1
        )

    def keep_last(child, row, values):
        t6x, j0, pair = bits(row, 3)
        for part in range(2):
            state[j0 * 16 + child * 4 + t6x * 2 + pair, part] = values[part]

    run(7, across, keep_last)

    def send(child, row, values):
        t7x, t7y, t6x, pair = bits(row, 4)
        line = 224 + child * 8 + row // 2
        cosine = table[line, 0, 8 * (row % 2) : 8 * (row % 2) + 8, :]
        sine = table[line, 1, 8 * (row % 2) : 8 * (row % 2) + 8, :]
        real, imaginary = values
        device = t6x * 32 + t7x * 16 + t7y * 2 + child
        for part, whole in enumerate(
            (real * cosine + imaginary * sine, imaginary * cosine - real * sine)
        ):
            for half, value in enumerate(halves(whole)):
                for upper in range(2):
                    place = (device + 64 * upper) * 8 + pair * 4 + half * 2 + part
                    out[pl.ds(place, 4, stride=32), :] = value[4 * upper : 4 * upper + 4]

    level(
        read, table, 192, highs, lows, last, 2, 16, True, fetches[2:], send, fetch_last
    )


def vmem(count):
    return [pl.BlockSpec(memory_space=pltpu.VMEM)] * count


def smem(count):
    return [pl.BlockSpec(memory_space=pltpu.SMEM)] * count


def far(count):
    return [pl.BlockSpec(memory_space=pltpu.HBM)] * count


def payload_kernel(place_far, amp_far, out_far, place, amp, out, arrive, leave):
    fetches = [
        pltpu.make_async_copy(place_far, place, arrive.at[0]),
        pltpu.make_async_copy(amp_far, amp, arrive.at[1]),
    ]
    for fetch in fetches:
        fetch.start()
    for fetch in fetches:
        fetch.wait()
    for k in range(2):
        out[pl.ds(k, DEVICES, stride=4), :] = place[k].astype(F32)
        out[pl.ds(2 + k, DEVICES, stride=4), :] = amp[k]
    store = pltpu.make_async_copy(out, out_far, leave)
    store.start()
    store.wait()


def make_payload(place, amp):
    return pl.pallas_call(
        payload_kernel,
        out_shape=jax.ShapeDtypeStruct((4 * DEVICES, 128), F32),
        in_specs=far(2),
        out_specs=far(1)[0],
        scratch_shapes=[
            pltpu.VMEM((2, DEVICES, 128), jnp.int32),
            pltpu.VMEM((2, DEVICES, 128), F32),
            pltpu.VMEM((4 * DEVICES, 128), F32),
            pltpu.SemaphoreType.DMA((2,)),
            pltpu.SemaphoreType.DMA,
        ],
        name="payload",
        compiler_params=pltpu.CompilerParams(vmem_limit_bytes=60 << 20),
    )(place, amp)


def inner_turns(block_first, block_second, slots):
    speeds = np.repeat(inner_speeds()[:, None], 128, axis=1)
    return pl.pallas_call(
        inner_turns_kernel,
        out_shape=jax.ShapeDtypeStruct((258, 2, 16, 256), F32),
        in_specs=smem(2) + far(3),
        out_specs=far(1)[0],
        scratch_shapes=[
            pltpu.VMEM((64, 256), jnp.int32),
            pltpu.VMEM((24, 256), F32),
            pltpu.VMEM((1024, 128), F32),
            pltpu.VMEM((258, 2, 16, 256), F32),
            pltpu.VMEM((2, 128, 128), F32),
            pltpu.VMEM((256, 8192), BF16),
            pltpu.VMEM((256, 8192), BF16),
            pltpu.SemaphoreType.DMA((3,)),
            pltpu.SemaphoreType.DMA((8,)),
        ],
        name="inner_turns",
        compiler_params=pltpu.CompilerParams(vmem_limit_bytes=60 << 20),
    )(block_first, block_second, slots, jnp.asarray(node_tables()), jnp.asarray(speeds))


def outer_turns(speeds):
    return pl.pallas_call(
        outer_turns_kernel,
        out_shape=jax.ShapeDtypeStruct((240, 2, 16, 256), F32),
        in_specs=vmem(2),
        out_specs=far(1)[0],
        scratch_shapes=[
            pltpu.VMEM((240, 2, 16, 256), F32),
            pltpu.SemaphoreType.DMA((7,)),
        ],
        name="outer_turns",
        compiler_params=pltpu.CompilerParams(vmem_limit_bytes=52 << 20),
    )(jnp.asarray(node_tables()), speeds)


LEVEL_SCRATCH = [
    pltpu.VMEM((32, 2, 8, 256), F32),
    pltpu.VMEM((4, 256, 128), F32),
    [pltpu.VMEM((256, 1024), BF16)] * 2,
    [pltpu.VMEM((256, 1024), BF16)] * 2,
]


def inner_levels(arrived, table):
    return pl.pallas_call(
        inner_kernel,
        out_shape=jax.ShapeDtypeStruct((1024, 128), F32),
        in_specs=vmem(1) + far(2),
        out_specs=vmem(1)[0],
        scratch_shapes=[
            pltpu.VMEM((1024, 512), BF16),
            pltpu.VMEM((1024, 512), BF16),
            pltpu.VMEM((258, 2, 16, 256), F32),
            pltpu.SemaphoreType.DMA((7,)),
            pltpu.VMEM((4096, 128), F32),
            pltpu.VMEM((3, 128, 128), F32),
            [pltpu.VMEM((256, 2048), BF16)] * 2,
            [pltpu.VMEM((512, 2048), BF16)] * 2,
            pltpu.VMEM((256, 512), F32),
        ]
        + LEVEL_SCRATCH
        + LEVEL_SCRATCH[:1],
        name="inner",
        compiler_params=pltpu.CompilerParams(vmem_limit_bytes=52 << 20),
    )(
        arrived,
        table,
        jnp.asarray(matrices()),
    )


def outer_levels(arrived, table):
    return pl.pallas_call(
        outer_kernel,
        out_shape=jax.ShapeDtypeStruct((1024, 128), F32),
        in_specs=vmem(1) + far(2),
        out_specs=vmem(1)[0],
        scratch_shapes=[
            pltpu.VMEM((240, 2, 16, 256), F32),
            pltpu.VMEM((1024, 512), BF16),
            pltpu.VMEM((512, 512), BF16),
            pltpu.SemaphoreType.DMA((10,)),
        ]
        + LEVEL_SCRATCH,
        name="outer",
        compiler_params=pltpu.CompilerParams(vmem_limit_bytes=52 << 20),
    )(
        arrived,
        table,
        jnp.asarray(matrices()),
    )


def reverse_bits(number, bit_count):
    result = jnp.zeros_like(number)
    for position in range(bit_count):
        result = result + jnp.left_shift(
            jnp.bitwise_and(jnp.right_shift(number, position), 1), bit_count - 1 - position
        )
    return result


def exchange(array):
    return lax.all_to_all(array, ("bx", "by"), split_axis=0, concat_axis=0, tiled=True)


def shards(src_pos, src_amp, box_slots):
    column = lax.axis_index("bx")
    row = lax.axis_index("by")
    device = column * BY + row
    block_first = reverse_bits(column, 3).astype(jnp.int32).reshape(1)
    block_second = reverse_bits(row, 4).astype(jnp.int32).reshape(1)
    payload = make_payload(src_pos.reshape(2, DEVICES, 128), src_amp.reshape(2, DEVICES, 128))
    arrived = exchange(payload.reshape(DEVICES, 4, 128)).reshape(512, 128)
    table = inner_turns(block_first, block_second, box_slots[0].T)
    arrived, table = lax.optimization_barrier((arrived, table))
    weights = inner_levels(arrived, table)
    weights = exchange(weights.reshape(DEVICES, 8, 128)).reshape(1024, 128)
    speeds = lax.dynamic_index_in_dim(jnp.asarray(outer_speeds()), device, 0, keepdims=False)
    speeds = jnp.broadcast_to(speeds[:, None], (7 * 256, 128))
    weights = outer_levels(weights, outer_turns(speeds))
    weights = exchange(weights.reshape(DEVICES, 8, 128))
    weights = weights.reshape(LEAVES, LEAVES, 2, 2, 128)
    weights = jnp.concatenate([weights[:, :, 0], weights[:, :, 1]], axis=-1)
    return weights.reshape(LEAVES, 1, LEAVES, 1, 2, BOX_NODES)


def solution(mesh):
    return jax.shard_map(
        shards,
        mesh=mesh,
        in_specs=(
            P(None, ("bx", "by"), None),
            P(None, ("bx", "by"), None),
            P(("bx", "by"), None, None),
        ),
        out_specs=P(None, "bx", None, "by", None, None),
        check_vma=False,
    )
```

```python
import functools
import math

import jax
import jax.numpy as jnp
import numpy as np
from jax import lax
from jax.experimental import pallas as pl
from jax.experimental.pallas import tpu as pltpu
from jax.sharding import PartitionSpec as P

NODES = 16
BOX_NODES = 256
DEVICES = 128
LEAVES = 16
BX = 8
BY = 16
BAND = 1024
F32 = jnp.float32
BF16 = jnp.bfloat16
ROUNDER = 12582912.0
SIN = (6.28305581, -41.33121471, 81.36682035, -74.47802935, 32.78144238)
COS = (0.99995995, -19.73105034, 64.67355678, -82.40422428, 45.64775943)


def chebyshev_points(point_count):
    indices = np.arange(point_count)
    return (1.0 - np.cos(np.pi * (2 * indices + 1) / (2 * point_count))) / 2.0


def lagrange_matrix(locations):
    points = chebyshev_points(NODES)
    matrix = np.ones((len(locations), NODES))
    for own in range(NODES):
        for other in range(NODES):
            if other != own:
                matrix[:, own] *= (locations - points[other]) / (points[own] - points[other])
    return matrix


def child_matrix(halves, child):
    if halves == 1:
        return np.eye(NODES)
    return lagrange_matrix((child + chebyshev_points(NODES)) / 2.0)


def stacked_matrix(halves_first, halves_second):
    pieces = [
        np.kron(child_matrix(halves_first, a), child_matrix(halves_second, b))
        for a in range(halves_first)
        for b in range(halves_second)
    ]
    return np.concatenate(pieces, axis=0)


def two_parts(matrix):
    exact = np.asarray(matrix, np.float32)
    high = exact.astype(jnp.bfloat16)
    low = (exact - high.astype(np.float32)).astype(jnp.bfloat16)
    return high, low


def velocity(first, second):
    return (2.0 + np.sin(2 * np.pi * first) * np.sin(2 * np.pi * second)) / 8.0


def bits(value, count):
    return [(value >> (count - 1 - k)) & 1 for k in range(count)]


def speed_change(first, second, level, split_first=True):
    count_second = 2.0**level
    count_first = 2.0 ** (level if split_first else level - 1)
    new = velocity((first + 0.5) / count_first, (second + 0.5) / count_second)
    above_first = first >> 1 if split_first else first
    old = velocity(
        (above_first + 0.5) / 2.0 ** (level - 1), ((second >> 1) + 0.5) / 2.0 ** (level - 1)
    )
    return new - old


def inner_speeds():
    table = np.zeros((4, 4, 8, 8))
    for child in range(4):
        x, y = bits(child, 2)
        for row in range(8):
            r0, r1, r2 = bits(row, 3)
            for sub in range(8):
                s0, s1, s2 = bits(sub, 3)
                table[0, child, row, sub] = speed_change(x, y, 1)
                table[1, child, row, sub] = speed_change(2 * r0 + x, 2 * r1 + y, 2)
                first, second = 2 * s0 + r2, 2 * s1 + s2
                table[2, child, row, sub] = speed_change(2 * first + x, 2 * second + y, 3)
                first, second = 2 * first + r0, 2 * second + r1
                table[3, child, row, sub] = speed_change(2 * first + x, 2 * second + y, 4)
    return table.reshape(1024).astype(np.float32)


def outer_speeds():
    tables = np.zeros((DEVICES, 7, 256))
    for device in range(DEVICES):
        coarse_first = device >> 3
        for child in range(4):
            x, y = bits(child, 2)
            for row in range(8):
                r0, r1, r2 = bits(row, 3)
                for sub in range(8):
                    s0, s1, s2 = bits(sub, 3)
                    place = child * 64 + row * 8 + sub
                    second = 2 * (device & 7) + s2
                    tables[device, 0, place] = speed_change(
                        2 * coarse_first + x, 2 * second + y, 5
                    )
                    tables[device, 1, place] = speed_change(
                        4 * coarse_first + 2 * r0 + x, 4 * second + 2 * r1 + y, 6
                    )
                    second = 2 * (device & 7) + r2
                    tables[device, 2, place] = speed_change(
                        8 * coarse_first + 4 * s0 + 2 * r0 + x,
                        8 * second + 4 * s1 + 2 * s2 + y,
                        7,
                    )
        for child in range(2):
            for row in range(16):
                r0, r1, r2, r3 = bits(row, 4)
                for sub in range(8):
                    s0, s1, s2 = bits(sub, 3)
                    place = child * 128 + row * 8 + sub
                    first = 8 * coarse_first + 4 * s0 + 2 * r2 + r0
                    second = 2 * (device & 7) + r3
                    second = 16 * second + 8 * s1 + 4 * s2 + 2 * r1 + child
                    tables[device, 3, place] = speed_change(first, second, 8, False)
                    tables[device, 4, place] = velocity((first + 0.5) / 128, (second + 0.5) / 256)
                    tables[device, 5, place] = 8 * (first + 0.5)
                    tables[device, 6, place] = 4 * (second + 0.5)
    return tables.reshape(DEVICES, 7 * 256).astype(np.float32)


def node_tables():
    points = chebyshev_points(NODES).astype(np.float32).astype(np.float64)
    first = np.repeat(points, NODES)
    second = np.tile(points, NODES)
    rows = np.zeros((24, BOX_NODES))
    for child in range(4):
        x, y = bits(child, 2)
        turns = (2 * x - 1) * 2 * first + (2 * y - 1) * second
        rows[child] = turns - np.round(turns)
    for child in range(2):
        rows[4 + child] = (2 * child - 1) * second
    rows[6] = 2 * first
    rows[7] = second
    rows[8] = np.round(first * 8192) / 8192
    rows[9] = first - rows[8]
    rows[10] = np.round(second * 8192) / 8192
    rows[11] = second - rows[10]
    for child in range(2):
        rows[16 + 2 * child] = np.cos(2 * np.pi * rows[child])
        rows[17 + 2 * child] = np.sin(2 * np.pi * rows[child])
    rows[12] = BAND * np.sqrt(first * first + second * second)
    return rows.astype(np.float32)


def basis_factors():
    points = chebyshev_points(NODES)
    return [
        float(np.float32(1.0 / np.prod([points[own] - points[k] for k in range(NODES) if k != own])))
        for own in range(NODES)
    ]


def second_basis():
    small = lagrange_matrix((np.arange(16) + 0.5) / 16.0)
    whole = np.zeros((16, 32, 32, 16))
    for k in range(32):
        whole[:, k, k, :] = small
    return whole.reshape(512, 512)


def turn(turns):
    part = turns - ((turns + ROUNDER) - ROUNDER)
    square = part * part
    sine = SIN[4]
    cosine = COS[4]
    for k in (3, 2, 1, 0):
        sine = sine * square + SIN[k]
        cosine = cosine * square + COS[k]
    return cosine, sine * part


def split(value):
    high = value.astype(BF16)
    return high, (value - high.astype(F32)).astype(BF16)


def bit(value, place):
    return (value >> place) & 1


def make_turns(
    table, first_line, box, level_number, speeds, speed_row, node, base_row, children, rows, stores=()
):
    scale = 4.0 * 2.0 ** (level_number - 1)
    pairs = rows // 2

    def step(index, carry):
        source = index // pairs
        pair = lax.rem(index, pairs)
        radius = []
        for k in range(2):
            first, second = box(source, 2 * pair + k)
            along = first + node[6:7, :]
            across = second + node[7:8, :]
            radius.append(scale * jnp.sqrt(along * along + across * across))
        radius = jnp.concatenate([jnp.broadcast_to(value, (8, BOX_NODES)) for value in radius])
        for child in range(children):
            place = pl.multiple_of(speed_row + child * rows * 8 + pair * 16, 16)
            change = speeds[pl.ds(place, 16), :]
            change = jnp.concatenate([change, change], axis=1)
            cosine, sine = turn(change * radius + node[base_row + child : base_row + child + 1, :])
            line = first_line + index * children + child
            table[line, 0] = cosine
            table[line, 1] = sine
        return carry

    if not stores:
        lax.fori_loop(0, (4 if children == 4 else 2) * pairs, step, 0)
    for source, store in enumerate(stores):
        lax.fori_loop(source * pairs, (source + 1) * pairs, step, 0)
        store.start()


def make_first_turns(table, box, node):
    def step(index, carry):
        radius = []
        for k in range(2):
            first, second = box(index // 4, 2 * (index % 4) + k)
            along = first + node[6:7, :]
            across = second + node[7:8, :]
            radius.append(0.5 * jnp.sqrt(along * along + across * across))
        cosine, sine = turn(jnp.concatenate(radius))
        for kind in range(2):
            base_cosine = node[16 + 2 * kind : 17 + 2 * kind, :]
            base_sine = node[17 + 2 * kind : 18 + 2 * kind, :]
            cosines = base_cosine * cosine
            sines = base_sine * sine
            mixed = base_sine * cosine
            other = base_cosine * sine
            line = 4 * index + kind
            mirror = 4 * index + 3 - kind
            if kind == 0:
                table[line, 0] = cosines - sines
                table[line, 1] = mixed + other
                table[mirror, 0] = cosines + sines
                table[mirror, 1] = other - mixed
            else:
                table[line, 0] = cosines + sines
                table[line, 1] = mixed - other
                table[mirror, 0] = cosines - sines
                table[mirror, 1] = -mixed - other
        return carry

    lax.fori_loop(0, 16, step, 0)


def whole_product(high, low, matrix):
    result = jnp.dot(
        jnp.concatenate([high, low], axis=1),
        jnp.concatenate([matrix, matrix], axis=0),
        preferred_element_type=F32,
    )
    return result[:, :BOX_NODES] + result[:, BOX_NODES:]


def level(
    read, table, first_line, highs, lows, matrix, children, rows, by_rows, ready, emit, matrix_ready=None
):
    sources = 4 if children == 4 else 2
    pairs = rows // 2
    columns = sources * BOX_NODES
    for half in range(2):
        high, low = highs[half], lows[half]
        if by_rows:
            chosen = list(range(children))
            near = list(range(half * pairs // 2, (half + 1) * pairs // 2))
        else:
            chosen = list(range(half * children // 2, (half + 1) * children // 2))
            near = list(range(pairs))
        height = 16 * len(near)
        for source in range(sources):
            lanes = slice(source * BOX_NODES, (source + 1) * BOX_NODES)
            if half == 0 and source < len(ready):
                ready[source].wait()
            for spot, pair in enumerate(near):
                group = source * rows + 2 * pair
                real, imaginary = (
                    jnp.concatenate([read(group, part), read(group + 1, part)])
                    for part in range(2)
                )
                for number, child in enumerate(chosen):
                    line = first_line + (source * pairs + pair) * children + child
                    cosine = table[line, 0]
                    sine = table[line, 1]
                    for part, value in enumerate(
                        (real * cosine - imaginary * sine, real * sine + imaginary * cosine)
                    ):
                        place = (number * 2 + part) * height + spot * 16
                        value_high, value_low = split(value)
                        high[place : place + 16, lanes] = value_high
                        low[place : place + 16, lanes] = value_low
        if half == 0 and matrix_ready is not None:
            matrix_ready.wait()
        result = whole_product(high[:, :columns], low[:, :columns], matrix[...])
        for number, child in enumerate(chosen):
            for spot, pair in enumerate(near):
                for k in range(2):
                    start = number * 2 * height + spot * 16 + 8 * k
                    emit(
                        child,
                        2 * pair + k,
                        [result[start + height * part : start + height * part + 8] for part in range(2)],
                    )


def matrices():
    basis = second_basis()
    rows = [
        stacked_matrix(2, 2),
        stacked_matrix(1, 2),
        basis[:, :256],
        basis[:, 256:],
    ]
    return np.concatenate(two_parts(np.concatenate(rows)), axis=1)


def sub_bits():
    row = lax.broadcasted_iota(jnp.int32, (8, BOX_NODES), 0)
    return [bit(row, 2 - k).astype(F32) for k in range(3)]


def find_mask(slots, table, entries, high_hot, low_hot):
    iota = lax.broadcasted_iota(jnp.int32, (16, 128), 0).astype(F32)
    rows = [(iota + 16.0 * k).astype(BF16) for k in range(8)]
    one = jnp.ones((16, 128), BF16)
    zero = jnp.zeros((16, 128), BF16)
    block = jnp.concatenate([slots[:, :128], slots[:, 128:]], axis=0)
    entries[0] = (block >> 7).astype(F32)
    entries[1] = (block & 127).astype(F32)

    def step(index, carry):
        for source, hot in enumerate((high_hot, low_hot)):
            for side in range(2):
                start = pl.multiple_of(index * 8 + 64 * side, 8)
                block = entries[source, pl.ds(start, 8), :]
                for k in range(8):
                    value = jnp.broadcast_to(block[k : k + 1], (16, 128)).astype(BF16)
                    lanes = pl.ds(pl.multiple_of(index * 1024 + 128 * k, 128), 128)
                    for place in range(8):
                        line = 128 * side + 16 * place
                        hot[line : line + 16, lanes] = jnp.where(value == rows[place], one, zero)
        return carry

    lax.fori_loop(0, 8, step, 0)
    parts = [
        lax.dot_general(
            high_hot[:, 4096 * k : 4096 * (k + 1)],
            low_hot[:, 4096 * k : 4096 * (k + 1)],
            (((1,), (1,)), ((), ())),
            preferred_element_type=F32,
        )
        for k in range(2)
    ]
    total = parts[0] + parts[1]
    mask = jnp.where(total[:128, :128] + total[128:, 128:] > 0.5, 1.0, 0.0)
    for k in range(8):
        lanes = slice(128 * (k % 2), 128 * (k % 2 + 1))
        table[256 + k // 4, k // 2 % 2, :, lanes] = mask[16 * k : 16 * (k + 1)]


def store_level(table, table_far, leave, index, size=64, first=0):
    lines = pl.ds(size * index, size)
    place = leave.at[index if first == 0 else first + index % 4]
    return pltpu.make_async_copy(table.at[lines], table_far.at[lines], place)


def fetch_level(table_far, table, arrive, index, size=64):
    lines = pl.ds(64 * index, size)
    return pltpu.make_async_copy(table_far.at[lines], table.at[lines], arrive.at[index])


def fetch_mask_lines(table_far, table, place):
    lines = pl.ds(256, 2)
    return pltpu.make_async_copy(table_far.at[lines], table.at[lines], place)


def inner_turns_kernel(
    block_first_ref,
    block_second_ref,
    slots_far,
    node_far,
    speeds_far,
    table_far,
    slots,
    node,
    speeds,
    table,
    entries,
    high_hot,
    low_hot,
    arrive,
    leave,
):
    fetches = [
        pltpu.make_async_copy(far, near, arrive.at[k])
        for k, (far, near) in enumerate(
            ((slots_far, slots), (node_far, node), (speeds_far, speeds))
        )
    ]
    for fetch in fetches:
        fetch.start()
    fetches[0].wait()
    find_mask(slots, table, entries, high_hot, low_hot)
    for fetch in fetches[1:]:
        fetch.wait()
    stores = [store_level(table, table_far, leave, k) for k in range(3)]
    stores += [store_level(table, table_far, leave, 12 + k, 16, 3) for k in range(4)]
    store_mask = store_level(table, table_far, leave, 128, 2, 7)
    store_mask.start()
    sub = sub_bits()
    block_first = block_first_ref[0]
    block_second = block_second_ref[0]

    def box(source, row):
        first = block_first * 16 + bit(source, 1) + 2 * bit(row, 2)
        second = block_second * 16 + bit(source, 0) + 2 * bit(row, 1) + 8 * bit(row, 0)
        return (
            2.0 * first.astype(F32) + (8.0 * sub[0] + 16.0 * sub[2]),
            second.astype(F32) + 4.0 * sub[1],
        )

    make_first_turns(table, box, node)
    stores[0].start()

    def box(source, row):
        first = block_first * 8 + bit(source, 1)
        second = block_second * 8 + bit(source, 0) + 4 * bit(row, 0)
        return (
            2.0 * first.astype(F32) + (4.0 * sub[0] + 8.0 * sub[2]),
            second.astype(F32) + 2.0 * sub[1],
        )

    make_turns(table, 64, box, 2, speeds, 256, node, 0, 4, 8)
    stores[1].start()

    def box(source, row):
        first = block_first * 4 + bit(source, 1) + 2 * bit(row, 2)
        second = block_second * 4 + bit(source, 0) + 2 * bit(row, 1)
        return 2.0 * first.astype(F32), second.astype(F32)

    make_turns(table, 128, box, 3, speeds, 512, node, 0, 4, 8)
    stores[2].start()

    def box(source, row):
        first = block_first * 2 + bit(source, 1)
        second = block_second * 2 + bit(source, 0)
        return 2.0 * first.astype(F32), second.astype(F32)

    make_turns(table, 192, box, 4, speeds, 768, node, 0, 4, 8, stores[3:])
    for store in stores + [store_mask]:
        store.wait()


def outer_turns_kernel(node, speeds, table_far, table, leave):
    stores = [store_level(table, table_far, leave, k) for k in range(3)]
    stores += [store_level(table, table_far, leave, 12 + k, 16, 3) for k in range(3)]
    sub = sub_bits()

    def box(source, row):
        first = bit(source, 1) + 2 * bit(row, 2) + 4 * bit(row, 1)
        second = bit(source, 0) + 2 * bit(row, 0)
        return 2.0 * first.astype(F32), second.astype(F32) + (4.0 * sub[0] + 8.0 * sub[1])

    make_turns(table, 0, box, 5, speeds, 0, node, 0, 4, 8)
    stores[0].start()

    def box(source, row):
        first = bit(source, 1) + 2 * bit(row, 0)
        second = bit(source, 0)
        return 2.0 * first.astype(F32), second.astype(F32) + (2.0 * sub[0] + 4.0 * sub[1])

    make_turns(table, 64, box, 6, speeds, 256, node, 0, 4, 8)
    stores[1].start()

    def box(source, row):
        first = bit(source, 1)
        second = bit(source, 0) + 2 * bit(row, 1)
        return 2.0 * first.astype(F32), second.astype(F32)

    make_turns(table, 128, box, 7, speeds, 512, node, 0, 4, 8)
    stores[2].start()

    def box(source, row):
        return jnp.float32(0.0), source.astype(F32)

    make_turns(table, 192, box, 8, speeds, 768, node, 4, 2, 16, stores[3:5])

    def last(index, carry):
        def column(table):
            value = speeds[pl.ds(pl.multiple_of(256 * table + index * 16, 16), 16), :]
            return jnp.concatenate([value, value], axis=1)

        first = column(5)
        second = column(6)
        turns = first * node[8:9, :]
        turns = turns - ((turns + ROUNDER) - ROUNDER)
        across = second * node[10:11, :]
        across = across - ((across + ROUNDER) - ROUNDER)
        around = column(4) * node[12:13, :]
        around = around - ((around + ROUNDER) - ROUNDER)
        turns = turns + across + around + first * node[9:10, :] + second * node[11:12, :]
        cosine, sine = turn(turns)
        table[224 + index, 0] = cosine
        table[224 + index, 1] = sine
        return carry

    lax.fori_loop(0, 16, last, 0)
    stores[5].start()
    for store in stores:
        store.wait()


def deposit(
    arrived, table, second, fetch_second, state, wide, cells, hots, spreads, grid
):
    points = [float(value) for value in chebyshev_points(NODES).astype(np.float32)]
    factors = basis_factors()

    def source_step(index, carry):
        rows = pl.ds(pl.multiple_of(index * 16, 16), 16)
        first, second, real, imaginary = (
            arrived[pl.ds(index * 64 + k, 16, stride=4), :] for k in range(4)
        )
        whole_first = first.astype(jnp.int32)
        whole_second = second.astype(jnp.int32)
        along = first + 0.5
        across = second + 0.5
        eighths = jnp.bitwise_and(whole_first + whole_second + 1, 7).astype(F32)
        cosine, sine = turn(
            0.125 * eighths + 0.0625 * jnp.sqrt(along * along + across * across)
        )
        lanes = pl.ds(pl.multiple_of(index % 2 * 128, 128), 128)
        live = table[256 + index // 4, index // 2 % 2, :, lanes]
        real = real * live
        imaginary = imaginary * live
        turned = (real * cosine - imaginary * sine, real * sine + imaginary * cosine)
        place = jnp.bitwise_and(whole_first, 31).astype(F32) * 0.03125 + 0.015625
        cells[0, rows, :] = jnp.bitwise_and(whole_second, 15).astype(F32)
        x = [bit(whole_first, 5 + k) for k in range(4)]
        y = [bit(whole_second, 4 + k) for k in range(4)]
        cells[1, rows, :] = (x[0] * 8 + y[0] * 4 + x[1] * 2 + y[1]).astype(F32)
        cells[2, rows, :] = (y[3] * 8 + x[2] * 4 + y[2] * 2 + x[3]).astype(F32)
        away = [place - value for value in points]
        before = [None] * NODES
        after = [None] * NODES
        for p in range(1, NODES):
            before[p] = away[p - 1] if p == 1 else before[p - 1] * away[p - 1]
            q = NODES - 1 - p
            after[q] = away[q + 1] if p == 1 else after[q + 1] * away[q + 1]
        for p in range(NODES):
            if p == 0:
                value = after[0]
            elif p == NODES - 1:
                value = before[p]
            else:
                value = before[p] * after[p]
            value = value * factors[p]
            for part in range(2):
                wide[pl.ds(index * 512 + part * 16 + p, 16, stride=32), :] = value * turned[part]
        return carry

    lax.fori_loop(0, 8, source_step, 0)

    iota = lax.broadcasted_iota(jnp.int32, (16, 128), 0).astype(F32).astype(BF16)
    one = jnp.ones((16, 128), BF16)
    zero = jnp.zeros((16, 128), BF16)

    def build(chunk, hot, spread):
        for k in range(16):
            sender = chunk * 16 + k
            lanes = slice(128 * k, 128 * (k + 1))

            def row(number, height):
                value = cells[number, pl.ds(sender, 1), :]
                return jnp.broadcast_to(value, (height, 128)).astype(BF16)

            value = wide[pl.ds(pl.multiple_of(sender * 32, 32), 32), :].astype(BF16)
            cell = row(0, 16)
            for c in range(16):
                chosen = cell == jnp.full((16, 128), c, BF16)
                for part in range(2):
                    spread[32 * c + 16 * part : 32 * c + 16 * (part + 1), lanes] = jnp.where(
                        chosen, value[16 * part : 16 * (part + 1)], zero
                    )
            inside = jnp.where(row(2, 16) == iota, one, zero)
            above = row(1, 16)
            for c in range(16):
                hot[16 * c : 16 * (c + 1), lanes] = jnp.where(
                    above == jnp.full((16, 128), c, BF16), inside, zero
                )

    grid[...] = jnp.zeros_like(grid)

    def spread_step(index, carry):
        for k in range(2):
            build(2 * index + k, hots[k], spreads[k])
        grid[...] += lax.dot_general(
            jnp.concatenate([hots[0][...], hots[1][...]], axis=1),
            jnp.concatenate([spreads[0][...], spreads[1][...]], axis=1),
            (((1,), (1,)), ((), ())),
            preferred_element_type=F32,
        )
        return carry

    lax.fori_loop(0, 4, spread_step, 0)

    grid_high, grid_low = split(grid[...])
    fetch_second.wait()
    for part in range(2):
        result = whole_product(grid_high, grid_low, second[512 * part : 512 * (part + 1), :])
        for group in range(32):
            state[group, part] = result[8 * group : 8 * group + 8, :]


def halves(value):
    return value[:, :128], value[:, 128:]


def inner_kernel(
    arrived,
    table_far,
    matrix_far,
    out,
    second,
    matrix,
    table,
    arrive,
    wide,
    cells,
    hots,
    spreads,
    grid,
    other,
    turned,
    highs,
    lows,
    state,
):
    fetch_mask = fetch_mask_lines(table_far, table, arrive.at[6])
    fetch_mask.start()
    fetch_second = pltpu.make_async_copy(matrix_far.at[pl.ds(1536, 1024)], second, arrive.at[4])
    fetch_second.start()
    fetches = [fetch_level(table_far, table, arrive, k) for k in range(4)]
    for fetch in fetches:
        fetch.start()
    fetch_matrix = pltpu.make_async_copy(matrix_far.at[pl.ds(0, 1024)], matrix, arrive.at[5])
    fetch_matrix.start()
    fetch_mask.wait()
    deposit(arrived, table, second, fetch_second, state, wide, cells, hots, spreads, grid)

    def run(number, read, emit):
        level(
            read,
            table,
            64 * (number - 1),
            highs,
            lows,
            matrix,
            4,
            8,
            number % 2 == 0,
            fetches[number - 1 : number],
            emit,
            fetch_matrix if number == 1 else None,
        )

    def leaf(group, part):
        return state[group, part]

    def read(group, part):
        return other[group, part]

    def keep(child, row, values):
        for part in range(2):
            other[(row // 2) * 8 + child * 2 + row % 2, part] = values[part]

    run(1, leaf, keep)

    def turn_over(child, row, values):
        start = ((row % 2 * 2 + child // 2) * 8 + row // 2 * 2 + child % 2) * 8
        for part in range(2):
            for half, value in enumerate(halves(values[part])):
                turned[2 * part + half, start : start + 8, :] = value

    run(2, read, turn_over)

    def across(group, part):
        b2x, b2y, b3x, b3y, t2x = bits(group, 5)
        start = (b3y * 2 + t2x) * 64 + b2x * 4 + b2y * 2 + b3x
        return jnp.concatenate(
            [turned.at[2 * part + half][pl.ds(start, 8, stride=8), :] for half in range(2)], axis=1
        )

    run(3, across, keep)

    def send(child, row, values):
        x, y = bits(child, 2)
        r0, r1, r2 = bits(row, 3)
        device = r2 * 32 + r0 * 16 + x * 8 + r1
        for upper in range(2):
            for part in range(2):
                for half, value in enumerate(halves(values[part])):
                    start = (device + 64 * upper) * 8 + y * 4 + half * 2 + part
                    out[pl.ds(start, 4, stride=16), :] = value[4 * upper : 4 * upper + 4]

    run(4, read, send)


def outer_kernel(
    arrived, table_far, matrix_far, out, table, matrix, last, arrive, state, turned, highs, lows
):
    first = [
        pltpu.make_async_copy(
            table_far.at[pl.ds(16 * k, 16)], table.at[pl.ds(16 * k, 16)], arrive.at[6 + k]
        )
        for k in range(4)
    ]
    fetches = [
        fetch_level(table_far, table, arrive, k, 64 if k < 3 else 48) for k in range(1, 4)
    ]
    fetch_matrix = pltpu.make_async_copy(matrix_far.at[pl.ds(0, 1024)], matrix, arrive.at[5])
    fetch_last = pltpu.make_async_copy(matrix_far.at[pl.ds(1024, 512)], last, arrive.at[4])
    for fetch in first + [fetch_matrix] + fetches + [fetch_last]:
        fetch.start()

    def first_read(group, part):
        i2, j3, i1, i0, j2 = bits(group, 5)
        source = i2 * 64 + i1 * 32 + i0 * 16 + j3 * 8 + j2 * 4
        return jnp.concatenate(
            [
                arrived[pl.ds(source * 8 + half * 2 + part, 8, stride=4), :]
                for half in range(2)
            ],
            axis=1,
        )

    def run(number, read, emit):
        level(
            read,
            table,
            64 * (number - 5),
            highs,
            lows,
            matrix,
            4,
            8,
            number % 2 == 0,
            first if number == 5 else fetches[number - 6 : number - 5],
            emit,
            fetch_matrix if number == 5 else None,
        )

    def read(group, part):
        return state[group, part]

    def keep(child, row, values):
        i1, i0, j2 = bits(row, 3)
        for part in range(2):
            state[(2 * i1 + j2) * 8 + child * 2 + i0, part] = values[part]

    run(5, first_read, keep)

    def turn_over(child, row, values):
        start = ((row % 2 * 2 + child // 2) * 8 + row // 2 * 2 + child % 2) * 8
        for part in range(2):
            for half, value in enumerate(halves(values[part])):
                turned[2 * part + half, start : start + 8, :] = value

    run(6, read, turn_over)

    def across(group, part):
        i0, j1, t6x, j0, pair = bits(group, 5)
        start = (i0 * 2 + t6x) * 64 + j1 * 4 + j0 * 2 + pair
        return jnp.concatenate(
            [turned.at[2 * part + half][pl.ds(start, 8, stride=8), :] for half in range(2)], axis=1
        )

    def keep_last(child, row, values):
        t6x, j0, pair = bits(row, 3)
        for part in range(2):
            state[j0 * 16 + child * 4 + t6x * 2 + pair, part] = values[part]

    run(7, across, keep_last)

    def send(child, row, values):
        t7x, t7y, t6x, pair = bits(row, 4)
        line = 224 + child * 8 + row // 2
        cosine = table[line, 0, 8 * (row % 2) : 8 * (row % 2) + 8, :]
        sine = table[line, 1, 8 * (row % 2) : 8 * (row % 2) + 8, :]
        real, imaginary = values
        device = t6x * 32 + t7x * 16 + t7y * 2 + child
        for part, whole in enumerate(
            (real * cosine + imaginary * sine, imaginary * cosine - real * sine)
        ):
            for half, value in enumerate(halves(whole)):
                for upper in range(2):
                    place = (device + 64 * upper) * 8 + pair * 4 + half * 2 + part
                    out[pl.ds(place, 4, stride=32), :] = value[4 * upper : 4 * upper + 4]

    level(
        read, table, 192, highs, lows, last, 2, 16, True, fetches[2:], send, fetch_last
    )


def vmem(count):
    return [pl.BlockSpec(memory_space=pltpu.VMEM)] * count


def smem(count):
    return [pl.BlockSpec(memory_space=pltpu.SMEM)] * count


def far(count):
    return [pl.BlockSpec(memory_space=pltpu.HBM)] * count


def payload_kernel(place_far, amp_far, out_far, place, amp, out, arrive, leave):
    fetches = [
        pltpu.make_async_copy(place_far, place, arrive.at[0]),
        pltpu.make_async_copy(amp_far, amp, arrive.at[1]),
    ]
    for fetch in fetches:
        fetch.start()
    for fetch in fetches:
        fetch.wait()
    for k in range(2):
        out[pl.ds(k, DEVICES, stride=4), :] = place[k].astype(F32)
        out[pl.ds(2 + k, DEVICES, stride=4), :] = amp[k]
    store = pltpu.make_async_copy(out, out_far, leave)
    store.start()
    store.wait()


def make_payload(place, amp):
    return pl.pallas_call(
        payload_kernel,
        out_shape=jax.ShapeDtypeStruct((4 * DEVICES, 128), F32),
        in_specs=far(2),
        out_specs=far(1)[0],
        scratch_shapes=[
            pltpu.VMEM((2, DEVICES, 128), jnp.int32),
            pltpu.VMEM((2, DEVICES, 128), F32),
            pltpu.VMEM((4 * DEVICES, 128), F32),
            pltpu.SemaphoreType.DMA((2,)),
            pltpu.SemaphoreType.DMA,
        ],
        name="payload",
        compiler_params=pltpu.CompilerParams(vmem_limit_bytes=60 << 20),
    )(place, amp)


def inner_turns(block_first, block_second, slots):
    speeds = np.repeat(inner_speeds()[:, None], 128, axis=1)
    return pl.pallas_call(
        inner_turns_kernel,
        out_shape=jax.ShapeDtypeStruct((258, 2, 16, 256), F32),
        in_specs=smem(2) + far(3),
        out_specs=far(1)[0],
        scratch_shapes=[
            pltpu.VMEM((64, 256), jnp.int32),
            pltpu.VMEM((24, 256), F32),
            pltpu.VMEM((1024, 128), F32),
            pltpu.VMEM((258, 2, 16, 256), F32),
            pltpu.VMEM((2, 128, 128), F32),
            pltpu.VMEM((256, 8192), BF16),
            pltpu.VMEM((256, 8192), BF16),
            pltpu.SemaphoreType.DMA((3,)),
            pltpu.SemaphoreType.DMA((8,)),
        ],
        name="inner_turns",
        compiler_params=pltpu.CompilerParams(vmem_limit_bytes=60 << 20),
    )(block_first, block_second, slots, jnp.asarray(node_tables()), jnp.asarray(speeds))


def outer_turns(speeds):
    return pl.pallas_call(
        outer_turns_kernel,
        out_shape=jax.ShapeDtypeStruct((240, 2, 16, 256), F32),
        in_specs=vmem(2),
        out_specs=far(1)[0],
        scratch_shapes=[
            pltpu.VMEM((240, 2, 16, 256), F32),
            pltpu.SemaphoreType.DMA((7,)),
        ],
        name="outer_turns",
        compiler_params=pltpu.CompilerParams(vmem_limit_bytes=52 << 20),
    )(jnp.asarray(node_tables()), speeds)


LEVEL_SCRATCH = [
    pltpu.VMEM((32, 2, 8, 256), F32),
    pltpu.VMEM((4, 256, 128), F32),
    [pltpu.VMEM((256, 1024), BF16)] * 2,
    [pltpu.VMEM((256, 1024), BF16)] * 2,
]


def inner_levels(arrived, table):
    return pl.pallas_call(
        inner_kernel,
        out_shape=jax.ShapeDtypeStruct((1024, 128), F32),
        in_specs=vmem(1) + far(2),
        out_specs=vmem(1)[0],
        scratch_shapes=[
            pltpu.VMEM((1024, 512), BF16),
            pltpu.VMEM((1024, 512), BF16),
            pltpu.VMEM((258, 2, 16, 256), F32),
            pltpu.SemaphoreType.DMA((7,)),
            pltpu.VMEM((4096, 128), F32),
            pltpu.VMEM((3, 128, 128), F32),
            [pltpu.VMEM((256, 2048), BF16)] * 2,
            [pltpu.VMEM((512, 2048), BF16)] * 2,
            pltpu.VMEM((256, 512), F32),
        ]
        + LEVEL_SCRATCH
        + LEVEL_SCRATCH[:1],
        name="inner",
        compiler_params=pltpu.CompilerParams(vmem_limit_bytes=52 << 20),
    )(
        arrived,
        table,
        jnp.asarray(matrices()),
    )


def outer_levels(arrived, table):
    return pl.pallas_call(
        outer_kernel,
        out_shape=jax.ShapeDtypeStruct((1024, 128), F32),
        in_specs=vmem(1) + far(2),
        out_specs=vmem(1)[0],
        scratch_shapes=[
            pltpu.VMEM((240, 2, 16, 256), F32),
            pltpu.VMEM((1024, 512), BF16),
            pltpu.VMEM((512, 512), BF16),
            pltpu.SemaphoreType.DMA((10,)),
        ]
        + LEVEL_SCRATCH,
        name="outer",
        compiler_params=pltpu.CompilerParams(vmem_limit_bytes=52 << 20),
    )(
        arrived,
        table,
        jnp.asarray(matrices()),
    )


def reverse_bits(number, bit_count):
    result = jnp.zeros_like(number)
    for position in range(bit_count):
        result = result + jnp.left_shift(
            jnp.bitwise_and(jnp.right_shift(number, position), 1), bit_count - 1 - position
        )
    return result


def exchange(array):
    return lax.all_to_all(array, ("bx", "by"), split_axis=0, concat_axis=0, tiled=True)


def shards(src_pos, src_amp, box_slots):
    column = lax.axis_index("bx")
    row = lax.axis_index("by")
    device = column * BY + row
    block_first = reverse_bits(column, 3).astype(jnp.int32).reshape(1)
    block_second = reverse_bits(row, 4).astype(jnp.int32).reshape(1)
    payload = make_payload(src_pos.reshape(2, DEVICES, 128), src_amp.reshape(2, DEVICES, 128))
    arrived = exchange(payload.reshape(DEVICES, 4, 128)).reshape(512, 128)
    table = inner_turns(block_first, block_second, box_slots[0].T)
    arrived, table = lax.optimization_barrier((arrived, table))
    weights = inner_levels(arrived, table)
    weights = exchange(weights.reshape(DEVICES, 8, 128)).reshape(1024, 128)
    speeds = lax.dynamic_index_in_dim(jnp.asarray(outer_speeds()), device, 0, keepdims=False)
    speeds = jnp.broadcast_to(speeds[:, None], (7 * 256, 128))
    weights = outer_levels(weights, outer_turns(speeds))
    weights = exchange(weights.reshape(DEVICES, 8, 128))
    weights = weights.reshape(LEAVES, LEAVES, 2, 2, 128)
    weights = jnp.concatenate([weights[:, :, 0], weights[:, :, 1]], axis=-1)
    return weights.reshape(LEAVES, 1, LEAVES, 1, 2, BOX_NODES)


def solution(mesh):
    return jax.shard_map(
        shards,
        mesh=mesh,
        in_specs=(
            P(None, ("bx", "by"), None),
            P(None, ("bx", "by"), None),
            P(("bx", "by"), None, None),
        ),
        out_specs=P(None, "bx", None, "by", None, None),
        check_vma=False,
    )
```

```python
import functools
import math

import jax
import jax.numpy as jnp
import numpy as np
from jax import lax
from jax.experimental import pallas as pl
from jax.experimental.pallas import tpu as pltpu
from jax.sharding import PartitionSpec as P

NODES = 16
BOX_NODES = 256
DEVICES = 128
LEAVES = 16
BX = 8
BY = 16
BAND = 1024
F32 = jnp.float32
BF16 = jnp.bfloat16
ROUNDER = 12582912.0
SIN = (6.28305581, -41.33121471, 81.36682035, -74.47802935, 32.78144238)
COS = (0.99995995, -19.73105034, 64.67355678, -82.40422428, 45.64775943)


def chebyshev_points(point_count):
    indices = np.arange(point_count)
    return (1.0 - np.cos(np.pi * (2 * indices + 1) / (2 * point_count))) / 2.0


def lagrange_matrix(locations):
    points = chebyshev_points(NODES)
    matrix = np.ones((len(locations), NODES))
    for own in range(NODES):
        for other in range(NODES):
            if other != own:
                matrix[:, own] *= (locations - points[other]) / (points[own] - points[other])
    return matrix


def child_matrix(halves, child):
    if halves == 1:
        return np.eye(NODES)
    return lagrange_matrix((child + chebyshev_points(NODES)) / 2.0)


def stacked_matrix(halves_first, halves_second):
    pieces = [
        np.kron(child_matrix(halves_first, a), child_matrix(halves_second, b))
        for a in range(halves_first)
        for b in range(halves_second)
    ]
    return np.concatenate(pieces, axis=0)


def two_parts(matrix):
    exact = np.asarray(matrix, np.float32)
    high = exact.astype(jnp.bfloat16)
    low = (exact - high.astype(np.float32)).astype(jnp.bfloat16)
    return high, low


def velocity(first, second):
    return (2.0 + np.sin(2 * np.pi * first) * np.sin(2 * np.pi * second)) / 8.0


def bits(value, count):
    return [(value >> (count - 1 - k)) & 1 for k in range(count)]


def speed_change(first, second, level, split_first=True):
    count_second = 2.0**level
    count_first = 2.0 ** (level if split_first else level - 1)
    new = velocity((first + 0.5) / count_first, (second + 0.5) / count_second)
    above_first = first >> 1 if split_first else first
    old = velocity(
        (above_first + 0.5) / 2.0 ** (level - 1), ((second >> 1) + 0.5) / 2.0 ** (level - 1)
    )
    return new - old


def inner_speeds():
    table = np.zeros((4, 4, 8, 8))
    for child in range(4):
        x, y = bits(child, 2)
        for row in range(8):
            r0, r1, r2 = bits(row, 3)
            for sub in range(8):
                s0, s1, s2 = bits(sub, 3)
                table[0, child, row, sub] = speed_change(x, y, 1)
                table[1, child, row, sub] = speed_change(2 * r0 + x, 2 * r1 + y, 2)
                first, second = 2 * s0 + r2, 2 * s1 + s2
                table[2, child, row, sub] = speed_change(2 * first + x, 2 * second + y, 3)
                first, second = 2 * first + r0, 2 * second + r1
                table[3, child, row, sub] = speed_change(2 * first + x, 2 * second + y, 4)
    return table.reshape(1024).astype(np.float32)


def outer_speeds():
    tables = np.zeros((DEVICES, 7, 256))
    for device in range(DEVICES):
        coarse_first = device >> 3
        for child in range(4):
            x, y = bits(child, 2)
            for row in range(8):
                r0, r1, r2 = bits(row, 3)
                for sub in range(8):
                    s0, s1, s2 = bits(sub, 3)
                    place = child * 64 + row * 8 + sub
                    second = 2 * (device & 7) + s2
                    tables[device, 0, place] = speed_change(
                        2 * coarse_first + x, 2 * second + y, 5
                    )
                    tables[device, 1, place] = speed_change(
                        4 * coarse_first + 2 * r0 + x, 4 * second + 2 * r1 + y, 6
                    )
                    second = 2 * (device & 7) + r2
                    tables[device, 2, place] = speed_change(
                        8 * coarse_first + 4 * s0 + 2 * r0 + x,
                        8 * second + 4 * s1 + 2 * s2 + y,
                        7,
                    )
        for child in range(2):
            for row in range(16):
                r0, r1, r2, r3 = bits(row, 4)
                for sub in range(8):
                    s0, s1, s2 = bits(sub, 3)
                    place = child * 128 + row * 8 + sub
                    first = 8 * coarse_first + 4 * s0 + 2 * r2 + r0
                    second = 2 * (device & 7) + r3
                    second = 16 * second + 8 * s1 + 4 * s2 + 2 * r1 + child
                    tables[device, 3, place] = speed_change(first, second, 8, False)
                    tables[device, 4, place] = velocity((first + 0.5) / 128, (second + 0.5) / 256)
                    tables[device, 5, place] = 8 * (first + 0.5)
                    tables[device, 6, place] = 4 * (second + 0.5)
    return tables.reshape(DEVICES, 7 * 256).astype(np.float32)


def node_tables():
    points = chebyshev_points(NODES).astype(np.float32).astype(np.float64)
    first = np.repeat(points, NODES)
    second = np.tile(points, NODES)
    rows = np.zeros((24, BOX_NODES))
    for child in range(4):
        x, y = bits(child, 2)
        turns = (2 * x - 1) * 2 * first + (2 * y - 1) * second
        rows[child] = turns - np.round(turns)
    for child in range(2):
        rows[4 + child] = (2 * child - 1) * second
    rows[6] = 2 * first
    rows[7] = second
    rows[8] = np.round(first * 8192) / 8192
    rows[9] = first - rows[8]
    rows[10] = np.round(second * 8192) / 8192
    rows[11] = second - rows[10]
    for child in range(2):
        rows[16 + 2 * child] = np.cos(2 * np.pi * rows[child])
        rows[17 + 2 * child] = np.sin(2 * np.pi * rows[child])
    rows[12] = BAND * np.sqrt(first * first + second * second)
    return rows.astype(np.float32)


def basis_factors():
    points = chebyshev_points(NODES)
    return [
        float(np.float32(1.0 / np.prod([points[own] - points[k] for k in range(NODES) if k != own])))
        for own in range(NODES)
    ]


def second_basis():
    small = lagrange_matrix((np.arange(16) + 0.5) / 16.0)
    whole = np.zeros((16, 32, 32, 16))
    for k in range(32):
        whole[:, k, k, :] = small
    return whole.reshape(512, 512)


def turn(turns):
    part = turns - ((turns + ROUNDER) - ROUNDER)
    square = part * part
    sine = SIN[4]
    cosine = COS[4]
    for k in (3, 2, 1, 0):
        sine = sine * square + SIN[k]
        cosine = cosine * square + COS[k]
    return cosine, sine * part


def split(value):
    high = value.astype(BF16)
    return high, (value - high.astype(F32)).astype(BF16)


def bit(value, place):
    return (value >> place) & 1


def make_turns(
    table, first_line, box, level_number, speeds, speed_row, node, base_row, children, rows, stores=()
):
    scale = 4.0 * 2.0 ** (level_number - 1)
    pairs = rows // 2

    def step(index, carry):
        source = index // pairs
        pair = lax.rem(index, pairs)
        radius = []
        for k in range(2):
            first, second = box(source, 2 * pair + k)
            along = first + node[6:7, :]
            across = second + node[7:8, :]
            radius.append(scale * jnp.sqrt(along * along + across * across))
        radius = jnp.concatenate([jnp.broadcast_to(value, (8, BOX_NODES)) for value in radius])
        for child in range(children):
            place = pl.multiple_of(speed_row + child * rows * 8 + pair * 16, 16)
            change = speeds[pl.ds(place, 16), :]
            change = jnp.concatenate([change, change], axis=1)
            cosine, sine = turn(change * radius + node[base_row + child : base_row + child + 1, :])
            line = first_line + index * children + child
            table[line, 0] = cosine
            table[line, 1] = sine
        return carry

    if not stores:
        lax.fori_loop(0, (4 if children == 4 else 2) * pairs, step, 0)
    for source, store in enumerate(stores):
        lax.fori_loop(source * pairs, (source + 1) * pairs, step, 0)
        store.start()


def make_first_turns(table, box, node):
    def step(index, carry):
        radius = []
        for k in range(2):
            first, second = box(index // 4, 2 * (index % 4) + k)
            along = first + node[6:7, :]
            across = second + node[7:8, :]
            radius.append(0.5 * jnp.sqrt(along * along + across * across))
        cosine, sine = turn(jnp.concatenate(radius))
        for kind in range(2):
            base_cosine = node[16 + 2 * kind : 17 + 2 * kind, :]
            base_sine = node[17 + 2 * kind : 18 + 2 * kind, :]
            cosines = base_cosine * cosine
            sines = base_sine * sine
            mixed = base_sine * cosine
            other = base_cosine * sine
            line = 4 * index + kind
            mirror = 4 * index + 3 - kind
            if kind == 0:
                table[line, 0] = cosines - sines
                table[line, 1] = mixed + other
                table[mirror, 0] = cosines + sines
                table[mirror, 1] = other - mixed
            else:
                table[line, 0] = cosines + sines
                table[line, 1] = mixed - other
                table[mirror, 0] = cosines - sines
                table[mirror, 1] = -mixed - other
        return carry

    lax.fori_loop(0, 16, step, 0)


def level(
    read, table, first_line, highs, lows, matrix, children, rows, by_rows, ready, emit, matrix_ready=None
):
    sources = 4 if children == 4 else 2
    pairs = rows // 2
    columns = sources * BOX_NODES
    for half in range(2):
        high, low = highs[half], lows[half]
        if by_rows:
            chosen = list(range(children))
            near = list(range(half * pairs // 2, (half + 1) * pairs // 2))
        else:
            chosen = list(range(half * children // 2, (half + 1) * children // 2))
            near = list(range(pairs))
        height = 16 * len(near)
        for source in range(sources):
            lanes = slice(source * BOX_NODES, (source + 1) * BOX_NODES)
            if half == 0 and source < len(ready):
                ready[source].wait()
            for spot, pair in enumerate(near):
                group = source * rows + 2 * pair
                real, imaginary = (
                    jnp.concatenate([read(group, part), read(group + 1, part)])
                    for part in range(2)
                )
                for number, child in enumerate(chosen):
                    line = first_line + (source * pairs + pair) * children + child
                    cosine = table[line, 0]
                    sine = table[line, 1]
                    for part, value in enumerate(
                        (real * cosine - imaginary * sine, real * sine + imaginary * cosine)
                    ):
                        place = (number * 2 + part) * height + spot * 16
                        value_high, value_low = split(value)
                        high[place : place + 16, lanes] = value_high
                        low[place : place + 16, lanes] = value_low
        if half == 0 and matrix_ready is not None:
            matrix_ready.wait()
        both = jnp.dot(high[:, :columns], matrix[...], preferred_element_type=F32)
        rest = jnp.dot(low[:, :columns], matrix[:, :BOX_NODES], preferred_element_type=F32)
        result = both[:, :BOX_NODES] + (both[:, BOX_NODES:] + rest)
        for number, child in enumerate(chosen):
            for spot, pair in enumerate(near):
                for k in range(2):
                    start = number * 2 * height + spot * 16 + 8 * k
                    emit(
                        child,
                        2 * pair + k,
                        [result[start + height * part : start + height * part + 8] for part in range(2)],
                    )


def matrices():
    basis = second_basis()
    rows = [
        stacked_matrix(2, 2),
        stacked_matrix(1, 2),
        basis[:, :256],
        basis[:, 256:],
    ]
    return np.concatenate(two_parts(np.concatenate(rows)), axis=1)


def sub_bits():
    row = lax.broadcasted_iota(jnp.int32, (8, BOX_NODES), 0)
    return [bit(row, 2 - k).astype(F32) for k in range(3)]


def find_mask(slots, table, entries, high_hot, low_hot):
    iota = lax.broadcasted_iota(jnp.int32, (16, 128), 0).astype(F32)
    rows = [(iota + 16.0 * k).astype(BF16) for k in range(8)]
    one = jnp.ones((16, 128), BF16)
    zero = jnp.zeros((16, 128), BF16)
    block = jnp.concatenate([slots[:, :128], slots[:, 128:]], axis=0)
    entries[0] = (block >> 7).astype(F32)
    entries[1] = (block & 127).astype(F32)

    def step(index, carry):
        for source, hot in enumerate((high_hot, low_hot)):
            for side in range(2):
                start = pl.multiple_of(index * 8 + 64 * side, 8)
                block = entries[source, pl.ds(start, 8), :]
                for k in range(8):
                    value = jnp.broadcast_to(block[k : k + 1], (16, 128)).astype(BF16)
                    lanes = pl.ds(pl.multiple_of(index * 1024 + 128 * k, 128), 128)
                    for place in range(8):
                        line = 128 * side + 16 * place
                        hot[line : line + 16, lanes] = jnp.where(value == rows[place], one, zero)
        return carry

    lax.fori_loop(0, 8, step, 0)
    parts = [
        lax.dot_general(
            high_hot[:, 4096 * k : 4096 * (k + 1)],
            low_hot[:, 4096 * k : 4096 * (k + 1)],
            (((1,), (1,)), ((), ())),
            preferred_element_type=F32,
        )
        for k in range(2)
    ]
    total = parts[0] + parts[1]
    mask = jnp.where(total[:128, :128] + total[128:, 128:] > 0.5, 1.0, 0.0)
    for k in range(8):
        lanes = slice(128 * (k % 2), 128 * (k % 2 + 1))
        table[256 + k // 4, k // 2 % 2, :, lanes] = mask[16 * k : 16 * (k + 1)]


def store_level(table, table_far, leave, index, size=64, first=0):
    lines = pl.ds(size * index, size)
    place = leave.at[index if first == 0 else first + index % 4]
    return pltpu.make_async_copy(table.at[lines], table_far.at[lines], place)


def fetch_level(table_far, table, arrive, index, size=64):
    lines = pl.ds(64 * index, size)
    return pltpu.make_async_copy(table_far.at[lines], table.at[lines], arrive.at[index])


def fetch_mask_lines(table_far, table, place):
    lines = pl.ds(256, 2)
    return pltpu.make_async_copy(table_far.at[lines], table.at[lines], place)


def inner_turns_kernel(
    block_first_ref,
    block_second_ref,
    slots_far,
    node_far,
    speeds_far,
    table_far,
    slots,
    node,
    speeds,
    table,
    entries,
    high_hot,
    low_hot,
    arrive,
    leave,
):
    fetches = [
        pltpu.make_async_copy(far, near, arrive.at[k])
        for k, (far, near) in enumerate(
            ((slots_far, slots), (node_far, node), (speeds_far, speeds))
        )
    ]
    for fetch in fetches:
        fetch.start()
    fetches[0].wait()
    find_mask(slots, table, entries, high_hot, low_hot)
    for fetch in fetches[1:]:
        fetch.wait()
    stores = [store_level(table, table_far, leave, k) for k in range(3)]
    stores += [store_level(table, table_far, leave, 12 + k, 16, 3) for k in range(4)]
    store_mask = store_level(table, table_far, leave, 128, 2, 7)
    store_mask.start()
    sub = sub_bits()
    block_first = block_first_ref[0]
    block_second = block_second_ref[0]

    def box(source, row):
        first = block_first * 16 + bit(source, 1) + 2 * bit(row, 2)
        second = block_second * 16 + bit(source, 0) + 2 * bit(row, 1) + 8 * bit(row, 0)
        return (
            2.0 * first.astype(F32) + (8.0 * sub[0] + 16.0 * sub[2]),
            second.astype(F32) + 4.0 * sub[1],
        )

    make_first_turns(table, box, node)
    stores[0].start()

    def box(source, row):
        first = block_first * 8 + bit(source, 1)
        second = block_second * 8 + bit(source, 0) + 4 * bit(row, 0)
        return (
            2.0 * first.astype(F32) + (4.0 * sub[0] + 8.0 * sub[2]),
            second.astype(F32) + 2.0 * sub[1],
        )

    make_turns(table, 64, box, 2, speeds, 256, node, 0, 4, 8)
    stores[1].start()

    def box(source, row):
        first = block_first * 4 + bit(source, 1) + 2 * bit(row, 2)
        second = block_second * 4 + bit(source, 0) + 2 * bit(row, 1)
        return 2.0 * first.astype(F32), second.astype(F32)

    make_turns(table, 128, box, 3, speeds, 512, node, 0, 4, 8)
    stores[2].start()

    def box(source, row):
        first = block_first * 2 + bit(source, 1)
        second = block_second * 2 + bit(source, 0)
        return 2.0 * first.astype(F32), second.astype(F32)

    make_turns(table, 192, box, 4, speeds, 768, node, 0, 4, 8, stores[3:])
    for store in stores + [store_mask]:
        store.wait()


def outer_turns_kernel(node, speeds, table_far, table, leave):
    stores = [store_level(table, table_far, leave, k) for k in range(3)]
    stores += [store_level(table, table_far, leave, 12 + k, 16, 3) for k in range(3)]
    sub = sub_bits()

    def box(source, row):
        first = bit(source, 1) + 2 * bit(row, 2) + 4 * bit(row, 1)
        second = bit(source, 0) + 2 * bit(row, 0)
        return 2.0 * first.astype(F32), second.astype(F32) + (4.0 * sub[0] + 8.0 * sub[1])

    make_turns(table, 0, box, 5, speeds, 0, node, 0, 4, 8)
    stores[0].start()

    def box(source, row):
        first = bit(source, 1) + 2 * bit(row, 0)
        second = bit(source, 0)
        return 2.0 * first.astype(F32), second.astype(F32) + (2.0 * sub[0] + 4.0 * sub[1])

    make_turns(table, 64, box, 6, speeds, 256, node, 0, 4, 8)
    stores[1].start()

    def box(source, row):
        first = bit(source, 1)
        second = bit(source, 0) + 2 * bit(row, 1)
        return 2.0 * first.astype(F32), second.astype(F32)

    make_turns(table, 128, box, 7, speeds, 512, node, 0, 4, 8)
    stores[2].start()

    def box(source, row):
        return jnp.float32(0.0), source.astype(F32)

    make_turns(table, 192, box, 8, speeds, 768, node, 4, 2, 16, stores[3:5])

    def last(index, carry):
        def column(table):
            value = speeds[pl.ds(pl.multiple_of(256 * table + index * 16, 16), 16), :]
            return jnp.concatenate([value, value], axis=1)

        first = column(5)
        second = column(6)
        turns = first * node[8:9, :]
        turns = turns - ((turns + ROUNDER) - ROUNDER)
        across = second * node[10:11, :]
        across = across - ((across + ROUNDER) - ROUNDER)
        around = column(4) * node[12:13, :]
        around = around - ((around + ROUNDER) - ROUNDER)
        turns = turns + across + around + first * node[9:10, :] + second * node[11:12, :]
        cosine, sine = turn(turns)
        table[224 + index, 0] = cosine
        table[224 + index, 1] = sine
        return carry

    lax.fori_loop(0, 16, last, 0)
    stores[5].start()
    for store in stores:
        store.wait()


def deposit(
    arrived, table, second, fetch_second, state, wide, cells, hots, spreads, grid
):
    points = [float(value) for value in chebyshev_points(NODES).astype(np.float32)]
    factors = basis_factors()

    def source_step(index, carry):
        rows = pl.ds(pl.multiple_of(index * 16, 16), 16)
        first, second, real, imaginary = (
            arrived[pl.ds(index * 64 + k, 16, stride=4), :] for k in range(4)
        )
        whole_first = first.astype(jnp.int32)
        whole_second = second.astype(jnp.int32)
        along = first + 0.5
        across = second + 0.5
        eighths = jnp.bitwise_and(whole_first + whole_second + 1, 7).astype(F32)
        cosine, sine = turn(
            0.125 * eighths + 0.0625 * jnp.sqrt(along * along + across * across)
        )
        lanes = pl.ds(pl.multiple_of(index % 2 * 128, 128), 128)
        live = table[256 + index // 4, index // 2 % 2, :, lanes]
        real = real * live
        imaginary = imaginary * live
        turned = (real * cosine - imaginary * sine, real * sine + imaginary * cosine)
        place = jnp.bitwise_and(whole_first, 31).astype(F32) * 0.03125 + 0.015625
        cells[0, rows, :] = jnp.bitwise_and(whole_second, 15).astype(F32)
        x = [bit(whole_first, 5 + k) for k in range(4)]
        y = [bit(whole_second, 4 + k) for k in range(4)]
        cells[1, rows, :] = (x[0] * 8 + y[0] * 4 + x[1] * 2 + y[1]).astype(F32)
        cells[2, rows, :] = (y[3] * 8 + x[2] * 4 + y[2] * 2 + x[3]).astype(F32)
        away = [place - value for value in points]
        before = [None] * NODES
        after = [None] * NODES
        for p in range(1, NODES):
            before[p] = away[p - 1] if p == 1 else before[p - 1] * away[p - 1]
            q = NODES - 1 - p
            after[q] = away[q + 1] if p == 1 else after[q + 1] * away[q + 1]
        for p in range(NODES):
            if p == 0:
                value = after[0]
            elif p == NODES - 1:
                value = before[p]
            else:
                value = before[p] * after[p]
            value = value * factors[p]
            for part in range(2):
                wide[pl.ds(index * 512 + part * 16 + p, 16, stride=32), :] = value * turned[part]
        return carry

    lax.fori_loop(0, 8, source_step, 0)

    iota = lax.broadcasted_iota(jnp.int32, (16, 128), 0).astype(F32).astype(BF16)
    one = jnp.ones((16, 128), BF16)
    zero = jnp.zeros((16, 128), BF16)

    def build(chunk, hot, spread):
        for k in range(16):
            sender = chunk * 16 + k
            lanes = slice(128 * k, 128 * (k + 1))

            def row(number, height):
                value = cells[number, pl.ds(sender, 1), :]
                return jnp.broadcast_to(value, (height, 128)).astype(BF16)

            value = wide[pl.ds(pl.multiple_of(sender * 32, 32), 32), :].astype(BF16)
            cell = row(0, 16)
            for c in range(16):
                chosen = cell == jnp.full((16, 128), c, BF16)
                for part in range(2):
                    spread[32 * c + 16 * part : 32 * c + 16 * (part + 1), lanes] = jnp.where(
                        chosen, value[16 * part : 16 * (part + 1)], zero
                    )
            inside = jnp.where(row(2, 16) == iota, one, zero)
            above = row(1, 16)
            for c in range(16):
                hot[16 * c : 16 * (c + 1), lanes] = jnp.where(
                    above == jnp.full((16, 128), c, BF16), inside, zero
                )

    grid[...] = jnp.zeros_like(grid)

    def spread_step(index, carry):
        for k in range(2):
            build(2 * index + k, hots[k], spreads[k])
        grid[...] += lax.dot_general(
            jnp.concatenate([hots[0][...], hots[1][...]], axis=1),
            jnp.concatenate([spreads[0][...], spreads[1][...]], axis=1),
            (((1,), (1,)), ((), ())),
            preferred_element_type=F32,
        )
        return carry

    lax.fori_loop(0, 4, spread_step, 0)

    grid_high, grid_low = split(grid[...])
    fetch_second.wait()
    for part in range(2):
        basis = second[512 * part : 512 * (part + 1), :]
        result = jnp.dot(grid_high, basis, preferred_element_type=F32)
        rest = jnp.dot(grid_low, basis[:, :BOX_NODES], preferred_element_type=F32)
        result = result[:, :BOX_NODES] + (result[:, BOX_NODES:] + rest)
        for group in range(32):
            state[group, part] = result[8 * group : 8 * group + 8, :]


def halves(value):
    return value[:, :128], value[:, 128:]


def inner_kernel(
    arrived,
    table_far,
    matrix_far,
    out,
    second,
    matrix,
    table,
    arrive,
    wide,
    cells,
    hots,
    spreads,
    grid,
    other,
    turned,
    highs,
    lows,
    state,
):
    fetch_mask = fetch_mask_lines(table_far, table, arrive.at[6])
    fetch_mask.start()
    fetch_second = pltpu.make_async_copy(matrix_far.at[pl.ds(1536, 1024)], second, arrive.at[4])
    fetch_second.start()
    fetches = [fetch_level(table_far, table, arrive, k) for k in range(4)]
    for fetch in fetches:
        fetch.start()
    fetch_matrix = pltpu.make_async_copy(matrix_far.at[pl.ds(0, 1024)], matrix, arrive.at[5])
    fetch_matrix.start()
    fetch_mask.wait()
    deposit(arrived, table, second, fetch_second, state, wide, cells, hots, spreads, grid)

    def run(number, read, emit):
        level(
            read,
            table,
            64 * (number - 1),
            highs,
            lows,
            matrix,
            4,
            8,
            number % 2 == 0,
            fetches[number - 1 : number],
            emit,
            fetch_matrix if number == 1 else None,
        )

    def leaf(group, part):
        return state[group, part]

    def read(group, part):
        return other[group, part]

    def keep(child, row, values):
        for part in range(2):
            other[(row // 2) * 8 + child * 2 + row % 2, part] = values[part]

    run(1, leaf, keep)

    def turn_over(child, row, values):
        start = ((row % 2 * 2 + child // 2) * 8 + row // 2 * 2 + child % 2) * 8
        for part in range(2):
            for half, value in enumerate(halves(values[part])):
                turned[2 * part + half, start : start + 8, :] = value

    run(2, read, turn_over)

    def across(group, part):
        b2x, b2y, b3x, b3y, t2x = bits(group, 5)
        start = (b3y * 2 + t2x) * 64 + b2x * 4 + b2y * 2 + b3x
        return jnp.concatenate(
            [turned.at[2 * part + half][pl.ds(start, 8, stride=8), :] for half in range(2)], axis=1
        )

    run(3, across, keep)

    def send(child, row, values):
        x, y = bits(child, 2)
        r0, r1, r2 = bits(row, 3)
        device = r2 * 32 + r0 * 16 + x * 8 + r1
        for upper in range(2):
            for part in range(2):
                for half, value in enumerate(halves(values[part])):
                    start = (device + 64 * upper) * 8 + y * 4 + half * 2 + part
                    out[pl.ds(start, 4, stride=16), :] = value[4 * upper : 4 * upper + 4]

    run(4, read, send)


def outer_kernel(
    arrived, table_far, matrix_far, out, table, matrix, last, arrive, state, turned, highs, lows
):
    first = [
        pltpu.make_async_copy(
            table_far.at[pl.ds(16 * k, 16)], table.at[pl.ds(16 * k, 16)], arrive.at[6 + k]
        )
        for k in range(4)
    ]
    fetches = [
        fetch_level(table_far, table, arrive, k, 64 if k < 3 else 48) for k in range(1, 4)
    ]
    fetch_matrix = pltpu.make_async_copy(matrix_far.at[pl.ds(0, 1024)], matrix, arrive.at[5])
    fetch_last = pltpu.make_async_copy(matrix_far.at[pl.ds(1024, 512)], last, arrive.at[4])
    for fetch in first + [fetch_matrix] + fetches + [fetch_last]:
        fetch.start()

    def first_read(group, part):
        i2, j3, i1, i0, j2 = bits(group, 5)
        source = i2 * 64 + i1 * 32 + i0 * 16 + j3 * 8 + j2 * 4
        return jnp.concatenate(
            [
                arrived[pl.ds(source * 8 + half * 2 + part, 8, stride=4), :]
                for half in range(2)
            ],
            axis=1,
        )

    def run(number, read, emit):
        level(
            read,
            table,
            64 * (number - 5),
            highs,
            lows,
            matrix,
            4,
            8,
            number % 2 == 0,
            first if number == 5 else fetches[number - 6 : number - 5],
            emit,
            fetch_matrix if number == 5 else None,
        )

    def read(group, part):
        return state[group, part]

    def keep(child, row, values):
        i1, i0, j2 = bits(row, 3)
        for part in range(2):
            state[(2 * i1 + j2) * 8 + child * 2 + i0, part] = values[part]

    run(5, first_read, keep)

    def turn_over(child, row, values):
        start = ((row % 2 * 2 + child // 2) * 8 + row // 2 * 2 + child % 2) * 8
        for part in range(2):
            for half, value in enumerate(halves(values[part])):
                turned[2 * part + half, start : start + 8, :] = value

    run(6, read, turn_over)

    def across(group, part):
        i0, j1, t6x, j0, pair = bits(group, 5)
        start = (i0 * 2 + t6x) * 64 + j1 * 4 + j0 * 2 + pair
        return jnp.concatenate(
            [turned.at[2 * part + half][pl.ds(start, 8, stride=8), :] for half in range(2)], axis=1
        )

    def keep_last(child, row, values):
        t6x, j0, pair = bits(row, 3)
        for part in range(2):
            state[j0 * 16 + child * 4 + t6x * 2 + pair, part] = values[part]

    run(7, across, keep_last)

    def send(child, row, values):
        t7x, t7y, t6x, pair = bits(row, 4)
        line = 224 + child * 8 + row // 2
        cosine = table[line, 0, 8 * (row % 2) : 8 * (row % 2) + 8, :]
        sine = table[line, 1, 8 * (row % 2) : 8 * (row % 2) + 8, :]
        real, imaginary = values
        device = t6x * 32 + t7x * 16 + t7y * 2 + child
        for part, whole in enumerate(
            (real * cosine + imaginary * sine, imaginary * cosine - real * sine)
        ):
            for half, value in enumerate(halves(whole)):
                for upper in range(2):
                    place = (device + 64 * upper) * 8 + pair * 4 + half * 2 + part
                    out[pl.ds(place, 4, stride=32), :] = value[4 * upper : 4 * upper + 4]

    level(
        read, table, 192, highs, lows, last, 2, 16, True, fetches[2:], send, fetch_last
    )


def vmem(count):
    return [pl.BlockSpec(memory_space=pltpu.VMEM)] * count


def smem(count):
    return [pl.BlockSpec(memory_space=pltpu.SMEM)] * count


def far(count):
    return [pl.BlockSpec(memory_space=pltpu.HBM)] * count


def payload_kernel(place_far, amp_far, out_far, place, amp, out, arrive, leave):
    fetches = [
        pltpu.make_async_copy(place_far, place, arrive.at[0]),
        pltpu.make_async_copy(amp_far, amp, arrive.at[1]),
    ]
    for fetch in fetches:
        fetch.start()
    for fetch in fetches:
        fetch.wait()
    for k in range(2):
        out[pl.ds(k, DEVICES, stride=4), :] = place[k].astype(F32)
        out[pl.ds(2 + k, DEVICES, stride=4), :] = amp[k]
    store = pltpu.make_async_copy(out, out_far, leave)
    store.start()
    store.wait()


def make_payload(place, amp):
    return pl.pallas_call(
        payload_kernel,
        out_shape=jax.ShapeDtypeStruct((4 * DEVICES, 128), F32),
        in_specs=far(2),
        out_specs=far(1)[0],
        scratch_shapes=[
            pltpu.VMEM((2, DEVICES, 128), jnp.int32),
            pltpu.VMEM((2, DEVICES, 128), F32),
            pltpu.VMEM((4 * DEVICES, 128), F32),
            pltpu.SemaphoreType.DMA((2,)),
            pltpu.SemaphoreType.DMA,
        ],
        name="payload",
        compiler_params=pltpu.CompilerParams(vmem_limit_bytes=60 << 20),
    )(place, amp)


def result_kernel(weights, out, leave):
    stores = [
        pltpu.make_async_copy(
            weights.at[:, :, half],
            out.at[:, 0, :, 0, :, pl.ds(128 * half, 128)],
            leave.at[half],
        )
        for half in range(2)
    ]
    for store in stores:
        store.start()
    for store in stores:
        store.wait()


def place_result(weights):
    return pl.pallas_call(
        result_kernel,
        out_shape=jax.ShapeDtypeStruct((LEAVES, 1, LEAVES, 1, 2, BOX_NODES), F32),
        in_specs=vmem(1),
        out_specs=far(1)[0],
        scratch_shapes=[pltpu.SemaphoreType.DMA((2,))],
        name="result",
        compiler_params=pltpu.CompilerParams(vmem_limit_bytes=16 << 20),
    )(weights)


def inner_turns(block_first, block_second, slots):
    speeds = np.repeat(inner_speeds()[:, None], 128, axis=1)
    return pl.pallas_call(
        inner_turns_kernel,
        out_shape=jax.ShapeDtypeStruct((258, 2, 16, 256), F32),
        in_specs=smem(2) + far(3),
        out_specs=far(1)[0],
        scratch_shapes=[
            pltpu.VMEM((64, 256), jnp.int32),
            pltpu.VMEM((24, 256), F32),
            pltpu.VMEM((1024, 128), F32),
            pltpu.VMEM((258, 2, 16, 256), F32),
            pltpu.VMEM((2, 128, 128), F32),
            pltpu.VMEM((256, 8192), BF16),
            pltpu.VMEM((256, 8192), BF16),
            pltpu.SemaphoreType.DMA((3,)),
            pltpu.SemaphoreType.DMA((8,)),
        ],
        name="inner_turns",
        compiler_params=pltpu.CompilerParams(vmem_limit_bytes=60 << 20),
    )(block_first, block_second, slots, jnp.asarray(node_tables()), jnp.asarray(speeds))


def outer_turns(speeds):
    return pl.pallas_call(
        outer_turns_kernel,
        out_shape=jax.ShapeDtypeStruct((240, 2, 16, 256), F32),
        in_specs=vmem(2),
        out_specs=far(1)[0],
        scratch_shapes=[
            pltpu.VMEM((240, 2, 16, 256), F32),
            pltpu.SemaphoreType.DMA((7,)),
        ],
        name="outer_turns",
        compiler_params=pltpu.CompilerParams(vmem_limit_bytes=52 << 20),
    )(jnp.asarray(node_tables()), speeds)


LEVEL_SCRATCH = [
    pltpu.VMEM((32, 2, 8, 256), F32),
    pltpu.VMEM((4, 256, 128), F32),
    [pltpu.VMEM((256, 1024), BF16)] * 2,
    [pltpu.VMEM((256, 1024), BF16)] * 2,
]


def inner_levels(arrived, table):
    return pl.pallas_call(
        inner_kernel,
        out_shape=jax.ShapeDtypeStruct((1024, 128), F32),
        in_specs=vmem(1) + far(2),
        out_specs=vmem(1)[0],
        scratch_shapes=[
            pltpu.VMEM((1024, 512), BF16),
            pltpu.VMEM((1024, 512), BF16),
            pltpu.VMEM((258, 2, 16, 256), F32),
            pltpu.SemaphoreType.DMA((7,)),
            pltpu.VMEM((4096, 128), F32),
            pltpu.VMEM((3, 128, 128), F32),
            [pltpu.VMEM((256, 2048), BF16)] * 2,
            [pltpu.VMEM((512, 2048), BF16)] * 2,
            pltpu.VMEM((256, 512), F32),
        ]
        + LEVEL_SCRATCH
        + LEVEL_SCRATCH[:1],
        name="inner",
        compiler_params=pltpu.CompilerParams(vmem_limit_bytes=52 << 20),
    )(
        arrived,
        table,
        jnp.asarray(matrices()),
    )


def outer_levels(arrived, table):
    return pl.pallas_call(
        outer_kernel,
        out_shape=jax.ShapeDtypeStruct((1024, 128), F32),
        in_specs=vmem(1) + far(2),
        out_specs=vmem(1)[0],
        scratch_shapes=[
            pltpu.VMEM((240, 2, 16, 256), F32),
            pltpu.VMEM((1024, 512), BF16),
            pltpu.VMEM((512, 512), BF16),
            pltpu.SemaphoreType.DMA((10,)),
        ]
        + LEVEL_SCRATCH,
        name="outer",
        compiler_params=pltpu.CompilerParams(vmem_limit_bytes=52 << 20),
    )(
        arrived,
        table,
        jnp.asarray(matrices()),
    )


def reverse_bits(number, bit_count):
    result = jnp.zeros_like(number)
    for position in range(bit_count):
        result = result + jnp.left_shift(
            jnp.bitwise_and(jnp.right_shift(number, position), 1), bit_count - 1 - position
        )
    return result


def exchange(array):
    return lax.all_to_all(array, ("bx", "by"), split_axis=0, concat_axis=0, tiled=True)


def shards(src_pos, src_amp, box_slots):
    column = lax.axis_index("bx")
    row = lax.axis_index("by")
    device = column * BY + row
    block_first = reverse_bits(column, 3).astype(jnp.int32).reshape(1)
    block_second = reverse_bits(row, 4).astype(jnp.int32).reshape(1)
    payload = make_payload(src_pos.reshape(2, DEVICES, 128), src_amp.reshape(2, DEVICES, 128))
    arrived = exchange(payload.reshape(DEVICES, 4, 128)).reshape(512, 128)
    table = inner_turns(block_first, block_second, box_slots[0].T)
    arrived, table = lax.optimization_barrier((arrived, table))
    weights = inner_levels(arrived, table)
    weights = exchange(weights.reshape(DEVICES, 8, 128)).reshape(1024, 128)
    speeds = lax.dynamic_index_in_dim(jnp.asarray(outer_speeds()), device, 0, keepdims=False)
    speeds = jnp.broadcast_to(speeds[:, None], (7 * 256, 128))
    weights = outer_levels(weights, outer_turns(speeds))
    weights = exchange(weights.reshape(DEVICES, 8, 128))
    return place_result(weights.reshape(LEAVES, LEAVES, 2, 2, 128))


def solution(mesh):
    return jax.shard_map(
        shards,
        mesh=mesh,
        in_specs=(
            P(None, ("bx", "by"), None),
            P(None, ("bx", "by"), None),
            P(("bx", "by"), None, None),
        ),
        out_specs=P(None, "bx", None, "by", None, None),
        check_vma=False,
    )
```

```python
import functools
import math

import jax
import jax.numpy as jnp
import numpy as np
from jax import lax
from jax.experimental import pallas as pl
from jax.experimental.pallas import tpu as pltpu
from jax.sharding import PartitionSpec as P

NODES = 16
BOX_NODES = 256
DEVICES = 128
LEAVES = 16
BX = 8
BY = 16
BAND = 1024
F32 = jnp.float32
BF16 = jnp.bfloat16
ROUNDER = 12582912.0
SIN = (6.28305581, -41.33121471, 81.36682035, -74.47802935, 32.78144238)
COS = (0.99995995, -19.73105034, 64.67355678, -82.40422428, 45.64775943)


def chebyshev_points(point_count):
    indices = np.arange(point_count)
    return (1.0 - np.cos(np.pi * (2 * indices + 1) / (2 * point_count))) / 2.0


def lagrange_matrix(locations):
    points = chebyshev_points(NODES)
    matrix = np.ones((len(locations), NODES))
    for own in range(NODES):
        for other in range(NODES):
            if other != own:
                matrix[:, own] *= (locations - points[other]) / (points[own] - points[other])
    return matrix


def child_matrix(halves, child):
    if halves == 1:
        return np.eye(NODES)
    return lagrange_matrix((child + chebyshev_points(NODES)) / 2.0)


def stacked_matrix(halves_first, halves_second):
    pieces = [
        np.kron(child_matrix(halves_first, a), child_matrix(halves_second, b))
        for a in range(halves_first)
        for b in range(halves_second)
    ]
    return np.concatenate(pieces, axis=0)


def two_parts(matrix):
    exact = np.asarray(matrix, np.float32)
    high = exact.astype(jnp.bfloat16)
    low = (exact - high.astype(np.float32)).astype(jnp.bfloat16)
    return high, low


def velocity(first, second):
    return (2.0 + np.sin(2 * np.pi * first) * np.sin(2 * np.pi * second)) / 8.0


def bits(value, count):
    return [(value >> (count - 1 - k)) & 1 for k in range(count)]


def speed_change(first, second, level, split_first=True):
    count_second = 2.0**level
    count_first = 2.0 ** (level if split_first else level - 1)
    new = velocity((first + 0.5) / count_first, (second + 0.5) / count_second)
    above_first = first >> 1 if split_first else first
    old = velocity(
        (above_first + 0.5) / 2.0 ** (level - 1), ((second >> 1) + 0.5) / 2.0 ** (level - 1)
    )
    return new - old


def inner_speeds():
    table = np.zeros((4, 4, 8, 8))
    for child in range(4):
        x, y = bits(child, 2)
        for row in range(8):
            r0, r1, r2 = bits(row, 3)
            for sub in range(8):
                s0, s1, s2 = bits(sub, 3)
                table[0, child, row, sub] = speed_change(x, y, 1)
                table[1, child, row, sub] = speed_change(2 * r0 + x, 2 * r1 + y, 2)
                first, second = 2 * s0 + r2, 2 * s1 + s2
                table[2, child, row, sub] = speed_change(2 * first + x, 2 * second + y, 3)
                first, second = 2 * first + r0, 2 * second + r1
                table[3, child, row, sub] = speed_change(2 * first + x, 2 * second + y, 4)
    return table.reshape(1024).astype(np.float32)


def outer_speeds():
    tables = np.zeros((DEVICES, 7, 256))
    for device in range(DEVICES):
        coarse_first = device >> 3
        for child in range(4):
            x, y = bits(child, 2)
            for row in range(8):
                r0, r1, r2 = bits(row, 3)
                for sub in range(8):
                    s0, s1, s2 = bits(sub, 3)
                    place = child * 64 + row * 8 + sub
                    second = 2 * (device & 7) + s2
                    tables[device, 0, place] = speed_change(
                        2 * coarse_first + x, 2 * second + y, 5
                    )
                    tables[device, 1, place] = speed_change(
                        4 * coarse_first + 2 * r0 + x, 4 * second + 2 * r1 + y, 6
                    )
                    second = 2 * (device & 7) + r2
                    tables[device, 2, place] = speed_change(
                        8 * coarse_first + 4 * s0 + 2 * r0 + x,
                        8 * second + 4 * s1 + 2 * s2 + y,
                        7,
                    )
        for child in range(2):
            for row in range(16):
                r0, r1, r2, r3 = bits(row, 4)
                for sub in range(8):
                    s0, s1, s2 = bits(sub, 3)
                    place = child * 128 + row * 8 + sub
                    first = 8 * coarse_first + 4 * s0 + 2 * r2 + r0
                    second = 2 * (device & 7) + r3
                    second = 16 * second + 8 * s1 + 4 * s2 + 2 * r1 + child
                    tables[device, 3, place] = speed_change(first, second, 8, False)
                    tables[device, 4, place] = velocity((first + 0.5) / 128, (second + 0.5) / 256)
                    tables[device, 5, place] = 8 * (first + 0.5)
                    tables[device, 6, place] = 4 * (second + 0.5)
    return tables.reshape(DEVICES, 7 * 256).astype(np.float32)


def node_tables():
    points = chebyshev_points(NODES).astype(np.float32).astype(np.float64)
    first = np.repeat(points, NODES)
    second = np.tile(points, NODES)
    rows = np.zeros((24, BOX_NODES))
    for child in range(4):
        x, y = bits(child, 2)
        turns = (2 * x - 1) * 2 * first + (2 * y - 1) * second
        rows[child] = turns - np.round(turns)
    for child in range(2):
        rows[4 + child] = (2 * child - 1) * second
    rows[6] = 2 * first
    rows[7] = second
    rows[8] = np.round(first * 8192) / 8192
    rows[9] = first - rows[8]
    rows[10] = np.round(second * 8192) / 8192
    rows[11] = second - rows[10]
    for child in range(2):
        rows[16 + 2 * child] = np.cos(2 * np.pi * rows[child])
        rows[17 + 2 * child] = np.sin(2 * np.pi * rows[child])
    rows[12] = BAND * np.sqrt(first * first + second * second)
    return rows.astype(np.float32)


def basis_factors():
    points = chebyshev_points(NODES)
    return [
        float(np.float32(1.0 / np.prod([points[own] - points[k] for k in range(NODES) if k != own])))
        for own in range(NODES)
    ]


def second_basis():
    small = lagrange_matrix((np.arange(16) + 0.5) / 16.0)
    whole = np.zeros((16, 32, 32, 16))
    for k in range(32):
        whole[:, k, k, :] = small
    return whole.reshape(512, 512)


def turn(turns):
    part = turns - ((turns + ROUNDER) - ROUNDER)
    square = part * part
    sine = SIN[4]
    cosine = COS[4]
    for k in (3, 2, 1, 0):
        sine = sine * square + SIN[k]
        cosine = cosine * square + COS[k]
    return cosine, sine * part


def split(value):
    high = value.astype(BF16)
    return high, (value - high.astype(F32)).astype(BF16)


def bit(value, place):
    return (value >> place) & 1


def make_turns(
    table, first_line, box, level_number, speeds, speed_row, node, base_row, children, rows, stores=()
):
    scale = 4.0 * 2.0 ** (level_number - 1)
    pairs = rows // 2

    def step(index, carry):
        source = index // pairs
        pair = lax.rem(index, pairs)
        radius = []
        for k in range(2):
            first, second = box(source, 2 * pair + k)
            along = first + node[6:7, :]
            across = second + node[7:8, :]
            radius.append(scale * jnp.sqrt(along * along + across * across))
        radius = jnp.concatenate([jnp.broadcast_to(value, (8, BOX_NODES)) for value in radius])
        for child in range(children):
            place = pl.multiple_of(speed_row + child * rows * 8 + pair * 16, 16)
            change = speeds[pl.ds(place, 16), :]
            change = jnp.concatenate([change, change], axis=1)
            cosine, sine = turn(change * radius + node[base_row + child : base_row + child + 1, :])
            line = first_line + index * children + child
            table[line, 0] = cosine
            table[line, 1] = sine
        return carry

    if not stores:
        lax.fori_loop(0, (4 if children == 4 else 2) * pairs, step, 0)
    for source, store in enumerate(stores):
        lax.fori_loop(source * pairs, (source + 1) * pairs, step, 0)
        store.start()


def make_first_turns(table, box, node):
    def step(index, carry):
        radius = []
        for k in range(2):
            first, second = box(index // 4, 2 * (index % 4) + k)
            along = first + node[6:7, :]
            across = second + node[7:8, :]
            radius.append(0.5 * jnp.sqrt(along * along + across * across))
        cosine, sine = turn(jnp.concatenate(radius))
        for kind in range(2):
            base_cosine = node[16 + 2 * kind : 17 + 2 * kind, :]
            base_sine = node[17 + 2 * kind : 18 + 2 * kind, :]
            cosines = base_cosine * cosine
            sines = base_sine * sine
            mixed = base_sine * cosine
            other = base_cosine * sine
            line = 4 * index + kind
            mirror = 4 * index + 3 - kind
            if kind == 0:
                table[line, 0] = cosines - sines
                table[line, 1] = mixed + other
                table[mirror, 0] = cosines + sines
                table[mirror, 1] = other - mixed
            else:
                table[line, 0] = cosines + sines
                table[line, 1] = mixed - other
                table[mirror, 0] = cosines - sines
                table[mirror, 1] = -mixed - other
        return carry

    lax.fori_loop(0, 16, step, 0)


def level(
    read, table, first_line, highs, lows, matrix, children, rows, by_rows, ready, emit, matrix_ready=None
):
    sources = 4 if children == 4 else 2
    pairs = rows // 2
    columns = sources * BOX_NODES
    for half in range(2):
        high, low = highs[half], lows[half]
        if by_rows:
            chosen = list(range(children))
            near = list(range(half * pairs // 2, (half + 1) * pairs // 2))
        else:
            chosen = list(range(half * children // 2, (half + 1) * children // 2))
            near = list(range(pairs))
        height = 16 * len(near)
        for source in range(sources):
            lanes = slice(source * BOX_NODES, (source + 1) * BOX_NODES)
            if half == 0 and source < len(ready):
                ready[source].wait()
            for spot, pair in enumerate(near):
                group = source * rows + 2 * pair
                real, imaginary = (
                    jnp.concatenate([read(group, part), read(group + 1, part)])
                    for part in range(2)
                )
                for number, child in enumerate(chosen):
                    line = first_line + (source * pairs + pair) * children + child
                    cosine = table[line, 0]
                    sine = table[line, 1]
                    for part, value in enumerate(
                        (real * cosine - imaginary * sine, real * sine + imaginary * cosine)
                    ):
                        place = (number * 2 + part) * height + spot * 16
                        value_high, value_low = split(value)
                        high[place : place + 16, lanes] = value_high
                        low[place : place + 16, lanes] = value_low
        if half == 0 and matrix_ready is not None:
            matrix_ready.wait()
        both = jnp.dot(high[:, :columns], matrix[...], preferred_element_type=F32)
        rest = jnp.dot(low[:, :columns], matrix[:, :BOX_NODES], preferred_element_type=F32)
        result = both[:, :BOX_NODES] + (both[:, BOX_NODES:] + rest)
        for number, child in enumerate(chosen):
            for spot, pair in enumerate(near):
                for k in range(2):
                    start = number * 2 * height + spot * 16 + 8 * k
                    emit(
                        child,
                        2 * pair + k,
                        [result[start + height * part : start + height * part + 8] for part in range(2)],
                    )


def matrices():
    basis = second_basis()
    rows = [
        stacked_matrix(2, 2),
        stacked_matrix(1, 2),
        basis[:, :256],
        basis[:, 256:],
    ]
    return np.concatenate(two_parts(np.concatenate(rows)), axis=1)


def sub_bits():
    row = lax.broadcasted_iota(jnp.int32, (8, BOX_NODES), 0)
    return [bit(row, 2 - k).astype(F32) for k in range(3)]


def find_mask(slots, table, entries, high_hot, low_hot):
    iota = lax.broadcasted_iota(jnp.int32, (16, 128), 0).astype(F32)
    rows = [(iota + 16.0 * k).astype(BF16) for k in range(8)]
    one = jnp.ones((16, 128), BF16)
    zero = jnp.zeros((16, 128), BF16)
    block = jnp.concatenate([slots[:, :128], slots[:, 128:]], axis=0)
    entries[0] = (block >> 7).astype(F32)
    entries[1] = (block & 127).astype(F32)

    def step(index, carry):
        for source, hot in enumerate((high_hot, low_hot)):
            for side in range(2):
                start = pl.multiple_of(index * 8 + 64 * side, 8)
                block = entries[source, pl.ds(start, 8), :]
                for k in range(8):
                    value = jnp.broadcast_to(block[k : k + 1], (16, 128)).astype(BF16)
                    lanes = pl.ds(pl.multiple_of(index * 1024 + 128 * k, 128), 128)
                    for place in range(8):
                        line = 128 * side + 16 * place
                        hot[line : line + 16, lanes] = jnp.where(value == rows[place], one, zero)
        return carry

    lax.fori_loop(0, 8, step, 0)
    parts = [
        lax.dot_general(
            high_hot[:, 4096 * k : 4096 * (k + 1)],
            low_hot[:, 4096 * k : 4096 * (k + 1)],
            (((1,), (1,)), ((), ())),
            preferred_element_type=F32,
        )
        for k in range(2)
    ]
    total = parts[0] + parts[1]
    mask = jnp.where(total[:128, :128] + total[128:, 128:] > 0.5, 1.0, 0.0)
    for k in range(8):
        lanes = slice(128 * (k % 2), 128 * (k % 2 + 1))
        table[256 + k // 4, k // 2 % 2, :, lanes] = mask[16 * k : 16 * (k + 1)]


def store_level(table, table_far, leave, index, size=64, first=0):
    lines = pl.ds(size * index, size)
    place = leave.at[index if first == 0 else first + index % 4]
    return pltpu.make_async_copy(table.at[lines], table_far.at[lines], place)


def fetch_level(table_far, table, arrive, index, size=64):
    lines = pl.ds(64 * index, size)
    return pltpu.make_async_copy(table_far.at[lines], table.at[lines], arrive.at[index])


def fetch_mask_lines(table_far, table, place):
    lines = pl.ds(256, 2)
    return pltpu.make_async_copy(table_far.at[lines], table.at[lines], place)


def inner_turns_kernel(
    block_first_ref,
    block_second_ref,
    slots_far,
    node_far,
    speeds_far,
    table_far,
    slots,
    node,
    speeds,
    table,
    entries,
    high_hot,
    low_hot,
    arrive,
    leave,
):
    fetches = [
        pltpu.make_async_copy(far, near, arrive.at[k])
        for k, (far, near) in enumerate(
            ((slots_far, slots), (node_far, node), (speeds_far, speeds))
        )
    ]
    for fetch in fetches:
        fetch.start()
    fetches[0].wait()
    find_mask(slots, table, entries, high_hot, low_hot)
    for fetch in fetches[1:]:
        fetch.wait()
    stores = [store_level(table, table_far, leave, k) for k in range(3)]
    stores += [store_level(table, table_far, leave, 12 + k, 16, 3) for k in range(4)]
    store_mask = store_level(table, table_far, leave, 128, 2, 7)
    store_mask.start()
    sub = sub_bits()
    block_first = block_first_ref[0]
    block_second = block_second_ref[0]

    def box(source, row):
        first = block_first * 16 + bit(source, 1) + 2 * bit(row, 2)
        second = block_second * 16 + bit(source, 0) + 2 * bit(row, 1) + 8 * bit(row, 0)
        return (
            2.0 * first.astype(F32) + (8.0 * sub[0] + 16.0 * sub[2]),
            second.astype(F32) + 4.0 * sub[1],
        )

    make_first_turns(table, box, node)
    stores[0].start()

    def box(source, row):
        first = block_first * 8 + bit(source, 1)
        second = block_second * 8 + bit(source, 0) + 4 * bit(row, 0)
        return (
            2.0 * first.astype(F32) + (4.0 * sub[0] + 8.0 * sub[2]),
            second.astype(F32) + 2.0 * sub[1],
        )

    make_turns(table, 64, box, 2, speeds, 256, node, 0, 4, 8)
    stores[1].start()

    def box(source, row):
        first = block_first * 4 + bit(source, 1) + 2 * bit(row, 2)
        second = block_second * 4 + bit(source, 0) + 2 * bit(row, 1)
        return 2.0 * first.astype(F32), second.astype(F32)

    make_turns(table, 128, box, 3, speeds, 512, node, 0, 4, 8)
    stores[2].start()

    def box(source, row):
        first = block_first * 2 + bit(source, 1)
        second = block_second * 2 + bit(source, 0)
        return 2.0 * first.astype(F32), second.astype(F32)

    make_turns(table, 192, box, 4, speeds, 768, node, 0, 4, 8, stores[3:])
    for store in stores + [store_mask]:
        store.wait()


def outer_turns_kernel(node, speeds, table_far, table, leave):
    stores = [store_level(table, table_far, leave, k) for k in range(3)]
    stores += [store_level(table, table_far, leave, 12 + k, 16, 3) for k in range(3)]
    sub = sub_bits()

    def box(source, row):
        first = bit(source, 1) + 2 * bit(row, 2) + 4 * bit(row, 1)
        second = bit(source, 0) + 2 * bit(row, 0)
        return 2.0 * first.astype(F32), second.astype(F32) + (4.0 * sub[0] + 8.0 * sub[1])

    make_turns(table, 0, box, 5, speeds, 0, node, 0, 4, 8)
    stores[0].start()

    def box(source, row):
        first = bit(source, 1) + 2 * bit(row, 0)
        second = bit(source, 0)
        return 2.0 * first.astype(F32), second.astype(F32) + (2.0 * sub[0] + 4.0 * sub[1])

    make_turns(table, 64, box, 6, speeds, 256, node, 0, 4, 8)
    stores[1].start()

    def box(source, row):
        first = bit(source, 1)
        second = bit(source, 0) + 2 * bit(row, 1)
        return 2.0 * first.astype(F32), second.astype(F32)

    make_turns(table, 128, box, 7, speeds, 512, node, 0, 4, 8)
    stores[2].start()

    def box(source, row):
        return jnp.float32(0.0), source.astype(F32)

    make_turns(table, 192, box, 8, speeds, 768, node, 4, 2, 16, stores[3:5])

    def last(index, carry):
        def column(table):
            value = speeds[pl.ds(pl.multiple_of(256 * table + index * 16, 16), 16), :]
            return jnp.concatenate([value, value], axis=1)

        first = column(5)
        second = column(6)
        turns = first * node[8:9, :]
        turns = turns - ((turns + ROUNDER) - ROUNDER)
        across = second * node[10:11, :]
        across = across - ((across + ROUNDER) - ROUNDER)
        around = column(4) * node[12:13, :]
        around = around - ((around + ROUNDER) - ROUNDER)
        turns = turns + across + around + first * node[9:10, :] + second * node[11:12, :]
        cosine, sine = turn(turns)
        table[224 + index, 0] = cosine
        table[224 + index, 1] = sine
        return carry

    lax.fori_loop(0, 16, last, 0)
    stores[5].start()
    for store in stores:
        store.wait()


def deposit(
    arrived, table, second, fetch_second, state, wide, cells, hots, spreads, grid
):
    points = [float(value) for value in chebyshev_points(NODES).astype(np.float32)]
    factors = basis_factors()

    def source_step(index, carry):
        rows = pl.ds(pl.multiple_of(index * 16, 16), 16)
        first, second, real, imaginary = (
            arrived[pl.ds(index * 64 + k, 16, stride=4), :] for k in range(4)
        )
        whole_first = first.astype(jnp.int32)
        whole_second = second.astype(jnp.int32)
        along = first + 0.5
        across = second + 0.5
        eighths = jnp.bitwise_and(whole_first + whole_second + 1, 7).astype(F32)
        cosine, sine = turn(
            0.125 * eighths + 0.0625 * jnp.sqrt(along * along + across * across)
        )
        lanes = pl.ds(pl.multiple_of(index % 2 * 128, 128), 128)
        live = table[256 + index // 4, index // 2 % 2, :, lanes]
        real = real * live
        imaginary = imaginary * live
        turned = (real * cosine - imaginary * sine, real * sine + imaginary * cosine)
        place = jnp.bitwise_and(whole_first, 31).astype(F32) * 0.03125 + 0.015625
        cells[0, rows, :] = jnp.bitwise_and(whole_second, 15).astype(F32)
        x = [bit(whole_first, 5 + k) for k in range(4)]
        y = [bit(whole_second, 4 + k) for k in range(4)]
        cells[1, rows, :] = (x[0] * 8 + y[0] * 4 + x[1] * 2 + y[1]).astype(F32)
        cells[2, rows, :] = (y[3] * 8 + x[2] * 4 + y[2] * 2 + x[3]).astype(F32)
        away = [place - value for value in points]
        before = [None] * NODES
        after = [None] * NODES
        for p in range(1, NODES):
            before[p] = away[p - 1] if p == 1 else before[p - 1] * away[p - 1]
            q = NODES - 1 - p
            after[q] = away[q + 1] if p == 1 else after[q + 1] * away[q + 1]
        for p in range(NODES):
            if p == 0:
                value = after[0]
            elif p == NODES - 1:
                value = before[p]
            else:
                value = before[p] * after[p]
            value = value * factors[p]
            for part in range(2):
                wide[pl.ds(index * 512 + part * 16 + p, 16, stride=32), :] = value * turned[part]
        return carry

    lax.fori_loop(0, 8, source_step, 0)

    iota = lax.broadcasted_iota(jnp.int32, (16, 128), 0).astype(F32).astype(BF16)
    one = jnp.ones((16, 128), BF16)
    zero = jnp.zeros((16, 128), BF16)

    def build(chunk, hot, spread):
        for k in range(16):
            sender = chunk * 16 + k
            lanes = slice(128 * k, 128 * (k + 1))

            def row(number, height):
                value = cells[number, pl.ds(sender, 1), :]
                return jnp.broadcast_to(value, (height, 128)).astype(BF16)

            value = wide[pl.ds(pl.multiple_of(sender * 32, 32), 32), :].astype(BF16)
            cell = row(0, 16)
            for c in range(16):
                chosen = cell == jnp.full((16, 128), c, BF16)
                for part in range(2):
                    spread[32 * c + 16 * part : 32 * c + 16 * (part + 1), lanes] = jnp.where(
                        chosen, value[16 * part : 16 * (part + 1)], zero
                    )
            inside = jnp.where(row(2, 16) == iota, one, zero)
            above = row(1, 16)
            for c in range(16):
                hot[16 * c : 16 * (c + 1), lanes] = jnp.where(
                    above == jnp.full((16, 128), c, BF16), inside, zero
                )

    grid[...] = jnp.zeros_like(grid)

    def spread_step(index, carry):
        for k in range(2):
            build(2 * index + k, hots[k], spreads[k])
        grid[...] += lax.dot_general(
            jnp.concatenate([hots[0][...], hots[1][...]], axis=1),
            jnp.concatenate([spreads[0][...], spreads[1][...]], axis=1),
            (((1,), (1,)), ((), ())),
            preferred_element_type=F32,
        )
        return carry

    lax.fori_loop(0, 4, spread_step, 0)

    grid_high, grid_low = split(grid[...])
    fetch_second.wait()
    for part in range(2):
        basis = second[512 * part : 512 * (part + 1), :]
        result = jnp.dot(grid_high, basis, preferred_element_type=F32)
        rest = jnp.dot(grid_low, basis[:, :BOX_NODES], preferred_element_type=F32)
        result = result[:, :BOX_NODES] + (result[:, BOX_NODES:] + rest)
        for group in range(32):
            state[group, part] = result[8 * group : 8 * group + 8, :]


def halves(value):
    return value[:, :128], value[:, 128:]


def inner_kernel(
    arrived,
    table_far,
    matrix_far,
    out,
    second,
    matrix,
    table,
    arrive,
    wide,
    cells,
    hots,
    spreads,
    grid,
    other,
    turned,
    highs,
    lows,
    state,
):
    fetch_mask = fetch_mask_lines(table_far, table, arrive.at[6])
    fetch_mask.start()
    fetch_second = pltpu.make_async_copy(matrix_far.at[pl.ds(1536, 1024)], second, arrive.at[4])
    fetch_second.start()
    fetches = [fetch_level(table_far, table, arrive, k) for k in range(4)]
    for fetch in fetches:
        fetch.start()
    fetch_matrix = pltpu.make_async_copy(matrix_far.at[pl.ds(0, 1024)], matrix, arrive.at[5])
    fetch_matrix.start()
    fetch_mask.wait()
    deposit(arrived, table, second, fetch_second, state, wide, cells, hots, spreads, grid)

    def run(number, read, emit):
        level(
            read,
            table,
            64 * (number - 1),
            highs,
            lows,
            matrix,
            4,
            8,
            number % 2 == 0,
            fetches[number - 1 : number],
            emit,
            fetch_matrix if number == 1 else None,
        )

    def leaf(group, part):
        return state[group, part]

    def read(group, part):
        return other[group, part]

    def keep(child, row, values):
        for part in range(2):
            other[(row // 2) * 8 + child * 2 + row % 2, part] = values[part]

    run(1, leaf, keep)

    def turn_over(child, row, values):
        start = ((row % 2 * 2 + child // 2) * 8 + row // 2 * 2 + child % 2) * 8
        for part in range(2):
            for half, value in enumerate(halves(values[part])):
                turned[2 * part + half, start : start + 8, :] = value

    run(2, read, turn_over)

    def across(group, part):
        b2x, b2y, b3x, b3y, t2x = bits(group, 5)
        start = (b3y * 2 + t2x) * 64 + b2x * 4 + b2y * 2 + b3x
        return jnp.concatenate(
            [turned.at[2 * part + half][pl.ds(start, 8, stride=8), :] for half in range(2)], axis=1
        )

    run(3, across, keep)

    def send(child, row, values):
        x, y = bits(child, 2)
        r0, r1, r2 = bits(row, 3)
        device = r2 * 32 + r0 * 16 + x * 8 + r1
        for upper in range(2):
            for part in range(2):
                for half, value in enumerate(halves(values[part])):
                    start = (device + 64 * upper) * 8 + y * 4 + half * 2 + part
                    out[pl.ds(start, 4, stride=16), :] = value[4 * upper : 4 * upper + 4]

    run(4, read, send)


def outer_kernel(
    arrived, table_far, matrix_far, out, table, matrix, last, arrive, state, turned, highs, lows
):
    first = [
        pltpu.make_async_copy(
            table_far.at[pl.ds(16 * k, 16)], table.at[pl.ds(16 * k, 16)], arrive.at[6 + k]
        )
        for k in range(4)
    ]
    fetches = [
        fetch_level(table_far, table, arrive, k, 64 if k < 3 else 48) for k in range(1, 4)
    ]
    fetch_matrix = pltpu.make_async_copy(matrix_far.at[pl.ds(0, 1024)], matrix, arrive.at[5])
    fetch_last = pltpu.make_async_copy(matrix_far.at[pl.ds(1024, 512)], last, arrive.at[4])
    for fetch in first + [fetch_matrix] + fetches + [fetch_last]:
        fetch.start()

    def first_read(group, part):
        i2, j3, i1, i0, j2 = bits(group, 5)
        source = i2 * 64 + i1 * 32 + i0 * 16 + j3 * 8 + j2 * 4
        return jnp.concatenate(
            [
                arrived[pl.ds(source * 8 + half * 2 + part, 8, stride=4), :]
                for half in range(2)
            ],
            axis=1,
        )

    def run(number, read, emit):
        level(
            read,
            table,
            64 * (number - 5),
            highs,
            lows,
            matrix,
            4,
            8,
            number % 2 == 0,
            first if number == 5 else fetches[number - 6 : number - 5],
            emit,
            fetch_matrix if number == 5 else None,
        )

    def read(group, part):
        return state[group, part]

    def keep(child, row, values):
        i1, i0, j2 = bits(row, 3)
        for part in range(2):
            state[(2 * i1 + j2) * 8 + child * 2 + i0, part] = values[part]

    run(5, first_read, keep)

    def turn_over(child, row, values):
        start = ((row % 2 * 2 + child // 2) * 8 + row // 2 * 2 + child % 2) * 8
        for part in range(2):
            for half, value in enumerate(halves(values[part])):
                turned[2 * part + half, start : start + 8, :] = value

    run(6, read, turn_over)

    def across(group, part):
        i0, j1, t6x, j0, pair = bits(group, 5)
        start = (i0 * 2 + t6x) * 64 + j1 * 4 + j0 * 2 + pair
        return jnp.concatenate(
            [turned.at[2 * part + half][pl.ds(start, 8, stride=8), :] for half in range(2)], axis=1
        )

    def keep_last(child, row, values):
        t6x, j0, pair = bits(row, 3)
        for part in range(2):
            state[j0 * 16 + child * 4 + t6x * 2 + pair, part] = values[part]

    run(7, across, keep_last)

    def send(child, row, values):
        t7x, t7y, t6x, pair = bits(row, 4)
        line = 224 + child * 8 + row // 2
        cosine = table[line, 0, 8 * (row % 2) : 8 * (row % 2) + 8, :]
        sine = table[line, 1, 8 * (row % 2) : 8 * (row % 2) + 8, :]
        real, imaginary = values
        device = t6x * 32 + t7x * 16 + t7y * 2 + child
        for part, whole in enumerate(
            (real * cosine + imaginary * sine, imaginary * cosine - real * sine)
        ):
            for half, value in enumerate(halves(whole)):
                for upper in range(2):
                    place = (device + 64 * upper) * 8 + pair * 4 + half * 2 + part
                    out[pl.ds(place, 4, stride=32), :] = value[4 * upper : 4 * upper + 4]

    level(
        read, table, 192, highs, lows, last, 2, 16, True, fetches[2:], send, fetch_last
    )


def vmem(count):
    return [pl.BlockSpec(memory_space=pltpu.VMEM)] * count


def smem(count):
    return [pl.BlockSpec(memory_space=pltpu.SMEM)] * count


def far(count):
    return [pl.BlockSpec(memory_space=pltpu.HBM)] * count


def payload_kernel(place_far, amp_far, out_far, place, amp, out, arrive, leave):
    part = DEVICES // 2
    fetches = [
        pltpu.make_async_copy(
            far_ref.at[:, pl.ds(part * half, part)],
            near_ref.at[:, pl.ds(part * half, part)],
            arrive.at[2 * half + k],
        )
        for half in range(2)
        for k, (far_ref, near_ref) in enumerate(((place_far, place), (amp_far, amp)))
    ]
    for fetch in fetches:
        fetch.start()
    stores = []
    for half in range(2):
        for fetch in fetches[2 * half : 2 * half + 2]:
            fetch.wait()
        chosen = slice(part * half, part * (half + 1))
        for k in range(2):
            start = 4 * part * half + k
            out[pl.ds(start, part, stride=4), :] = place[k, chosen].astype(F32)
            out[pl.ds(start + 2, part, stride=4), :] = amp[k, chosen]
        rows = pl.ds(4 * part * half, 4 * part)
        stores.append(pltpu.make_async_copy(out.at[rows], out_far.at[rows], leave.at[half]))
        stores[half].start()
    for store in stores:
        store.wait()


def make_payload(place, amp):
    return pl.pallas_call(
        payload_kernel,
        out_shape=jax.ShapeDtypeStruct((4 * DEVICES, 128), F32),
        in_specs=far(2),
        out_specs=far(1)[0],
        scratch_shapes=[
            pltpu.VMEM((2, DEVICES, 128), jnp.int32),
            pltpu.VMEM((2, DEVICES, 128), F32),
            pltpu.VMEM((4 * DEVICES, 128), F32),
            pltpu.SemaphoreType.DMA((4,)),
            pltpu.SemaphoreType.DMA((2,)),
        ],
        name="payload",
        compiler_params=pltpu.CompilerParams(vmem_limit_bytes=60 << 20),
    )(place, amp)


def result_kernel(weights, out, leave):
    stores = [
        pltpu.make_async_copy(
            weights.at[:, :, half],
            out.at[:, 0, :, 0, :, pl.ds(128 * half, 128)],
            leave.at[half],
        )
        for half in range(2)
    ]
    for store in stores:
        store.start()
    for store in stores:
        store.wait()


def place_result(weights):
    return pl.pallas_call(
        result_kernel,
        out_shape=jax.ShapeDtypeStruct((LEAVES, 1, LEAVES, 1, 2, BOX_NODES), F32),
        in_specs=vmem(1),
        out_specs=far(1)[0],
        scratch_shapes=[pltpu.SemaphoreType.DMA((2,))],
        name="result",
        compiler_params=pltpu.CompilerParams(vmem_limit_bytes=16 << 20),
    )(weights)


def inner_turns(block_first, block_second, slots):
    speeds = np.repeat(inner_speeds()[:, None], 128, axis=1)
    return pl.pallas_call(
        inner_turns_kernel,
        out_shape=jax.ShapeDtypeStruct((258, 2, 16, 256), F32),
        in_specs=smem(2) + far(3),
        out_specs=far(1)[0],
        scratch_shapes=[
            pltpu.VMEM((64, 256), jnp.int32),
            pltpu.VMEM((24, 256), F32),
            pltpu.VMEM((1024, 128), F32),
            pltpu.VMEM((258, 2, 16, 256), F32),
            pltpu.VMEM((2, 128, 128), F32),
            pltpu.VMEM((256, 8192), BF16),
            pltpu.VMEM((256, 8192), BF16),
            pltpu.SemaphoreType.DMA((3,)),
            pltpu.SemaphoreType.DMA((8,)),
        ],
        name="inner_turns",
        compiler_params=pltpu.CompilerParams(vmem_limit_bytes=60 << 20),
    )(block_first, block_second, slots, jnp.asarray(node_tables()), jnp.asarray(speeds))


def outer_turns(speeds):
    return pl.pallas_call(
        outer_turns_kernel,
        out_shape=jax.ShapeDtypeStruct((240, 2, 16, 256), F32),
        in_specs=vmem(2),
        out_specs=far(1)[0],
        scratch_shapes=[
            pltpu.VMEM((240, 2, 16, 256), F32),
            pltpu.SemaphoreType.DMA((7,)),
        ],
        name="outer_turns",
        compiler_params=pltpu.CompilerParams(vmem_limit_bytes=52 << 20),
    )(jnp.asarray(node_tables()), speeds)


LEVEL_SCRATCH = [
    pltpu.VMEM((32, 2, 8, 256), F32),
    pltpu.VMEM((4, 256, 128), F32),
    [pltpu.VMEM((256, 1024), BF16)] * 2,
    [pltpu.VMEM((256, 1024), BF16)] * 2,
]


def inner_levels(arrived, table):
    return pl.pallas_call(
        inner_kernel,
        out_shape=jax.ShapeDtypeStruct((1024, 128), F32),
        in_specs=vmem(1) + far(2),
        out_specs=vmem(1)[0],
        scratch_shapes=[
            pltpu.VMEM((1024, 512), BF16),
            pltpu.VMEM((1024, 512), BF16),
            pltpu.VMEM((258, 2, 16, 256), F32),
            pltpu.SemaphoreType.DMA((7,)),
            pltpu.VMEM((4096, 128), F32),
            pltpu.VMEM((3, 128, 128), F32),
            [pltpu.VMEM((256, 2048), BF16)] * 2,
            [pltpu.VMEM((512, 2048), BF16)] * 2,
            pltpu.VMEM((256, 512), F32),
        ]
        + LEVEL_SCRATCH
        + LEVEL_SCRATCH[:1],
        name="inner",
        compiler_params=pltpu.CompilerParams(vmem_limit_bytes=52 << 20),
    )(
        arrived,
        table,
        jnp.asarray(matrices()),
    )


def outer_levels(arrived, table):
    return pl.pallas_call(
        outer_kernel,
        out_shape=jax.ShapeDtypeStruct((1024, 128), F32),
        in_specs=vmem(1) + far(2),
        out_specs=vmem(1)[0],
        scratch_shapes=[
            pltpu.VMEM((240, 2, 16, 256), F32),
            pltpu.VMEM((1024, 512), BF16),
            pltpu.VMEM((512, 512), BF16),
            pltpu.SemaphoreType.DMA((10,)),
        ]
        + LEVEL_SCRATCH,
        name="outer",
        compiler_params=pltpu.CompilerParams(vmem_limit_bytes=52 << 20),
    )(
        arrived,
        table,
        jnp.asarray(matrices()),
    )


def reverse_bits(number, bit_count):
    result = jnp.zeros_like(number)
    for position in range(bit_count):
        result = result + jnp.left_shift(
            jnp.bitwise_and(jnp.right_shift(number, position), 1), bit_count - 1 - position
        )
    return result


def exchange(array):
    return lax.all_to_all(array, ("bx", "by"), split_axis=0, concat_axis=0, tiled=True)


def shards(src_pos, src_amp, box_slots):
    column = lax.axis_index("bx")
    row = lax.axis_index("by")
    device = column * BY + row
    block_first = reverse_bits(column, 3).astype(jnp.int32).reshape(1)
    block_second = reverse_bits(row, 4).astype(jnp.int32).reshape(1)
    payload = make_payload(src_pos.reshape(2, DEVICES, 128), src_amp.reshape(2, DEVICES, 128))
    arrived = exchange(payload.reshape(DEVICES, 4, 128)).reshape(512, 128)
    table = inner_turns(block_first, block_second, box_slots[0].T)
    arrived, table = lax.optimization_barrier((arrived, table))
    weights = inner_levels(arrived, table)
    weights = exchange(weights.reshape(DEVICES, 8, 128)).reshape(1024, 128)
    speeds = lax.dynamic_index_in_dim(jnp.asarray(outer_speeds()), device, 0, keepdims=False)
    speeds = jnp.broadcast_to(speeds[:, None], (7 * 256, 128))
    weights = outer_levels(weights, outer_turns(speeds))
    weights = exchange(weights.reshape(DEVICES, 8, 128))
    return place_result(weights.reshape(LEAVES, LEAVES, 2, 2, 128))


def solution(mesh):
    return jax.shard_map(
        shards,
        mesh=mesh,
        in_specs=(
            P(None, ("bx", "by"), None),
            P(None, ("bx", "by"), None),
            P(("bx", "by"), None, None),
        ),
        out_specs=P(None, "bx", None, "by", None, None),
        check_vma=False,
    )
```
